128 devices in a mesh: blk: 16 (over z, x_lo, core), head: 8 (over y, x_hi).
Axes of the slice: x: 4 (x_hi: 2, x_lo: 2; x = x_hi * 2 + x_lo), y: 4, z: 4, core: 2. Of those that a mesh axis runs over, the one named last changes fastest.
Arguments:
- inputs: bfloat16 [2, 8192, 1280], P(None, ('blk', 'head')), may hold values from -6 to 6
- segment_ids: int32 [2, 8192], replicated, may hold values from 0 to 8, as said below
- norm1_gain: bfloat16 [1280], P(('blk', 'head')), may hold values from 0.099609375 to 1.8984375
- w_query: bfloat16 [1280, 1280], P(('blk', 'head')), may hold values from -0.15625 to 0.15625
- w_key: bfloat16 [1280, 1280], P(('blk', 'head')), may hold values from -0.15625 to 0.15625
- w_value: bfloat16 [1280, 1280], P(('blk', 'head')), may hold values from -0.15625 to 0.15625
- query_bias: bfloat16 [1280], P(('blk', 'head')), may hold values from -3 to 3
- value_bias: bfloat16 [1280], P(('blk', 'head')), may hold values from -3 to 3
- w_out: bfloat16 [1280, 1280], P(('blk', 'head')), may hold values from -1.25 to 1.25
- out_bias: bfloat16 [1280], P(('blk', 'head')), may hold values from -3 to 3
- norm2_gain: bfloat16 [1280], P(('blk', 'head')), may hold values from 0.099609375 to 1.8984375
- w_hidden: bfloat16 [1280, 1280], P(('blk', 'head')), may hold values from -0.15625 to 0.15625
- hidden_bias: bfloat16 [1280], P(('blk', 'head')), may hold values from -3 to 3
- w_proj: bfloat16 [1280, 1280], P(('blk', 'head')), may hold values from -0.15625 to 0.15625
- proj_bias: bfloat16 [1280], P(('blk', 'head')), may hold values from -3 to 3
- dim_scale: float32 [80], replicated, may hold values from -1 to 1
- cotangent: bfloat16 [2, 8192, 1280], P(None, ('blk', 'head')), may hold values from -6 to 6
Outputs:
- layer_out: bfloat16 [2, 8192, 1280], P(None, ('blk', 'head'))
- input_grad: bfloat16 [2, 8192, 1280], P(None, ('blk', 'head'))
- norm1_gain_grad: float32 [1280], P(('blk', 'head'))
- w_query_grad: float32 [1280, 1280], P(('blk', 'head'))
- w_key_grad: float32 [1280, 1280], P(('blk', 'head'))
- w_value_grad: float32 [1280, 1280], P(('blk', 'head'))
- query_bias_grad: float32 [1280], P(('blk', 'head'))
- value_bias_grad: float32 [1280], P(('blk', 'head'))
- w_out_grad: float32 [1280, 1280], P(('blk', 'head'))
- out_bias_grad: float32 [1280], P(('blk', 'head'))
- norm2_gain_grad: float32 [1280], P(('blk', 'head'))
- w_hidden_grad: float32 [1280, 1280], P(('blk', 'head'))
- hidden_bias_grad: float32 [1280], P(('blk', 'head'))
- w_proj_grad: float32 [1280, 1280], P(('blk', 'head'))
- proj_bias_grad: float32 [1280], P(('blk', 'head'))
- dim_scale_grad: float32 [80], replicated
The draws below stay inside these ranges and needn't reach their ends.
Inputs may be any that keep to these rules, and one draw needn't show every extreme that they name: `segment_ids`: ids never fall along a sequence. In each micro-batch one document starts before position 512 and ends at or after position 7680; the others are short and lie at the two ends.
All inputs are finite; a program needn't handle non-finite values.
Results may differ from the reference program's by a relative error of at most 0.024.
Values may be sent and summed in bfloat16 or wider, within the bound.
A program may use at most 256 MiB of HBM per device.

```python
import math
import jax
import jax.numpy as jnp
from jax import lax

D = 1280
H = 16
HD = 80
FF = 1280
MICRO = 2
SEQ = 8192
QBLK = 512


def draw_segment_ids(key, part):
    key = jax.random.fold_in(key, 11)
    head_cuts = jax.random.randint(jax.random.fold_in(key, 1), (MICRO, 4), 1, QBLK)
    tail_cuts = jax.random.randint(jax.random.fold_in(key, 2), (MICRO, 4), SEQ - QBLK + 1, SEQ)
    positions = jnp.arange(SEQ, dtype=jnp.int32)
    before = jnp.sum((positions[None, :, None] >= head_cuts[:, None, :]).astype(jnp.int32), axis=-1)
    after = jnp.sum((positions[None, :, None] >= tail_cuts[:, None, :]).astype(jnp.int32), axis=-1)
    return (before + after).astype(jnp.int32)


def levels(rng, shape, split, low, top_value):
    def one(axis_at, shards_of):
        heights = jax.random.uniform(jax.random.fold_in(jax.random.fold_in(rng, 6), axis_at), (shards_of,), jnp.float32, low / len(split), top_value / len(split))
        return jnp.repeat(jnp.exp(heights), shape[axis_at] // shards_of).reshape((-1,) + (1,) * (len(shape) - axis_at - 1))

    factor_of = one(*split[0])
    for cut in split[1:]:
        factor_of = factor_of * one(*cut)
    return factor_of


def noise(rng, shape, spread, limit, shards=(), kind=jnp.bfloat16):
    factor_of = levels(rng, shape, shards, -0.22, 0.18) if shards else 1.0
    result = jax.random.normal(rng, shape, jnp.float32) * spread * factor_of
    return jnp.minimum(jnp.maximum(result, -limit), limit).astype(kind)


def setup_inputs(seed: int = 0) -> dict:
    arg_keys = jax.random.split(jax.random.key(seed), 18)
    inputs = noise(arg_keys[0], (MICRO, SEQ, D), 1.0, 6.0, ((1, 128),))
    segment_ids = draw_segment_ids(jax.random.fold_in(arg_keys[17], 71), 0)
    norm1_gain = jnp.clip(1.0 + 0.18 * jax.random.normal(arg_keys[2], (D,), jnp.float32), 0.099609375, 1.8984375).astype(jnp.bfloat16)
    w_query = noise(arg_keys[3], (D, D), D ** -0.5, 0.15625, ((0, 128),))
    w_key = noise(arg_keys[4], (D, D), D ** -0.5, 0.15625, ((0, 128),))
    w_value = noise(arg_keys[5], (D, D), D ** -0.5, 0.15625, ((0, 128),))
    query_bias = noise(arg_keys[6], (D,), 0.5, 3.0, ((0, 128),))
    value_bias = noise(arg_keys[7], (D,), 0.5, 3.0, ((0, 128),))
    w_out = noise(arg_keys[8], (D, D), (D // 64) ** -0.5, 1.25, ((0, 128),))
    out_bias = noise(arg_keys[9], (D,), 0.5, 3.0, ((0, 128),))
    norm2_gain = jnp.clip(1.0 + 0.18 * jax.random.normal(arg_keys[10], (D,), jnp.float32), 0.099609375, 1.8984375).astype(jnp.bfloat16)
    w_hidden = noise(arg_keys[11], (D, FF), D ** -0.5, 0.15625, ((0, 128),))
    hidden_bias = noise(arg_keys[12], (FF,), 0.5, 3.0, ((0, 128),))
    w_proj = noise(arg_keys[13], (FF, D), FF ** -0.5, 0.15625, ((0, 128),))
    proj_bias = noise(arg_keys[14], (D,), 0.5, 3.0, ((0, 128),))
    dim_scale = jnp.clip(jax.random.uniform(arg_keys[15], (HD,), jnp.float32, -1.0, 1.0), -1.0, 1.0)
    cotangent = noise(arg_keys[16], (MICRO, SEQ, D), 1.0, 6.0, ((1, 128),))
    return {"inputs": inputs, "segment_ids": segment_ids, "norm1_gain": norm1_gain, "w_query": w_query, "w_key": w_key, "w_value": w_value, "query_bias": query_bias, "value_bias": value_bias, "w_out": w_out, "out_bias": out_bias, "norm2_gain": norm2_gain, "w_hidden": w_hidden, "hidden_bias": hidden_bias, "w_proj": w_proj, "proj_bias": proj_bias, "dim_scale": dim_scale, "cotangent": cotangent}


HIGHEST = lax.Precision.HIGHEST

@jax.custom_vjp
def low(v):
    return lax.optimization_barrier(v.astype(jnp.bfloat16)).astype(jnp.float32)

@jax.custom_vjp
def low_back(v):
    return v

def low_keep(v):
    return (low(v), None)

def low_pass(kept, grad):
    return (grad,)

def back_keep(v):
    return (v, None)

def back_low(kept, grad):
    return (low(grad),)
low.defvjp(low_keep, low_pass)
low_back.defvjp(back_keep, back_low)

def inverse_rms(values):
    return lax.rsqrt(lax.optimization_barrier(jnp.mean(values * values, axis=-1, keepdims=True)) + 1e-06)

def matmul(left_side, right_side):
    return jnp.dot(left_side, right_side, precision=HIGHEST)

def attention(scaled, key_proj, value_proj, segment_row):
    row_block = min(512, SEQ)
    key_positions = jnp.arange(SEQ, dtype=jnp.int32)

    def one_block(block_number):
        start_row = (block_number * row_block).astype(jnp.int32)
        queries = lax.dynamic_slice_in_dim(scaled, start_row, row_block, 0)
        row_segments = lax.dynamic_slice_in_dim(segment_row, start_row, row_block, 0)
        row_positions = start_row + jnp.arange(row_block, dtype=jnp.int32)
        scores = low_back(jnp.einsum('qhd,khd->hqk', queries, key_proj, precision=HIGHEST))
        allowed = (row_segments[:, None] == segment_row[None, :]) & (key_positions[None, :] <= row_positions[:, None])
        masked = jnp.where(allowed[None], scores, -1e+30)
        row_top = lax.optimization_barrier(jnp.max(masked, axis=-1, keepdims=True))
        weights = jnp.where(allowed[None], jnp.exp(masked - row_top), 0.0)
        probabilities = weights / lax.optimization_barrier(jnp.sum(weights, axis=-1, keepdims=True))
        return jnp.einsum('hqk,khd->qhd', low(probabilities), value_proj, precision=HIGHEST)
    blocks = lax.map(jax.checkpoint(one_block), jnp.arange(SEQ // row_block, dtype=jnp.int32))
    return blocks.reshape(SEQ, H * HD)

def layer_forward(tokens_all, norm1_gain, w_query, w_key, w_value, query_bias, value_bias, w_out, out_bias, norm2_gain, w_hidden, hidden_bias, w_proj, proj_bias, dim_scale, segment_ids):
    softplus_scale = 1.442695041 / math.sqrt(HD) * jax.nn.softplus(dim_scale)
    results = []
    for batch_index in range(MICRO):
        tokens = tokens_all[batch_index]
        normed = low(tokens * inverse_rms(tokens) * norm1_gain)
        query_full = low_back(matmul(normed, w_query) + query_bias)
        scaled = low(low_back(query_full.reshape(SEQ, H, HD) * softplus_scale))
        key_proj = low(low_back(matmul(normed, w_key))).reshape(SEQ, H, HD)
        value_proj = low(low_back(matmul(normed, w_value) + value_bias)).reshape(SEQ, H, HD)
        attended = low(low_back(attention(scaled, key_proj, value_proj, segment_ids[batch_index])))
        branch = low_back(matmul(attended, w_out) + out_bias)
        residual = tokens + branch
        normed_two = low(residual * inverse_rms(residual) * norm2_gain)
        pre_act = low_back(matmul(normed_two, w_hidden) + hidden_bias)
        activated = low(jax.nn.silu(pre_act))
        results.append(residual + matmul(activated, w_proj) + proj_bias)
    return jnp.stack(results)

def reference(inputs, segment_ids, norm1_gain, w_query, w_key, w_value, query_bias, value_bias, w_out, out_bias, norm2_gain, w_hidden, hidden_bias, w_proj, proj_bias, dim_scale, cotangent):
    initials = (inputs, norm1_gain, w_query, w_key, w_value, query_bias, value_bias, w_out, out_bias, norm2_gain, w_hidden, hidden_bias, w_proj, proj_bias, dim_scale)
    floats = tuple((entry_item.astype(jnp.float32) for entry_item in initials))

    def forward(*arrays):
        return layer_forward(*arrays, segment_ids)
    layer_out, pullback = jax.vjp(forward, *floats)
    gradients = pullback(cotangent.astype(jnp.float32))
    return (layer_out.astype(jnp.bfloat16), gradients[0].astype(jnp.bfloat16), gradients[1], gradients[2], gradients[3], gradients[4], gradients[5], gradients[6], gradients[7], gradients[8], gradients[9], gradients[10], gradients[11], gradients[12], gradients[13], gradients[14])
```

```python
import functools
import math

import jax
import jax.numpy as jnp
from jax import lax
from jax.experimental import pallas as pl
from jax.experimental.pallas import tpu as pltpu
from jax.sharding import PartitionSpec as P

D = 1280
H = 16
HD = 80
FF = 1280
B = 512
TOK = 64
PAIRS = 32
LANES = 256
ROWS = 64
EPSILON = 1e-06
LOG2E = 1.442695041
NEGATIVE = -1e30
MESH = pl.DeviceIdType.MESH
f32 = jnp.float32
bf16 = jnp.bfloat16

PARTS = (((0, 512), "xyz"), ((512, 384), "yzx"), ((896, 384), "zxy"))


def inverse_rms(values):
    return lax.rsqrt(jnp.mean(values * values, axis=-1, keepdims=True) + EPSILON)


def norm_back(upstream, values, inverse):
    return inverse * upstream - values * inverse**3 * jnp.mean(
        upstream * values, axis=-1, keepdims=True
    )


def nn(a, b):
    return lax.dot_general(a, b, (((1,), (0,)), ((), ())), preferred_element_type=f32)


def nt(a, b):
    return lax.dot_general(a, b, (((1,), (1,)), ((), ())), preferred_element_type=f32)


def tn(a, b):
    return lax.dot_general(a, b, (((0,), (0,)), ((), ())), preferred_element_type=f32)


def my_place():
    blk = lax.axis_index("blk")
    head = lax.axis_index("head")
    return {
        "x": (head % 2) * 2 + (blk // 2) % 2,
        "y": head // 2,
        "z": blk // 4,
        "c": blk % 2,
    }


def device_at(place):
    x, y, z, c = place["x"], place["y"], place["z"], place["c"]
    return (z * 4 + (x % 2) * 2 + c, y * 2 + x // 2)


def linear_at(place):
    blk, head = device_at(place)
    return blk * 8 + head


def moved(place, axis, value):
    other = dict(place)
    other[axis] = value
    return other


def greet(peers):
    barrier = pltpu.get_barrier_semaphore()
    for peer in peers:
        pl.semaphore_signal(barrier, inc=1, device_id=peer, device_id_type=MESH)
    pl.semaphore_wait(barrier, len(peers))


def greet_all():
    barrier = pltpu.get_barrier_semaphore()
    me = lax.axis_index("blk") * 8 + lax.axis_index("head")

    @pl.loop(1, 128)
    def _(k):
        other = (me + k) % 128
        pl.semaphore_signal(
            barrier, inc=1, device_id=(other // 8, other % 8), device_id_type=MESH
        )

    pl.semaphore_wait(barrier, 127)


def ring_peers(place):
    peers = [device_at(moved(place, "c", 1 - place["c"]))]
    for axis in "xyz":
        for step in (1, 3, 2):
            peers.append(device_at(moved(place, axis, (place[axis] + step) % 4)))
    return peers


def wait_bytes(ref, sem):
    pltpu.make_async_copy(ref, ref, sem).wait()


def remote(src, dst, send, recv, device):
    return pltpu.make_async_remote_copy(
        src_ref=src, dst_ref=dst, send_sem=send, recv_sem=recv, device_id=device, device_id_type=MESH
    )


def varied(place, axes, number):
    other = dict(place)
    for axis in axes:
        other[axis] = number % 4
        number = number // 4
    return other


def gather_kernel(pack, out, send, recv, own_sem):
    place = my_place()
    me = linear_at(place)
    own = pltpu.make_async_copy(pack, out.at[me], own_sem)
    own.start()
    greet(ring_peers(place))
    own.wait()
    for stage in range(3):
        count = 4**stage
        for part, ((first, width), order) in enumerate(PARTS):
            cols = pl.ds(first, width)
            if stage:
                wait_bytes(
                    out.at[pl.ds(0, 3 * count // 4), :, cols], recv.at[part, stage - 1]
                )

            @pl.loop(0, count)
            def _(number, part=part, cols=cols, order=order, stage=stage):
                chunk = linear_at(varied(place, order[:stage], number))
                axis = order[stage]
                for step in (1, 3, 2):
                    target = moved(place, axis, (place[axis] + step) % 4)
                    remote(
                        out.at[chunk, :, cols],
                        out.at[chunk, :, cols],
                        send.at[part, stage],
                        recv.at[part, stage],
                        device_at(target),
                    ).start()

    for part, ((first, width), order) in enumerate(PARTS):
        wait_bytes(out.at[pl.ds(0, 48), :, pl.ds(first, width)], recv.at[part, 2])
    sibling = device_at(moved(place, "c", 1 - place["c"]))

    @pl.loop(0, 8)
    def _(number):
        rows = pl.ds(number * 16 + place["c"] * 8, 8)
        remote(out.at[rows], out.at[rows], send.at[3, 0], recv.at[3, 0], sibling).start()

    wait_bytes(out.at[pl.ds(0, 64)], recv.at[3, 0])
    wait_bytes(out.at[pl.ds(0, 64)], send.at[3, 0])
    for stage in range(3):
        for part, ((first, width), order) in enumerate(PARTS):
            wait_bytes(
                out.at[pl.ds(0, 3 * 4**stage), :, pl.ds(first, width)], send.at[part, stage]
            )


def gather_weights(pack):
    return pl.pallas_call(
        gather_kernel,
        out_shape=jax.ShapeDtypeStruct((128, ROWS, D), bf16),
        in_specs=[pl.BlockSpec(memory_space=pl.ANY)],
        out_specs=pl.BlockSpec(memory_space=pl.ANY),
        scratch_shapes=[
            pltpu.SemaphoreType.DMA((4, 3)),
            pltpu.SemaphoreType.DMA((4, 3)),
            pltpu.SemaphoreType.DMA,
        ],
        compiler_params=pltpu.CompilerParams(
            collective_id=0, has_side_effects=True, vmem_limit_bytes=32 * 2**20
        ),
        name="gather_weights",
    )(pack)


def scatter_kernel(
    grads, out, mine, pair, land_one, land_two, land_three, half_one, half_two, send, recv, own_sem
):
    place = my_place()
    sibling = device_at(moved(place, "c", 1 - place["c"]))
    loads = []
    for number in range(8):
        rows = pl.ds(number * 16 + place["c"] * 8, 8)
        loads.append(
            pltpu.make_async_copy(grads.at[rows], mine.at[pl.ds(number * 8, 8)], own_sem.at[number])
        )
        loads[-1].start()
    greet(ring_peers(place))
    sends = []
    for number in range(8):
        rows = pl.ds(number * 16 + (1 - place["c"]) * 8, 8)
        sends.append(
            remote(
                grads.at[rows],
                pair.at[pl.ds(number * 8, 8)],
                send.at[3, number],
                recv.at[3, number],
                sibling,
            )
        )
        sends[-1].start()
    for number in range(8):
        loads[number].wait()
        sends[number].wait()

        @pl.loop(0, 8)
        def _(inner, number=number):
            at = number * 8 + inner
            mine[at] = (mine[at].astype(f32) + pair[at].astype(f32)).astype(bf16)

    def slot(where):
        return (where["z"] * 2 + where["x"] % 2) * 8 + where["y"] * 2 + where["x"] // 2

    lands = (land_one, land_two, land_three)
    for stage in range(3):
        count = 16 // 4**stage
        for part, ((first, width), order) in enumerate(PARTS):
            cols = pl.ds(first, width)
            axis = order[2 - stage]
            rest = order[: 2 - stage]

            @pl.loop(0, count)
            def _(number, part=part, cols=cols, axis=axis, rest=rest, stage=stage):
                for step in (1, 3, 2):
                    target = moved(place, axis, (place[axis] + step) % 4)
                    if stage == 0:
                        source = mine.at[slot(varied(target, rest, number)), :, cols]
                    elif stage == 1:
                        source = half_one.at[target[axis], number, :, cols]
                    else:
                        source = half_two.at[target[axis], :, cols]
                    remote(
                        source,
                        lands[stage].at[step - 1, number, :, cols],
                        send.at[part, stage],
                        recv.at[part, stage],
                        device_at(target),
                    ).start()

        for part, ((first, width), order) in enumerate(PARTS):
            cols = pl.ds(first, width)
            axis = order[2 - stage]
            rest = order[: 2 - stage]
            wait_bytes(lands[stage].at[:, :, :, cols], recv.at[part, stage])

            @pl.loop(0, count)
            def _(number, cols=cols, axis=axis, rest=rest, stage=stage):
                if stage == 0:
                    total = mine[slot(varied(place, rest, number)), :, cols].astype(f32)
                elif stage == 1:
                    total = half_one[place[axis], number, :, cols].astype(f32)
                else:
                    total = half_two[place[axis], :, cols].astype(f32)
                for source in range(3):
                    total = total + lands[stage][source, number, :, cols].astype(f32)
                if stage == 0:
                    half_one[number // 4, number % 4, :, cols] = total.astype(bf16)
                elif stage == 1:
                    half_two[number, :, cols] = total.astype(bf16)
                else:
                    out[:, cols] = total

    for stage in range(3):
        for part, ((first, width), order) in enumerate(PARTS):
            wait_bytes(lands[stage].at[:, :, :, pl.ds(first, width)], send.at[part, stage])


def scatter_grads(grads):
    return pl.pallas_call(
        scatter_kernel,
        out_shape=jax.ShapeDtypeStruct((ROWS, D), f32),
        in_specs=[pl.BlockSpec(memory_space=pl.ANY)],
        out_specs=pl.BlockSpec(memory_space=pltpu.VMEM),
        scratch_shapes=[
            pltpu.VMEM((64, ROWS, D), bf16),
            pltpu.VMEM((64, ROWS, D), bf16),
            pltpu.VMEM((3, 16, ROWS, D), bf16),
            pltpu.VMEM((3, 4, ROWS, D), bf16),
            pltpu.VMEM((3, 1, ROWS, D), bf16),
            pltpu.VMEM((4, 4, ROWS, D), bf16),
            pltpu.VMEM((4, ROWS, D), bf16),
            pltpu.SemaphoreType.DMA((4, 8)),
            pltpu.SemaphoreType.DMA((4, 8)),
            pltpu.SemaphoreType.DMA((8,)),
        ],
        compiler_params=pltpu.CompilerParams(
            collective_id=3, has_side_effects=True, vmem_limit_bytes=56 * 2**20
        ),
        name="scatter_grads",
    )(grads)


def quarter_of(blk):
    inner = blk % 4
    return jnp.where((blk // 4) % 2 == 0, inner, 3 - inner)


def query_block(quarter, j):
    return j * 4 + (quarter if j % 2 == 0 else 3 - quarter)


def core_block(core, number):
    z = number // 2
    return z * 4 + (core + z) % 2 + 2 * (number % 2)


def mask_of(key_block, block, start):
    key_at = key_block * B + lax.broadcasted_iota(jnp.int32, (B, B), 0)
    query_at = block * B + lax.broadcasted_iota(jnp.int32, (B, B), 1)
    return (key_at >= start) & (key_at <= query_at)


def over_keys(block, step, state):
    state = step(0, state, True)

    def middle(masked):
        return lambda s: lax.fori_loop(1, block, lambda k, t: step(k, t, masked), s)

    state = lax.cond(block == 15, middle(True), middle(False), state)
    return lax.cond(block > 0, lambda s: step(block, s, True), lambda s: s, state)


def shift_matrix(rows, cols, by):
    row = lax.broadcasted_iota(jnp.int32, (rows, cols), 0)
    col = lax.broadcasted_iota(jnp.int32, (rows, cols), 1)
    return jnp.where((row - col == by) & (jnp.minimum(row, col) < HD), 1.0, 0.0).astype(bf16)


def forward_block(j, block, kv, value_t, queries, starts, out_t, log_norms):
    q = queries[j]
    start = starts[j]

    def step(key_block, state, masked):
        top, total, acc = state
        s = nt(kv[key_block, :, :128], q)
        if masked:
            s = jnp.where(mask_of(key_block, block, start), s, NEGATIVE)
        new_top = jnp.maximum(top, jnp.max(s, axis=0, keepdims=True))
        p = jnp.exp(s - new_top)
        scale = jnp.exp(top - new_top)
        total = total * scale + jnp.sum(p, axis=0, keepdims=True)
        return (new_top, total, acc * scale + nn(value_t[key_block], p.astype(bf16)))

    state = (
        jnp.full((1, B), NEGATIVE, f32),
        jnp.zeros((1, B), f32),
        jnp.zeros((128, B), f32),
    )
    top, total, acc = over_keys(block, step, state)
    result = acc / acc[112:113]
    out_t[j] = result
    log_norms[j] = top + jnp.log(total)
    return result


def forward_kernel(
    pack,
    starts,
    kv_out,
    queries,
    out_t,
    log_norms,
    attended,
    kv,
    value_t,
    rounded,
    landed,
    send,
    recv,
    core_send,
    core_recv,
    back_send,
    back_recv,
    kv_sem,
):
    blk = lax.axis_index("blk")
    head = lax.axis_index("head")
    core = blk % 2
    quarter = blk % 4
    pair = (blk // 4) * 8 + head
    to_quarter = quarter_of(blk)
    even = (blk // 4) % 2 == 0
    greet_all()

    @pl.loop(0, PAIRS)
    def _(k):
        p = (pair + k) % PAIRS
        dst = kv.at[blk, pl.ds(head * TOK, TOK)]
        mine = (k == 0) & even

        @pl.when(mine)
        def _():
            pltpu.make_async_copy(pack.at[p], dst, recv).start()

        @pl.when(jnp.logical_not(mine))
        def _():
            remote(pack.at[p], dst, send, recv, ((p // 8) * 4 + to_quarter, p % 8)).start()

        remote(
            pack.at[p], dst, send, recv, ((p // 8) * 4 + (to_quarter + 2) % 4, p % 8)
        ).start()

    wait_bytes(kv.at[pl.ds(0, 8)], recv)
    sibling = (blk + 1 - 2 * core, head)

    @pl.loop(0, 8)
    def _(number):
        b = core_block(core, number)
        remote(kv.at[b], kv.at[b], core_send, core_recv, sibling).start()

    wait_bytes(kv.at[pl.ds(0, 8)], core_recv)
    keep = pltpu.make_async_copy(kv, kv_out, kv_sem)
    keep.start()

    @pl.loop(0, 16)
    def _(b):
        value_t[b] = kv[b, :, 128:].T

    pick = shift_matrix(LANES, 128, HD)
    for j in range(4):
        queries[j] = nn(kv[query_block(quarter, j)], pick).astype(bf16)
    for j in (3, 2, 1, 0):
        block = query_block(quarter, j)
        result = forward_block(j, block, kv, value_t, queries, starts, out_t, log_norms)
        rounded[j] = result.T.astype(bf16)

        @pl.loop(0, 8)
        def _(k, j=j, block=block):
            h = (head + k) % 8
            src = rounded.at[j, pl.ds(h * TOK, TOK)]
            mine = (k == 0) & (block == blk)

            @pl.when(mine)
            def _():
                pltpu.make_async_copy(src, landed.at[pair], back_recv).start()

            @pl.when(jnp.logical_not(mine))
            def _():
                remote(src, landed.at[pair], back_send, back_recv, (block, h)).start()

    wait_bytes(landed, back_recv)
    attended[...] = landed[...]
    keep.wait()
    wait_bytes(kv.at[pl.ds(0, 8)], core_send)
    wait_bytes(pack, send)
    wait_bytes(pack.at[pl.ds(0, 31)], send)
    wait_bytes(landed.at[pl.ds(0, 31)], back_send)

    @pl.when(jnp.logical_not(even))
    def _():
        wait_bytes(pack.at[0], send)
        wait_bytes(landed.at[0], back_send)


VMEM = pl.BlockSpec(memory_space=pltpu.VMEM)
HBM = pl.BlockSpec(memory_space=pl.ANY)


def attend(pack, starts):
    return pl.pallas_call(
        forward_kernel,
        out_shape=(
            jax.ShapeDtypeStruct((16, B, LANES), bf16),
            jax.ShapeDtypeStruct((4, B, 128), bf16),
            jax.ShapeDtypeStruct((4, 128, B), f32),
            jax.ShapeDtypeStruct((4, 1, B), f32),
            jax.ShapeDtypeStruct((PAIRS, TOK, 128), bf16),
        ),
        in_specs=[VMEM, VMEM],
        out_specs=(HBM, VMEM, VMEM, VMEM, VMEM),
        scratch_shapes=[
            pltpu.VMEM((16, B, LANES), bf16),
            pltpu.VMEM((16, 128, B), bf16),
            pltpu.VMEM((4, B, 128), bf16),
            pltpu.VMEM((PAIRS, TOK, 128), bf16),
        ]
        + [pltpu.SemaphoreType.DMA] * 7,
        compiler_params=pltpu.CompilerParams(
            collective_id=1, has_side_effects=True, vmem_limit_bytes=48 * 2**20
        ),
        name="attend",
    )(pack, starts)


def backward_block(j, block, kv, key_t, queries, d_out, starts, out_t, log_norms, d_kv):
    q = queries[j]
    do = d_out[j]
    start = starts[j]
    log_norm = log_norms[j]
    delta = jnp.sum(do.astype(f32).T * out_t[j], axis=0, keepdims=True)

    def step(key_block, acc, masked):
        s = nt(kv[key_block, :, :128], q)
        p = jnp.exp(s - log_norm)
        if masked:
            p = jnp.where(mask_of(key_block, block, start), p, 0.0)
        dp = nt(kv[key_block, :, 128:], do)
        ds = (p * (dp - delta)).astype(bf16)
        d_kv[key_block, :, :128] += nn(ds, q)
        d_kv[key_block, :, 128:] += nn(p.astype(bf16), do)
        return acc + nn(key_t[key_block], ds)

    return over_keys(block, step, jnp.zeros((128, B), f32))


def backward_kernel(
    pack,
    kv,
    queries,
    starts,
    out_t,
    log_norms,
    own_out,
    other_out,
    d_out,
    key_t,
    d_kv,
    d_query,
    half,
    half_in,
    total,
    own_in,
    other_in,
    send,
    recv,
    core_send,
    core_recv,
    back_send,
    own_recv,
    other_recv,
):
    blk = lax.axis_index("blk")
    head = lax.axis_index("head")
    core = blk % 2
    quarter = blk % 4
    pair = (blk // 4) * 8 + head
    to_quarter = quarter_of(blk)
    even = (blk // 4) % 2 == 0
    greet_all()

    @pl.loop(0, PAIRS)
    def _(k):
        p = (pair + k) % PAIRS
        dst = d_out.at[blk // 4, pl.ds(head * TOK, TOK)]
        mine = (k == 0) & even

        @pl.when(mine)
        def _():
            pltpu.make_async_copy(pack.at[p], dst, recv).start()

        @pl.when(jnp.logical_not(mine))
        def _():
            remote(pack.at[p], dst, send, recv, ((p // 8) * 4 + to_quarter, p % 8)).start()

    @pl.loop(0, 16)
    def _(b):
        key_t[b] = kv[b, :, :128].T
        d_kv[b] = jnp.zeros((B, LANES), f32)

    wait_bytes(d_out, recv)
    for j in (3, 2, 1, 0):
        block = query_block(quarter, j)
        d_query[j] = backward_block(
            j, block, kv, key_t, queries, d_out, starts, out_t, log_norms, d_kv
        ).astype(bf16)
    sibling = (blk + 1 - 2 * core, head)

    @pl.loop(0, 8)
    def _(number):
        half[number] = d_kv[core_block(1 - core, number)].astype(bf16)
        remote(
            half.at[number], half_in.at[number], core_send, core_recv, sibling
        ).start()

    wait_bytes(half_in, core_recv)
    place = shift_matrix(128, LANES, -HD)
    x_low = (blk // 2) % 2
    for z in range(4):
        own = z * 2 + (x_low if z % 2 == 0 else 1 - x_low)
        other = z * 4 + 1 - own
        block = core_block(core, own)
        total[own] = (
            d_kv[block] + half_in[own].astype(f32) + nn(d_query[z].T, place)
        ).astype(bf16)
        block_two = core_block(core, other)
        total[other] = (d_kv[block_two] + half_in[other].astype(f32)).astype(bf16)

        @pl.loop(0, 8)
        def _(k, own=own, other=other, block=block, block_two=block_two):
            h = (head + k) % 8
            src = total.at[own, pl.ds(h * TOK, TOK)]
            mine = (k == 0) & (block == blk)

            @pl.when(mine)
            def _():
                pltpu.make_async_copy(src, own_in.at[pair], own_recv).start()

            @pl.when(jnp.logical_not(mine))
            def _():
                remote(src, own_in.at[pair], back_send, own_recv, (block, h)).start()

            remote(
                total.at[other, pl.ds(h * TOK, TOK)],
                other_in.at[pair],
                back_send,
                other_recv,
                (block_two, h),
            ).start()

    wait_bytes(own_in, own_recv)
    own_out[...] = own_in[...]
    wait_bytes(other_in, other_recv)
    other_out[...] = other_in[...]
    wait_bytes(half, core_send)
    wait_bytes(pack.at[pl.ds(0, 31)], send)
    wait_bytes(own_in, back_send)
    wait_bytes(own_in.at[pl.ds(0, 31)], back_send)

    @pl.when(jnp.logical_not(even))
    def _():
        wait_bytes(pack.at[0], send)
        wait_bytes(own_in.at[0], back_send)


def attend_back(pack, kv, queries, starts, out_t, log_norms):
    return pl.pallas_call(
        backward_kernel,
        out_shape=(
            jax.ShapeDtypeStruct((PAIRS, TOK, LANES), bf16),
            jax.ShapeDtypeStruct((PAIRS, TOK, LANES), bf16),
        ),
        in_specs=[VMEM] * 6,
        out_specs=(VMEM, VMEM),
        scratch_shapes=[
            pltpu.VMEM((4, B, 128), bf16),
            pltpu.VMEM((16, 128, B), bf16),
            pltpu.VMEM((16, B, LANES), f32),
            pltpu.VMEM((4, 128, B), bf16),
            pltpu.VMEM((8, B, LANES), bf16),
            pltpu.VMEM((8, B, LANES), bf16),
            pltpu.VMEM((8, B, LANES), bf16),
            pltpu.VMEM((PAIRS, TOK, LANES), bf16),
            pltpu.VMEM((PAIRS, TOK, LANES), bf16),
        ]
        + [pltpu.SemaphoreType.DMA] * 7,
        compiler_params=pltpu.CompilerParams(
            collective_id=2, has_side_effects=True, vmem_limit_bytes=56 * 2**20
        ),
        name="attend_back",
    )(pack, kv, queries, starts, out_t, log_norms)


def pack_vectors(vectors):
    flat = jnp.concatenate(vectors, axis=-1)
    return jnp.pad(flat, [(0, 0)] * (flat.ndim - 1) + [(0, D - flat.shape[-1])])


def by_head(values):
    return values.reshape(2, TOK, H, HD).transpose(0, 2, 1, 3).reshape(PAIRS, TOK, HD)


def by_token(values):
    return values.reshape(2, H, TOK, HD).transpose(0, 2, 1, 3).reshape(2 * TOK, D)


def on_device(
    inputs,
    segment_ids,
    norm1_gain,
    w_query,
    w_key,
    w_value,
    query_bias,
    value_bias,
    w_out,
    out_bias,
    norm2_gain,
    w_hidden,
    hidden_bias,
    w_proj,
    proj_bias,
    dim_scale,
    cotangent,
):
    blk = lax.axis_index("blk")
    head = lax.axis_index("head")
    vectors = [
        norm1_gain, query_bias, value_bias, out_bias, norm2_gain, hidden_bias, proj_bias
    ]
    zero_row = jnp.zeros((1, D), bf16)
    pack = jnp.concatenate(
        [w_query, w_key, w_value, pack_vectors(vectors)[None], zero_row]
        + [w_out, w_hidden, w_proj, zero_row, zero_row],
        axis=0,
    )
    full = gather_weights(pack)

    def weight(first):
        return full[:, first : first + 10].reshape(D, D)

    query_w, key_w, value_w = weight(0), weight(10), weight(20)
    out_w, hidden_w, proj_w = weight(32), weight(42), weight(52)
    every = full[:, 30, :70].reshape(128, 7, 10).transpose(1, 0, 2).reshape(7, D).astype(f32)
    gain_one, query_b, value_b, out_b, gain_two, hidden_b, proj_b = [every[i] for i in range(7)]

    micro = blk // 8
    segment_row = lax.dynamic_index_in_dim(segment_ids, micro, 0, keepdims=False)
    starts = jnp.zeros_like(segment_row)
    for value in range(1, 9):
        before = jnp.sum((segment_row < value).astype(jnp.int32))
        starts = jnp.where(segment_row == value, before, starts)
    quarter = blk % 4
    starts = starts.reshape(16, 1, B)
    starts = jnp.stack([starts[query_block(quarter, j)] for j in range(4)])

    tokens = inputs.reshape(2 * TOK, D).astype(f32)
    inverse_one = inverse_rms(tokens)
    normed = (tokens * inverse_one * gain_one).astype(bf16)
    softplus_scale = LOG2E / math.sqrt(HD) * jax.nn.softplus(dim_scale)
    wide_scale = jnp.tile(softplus_scale, H)
    query_full = nn(normed, query_w) + query_b
    scaled = (query_full * wide_scale).astype(bf16)
    key_proj = nn(normed, key_w).astype(bf16)
    value_proj = (nn(normed, value_w) + value_b).astype(bf16)
    packed = jnp.concatenate(
        [
            by_head(key_proj),
            by_head(scaled),
            by_head(value_proj),
            jnp.ones((PAIRS, TOK, 1), bf16),
            jnp.zeros((PAIRS, TOK, LANES - 3 * HD - 1), bf16),
        ],
        axis=-1,
    )
    kv, queries, out_t, log_norms, landed = attend(packed, starts)
    attended = by_token(landed[:, :, 32:112])

    residual = tokens + nn(attended, out_w) + out_b
    inverse_two = inverse_rms(residual)
    normed_two = (residual * inverse_two * gain_two).astype(bf16)
    pre_act = nn(normed_two, hidden_w) + hidden_b
    gate = jax.nn.sigmoid(pre_act)
    activated = (pre_act * gate).astype(bf16)
    layer_out = (residual + nn(activated, proj_w) + proj_b).astype(bf16)

    upstream_low = cotangent.reshape(2 * TOK, D)
    upstream = upstream_low.astype(f32)
    d_pre = (nt(upstream_low, proj_w) * gate * (1.0 + pre_act * (1.0 - gate))).astype(bf16)
    d_normed_two = nt(d_pre, hidden_w)
    d_residual = upstream + norm_back(d_normed_two * gain_two, residual, inverse_two)
    d_branch = d_residual.astype(bf16)
    d_attended = nt(d_branch, out_w).astype(bf16)
    d_pack = jnp.pad(by_head(d_attended), ((0, 0), (0, 0), (32, 16)))
    own, other = attend_back(d_pack, kv, queries, starts, out_t, log_norms)
    back = own.astype(f32) + other.astype(f32)
    d_keys = by_token(back[:, :, :HD]).astype(bf16)
    d_scaled = by_token(back[:, :, HD : 2 * HD])
    d_values = by_token(back[:, :, 2 * HD : 3 * HD]).astype(bf16)
    scale_terms = jnp.sum((d_scaled * query_full).reshape(2 * TOK * H, HD), axis=0)
    d_query = (d_scaled * wide_scale).astype(bf16)
    d_normed = nt(d_query, query_w) + nt(d_keys, key_w) + nt(d_values, value_w)
    input_grad = (
        d_residual + norm_back(d_normed * gain_one, tokens, inverse_one)
    ).astype(bf16)

    def pieces(left, right):
        return tn(left, right).astype(bf16).reshape(128, 10, D)

    def total(values):
        return jnp.sum(values.astype(f32), axis=0).reshape(128, 10)

    vector_grads = [
        total(d_normed * tokens * inverse_one),
        total(d_query),
        total(d_values),
        total(d_branch),
        total(d_normed_two * residual * inverse_two),
        total(d_pre),
        total(upstream),
        jnp.broadcast_to(scale_terms, (128, HD)),
    ]
    zero_rows = jnp.zeros((128, 1, D), bf16)
    grads = jnp.concatenate(
        [
            pieces(normed, d_query),
            pieces(normed, d_keys),
            pieces(normed, d_values),
            pack_vectors(vector_grads)[:, None].astype(bf16),
            zero_rows,
            pieces(attended, d_branch),
            pieces(normed_two, d_pre),
            pieces(activated, upstream_low),
            zero_rows,
            zero_rows,
        ],
        axis=1,
    )
    summed = scatter_grads(grads)
    vector = [summed[30, 10 * i : 10 * i + 10] for i in range(7)]
    scale_grad = summed[30, 70:150] * (LOG2E / math.sqrt(HD)) * jax.nn.sigmoid(dim_scale)
    return (
        layer_out.reshape(2, TOK, D),
        input_grad.reshape(2, TOK, D),
        vector[0],
        summed[0:10],
        summed[10:20],
        summed[20:30],
        vector[1],
        vector[2],
        summed[32:42],
        vector[3],
        vector[4],
        summed[42:52],
        vector[5],
        summed[52:62],
        vector[6],
        scale_grad,
    )


def solution(mesh):
    rows = P(("blk", "head"), None)
    vec = P(("blk", "head"))
    tok = P(None, ("blk", "head"), None)
    in_specs = (
        tok, P(), vec, rows, rows, rows, vec, vec, rows, vec, vec, rows, vec, rows, vec, P(), tok
    )
    out_specs = (
        tok, tok, vec, rows, rows, rows, vec, vec, rows, vec, vec, rows, vec, rows, vec, P()
    )
    return jax.shard_map(
        on_device, mesh=mesh, in_specs=in_specs, out_specs=out_specs, check_vma=False
    )
```

```python
import functools
import math

import jax
import jax.numpy as jnp
import numpy as np
from jax import lax
from jax.experimental import pallas as pl
from jax.experimental.pallas import tpu as pltpu
from jax.sharding import PartitionSpec as P

D = 1280
H = 16
HD = 80
FF = 1280
B = 512
TOK = 64
PAIRS = 32
LANES = 256
ROWS = 32
WIDE = H * LANES
OUT_WIDE = H * 128
GROUP = 80
EPSILON = 1e-06
LOG2E = 1.442695041
NEGATIVE = -1e30
MESH = pl.DeviceIdType.MESH
f32 = jnp.float32
bf16 = jnp.bfloat16

PARTS = (((0, 512), "xyz"), ((512, 384), "yzx"), ((896, 384), "zxy"))


def inverse_rms(values):
    return lax.rsqrt(jnp.mean(values * values, axis=-1, keepdims=True) + EPSILON)


def norm_back(upstream, values, inverse):
    return inverse * upstream - values * inverse**3 * jnp.mean(
        upstream * values, axis=-1, keepdims=True
    )


def nn(a, b):
    return lax.dot_general(a, b, (((1,), (0,)), ((), ())), preferred_element_type=f32)


def nt(a, b):
    return lax.dot_general(a, b, (((1,), (1,)), ((), ())), preferred_element_type=f32)


def tn(a, b):
    return lax.dot_general(a, b, (((0,), (0,)), ((), ())), preferred_element_type=f32)


def my_place():
    blk = lax.axis_index("blk")
    head = lax.axis_index("head")
    return {
        "x": (head % 2) * 2 + (blk // 2) % 2,
        "y": head // 2,
        "z": blk // 4,
        "c": blk % 2,
    }


def device_at(place):
    x, y, z, c = place["x"], place["y"], place["z"], place["c"]
    return (z * 4 + (x % 2) * 2 + c, y * 2 + x // 2)


def chunk_of(ref, place, cols, lead=()):
    blk, head = device_at(place)
    return ref.at[(*lead, blk, pl.ds(head * ROWS, ROWS), cols)]


def moved(place, axis, value):
    other = dict(place)
    other[axis] = value
    return other


def greet(peers):
    barrier = pltpu.get_barrier_semaphore()
    for peer in peers:
        pl.semaphore_signal(barrier, inc=1, device_id=peer, device_id_type=MESH)
    pl.semaphore_wait(barrier, len(peers))


def greet_all():
    barrier = pltpu.get_barrier_semaphore()
    me = lax.axis_index("blk") * 8 + lax.axis_index("head")

    @pl.loop(1, 128)
    def _(k):
        other = (me + k) % 128
        pl.semaphore_signal(
            barrier, inc=1, device_id=(other // 8, other % 8), device_id_type=MESH
        )

    pl.semaphore_wait(barrier, 127)


def ring_peers(place):
    peers = [device_at(moved(place, "c", 1 - place["c"]))]
    for axis in "xyz":
        for step in (1, 3, 2):
            peers.append(device_at(moved(place, axis, (place[axis] + step) % 4)))
    return peers


def wait_bytes(ref, sem):
    pltpu.make_async_copy(ref, ref, sem).wait()


def remote(src, dst, send, recv, device):
    return pltpu.make_async_remote_copy(
        src_ref=src, dst_ref=dst, send_sem=send, recv_sem=recv, device_id=device, device_id_type=MESH
    )


def varied(place, axes, number):
    other = dict(place)
    for axis in axes:
        other[axis] = number % 4
        number = number // 4
    return other


def selections():
    take = np.zeros((3, GROUP, 256), np.float32)
    last = np.zeros((5, GROUP, 256), np.float32)
    for i in range(8):
        for j in range(10):
            for w in range(3):
                take[w, i * 10 + j, i * ROWS + w * 10 + j] = 1
            last[j % 5, i * 10 + j, i * ROWS + 30 + j // 5] = 1
    spread = np.zeros((128, 256), np.float32)
    spread[32:112] = take[0]
    return take, last, spread


TAKE, LAST, SPREAD = selections()
LANE_OF = np.zeros((128, D), np.float32)
LANE_OF[112 + np.arange(D) % 10, np.arange(D)] = 1
ROW_OF = np.zeros((16, D), np.float32)
ROW_OF[np.arange(D) % 10, np.arange(D)] = 1
TENTH = (np.arange(D) // 10).astype(np.int32)
SCALE_ROWS = np.zeros((256, 16), np.float32)
for _i in range(8):
    for _j in range(8):
        SCALE_ROWS[_i * ROWS + _j, _j] = 1


class Gather:
    def __init__(self, buf, send, recv, place):
        self.buf, self.send, self.recv, self.place = buf, send, recv, place
        self.sibling = device_at(moved(place, "c", 1 - place["c"]))

    def begin(self, pack, sem):
        own = pltpu.make_async_copy(
            pack, chunk_of(self.buf, self.place, pl.ds(0, D)), sem
        )
        own.start()
        return own

    def forward(self, part, axes, fixed, count):
        first, width = PARTS[part][0]
        cols = pl.ds(first, width)

        @pl.loop(0, count)
        def _(number):
            where = dict(varied(self.place, axes, number), **fixed)
            piece = chunk_of(self.buf, where, cols)
            remote(
                piece, piece, self.send.at[part, 3], self.recv.at[part, 5], self.sibling
            ).start()

    def stage(self, stage):
        for part, ((first, width), order) in enumerate(PARTS):
            cols = pl.ds(first, width)
            if stage:
                wait_bytes(
                    self.buf.at[0, pl.ds(0, 3 * 4 ** (stage - 1) * ROWS), cols]
                    if stage == 1
                    else self.buf.at[pl.ds(0, 3), pl.ds(0, 4 * ROWS), cols],
                    self.recv.at[part, stage - 1],
                )

            @pl.loop(0, 4**stage)
            def _(number, part=part, cols=cols, order=order):
                piece = chunk_of(self.buf, varied(self.place, order[:stage], number), cols)
                axis = order[stage]
                for step in (1, 3, 2):
                    target = moved(self.place, axis, (self.place[axis] + step) % 4)
                    slot = stage if stage < 2 else 1 + step
                    remote(
                        piece,
                        piece,
                        self.send.at[part, stage],
                        self.recv.at[part, slot],
                        device_at(target),
                    ).start()

        for part, (_, order) in enumerate(PARTS):
            if stage == 0:
                self.forward(part, "", {}, 1)
            else:
                axis = order[stage - 1]
                for step in (1, 3, 2):
                    self.forward(
                        part,
                        order[: stage - 1],
                        {axis: (self.place[axis] + 4 - step) % 4},
                        4 ** (stage - 1),
                    )

    def finish(self):
        for step in (1, 3, 2):
            for part, ((first, width), order) in enumerate(PARTS):
                wait_bytes(
                    self.buf.at[pl.ds(0, 2), :, pl.ds(first, width)],
                    self.recv.at[part, 1 + step],
                )
                axis = order[2]
                self.forward(
                    part, order[:2], {axis: (self.place[axis] + 4 - step) % 4}, 16
                )
        for part, ((first, width), order) in enumerate(PARTS):
            cols = pl.ds(first, width)
            half = self.buf.at[pl.ds(0, 8), :, cols]
            wait_bytes(half, self.recv.at[part, 5])
            wait_bytes(half, self.send.at[part, 3])
            wait_bytes(self.buf.at[0, pl.ds(0, 3 * ROWS), cols], self.send.at[part, 0])
            wait_bytes(
                self.buf.at[pl.ds(0, 3), pl.ds(0, 4 * ROWS), cols], self.send.at[part, 1]
            )
            wait_bytes(self.buf.at[pl.ds(0, 6), :, cols], self.send.at[part, 2])


def gather_kernel(
    pack_one,
    pack_two,
    take,
    last,
    spread,
    lane_of,
    row_of,
    tenth_row,
    tenth_col,
    wide,
    out_w,
    hidden_w,
    proj_w,
    vectors,
    buf_one,
    buf_two,
    vec_tile,
    stage_one,
    stage_two,
    send,
    recv,
    own_sem,
    out_sem,
):
    place = my_place()
    one = Gather(buf_one, send.at[0], recv.at[0], place)
    two = Gather(buf_two, send.at[1], recv.at[1], place)
    first = one.begin(pack_one, own_sem.at[0])
    second = two.begin(pack_two, own_sem.at[1])
    greet(ring_peers(place))
    first.wait()
    second.wait()
    for stage in range(3):
        one.stage(stage)
    one.finish()
    for stage in range(3):
        two.stage(stage)

    def rows(ref, g, count):
        return ref.at[pl.ds(pl.multiple_of(g * count, 16), count)]

    @pl.loop(0, 16)
    def _(g):
        slot = g % 2
        out = pltpu.make_async_copy(stage_one.at[slot], rows(wide, g, GROUP), out_sem.at[0, slot])

        @pl.when(g >= 2)
        def _():
            out.wait()

        for w in range(3):
            stage_one[slot, :, w * D : (w + 1) * D] = nn(take[w], buf_one[g]).astype(bf16)
        head = jnp.zeros((GROUP, LANES), f32)
        for cell in range(5):
            head = head + nn(last[cell], buf_one[g, :, cell * LANES : (cell + 1) * LANES])
        stage_one[slot, :, 3 * D :] = head.astype(bf16)
        vec_tile[pl.ds(pl.multiple_of(g * GROUP, 16), GROUP)] = stage_one[slot, :, 128:256]
        out.start()

    for slot in range(2):
        pltpu.make_async_copy(stage_one.at[slot], rows(wide, 0, GROUP), out_sem.at[0, slot]).wait()
    spread_out = nn(vec_tile[...], lane_of[...])
    spread_out = jnp.where(tenth_col[...] == tenth_row[...], spread_out, 0.0).astype(bf16)
    vectors[...] = nn(row_of[...], spread_out)
    two.finish()

    @pl.loop(0, 16)
    def _(g):
        slot = g % 2
        outs = [
            pltpu.make_async_copy(
                stage_two.at[slot, pl.ds(0, 128)], rows(out_w, g, 128), out_sem.at[1, slot]
            ),
            pltpu.make_async_copy(
                stage_two.at[slot, pl.ds(128, GROUP)], rows(hidden_w, g, GROUP), out_sem.at[2, slot]
            ),
            pltpu.make_async_copy(
                stage_two.at[slot, pl.ds(208, GROUP)], rows(proj_w, g, GROUP), out_sem.at[3, slot]
            ),
        ]

        @pl.when(g >= 2)
        def _():
            for out in outs:
                out.wait()

        stage_two[slot, 0:128] = nn(spread[...], buf_two[g]).astype(bf16)
        stage_two[slot, 128:208] = nn(take[1], buf_two[g]).astype(bf16)
        stage_two[slot, 208:288] = nn(take[2], buf_two[g]).astype(bf16)
        for out in outs:
            out.start()

    for slot in range(2):
        for at, count in ((0, 128), (128, GROUP), (208, GROUP)):
            pltpu.make_async_copy(
                stage_two.at[slot, pl.ds(at, count)],
                (out_w if at == 0 else hidden_w).at[pl.ds(0, count)],
                out_sem.at[1 + (at > 0) + (at > 200), slot],
            ).wait()


VMEM = pl.BlockSpec(memory_space=pltpu.VMEM)
HBM = pl.BlockSpec(memory_space=pl.ANY)


def gather_weights(pack_one, pack_two):
    return pl.pallas_call(
        gather_kernel,
        out_shape=(
            jax.ShapeDtypeStruct((D, WIDE), bf16),
            jax.ShapeDtypeStruct((OUT_WIDE, D), bf16),
            jax.ShapeDtypeStruct((D, D), bf16),
            jax.ShapeDtypeStruct((D, D), bf16),
            jax.ShapeDtypeStruct((16, D), f32),
        ),
        in_specs=[VMEM] * 9,
        out_specs=(HBM, HBM, HBM, HBM, VMEM),
        scratch_shapes=[
            pltpu.VMEM((16, 256, D), bf16),
            pltpu.VMEM((16, 256, D), bf16),
            pltpu.VMEM((D, 128), bf16),
            pltpu.VMEM((2, GROUP, WIDE), bf16),
            pltpu.VMEM((2, 288, D), bf16),
            pltpu.SemaphoreType.DMA((2, 3, 4)),
            pltpu.SemaphoreType.DMA((2, 3, 6)),
            pltpu.SemaphoreType.DMA((2,)),
            pltpu.SemaphoreType.DMA((4, 2)),
        ],
        compiler_params=pltpu.CompilerParams(
            collective_id=0, has_side_effects=True, vmem_limit_bytes=56 * 2**20
        ),
        name="gather_weights",
    )(
        pack_one,
        pack_two,
        jnp.asarray(TAKE, bf16),
        jnp.asarray(LAST, bf16),
        jnp.asarray(SPREAD, bf16),
        jnp.asarray(LANE_OF, bf16),
        jnp.asarray(ROW_OF, bf16),
        jnp.asarray(TENTH[None, :]),
        jnp.asarray(TENTH[:, None]),
    )


class Scatter:
    def __init__(self, away, mine, pair, lands, halves, send, recv, place):
        self.away, self.mine, self.pair = away, mine, pair
        self.lands, self.halves = lands, halves
        self.send, self.recv, self.place = send, recv, place
        self.sibling = device_at(moved(place, "c", 1 - place["c"]))

    def swap(self, number):
        return remote(
            self.away.at[number],
            self.pair.at[number],
            self.send.at[3, number],
            self.recv.at[3, number],
            self.sibling,
        )

    def add_pair(self, number):
        self.swap(number).wait()
        self.mine[number] = (
            self.mine[number].astype(f32) + self.pair[number].astype(f32)
        ).astype(bf16)

    def own_piece(self, where, cols):
        half = where["z"] * 2 + where["x"] % 2
        return self.mine.at[half, pl.ds((where["y"] * 2 + where["x"] // 2) * ROWS, ROWS), cols]

    def start(self, stage):
        for part, ((first, width), order) in enumerate(PARTS):
            cols = pl.ds(first, width)
            axis = order[2 - stage]
            rest = order[: 2 - stage]

            @pl.loop(0, 16 // 4**stage)
            def _(number, part=part, cols=cols, axis=axis, rest=rest):
                for step in (1, 3, 2):
                    target = moved(self.place, axis, (self.place[axis] + step) % 4)
                    if stage == 0:
                        source = self.own_piece(varied(target, rest, number), cols)
                    elif stage == 1:
                        source = self.halves[0].at[target[axis], number, :, cols]
                    else:
                        source = self.halves[1].at[target[axis], :, cols]
                    remote(
                        source,
                        self.lands[stage].at[step - 1, number, :, cols],
                        self.send.at[part, stage],
                        self.recv.at[part, stage],
                        device_at(target),
                    ).start()

    def add(self, stage, out=None):
        for part, ((first, width), order) in enumerate(PARTS):
            cols = pl.ds(first, width)
            axis = order[2 - stage]
            rest = order[: 2 - stage]
            wait_bytes(self.lands[stage].at[:, :, :, cols], self.recv.at[part, stage])

            @pl.loop(0, 16 // 4**stage)
            def _(number, cols=cols, axis=axis, rest=rest):
                if stage == 0:
                    total = self.own_piece(varied(self.place, rest, number), cols)[...]
                elif stage == 1:
                    total = self.halves[0][self.place[axis], number, :, cols]
                else:
                    total = self.halves[1][self.place[axis], :, cols]
                total = total.astype(f32)
                for source in range(3):
                    total = total + self.lands[stage][source, number, :, cols].astype(f32)
                if stage == 0:
                    self.halves[0][number // 4, number % 4, :, cols] = total.astype(bf16)
                elif stage == 1:
                    self.halves[1][number, :, cols] = total.astype(bf16)
                else:
                    out[:, cols] = total

    def finish(self):
        for stage in range(3):
            for part, ((first, width), order) in enumerate(PARTS):
                wait_bytes(
                    self.lands[stage].at[:, :, :, pl.ds(first, width)], self.send.at[part, stage]
                )


def scatter_scratch():
    return [
        pltpu.VMEM((8, 256, D), bf16),
        pltpu.VMEM((8, 256, D), bf16),
        pltpu.VMEM((8, 256, D), bf16),
        pltpu.VMEM((3, 16, ROWS, D), bf16),
        pltpu.VMEM((3, 4, ROWS, D), bf16),
        pltpu.VMEM((3, 1, ROWS, D), bf16),
        pltpu.VMEM((4, 4, ROWS, D), bf16),
        pltpu.VMEM((4, ROWS, D), bf16),
        pltpu.SemaphoreType.DMA((4, 8)),
        pltpu.SemaphoreType.DMA((4, 8)),
    ]


def scatter_of(scratch, place):
    away, mine, pair, l0, l1, l2, h0, h1, send, recv = scratch
    return Scatter(away, mine, pair, (l0, l1, l2), (h0, h1), send, recv, place)


def turned(ref, cols):
    return ref[:, cols].T


def scatter_kernel(
    normed,
    d_wide,
    attended,
    d_branch,
    normed_two,
    d_pre,
    activated,
    upstream,
    vector_grads,
    scale_tile,
    take_t,
    last_t,
    lane_of_t,
    row_of_t,
    scale_rows,
    tenth_row,
    tenth_col,
    out_one,
    out_two,
    normed_t,
    attended_t,
    normed_two_t,
    activated_t,
    right_one,
    right_two,
    vec_tile,
    *scratch,
):
    place = my_place()
    one = scatter_of(scratch[:10], place)
    two = scatter_of(scratch[10:], place)
    for n in range(D // 128):
        lanes = slice(n * 128, n * 128 + 128)
        normed_t[lanes] = turned(normed, lanes)
        normed_two_t[lanes] = turned(normed_two, lanes)
        activated_t[lanes] = turned(activated, lanes)
    for n in range(H):
        lanes = slice(n * 128, n * 128 + 128)
        attended_t[lanes] = turned(attended, lanes)
    for w in range(3):
        right_one[w * 128 : w * 128 + 128] = d_wide[:, w * D : (w + 1) * D]
    for cell in range(5):
        right_one[384:512, cell * LANES : (cell + 1) * LANES] = d_wide[:, 3 * D :]
    right_two[0:128] = d_branch[...]
    right_two[128:256] = d_pre[...]
    right_two[256:384] = upstream[...]
    by_row = nn(row_of_t[...], vector_grads[...])
    by_row = jnp.where(tenth_col[...] == tenth_row[...], by_row, 0.0).astype(bf16)
    vec_tile[...] = nn(by_row, lane_of_t[...]).astype(bf16)
    greet(ring_peers(place))

    def produce(number, core, into_one, into_two):
        group = number * 2 + core
        rows = pl.ds(pl.multiple_of(group * GROUP, 16), GROUP)
        piece = normed_t[rows]
        lefts = [nn(take_t[w], piece).astype(bf16) for w in range(3)]
        for cell in range(5):
            left = jnp.concatenate(lefts + [nn(last_t[cell], piece).astype(bf16)], axis=1)
            lanes = slice(cell * LANES, (cell + 1) * LANES)
            block = nn(left, right_one[:, lanes])
            if cell == 0:
                block = block + jnp.concatenate(
                    [jnp.zeros((256, 128), f32), nn(take_t[0], vec_tile[rows])], axis=1
                )
            if cell == 1:
                block = block + jnp.concatenate(
                    [jnp.zeros((256, 128), f32), nn(scale_rows[...], scale_tile[...])], axis=1
                )
            into_one[number, :, lanes] = block.astype(bf16)
        out_rows = pl.ds(pl.multiple_of(group * 128 + 32, 16), GROUP)
        left = jnp.concatenate(
            [
                nn(take_t[0], attended_t[out_rows]).astype(bf16),
                nn(take_t[1], normed_two_t[rows]).astype(bf16),
                nn(take_t[2], activated_t[rows]).astype(bf16),
            ],
            axis=1,
        )
        for cell in range(5):
            lanes = slice(cell * LANES, (cell + 1) * LANES)
            into_two[number, :, lanes] = nn(left, right_two[:, lanes]).astype(bf16)

    @pl.loop(0, 8)
    def _(number):
        produce(number, 1 - place["c"], one.away, two.away)
        one.swap(number).start()
        two.swap(number).start()

    @pl.loop(0, 8)
    def _(number):
        produce(number, place["c"], one.mine, two.mine)
        one.add_pair(number)
        two.add_pair(number)

    for stage in range(3):
        one.start(stage)
        two.start(stage)
        one.add(stage, out_one)
        two.add(stage, out_two)
    one.finish()
    two.finish()


def scatter_grads(*operands):
    return pl.pallas_call(
        scatter_kernel,
        out_shape=(
            jax.ShapeDtypeStruct((ROWS, D), f32),
            jax.ShapeDtypeStruct((ROWS, D), f32),
        ),
        in_specs=[VMEM] * 17,
        out_specs=(VMEM, VMEM),
        scratch_shapes=[
            pltpu.VMEM((D, 128), bf16),
            pltpu.VMEM((OUT_WIDE, 128), bf16),
            pltpu.VMEM((D, 128), bf16),
            pltpu.VMEM((D, 128), bf16),
            pltpu.VMEM((512, D), bf16),
            pltpu.VMEM((384, D), bf16),
            pltpu.VMEM((D, 128), bf16),
        ]
        + scatter_scratch()
        + scatter_scratch(),
        compiler_params=pltpu.CompilerParams(
            collective_id=3, has_side_effects=True, vmem_limit_bytes=60 * 2**20
        ),
        name="scatter_grads",
    )(
        *operands,
        jnp.asarray(TAKE.transpose(0, 2, 1), bf16),
        jnp.asarray(LAST.transpose(0, 2, 1), bf16),
        jnp.asarray(LANE_OF.T, bf16),
        jnp.asarray(ROW_OF.T, bf16),
        jnp.asarray(SCALE_ROWS, bf16),
        jnp.asarray(TENTH[None, :]),
        jnp.asarray(TENTH[:, None]),
    )


def quarter_of(blk):
    inner = blk % 4
    return jnp.where((blk // 4) % 2 == 0, inner, 3 - inner)


def query_block(quarter, j):
    return j * 4 + (quarter if j % 2 == 0 else 3 - quarter)


def core_block(core, number):
    z = number // 2
    return z * 4 + (core + z) % 2 + 2 * (number % 2)


def cell_of(ref, pair, width):
    return ref.at[pl.ds(pair // H * TOK, TOK), pl.ds(pair % H * width, width)]


def mask_of(key_block, block, start):
    key_at = key_block * B + lax.broadcasted_iota(jnp.int32, (B, B), 0)
    query_at = block * B + lax.broadcasted_iota(jnp.int32, (B, B), 1)
    return (key_at >= start) & (key_at <= query_at)


def over_keys(block, step, state):
    state = step(0, state, True)

    def middle(masked):
        return lambda s: lax.fori_loop(1, block, lambda k, t: step(k, t, masked), s)

    state = lax.cond(block == 15, middle(True), middle(False), state)
    return lax.cond(block > 0, lambda s: step(block, s, True), lambda s: s, state)


def shift_matrix(rows, cols, by):
    row = lax.broadcasted_iota(jnp.int32, (rows, cols), 0)
    col = lax.broadcasted_iota(jnp.int32, (rows, cols), 1)
    return jnp.where((row - col == by) & (jnp.minimum(row, col) < HD), 1.0, 0.0).astype(bf16)


def wait_cells(ref, sem, fewer, width):
    wait_bytes(ref.at[:, pl.ds(0, 15 * width)], sem)
    wait_bytes(cell_of(ref, 0, width), sem)

    @pl.when(jnp.logical_not(fewer))
    def _():
        wait_bytes(cell_of(ref, 0, width), sem)


def forward_block(j, block, kv, value_t, queries, starts, out_t, log_norms):
    q = queries[j]
    start = starts[j]

    def step(key_block, state, masked):
        top, total, acc = state
        s = nt(kv[key_block, :, :128], q)
        if masked:
            s = jnp.where(mask_of(key_block, block, start), s, NEGATIVE)
        new_top = jnp.maximum(top, jnp.max(s, axis=0, keepdims=True))
        p = jnp.exp(s - new_top)
        scale = jnp.exp(top - new_top)
        total = total * scale + jnp.sum(p, axis=0, keepdims=True)
        return (new_top, total, acc * scale + nn(value_t[key_block], p.astype(bf16)))

    state = (
        jnp.full((1, B), NEGATIVE, f32),
        jnp.zeros((1, B), f32),
        jnp.zeros((128, B), f32),
    )
    top, total, acc = over_keys(block, step, state)
    result = acc / acc[112:113]
    out_t[j] = result
    log_norms[j] = top + jnp.log(total)
    return result


def forward_kernel(
    pack,
    starts,
    kv_out,
    queries,
    out_t,
    log_norms,
    attended,
    kv,
    value_t,
    rounded,
    landed,
    send,
    recv,
    core_send,
    core_recv,
    back_send,
    back_recv,
    kv_sem,
):
    blk = lax.axis_index("blk")
    head = lax.axis_index("head")
    core = blk % 2
    quarter = blk % 4
    pair = (blk // 4) * 8 + head
    to_quarter = quarter_of(blk)
    even = (blk // 4) % 2 == 0
    greet_all()

    @pl.loop(0, PAIRS)
    def _(k):
        p = (pair + k) % PAIRS
        src = cell_of(pack, p, LANES)
        dst = kv.at[blk, pl.ds(head * TOK, TOK)]
        mine = (k == 0) & even

        @pl.when(mine)
        def _():
            pltpu.make_async_copy(src, dst, recv).start()

        @pl.when(jnp.logical_not(mine))
        def _():
            remote(src, dst, send, recv, ((p // 8) * 4 + to_quarter, p % 8)).start()

        remote(
            src, dst, send, recv, ((p // 8) * 4 + (to_quarter + 2) % 4, p % 8)
        ).start()

    wait_bytes(kv.at[pl.ds(0, 8)], recv)
    sibling = (blk + 1 - 2 * core, head)

    @pl.loop(0, 8)
    def _(number):
        b = core_block(core, number)
        remote(kv.at[b], kv.at[b], core_send, core_recv, sibling).start()

    wait_bytes(kv.at[pl.ds(0, 8)], core_recv)
    keep = pltpu.make_async_copy(kv, kv_out, kv_sem)
    keep.start()

    @pl.loop(0, 16)
    def _(b):
        value_t[b] = kv[b, :, 128:].T

    pick = shift_matrix(LANES, 128, HD)
    for j in range(4):
        queries[j] = nn(kv[query_block(quarter, j)], pick).astype(bf16)
    for j in (3, 2, 1, 0):
        block = query_block(quarter, j)
        result = forward_block(j, block, kv, value_t, queries, starts, out_t, log_norms)
        rounded[j] = result.T.astype(bf16)

        @pl.loop(0, 8)
        def _(k, j=j, block=block):
            h = (head + k) % 8
            src = rounded.at[j, pl.ds(h * TOK, TOK)]
            mine = (k == 0) & (block == blk)

            @pl.when(mine)
            def _():
                pltpu.make_async_copy(src, cell_of(landed, pair, 128), back_recv).start()

            @pl.when(jnp.logical_not(mine))
            def _():
                remote(
                    src, cell_of(landed, pair, 128), back_send, back_recv, (block, h)
                ).start()

    wait_bytes(landed, back_recv)
    attended[...] = landed[...]
    keep.wait()
    wait_bytes(kv.at[pl.ds(0, 8)], core_send)
    wait_bytes(pack, send)
    wait_cells(pack, send, even, LANES)
    wait_cells(landed, back_send, even, 128)


def attend(pack, starts):
    return pl.pallas_call(
        forward_kernel,
        out_shape=(
            jax.ShapeDtypeStruct((16, B, LANES), bf16),
            jax.ShapeDtypeStruct((4, B, 128), bf16),
            jax.ShapeDtypeStruct((4, 128, B), f32),
            jax.ShapeDtypeStruct((4, 1, B), f32),
            jax.ShapeDtypeStruct((2 * TOK, OUT_WIDE), bf16),
        ),
        in_specs=[VMEM, VMEM],
        out_specs=(HBM, VMEM, VMEM, VMEM, VMEM),
        scratch_shapes=[
            pltpu.VMEM((16, B, LANES), bf16),
            pltpu.VMEM((16, 128, B), bf16),
            pltpu.VMEM((4, B, 128), bf16),
            pltpu.VMEM((2 * TOK, OUT_WIDE), bf16),
        ]
        + [pltpu.SemaphoreType.DMA] * 7,
        compiler_params=pltpu.CompilerParams(
            collective_id=1, has_side_effects=True, vmem_limit_bytes=48 * 2**20
        ),
        name="attend",
    )(pack, starts)


def backward_block(j, block, kv, key_t, queries, d_out, starts, out_t, log_norms, d_kv):
    q = queries[j]
    do = d_out[j]
    start = starts[j]
    log_norm = log_norms[j]
    delta = jnp.sum(do.astype(f32).T * out_t[j], axis=0, keepdims=True)

    def step(key_block, acc, masked):
        s = nt(kv[key_block, :, :128], q)
        p = jnp.exp(s - log_norm)
        if masked:
            p = jnp.where(mask_of(key_block, block, start), p, 0.0)
        dp = nt(kv[key_block, :, 128:], do)
        ds = (p * (dp - delta)).astype(bf16)
        d_kv[key_block, :, :128] += nn(ds, q)
        d_kv[key_block, :, 128:] += nn(p.astype(bf16), do)
        return acc + nn(key_t[key_block], ds)

    return over_keys(block, step, jnp.zeros((128, B), f32))


def backward_kernel(
    pack,
    kv,
    queries,
    starts,
    out_t,
    log_norms,
    own_out,
    other_out,
    d_out,
    key_t,
    d_kv,
    d_query,
    half,
    half_in,
    total,
    own_in,
    other_in,
    send,
    recv,
    core_send,
    core_recv,
    back_send,
    own_recv,
    other_recv,
):
    blk = lax.axis_index("blk")
    head = lax.axis_index("head")
    core = blk % 2
    quarter = blk % 4
    pair = (blk // 4) * 8 + head
    to_quarter = quarter_of(blk)
    even = (blk // 4) % 2 == 0
    greet_all()

    @pl.loop(0, PAIRS)
    def _(k):
        p = (pair + k) % PAIRS
        src = cell_of(pack, p, 128)
        dst = d_out.at[blk // 4, pl.ds(head * TOK, TOK)]
        mine = (k == 0) & even

        @pl.when(mine)
        def _():
            pltpu.make_async_copy(src, dst, recv).start()

        @pl.when(jnp.logical_not(mine))
        def _():
            remote(src, dst, send, recv, ((p // 8) * 4 + to_quarter, p % 8)).start()

    @pl.loop(0, 16)
    def _(b):
        key_t[b] = kv[b, :, :128].T
        d_kv[b] = jnp.zeros((B, LANES), f32)

    wait_bytes(d_out, recv)
    for j in (3, 2, 1, 0):
        block = query_block(quarter, j)
        d_query[j] = backward_block(
            j, block, kv, key_t, queries, d_out, starts, out_t, log_norms, d_kv
        ).astype(bf16)
    sibling = (blk + 1 - 2 * core, head)

    @pl.loop(0, 8)
    def _(number):
        half[number] = d_kv[core_block(1 - core, number)].astype(bf16)
        remote(
            half.at[number], half_in.at[number], core_send, core_recv, sibling
        ).start()

    wait_bytes(half_in, core_recv)
    place = shift_matrix(128, LANES, -HD)
    x_low = (blk // 2) % 2
    for z in range(4):
        own = z * 2 + (x_low if z % 2 == 0 else 1 - x_low)
        other = z * 4 + 1 - own
        block = core_block(core, own)
        total[own] = (
            d_kv[block] + half_in[own].astype(f32) + nn(d_query[z].T, place)
        ).astype(bf16)
        block_two = core_block(core, other)
        total[other] = (d_kv[block_two] + half_in[other].astype(f32)).astype(bf16)

        @pl.loop(0, 8)
        def _(k, own=own, other=other, block=block, block_two=block_two):
            h = (head + k) % 8
            src = total.at[own, pl.ds(h * TOK, TOK)]
            mine = (k == 0) & (block == blk)

            @pl.when(mine)
            def _():
                pltpu.make_async_copy(src, cell_of(own_in, pair, LANES), own_recv).start()

            @pl.when(jnp.logical_not(mine))
            def _():
                remote(
                    src, cell_of(own_in, pair, LANES), back_send, own_recv, (block, h)
                ).start()

            remote(
                total.at[other, pl.ds(h * TOK, TOK)],
                cell_of(other_in, pair, LANES),
                back_send,
                other_recv,
                (block_two, h),
            ).start()

    wait_bytes(own_in, own_recv)
    own_out[...] = own_in[...]
    wait_bytes(other_in, other_recv)
    other_out[...] = other_in[...]
    wait_bytes(half, core_send)
    wait_cells(pack, send, even, 128)
    wait_bytes(own_in, back_send)
    wait_cells(own_in, back_send, even, LANES)


def attend_back(pack, kv, queries, starts, out_t, log_norms):
    return pl.pallas_call(
        backward_kernel,
        out_shape=(
            jax.ShapeDtypeStruct((2 * TOK, WIDE), bf16),
            jax.ShapeDtypeStruct((2 * TOK, WIDE), bf16),
        ),
        in_specs=[VMEM] * 6,
        out_specs=(VMEM, VMEM),
        scratch_shapes=[
            pltpu.VMEM((4, B, 128), bf16),
            pltpu.VMEM((16, 128, B), bf16),
            pltpu.VMEM((16, B, LANES), f32),
            pltpu.VMEM((4, 128, B), bf16),
            pltpu.VMEM((8, B, LANES), bf16),
            pltpu.VMEM((8, B, LANES), bf16),
            pltpu.VMEM((8, B, LANES), bf16),
            pltpu.VMEM((2 * TOK, WIDE), bf16),
            pltpu.VMEM((2 * TOK, WIDE), bf16),
        ]
        + [pltpu.SemaphoreType.DMA] * 7,
        compiler_params=pltpu.CompilerParams(
            collective_id=2, has_side_effects=True, vmem_limit_bytes=56 * 2**20
        ),
        name="attend_back",
    )(pack, kv, queries, starts, out_t, log_norms)


def on_device(
    inputs,
    segment_ids,
    norm1_gain,
    w_query,
    w_key,
    w_value,
    query_bias,
    value_bias,
    w_out,
    out_bias,
    norm2_gain,
    w_hidden,
    hidden_bias,
    w_proj,
    proj_bias,
    dim_scale,
    cotangent,
):
    blk = lax.axis_index("blk")
    vectors = jnp.stack(
        [norm1_gain, query_bias, value_bias, out_bias, norm2_gain, hidden_bias, proj_bias]
    )
    spare = jnp.pad(vectors[:, None], ((0, 3), (0, H - 1), (0, 6)))
    rows = jnp.concatenate(
        [w.reshape(10, H, HD) for w in (w_key, w_query, w_value)] + [spare], axis=2
    )
    pack_one = jnp.concatenate(
        [rows[:, w * 5 : w * 5 + 5].reshape(10, D) for w in range(3)]
        + [rows[:, 15].reshape(2, D)],
        axis=0,
    )
    pack_two = jnp.concatenate([w_out, w_hidden, w_proj, jnp.zeros((2, D), bf16)], axis=0)
    wide_w, out_w, hidden_w, proj_w, every = gather_weights(pack_one, pack_two)
    gain_one, query_b, value_b, out_b, gain_two, hidden_b, proj_b = [every[i] for i in range(7)]

    micro = blk // 8
    segment_row = lax.dynamic_index_in_dim(segment_ids, micro, 0, keepdims=False)
    starts = jnp.zeros_like(segment_row)
    for value in range(1, 9):
        before = jnp.sum((segment_row < value).astype(jnp.int32))
        starts = jnp.where(segment_row == value, before, starts)
    quarter = blk % 4
    starts = starts.reshape(16, 1, B)
    starts = jnp.stack([starts[query_block(quarter, j)] for j in range(4)])

    def lanes_of(key, query, value, spare_lanes):
        parts = [jnp.broadcast_to(part.reshape(-1, HD), (H, HD)) for part in (key, query, value)]
        return jnp.concatenate(parts + [jnp.broadcast_to(spare_lanes, (H, 16))], 1).reshape(WIDE)

    tokens = inputs.reshape(2 * TOK, D).astype(f32)
    inverse_one = inverse_rms(tokens)
    normed = (tokens * inverse_one * gain_one).astype(bf16)
    softplus_scale = LOG2E / math.sqrt(HD) * jax.nn.softplus(dim_scale)
    ones = jnp.ones((HD,), f32)
    zeros = jnp.zeros((HD,), f32)
    none = jnp.zeros((16,), f32)
    wide_bias = lanes_of(zeros, query_b, value_b, none)
    wide_scale = lanes_of(ones, softplus_scale, ones, none)
    wide_one = lanes_of(zeros, zeros, zeros, none.at[0].set(1.0))
    wide_full = nn(normed, wide_w) + wide_bias
    packed = (wide_full * wide_scale + wide_one).astype(bf16)
    kv, queries, out_t, log_norms, attended = attend(packed, starts)

    residual = tokens + nn(attended, out_w) + out_b
    inverse_two = inverse_rms(residual)
    normed_two = (residual * inverse_two * gain_two).astype(bf16)
    pre_act = nn(normed_two, hidden_w) + hidden_b
    gate = jax.nn.sigmoid(pre_act)
    activated = (pre_act * gate).astype(bf16)
    layer_out = (residual + nn(activated, proj_w) + proj_b).astype(bf16)

    upstream_low = cotangent.reshape(2 * TOK, D)
    upstream = upstream_low.astype(f32)
    d_pre = (nt(upstream_low, proj_w) * gate * (1.0 + pre_act * (1.0 - gate))).astype(bf16)
    d_normed_two = nt(d_pre, hidden_w)
    d_residual = upstream + norm_back(d_normed_two * gain_two, residual, inverse_two)
    d_branch = d_residual.astype(bf16)
    d_attended = nt(d_branch, out_w).astype(bf16)
    own, other = attend_back(d_attended, kv, queries, starts, out_t, log_norms)
    d_scaled = own.astype(f32) + other.astype(f32)
    query_lanes = lanes_of(zeros, ones, zeros, none)
    scale_terms = jnp.sum(d_scaled * wide_full, axis=0) * query_lanes
    scale_terms = jnp.sum(scale_terms.reshape(H, LANES), axis=0)[HD : 2 * HD]
    d_wide = (d_scaled.astype(bf16).astype(f32) * wide_scale).astype(bf16)
    d_normed = nt(d_wide, wide_w)
    input_grad = (
        d_residual + norm_back(d_normed * gain_one, tokens, inverse_one)
    ).astype(bf16)

    def total(values):
        return jnp.sum(values.astype(f32), axis=0)

    d_bias = total(d_wide).reshape(H, LANES)
    vector_grads = jnp.stack(
        [
            total(d_normed * tokens * inverse_one),
            d_bias[:, HD : 2 * HD].reshape(D),
            d_bias[:, 2 * HD : 3 * HD].reshape(D),
            total(d_branch),
            total(d_normed_two * residual * inverse_two),
            total(d_pre),
            total(upstream),
        ]
    )
    vector_grads = jnp.pad(vector_grads, ((0, 9), (0, 0))).astype(bf16)
    scale_tile = jnp.pad(scale_terms.reshape(8, 10), ((0, 8), (112, 6))).astype(bf16)
    one, two = scatter_grads(
        normed, d_wide, attended, d_branch, normed_two, d_pre, activated, upstream_low,
        vector_grads, scale_tile,
    )
    rows = jnp.concatenate(
        [one[w * 10 : w * 10 + 10].reshape(10, 5, LANES) for w in range(3)]
        + [one[30:32].reshape(10, 1, LANES)],
        axis=1,
    )
    d_key_w, d_query_w, d_value_w = [
        rows[:, :, i * HD : (i + 1) * HD].reshape(10, D) for i in range(3)
    ]
    vector = [one[i, 240:250] for i in range(7)]
    scale_grad = one[0:8, 496:506].reshape(HD)
    scale_grad = scale_grad * (LOG2E / math.sqrt(HD)) * jax.nn.sigmoid(dim_scale)
    return (
        layer_out.reshape(2, TOK, D),
        input_grad.reshape(2, TOK, D),
        vector[0],
        d_query_w,
        d_key_w,
        d_value_w,
        vector[1],
        vector[2],
        two[0:10],
        vector[3],
        vector[4],
        two[10:20],
        vector[5],
        two[20:30],
        vector[6],
        scale_grad,
    )


def solution(mesh):
    rows = P(("blk", "head"), None)
    vec = P(("blk", "head"))
    tok = P(None, ("blk", "head"), None)
    in_specs = (
        tok, P(), vec, rows, rows, rows, vec, vec, rows, vec, vec, rows, vec, rows, vec, P(), tok
    )
    out_specs = (
        tok, tok, vec, rows, rows, rows, vec, vec, rows, vec, vec, rows, vec, rows, vec, P()
    )
    return jax.shard_map(
        on_device, mesh=mesh, in_specs=in_specs, out_specs=out_specs, check_vma=False
    )
```

```python
import functools
import math

import jax
import jax.numpy as jnp
import numpy as np
from jax import lax
from jax.experimental import pallas as pl
from jax.experimental.pallas import tpu as pltpu
from jax.sharding import PartitionSpec as P

D = 1280
H = 16
HD = 80
FF = 1280
B = 512
TOK = 64
PAIRS = 32
LANES = 256
ROWS = 32
WIDE = H * LANES
OUT_WIDE = H * 128
GROUP = 80
EPSILON = 1e-06
LOG2E = 1.442695041
NEGATIVE = -1e30
MESH = pl.DeviceIdType.MESH
f32 = jnp.float32
bf16 = jnp.bfloat16

PARTS = (((0, 512), "xyz"), ((512, 384), "yzx"), ((896, 384), "zxy"))
PARTS_TWO = (((0, 640), "xyz"), ((640, 640), "xzy"))


def inverse_rms(values):
    return lax.rsqrt(jnp.mean(values * values, axis=-1, keepdims=True) + EPSILON)


def norm_back(upstream, values, inverse):
    return inverse * upstream - values * inverse**3 * jnp.mean(
        upstream * values, axis=-1, keepdims=True
    )


def nn(a, b):
    return lax.dot_general(a, b, (((1,), (0,)), ((), ())), preferred_element_type=f32)


def nt(a, b):
    return lax.dot_general(a, b, (((1,), (1,)), ((), ())), preferred_element_type=f32)


def tn(a, b):
    return lax.dot_general(a, b, (((0,), (0,)), ((), ())), preferred_element_type=f32)


def my_place():
    blk = lax.axis_index("blk")
    head = lax.axis_index("head")
    return {
        "x": (head % 2) * 2 + (blk // 2) % 2,
        "y": head // 2,
        "z": blk // 4,
        "c": blk % 2,
    }


def device_at(place):
    x, y, z, c = place["x"], place["y"], place["z"], place["c"]
    return (z * 4 + (x % 2) * 2 + c, y * 2 + x // 2)


def chunk_of(ref, place, cols, lead=()):
    blk, head = device_at(place)
    return ref.at[(*lead, blk, pl.ds(head * ROWS, ROWS), cols)]


def moved(place, axis, value):
    other = dict(place)
    other[axis] = value
    return other


def greet(peers):
    barrier = pltpu.get_barrier_semaphore()
    for peer in peers:
        pl.semaphore_signal(barrier, inc=1, device_id=peer, device_id_type=MESH)
    pl.semaphore_wait(barrier, len(peers))


def greet_all():
    barrier = pltpu.get_barrier_semaphore()
    me = lax.axis_index("blk") * 8 + lax.axis_index("head")

    @pl.loop(1, 128)
    def _(k):
        other = (me + k) % 128
        pl.semaphore_signal(
            barrier, inc=1, device_id=(other // 8, other % 8), device_id_type=MESH
        )

    pl.semaphore_wait(barrier, 127)


def ring_peers(place):
    peers = [device_at(moved(place, "c", 1 - place["c"]))]
    for axis in "xyz":
        for step in (1, 3, 2):
            peers.append(device_at(moved(place, axis, (place[axis] + step) % 4)))
    return peers


def wait_bytes(ref, sem):
    pltpu.make_async_copy(ref, ref, sem).wait()


def remote(src, dst, send, recv, device):
    return pltpu.make_async_remote_copy(
        src_ref=src, dst_ref=dst, send_sem=send, recv_sem=recv, device_id=device, device_id_type=MESH
    )


def varied(place, axes, number):
    other = dict(place)
    for axis in axes:
        other[axis] = number % 4
        number = number // 4
    return other


def selections():
    take = np.zeros((3, GROUP, 256), np.float32)
    last = np.zeros((5, GROUP, 256), np.float32)
    for i in range(8):
        for j in range(10):
            for w in range(3):
                take[w, i * 10 + j, i * ROWS + w * 10 + j] = 1
            last[j % 5, i * 10 + j, i * ROWS + 30 + j // 5] = 1
    spread = np.zeros((128, 256), np.float32)
    spread[32:112] = take[0]
    return take, last, spread


TAKE, LAST, SPREAD = selections()
LANE_OF = np.zeros((128, D), np.float32)
LANE_OF[112 + np.arange(D) % 10, np.arange(D)] = 1
ROW_OF = np.zeros((16, D), np.float32)
ROW_OF[np.arange(D) % 10, np.arange(D)] = 1
TENTH = (np.arange(D) // 10).astype(np.int32)
SCALE_ROWS = np.zeros((256, 16), np.float32)
for _i in range(8):
    for _j in range(8):
        SCALE_ROWS[_i * ROWS + _j, _j] = 1


class Gather:
    def __init__(self, parts, buf, send, recv, place):
        self.parts, self.place = parts, place
        self.buf, self.send, self.recv = buf, send, recv
        self.sibling = device_at(moved(place, "c", 1 - place["c"]))

    def begin(self, pack, sem):
        own = pltpu.make_async_copy(
            pack, chunk_of(self.buf, self.place, pl.ds(0, D)), sem
        )
        own.start()
        return own

    def forward(self, part, axes, fixed, count):
        first, width = self.parts[part][0]
        cols = pl.ds(first, width)

        @pl.loop(0, count)
        def _(number):
            where = dict(varied(self.place, axes, number), **fixed)
            piece = chunk_of(self.buf, where, cols)
            remote(
                piece, piece, self.send.at[part, 3], self.recv.at[part, 5], self.sibling
            ).start()

    def stage(self, stage):
        for part, ((first, width), order) in enumerate(self.parts):
            cols = pl.ds(first, width)
            if stage:
                wait_bytes(
                    self.buf.at[0, pl.ds(0, 3 * 4 ** (stage - 1) * ROWS), cols]
                    if stage == 1
                    else self.buf.at[pl.ds(0, 3), pl.ds(0, 4 * ROWS), cols],
                    self.recv.at[part, stage - 1],
                )

            @pl.loop(0, 4**stage)
            def _(number, part=part, cols=cols, order=order):
                piece = chunk_of(self.buf, varied(self.place, order[:stage], number), cols)
                axis = order[stage]
                for step in (1, 3, 2):
                    target = moved(self.place, axis, (self.place[axis] + step) % 4)
                    slot = stage if stage < 2 else 1 + step
                    remote(
                        piece,
                        piece,
                        self.send.at[part, stage],
                        self.recv.at[part, slot],
                        device_at(target),
                    ).start()

        for part, (_, order) in enumerate(self.parts):
            if stage == 0:
                self.forward(part, "", {}, 1)
            else:
                axis = order[stage - 1]
                for step in (1, 3, 2):
                    self.forward(
                        part,
                        order[: stage - 1],
                        {axis: (self.place[axis] + 4 - step) % 4},
                        4 ** (stage - 1),
                    )

    def finish(self):
        for step in (1, 3, 2):
            for part, ((first, width), order) in enumerate(self.parts):
                wait_bytes(
                    self.buf.at[pl.ds(0, 2), :, pl.ds(first, width)],
                    self.recv.at[part, 1 + step],
                )
                axis = order[2]
                self.forward(
                    part, order[:2], {axis: (self.place[axis] + 4 - step) % 4}, 16
                )
        for part, ((first, width), order) in enumerate(self.parts):
            cols = pl.ds(first, width)
            half = self.buf.at[pl.ds(0, 8), :, cols]
            wait_bytes(half, self.recv.at[part, 5])
            wait_bytes(half, self.send.at[part, 3])
            wait_bytes(self.buf.at[0, pl.ds(0, 3 * ROWS), cols], self.send.at[part, 0])
            wait_bytes(
                self.buf.at[pl.ds(0, 3), pl.ds(0, 4 * ROWS), cols], self.send.at[part, 1]
            )
            wait_bytes(self.buf.at[pl.ds(0, 6), :, cols], self.send.at[part, 2])


def row_block(ref, g, count):
    return ref.at[pl.ds(pl.multiple_of(g * count, 16), count)]


def gather_kernel(
    pack, take, last, lane_of, row_of, tenth_row, tenth_col, wide, vectors,
    buf, vec_tile, staged, send, recv, own_sem, out_sem,
):
    place = my_place()
    gather = Gather(PARTS, buf, send, recv, place)
    own = gather.begin(pack, own_sem)
    greet(ring_peers(place))
    own.wait()
    for stage in range(3):
        gather.stage(stage)
    gather.finish()

    @pl.loop(0, 16)
    def _(g):
        slot = g % 2
        out = pltpu.make_async_copy(staged.at[slot], row_block(wide, g, GROUP), out_sem.at[slot])

        @pl.when(g >= 2)
        def _():
            out.wait()

        for w in range(3):
            staged[slot, :, w * D : (w + 1) * D] = nn(take[w], buf[g]).astype(bf16)
        head = jnp.zeros((GROUP, LANES), f32)
        for cell in range(5):
            head = head + nn(last[cell], buf[g, :, cell * LANES : (cell + 1) * LANES])
        staged[slot, :, 3 * D :] = head.astype(bf16)
        vec_tile[pl.ds(pl.multiple_of(g * GROUP, 16), GROUP)] = staged[slot, :, 128:256]
        out.start()

    spread_out = nn(vec_tile[...], lane_of[...])
    spread_out = jnp.where(tenth_col[...] == tenth_row[...], spread_out, 0.0).astype(bf16)
    vectors[...] = nn(row_of[...], spread_out)
    for slot in range(2):
        pltpu.make_async_copy(staged.at[slot], row_block(wide, 0, GROUP), out_sem.at[slot]).wait()


VMEM = pl.BlockSpec(memory_space=pltpu.VMEM)
HBM = pl.BlockSpec(memory_space=pl.ANY)


def gather_semaphores(parts):
    return [pltpu.SemaphoreType.DMA((parts, 4)), pltpu.SemaphoreType.DMA((parts, 6))]


def gather_weights(pack):
    return pl.pallas_call(
        gather_kernel,
        out_shape=(
            jax.ShapeDtypeStruct((D, WIDE), bf16),
            jax.ShapeDtypeStruct((16, D), f32),
        ),
        in_specs=[VMEM] * 7,
        out_specs=(HBM, VMEM),
        scratch_shapes=[
            pltpu.VMEM((16, 256, D), bf16),
            pltpu.VMEM((D, 128), bf16),
            pltpu.VMEM((2, GROUP, WIDE), bf16),
        ]
        + gather_semaphores(3)
        + [
            pltpu.SemaphoreType.DMA,
            pltpu.SemaphoreType.DMA((2,)),
        ],
        compiler_params=pltpu.CompilerParams(
            collective_id=0, has_side_effects=True, vmem_limit_bytes=40 * 2**20
        ),
        name="gather_weights",
    )(
        pack,
        jnp.asarray(TAKE, bf16),
        jnp.asarray(LAST, bf16),
        jnp.asarray(LANE_OF, bf16),
        jnp.asarray(ROW_OF, bf16),
        jnp.asarray(TENTH[None, :]),
        jnp.asarray(TENTH[:, None]),
    )


def unpack_two(buf, staged, spread, take, out_w, hidden_w, proj_w, out_sem):
    spans = ((0, 128, out_w), (128, GROUP, hidden_w), (208, GROUP, proj_w))

    @pl.loop(0, 16)
    def _(g):
        slot = g % 2
        outs = [
            pltpu.make_async_copy(
                staged.at[slot, pl.ds(at, count)], row_block(ref, g, count), out_sem.at[i, slot]
            )
            for i, (at, count, ref) in enumerate(spans)
        ]

        @pl.when(g >= 2)
        def _():
            for out in outs:
                out.wait()

        staged[slot, 0:128] = nn(spread[...], buf[g]).astype(bf16)
        staged[slot, 128:208] = nn(take[1], buf[g]).astype(bf16)
        staged[slot, 208:288] = nn(take[2], buf[g]).astype(bf16)
        for out in outs:
            out.start()

    for slot in range(2):
        for i, (at, count, ref) in enumerate(spans):
            pltpu.make_async_copy(
                staged.at[slot, pl.ds(at, count)], row_block(ref, 0, count), out_sem.at[i, slot]
            ).wait()


class Scatter:
    def __init__(self, parts, away, mine, pair, lands, halves, send, recv, place):
        self.parts = parts
        self.away, self.mine, self.pair = away, mine, pair
        self.lands, self.halves = lands, halves
        self.send, self.recv, self.place = send, recv, place
        self.sibling = device_at(moved(place, "c", 1 - place["c"]))

    def swap(self, number):
        return remote(
            self.away.at[number],
            self.pair.at[number],
            self.send.at[len(self.parts), number],
            self.recv.at[len(self.parts), number],
            self.sibling,
        )

    def add_pair(self, number):
        self.swap(number).wait()
        self.mine[number] = (
            self.mine[number].astype(f32) + self.pair[number].astype(f32)
        ).astype(bf16)

    def own_piece(self, where, cols):
        half = where["z"] * 2 + where["x"] % 2
        return self.mine.at[half, pl.ds((where["y"] * 2 + where["x"] // 2) * ROWS, ROWS), cols]

    def start(self, stage):
        for part, ((first, width), order) in enumerate(self.parts):
            cols = pl.ds(first, width)
            axis = order[2 - stage]
            rest = order[: 2 - stage]

            @pl.loop(0, 16 // 4**stage)
            def _(number, part=part, cols=cols, axis=axis, rest=rest):
                for step in (1, 3, 2):
                    target = moved(self.place, axis, (self.place[axis] + step) % 4)
                    if stage == 0:
                        source = self.own_piece(varied(target, rest, number), cols)
                    elif stage == 1:
                        source = self.halves[0].at[target[axis], number, :, cols]
                    else:
                        source = self.halves[1].at[target[axis], :, cols]
                    remote(
                        source,
                        self.lands[stage].at[step - 1, number, :, cols],
                        self.send.at[part, stage],
                        self.recv.at[part, stage],
                        device_at(target),
                    ).start()

    def add(self, stage, out=None):
        for part, ((first, width), order) in enumerate(self.parts):
            cols = pl.ds(first, width)
            axis = order[2 - stage]
            rest = order[: 2 - stage]
            wait_bytes(self.lands[stage].at[:, :, :, cols], self.recv.at[part, stage])

            @pl.loop(0, 16 // 4**stage)
            def _(number, cols=cols, axis=axis, rest=rest):
                if stage == 0:
                    total = self.own_piece(varied(self.place, rest, number), cols)[...]
                elif stage == 1:
                    total = self.halves[0][self.place[axis], number, :, cols]
                else:
                    total = self.halves[1][self.place[axis], :, cols]
                total = total.astype(f32)
                for source in range(3):
                    total = total + self.lands[stage][source, number, :, cols].astype(f32)
                if stage == 0:
                    self.halves[0][number // 4, number % 4, :, cols] = total.astype(bf16)
                elif stage == 1:
                    self.halves[1][number, :, cols] = total.astype(bf16)
                else:
                    out[:, cols] = total

    def finish(self):
        for stage in range(3):
            for part, ((first, width), order) in enumerate(self.parts):
                wait_bytes(
                    self.lands[stage].at[:, :, :, pl.ds(first, width)], self.send.at[part, stage]
                )


def scatter_scratch(parts):
    return [
        pltpu.VMEM((8, 256, D), bf16),
        pltpu.VMEM((8, 256, D), bf16),
        pltpu.VMEM((8, 256, D), bf16),
        pltpu.VMEM((3, 16, ROWS, D), bf16),
        pltpu.VMEM((3, 4, ROWS, D), bf16),
        pltpu.VMEM((3, 1, ROWS, D), bf16),
        pltpu.VMEM((4, 4, ROWS, D), bf16),
        pltpu.VMEM((4, ROWS, D), bf16),
        pltpu.SemaphoreType.DMA((parts + 1, 8)),
        pltpu.SemaphoreType.DMA((parts + 1, 8)),
    ]


def scatter_of(parts, scratch, place):
    away, mine, pair, l0, l1, l2, h0, h1, send, recv = scratch
    return Scatter(parts, away, mine, pair, (l0, l1, l2), (h0, h1), send, recv, place)


def scatter_kernel(
    normed, d_wide, vector_grads, scale_tile,
    take_t, last_t, lane_of_t, row_of_t, scale_rows, tenth_row, tenth_col,
    out, normed_t, right, vec_tile, *scratch,
):
    place = my_place()
    scatter = scatter_of(PARTS, scratch, place)
    for n in range(D // 128):
        lanes = slice(n * 128, n * 128 + 128)
        normed_t[lanes] = normed[:, lanes].T
    for w in range(3):
        right[w * 128 : w * 128 + 128] = d_wide[:, w * D : (w + 1) * D]
    for cell in range(5):
        right[384:512, cell * LANES : (cell + 1) * LANES] = d_wide[:, 3 * D :]
    by_row = nn(row_of_t[...], vector_grads[...])
    by_row = jnp.where(tenth_col[...] == tenth_row[...], by_row, 0.0).astype(bf16)
    vec_tile[...] = nn(by_row, lane_of_t[...]).astype(bf16)
    greet(ring_peers(place))

    def produce(number, core, into):
        group = number * 2 + core
        rows = pl.ds(pl.multiple_of(group * GROUP, 16), GROUP)
        piece = normed_t[rows]
        lefts = [nn(take_t[w], piece).astype(bf16) for w in range(3)]
        for cell in range(5):
            left = jnp.concatenate(lefts + [nn(last_t[cell], piece).astype(bf16)], axis=1)
            lanes = slice(cell * LANES, (cell + 1) * LANES)
            block = nn(left, right[:, lanes])
            if cell == 0:
                block = block + jnp.concatenate(
                    [jnp.zeros((256, 128), f32), nn(take_t[0], vec_tile[rows])], axis=1
                )
            if cell == 1:
                block = block + jnp.concatenate(
                    [jnp.zeros((256, 128), f32), nn(scale_rows[...], scale_tile[...])], axis=1
                )
            into[number, :, lanes] = block.astype(bf16)

    @pl.loop(0, 8)
    def _(number):
        produce(number, 1 - place["c"], scatter.away)
        scatter.swap(number).start()

    @pl.loop(0, 8)
    def _(number):
        produce(number, place["c"], scatter.mine)
        scatter.add_pair(number)

    for stage in range(3):
        scatter.start(stage)
        scatter.add(stage, out)
    scatter.finish()


def scatter_grads(*operands):
    return pl.pallas_call(
        scatter_kernel,
        out_shape=jax.ShapeDtypeStruct((ROWS, D), f32),
        in_specs=[VMEM] * 11,
        out_specs=VMEM,
        scratch_shapes=[
            pltpu.VMEM((D, 128), bf16),
            pltpu.VMEM((512, D), bf16),
            pltpu.VMEM((D, 128), bf16),
        ]
        + scatter_scratch(3),
        compiler_params=pltpu.CompilerParams(
            collective_id=3, has_side_effects=True, vmem_limit_bytes=48 * 2**20
        ),
        name="scatter_grads",
    )(
        *operands,
        jnp.asarray(TAKE.transpose(0, 2, 1), bf16),
        jnp.asarray(LAST.transpose(0, 2, 1), bf16),
        jnp.asarray(LANE_OF.T, bf16),
        jnp.asarray(ROW_OF.T, bf16),
        jnp.asarray(SCALE_ROWS, bf16),
        jnp.asarray(TENTH[None, :]),
        jnp.asarray(TENTH[:, None]),
    )


def quarter_of(blk):
    inner = blk % 4
    return jnp.where((blk // 4) % 2 == 0, inner, 3 - inner)


def query_block(quarter, j):
    return j * 4 + jnp.where(j % 2 == 0, quarter, 3 - quarter)


def chip_block(x_low, n):
    z = n // 2
    return z * 4 + 2 * ((z + x_low) % 2) + n % 2


def cell_of(ref, pair, width):
    return ref.at[pl.ds(pair // H * TOK, TOK), pl.ds(pair % H * width, width)]


def mask_of(key_block, block, start):
    key_at = key_block * B + lax.broadcasted_iota(jnp.int32, (B, B), 0)
    query_at = block * B + lax.broadcasted_iota(jnp.int32, (B, B), 1)
    return (key_at >= start) & (key_at <= query_at)


def has_mask(key_block, block):
    return (key_block == 0) | (key_block == block) | (block == 15)


def shift_matrix(rows, cols, by):
    row = lax.broadcasted_iota(jnp.int32, (rows, cols), 0)
    col = lax.broadcasted_iota(jnp.int32, (rows, cols), 1)
    return jnp.where((row - col == by) & (jnp.minimum(row, col) < HD), 1.0, 0.0).astype(bf16)


def wait_cells(ref, sem, fewer, width):
    wait_bytes(ref.at[:, pl.ds(0, 15 * width)], sem)
    wait_bytes(cell_of(ref, 0, width), sem)

    @pl.when(jnp.logical_not(fewer))
    def _():
        wait_bytes(cell_of(ref, 0, width), sem)


def forward_kernel(
    pack, starts, pack_two, spread, take,
    kv_out, queries, out_t, log_norms, attended, out_w, hidden_w, proj_w,
    kv, value_t, tops, totals, rounded, landed, buf, staged,
    two_send, two_recv, send, recv, core_send, core_recv, x_send, x_recv,
    pass_send, pass_recv, back_send, back_recv, kv_sem, own_sem, out_sem,
):
    blk = lax.axis_index("blk")
    head = lax.axis_index("head")
    core = blk % 2
    x_low = (blk // 2) % 2
    quarter = blk % 4
    pair = (blk // 4) * 8 + head
    to_quarter = quarter_of(blk)
    even = (blk // 4) % 2 == 0
    place = my_place()
    two = Gather(PARTS_TWO, buf, two_send, two_recv, place)
    own = two.begin(pack_two, own_sem)
    greet_all()

    @pl.loop(0, PAIRS)
    def _(k):
        p = (pair + k) % PAIRS
        src = cell_of(pack, p, LANES)
        dst = kv.at[blk, pl.ds(head * TOK, TOK)]
        mine = (k == 0) & even

        @pl.when(mine)
        def _():
            pltpu.make_async_copy(src, dst, recv).start()

        @pl.when(jnp.logical_not(mine))
        def _():
            remote(src, dst, send, recv, ((p // 8) * 4 + to_quarter, p % 8)).start()

    own.wait()
    two.stage(0)
    sibling = (blk + 1 - 2 * core, head)
    partner = (blk + 2 - 4 * x_low, head)
    wait_bytes(kv.at[pl.ds(0, 4)], recv)

    @pl.loop(0, 4)
    def _(j):
        block = kv.at[query_block(quarter, j)]
        remote(block, block, core_send, core_recv, sibling).start()
        remote(block, block, x_send, x_recv, partner).start()

    two.stage(1)
    pick = shift_matrix(LANES, 128, HD)

    @pl.loop(0, 4)
    def _(j):
        queries[j] = nn(kv[query_block(quarter, j)], pick).astype(bf16)
        tops[j] = jnp.full((1, B), NEGATIVE, f32)
        totals[j] = jnp.zeros((1, B), f32)
        out_t[j] = jnp.zeros((128, B), f32)

    wait_bytes(kv.at[pl.ds(0, 4)], core_recv)

    @pl.loop(0, 8)
    def _(n):
        b = chip_block(x_low, n)
        value_t[b] = kv[b, :, 128:].T

    two.stage(2)

    def step(j, block, key_block):
        def tile(masked):
            s = nt(kv[key_block, :, :128], queries[j])
            if masked:
                s = jnp.where(mask_of(key_block, block, starts[j]), s, NEGATIVE)
            top = tops[j]
            new_top = jnp.maximum(top, jnp.max(s, axis=0, keepdims=True))
            p = jnp.exp(s - new_top)
            scale = jnp.exp(top - new_top)
            tops[j] = new_top
            totals[j] = totals[j] * scale + jnp.sum(p, axis=0, keepdims=True)
            out_t[j] = out_t[j] * scale + nn(value_t[key_block], p.astype(bf16))

        masked = has_mask(key_block, block)
        pl.when(masked)(lambda: tile(True))
        pl.when(jnp.logical_not(masked))(lambda: tile(False))

    @pl.loop(0, 4)
    def _(j):
        block = query_block(quarter, j)

        @pl.loop(0, 2 * j + block % 2 + 1)
        def _(n):
            step(j, block, chip_block(x_low, n))

    wait_bytes(kv.at[pl.ds(0, 4)], x_recv)

    @pl.loop(0, 4)
    def _(j):
        block = kv.at[query_block((quarter + 2) % 4, j)]
        remote(block, block, pass_send, pass_recv, sibling).start()

    wait_bytes(kv.at[pl.ds(0, 4)], pass_recv)
    keep = pltpu.make_async_copy(kv, kv_out, kv_sem)
    keep.start()

    @pl.loop(0, 8)
    def _(n):
        b = chip_block(1 - x_low, n)
        value_t[b] = kv[b, :, 128:].T

    @pl.loop(0, 4)
    def _(i):
        j = 3 - i
        block = query_block(quarter, j)

        @pl.loop(0, 2 * j + 2 * ((j + x_low) % 2))
        def _(n):
            step(j, block, chip_block(1 - x_low, n))

        acc = out_t[j]
        result = acc / acc[112:113]
        out_t[j] = result
        log_norms[j] = tops[j] + jnp.log(totals[j])
        rounded[j] = result.T.astype(bf16)

        @pl.loop(0, 8)
        def _(k):
            h = (head + k) % 8
            src = rounded.at[j, pl.ds(h * TOK, TOK)]
            dst = cell_of(landed, pair, 128)
            mine = (k == 0) & (block == blk)

            @pl.when(mine)
            def _():
                pltpu.make_async_copy(src, dst, back_recv).start()

            @pl.when(jnp.logical_not(mine))
            def _():
                remote(src, dst, back_send, back_recv, (block, h)).start()

    two.finish()
    unpack_two(buf, staged, spread, take, out_w, hidden_w, proj_w, out_sem)
    wait_bytes(landed, back_recv)
    attended[...] = landed[...]
    keep.wait()
    for sem in (core_send, x_send, pass_send):
        wait_bytes(kv.at[pl.ds(0, 4)], sem)
    wait_cells(pack, send, even, LANES)
    wait_cells(landed, back_send, even, 128)


def attend(pack, starts, pack_two):
    return pl.pallas_call(
        forward_kernel,
        out_shape=(
            jax.ShapeDtypeStruct((16, B, LANES), bf16),
            jax.ShapeDtypeStruct((4, B, 128), bf16),
            jax.ShapeDtypeStruct((4, 128, B), f32),
            jax.ShapeDtypeStruct((4, 1, B), f32),
            jax.ShapeDtypeStruct((2 * TOK, OUT_WIDE), bf16),
            jax.ShapeDtypeStruct((OUT_WIDE, D), bf16),
            jax.ShapeDtypeStruct((D, D), bf16),
            jax.ShapeDtypeStruct((D, D), bf16),
        ),
        in_specs=[VMEM] * 5,
        out_specs=(HBM, VMEM, VMEM, VMEM, VMEM, HBM, HBM, HBM),
        scratch_shapes=[
            pltpu.VMEM((16, B, LANES), bf16),
            pltpu.VMEM((16, 128, B), bf16),
            pltpu.VMEM((4, 1, B), f32),
            pltpu.VMEM((4, 1, B), f32),
            pltpu.VMEM((4, B, 128), bf16),
            pltpu.VMEM((2 * TOK, OUT_WIDE), bf16),
            pltpu.VMEM((16, 256, D), bf16),
            pltpu.VMEM((2, 288, D), bf16),
        ]
        + gather_semaphores(2)
        + [pltpu.SemaphoreType.DMA] * 12
        + [pltpu.SemaphoreType.DMA((3, 2))],
        compiler_params=pltpu.CompilerParams(
            collective_id=1, has_side_effects=True, vmem_limit_bytes=48 * 2**20
        ),
        name="attend",
    )(pack, starts, pack_two, jnp.asarray(SPREAD, bf16), jnp.asarray(TAKE, bf16))


def backward_kernel(
    pack, kv, queries, starts, out_t, log_norms,
    attended, d_branch, normed_two, d_pre, activated, upstream, take_t,
    wide_out, two_out,
    d_out, key_t, deltas, d_query, d_kv, mine_kv, half, half_in, cross, cross_in, final, landed,
    attended_t, normed_two_t, activated_t, right,
    send, recv, core_send, core_recv, x_send, x_recv, back_send, back_recv,
    *scratch,
):
    blk = lax.axis_index("blk")
    head = lax.axis_index("head")
    core = blk % 2
    x_low = (blk // 2) % 2
    quarter = blk % 4
    pair = (blk // 4) * 8 + head
    to_quarter = quarter_of(blk)
    even = (blk // 4) % 2 == 0
    place = my_place()
    two = scatter_of(PARTS_TWO, scratch, place)
    greet_all()

    @pl.loop(0, PAIRS)
    def _(k):
        p = (pair + k) % PAIRS
        src = cell_of(pack, p, 128)
        dst = d_out.at[blk // 4, pl.ds(head * TOK, TOK)]
        mine = (k == 0) & even

        @pl.when(mine)
        def _():
            pltpu.make_async_copy(src, dst, recv).start()

        @pl.when(jnp.logical_not(mine))
        def _():
            remote(src, dst, send, recv, ((p // 8) * 4 + to_quarter, p % 8)).start()

    for n in range(D // 128):
        lanes = slice(n * 128, n * 128 + 128)
        normed_two_t[lanes] = normed_two[:, lanes].T
        activated_t[lanes] = activated[:, lanes].T
    for n in range(H):
        lanes = slice(n * 128, n * 128 + 128)
        attended_t[lanes] = attended[:, lanes].T
    right[0:128] = d_branch[...]
    right[128:256] = d_pre[...]
    right[256:384] = upstream[...]

    def produce(number, of_core, into):
        group = number * 2 + of_core
        rows = pl.ds(pl.multiple_of(group * GROUP, 16), GROUP)
        out_rows = pl.ds(pl.multiple_of(group * 128 + 32, 16), GROUP)
        left = jnp.concatenate(
            [
                nn(take_t[0], attended_t[out_rows]).astype(bf16),
                nn(take_t[1], normed_two_t[rows]).astype(bf16),
                nn(take_t[2], activated_t[rows]).astype(bf16),
            ],
            axis=1,
        )
        for cell in range(5):
            lanes = slice(cell * LANES, (cell + 1) * LANES)
            into[number, :, lanes] = nn(left, right[:, lanes]).astype(bf16)

    @pl.loop(0, 8)
    def _(number):
        produce(number, 1 - core, two.away)
        two.swap(number).start()

    @pl.loop(0, 8)
    def _(number):
        produce(number, core, two.mine)

    @pl.loop(0, 16)
    def _(b):
        key_t[b] = kv[b, :, :128].T

    @pl.loop(0, 8)
    def _(number):
        two.add_pair(number)

    two.start(0)
    wait_bytes(d_out, recv)

    @pl.loop(0, 4)
    def _(j):
        deltas[j] = jnp.sum(d_out[j].astype(f32).T * out_t[j], axis=0, keepdims=True)
        d_query[j] = jnp.zeros((128, B), f32)

    sibling = (blk + 1 - 2 * core, head)
    partner = (blk + 2 - 4 * x_low, head)

    def step(j, block, key_block):
        def tile(masked):
            q = queries[j]
            do = d_out[j]
            p = jnp.exp(nt(kv[key_block, :, :128], q) - log_norms[j])
            if masked:
                p = jnp.where(mask_of(key_block, block, starts[j]), p, 0.0)
            dp = nt(kv[key_block, :, 128:], do)
            ds = (p * (dp - deltas[j])).astype(bf16)
            d_kv[:, :128] += nn(ds, q)
            d_kv[:, 128:] += nn(p.astype(bf16), do)
            d_query[j] += nn(key_t[key_block], ds)

        masked = has_mask(key_block, block)
        pl.when(masked)(lambda: tile(True))
        pl.when(jnp.logical_not(masked))(lambda: tile(False))

    def swap(n):
        return remote(
            half.at[n], half_in.at[n], core_send.at[n], core_recv.at[n], sibling
        )

    def cross_swap(z):
        return remote(cross.at[z], cross_in.at[z], x_send.at[z], x_recv.at[z], partner)

    def own_number(z):
        return 2 * z + (x_low + z) % 2

    def core_sum(z):
        own = own_number(z)
        other = 4 * z + 1 - own
        swap(other).wait()
        cross[z] = (mine_kv[other] + half_in[other].astype(f32)).astype(bf16)
        cross_swap(z).start()
        swap(own).wait()
        mine_kv[own] = mine_kv[own] + half_in[own].astype(f32)

    shift = shift_matrix(128, LANES, -HD)

    def finish(z):
        block = query_block(quarter, z)
        cross_swap(z).wait()
        final[z] = (
            mine_kv[own_number(z)]
            + cross_in[z].astype(f32)
            + nn(d_query[z].T.astype(bf16), shift)
        ).astype(bf16)

        @pl.loop(0, 8)
        def _(k):
            h = (head + k) % 8
            src = final.at[z, pl.ds(h * TOK, TOK)]
            dst = cell_of(landed, pair, LANES)
            mine = (k == 0) & (block == blk)

            @pl.when(mine)
            def _():
                pltpu.make_async_copy(src, dst, back_recv).start()

            @pl.when(jnp.logical_not(mine))
            def _():
                remote(src, dst, back_send, back_recv, (block, h)).start()

    @pl.loop(0, 8)
    def _(part):
        z = part // 2

        @pl.loop(2 * part, 2 * part + 2)
        def _(key_block):
            d_kv[...] = jnp.zeros((B, LANES), f32)
            first = z + (query_block(quarter, z) < key_block).astype(jnp.int32)

            @pl.loop(first, 4)
            def _(j):
                step(j, query_block(quarter, j), key_block)

            n = 2 * z + (key_block % 4) // 2

            @pl.when((key_block + z + core) % 2 == 0)
            def _():
                mine_kv[n] = d_kv[...]

            @pl.when((key_block + z + core) % 2 == 1)
            def _():
                half[n] = d_kv[...].astype(bf16)
                swap(n).start()

        @pl.when((part % 2 == 0) & (part > 0))
        def _():
            core_sum(z - 1)

        @pl.when((part % 2 == 1) & (part > 1))
        def _():
            finish(z - 1)

        @pl.when(part == 4)
        def _():
            two.add(0)
            two.start(1)

        @pl.when(part == 6)
        def _():
            two.add(1)
            two.start(2)

    core_sum(3)
    two.add(2, two_out)
    finish(3)
    two.finish()
    wait_bytes(landed, back_recv)
    wide_out[...] = landed[...]
    wait_cells(pack, send, even, 128)
    wait_cells(landed, back_send, even, LANES)


def attend_back(*operands):
    return pl.pallas_call(
        backward_kernel,
        out_shape=(
            jax.ShapeDtypeStruct((2 * TOK, WIDE), bf16),
            jax.ShapeDtypeStruct((ROWS, D), f32),
        ),
        in_specs=[VMEM] * 13,
        out_specs=(VMEM, VMEM),
        scratch_shapes=[
            pltpu.VMEM((4, B, 128), bf16),
            pltpu.VMEM((16, 128, B), bf16),
            pltpu.VMEM((4, 1, B), f32),
            pltpu.VMEM((4, 128, B), f32),
            pltpu.VMEM((B, LANES), f32),
            pltpu.VMEM((8, B, LANES), f32),
            pltpu.VMEM((8, B, LANES), bf16),
            pltpu.VMEM((8, B, LANES), bf16),
            pltpu.VMEM((4, B, LANES), bf16),
            pltpu.VMEM((4, B, LANES), bf16),
            pltpu.VMEM((4, B, LANES), bf16),
            pltpu.VMEM((2 * TOK, WIDE), bf16),
            pltpu.VMEM((OUT_WIDE, 128), bf16),
            pltpu.VMEM((D, 128), bf16),
            pltpu.VMEM((D, 128), bf16),
            pltpu.VMEM((384, D), bf16),
            pltpu.SemaphoreType.DMA,
            pltpu.SemaphoreType.DMA,
            pltpu.SemaphoreType.DMA((8,)),
            pltpu.SemaphoreType.DMA((8,)),
            pltpu.SemaphoreType.DMA((4,)),
            pltpu.SemaphoreType.DMA((4,)),
            pltpu.SemaphoreType.DMA,
            pltpu.SemaphoreType.DMA,
        ]
        + scatter_scratch(2),
        compiler_params=pltpu.CompilerParams(
            collective_id=2, has_side_effects=True, vmem_limit_bytes=60 * 2**20
        ),
        name="attend_back",
    )(*operands, jnp.asarray(TAKE.transpose(0, 2, 1), bf16))


def on_device(
    inputs,
    segment_ids,
    norm1_gain,
    w_query,
    w_key,
    w_value,
    query_bias,
    value_bias,
    w_out,
    out_bias,
    norm2_gain,
    w_hidden,
    hidden_bias,
    w_proj,
    proj_bias,
    dim_scale,
    cotangent,
):
    blk = lax.axis_index("blk")
    vectors = jnp.stack(
        [norm1_gain, query_bias, value_bias, out_bias, norm2_gain, hidden_bias, proj_bias]
    )
    spare = jnp.pad(vectors[:, None], ((0, 3), (0, H - 1), (0, 6)))
    rows = jnp.concatenate(
        [w.reshape(10, H, HD) for w in (w_key, w_query, w_value)] + [spare], axis=2
    )
    pack_one = jnp.concatenate(
        [rows[:, w * 5 : w * 5 + 5].reshape(10, D) for w in range(3)]
        + [rows[:, 15].reshape(2, D)],
        axis=0,
    )
    pack_two = jnp.concatenate([w_out, w_hidden, w_proj, jnp.zeros((2, D), bf16)], axis=0)
    wide_w, every = gather_weights(pack_one)
    gain_one, query_b, value_b, out_b, gain_two, hidden_b, proj_b = [every[i] for i in range(7)]

    micro = blk // 8
    segment_row = lax.dynamic_index_in_dim(segment_ids, micro, 0, keepdims=False)
    starts = jnp.zeros_like(segment_row)
    for value in range(1, 9):
        before = jnp.sum((segment_row < value).astype(jnp.int32))
        starts = jnp.where(segment_row == value, before, starts)
    quarter = blk % 4
    starts = starts.reshape(16, 1, B)
    starts = jnp.stack([starts[query_block(quarter, j)] for j in range(4)])

    def lanes_of(key, query, value, spare_lanes):
        parts = [jnp.broadcast_to(part.reshape(-1, HD), (H, HD)) for part in (key, query, value)]
        return jnp.concatenate(parts + [jnp.broadcast_to(spare_lanes, (H, 16))], 1).reshape(WIDE)

    tokens = inputs.reshape(2 * TOK, D).astype(f32)
    inverse_one = inverse_rms(tokens)
    normed = (tokens * inverse_one * gain_one).astype(bf16)
    softplus_scale = LOG2E / math.sqrt(HD) * jax.nn.softplus(dim_scale)
    ones = jnp.ones((HD,), f32)
    zeros = jnp.zeros((HD,), f32)
    none = jnp.zeros((16,), f32)
    wide_bias = lanes_of(zeros, query_b, value_b, none)
    wide_scale = lanes_of(ones, softplus_scale, ones, none)
    wide_one = lanes_of(zeros, zeros, zeros, none.at[0].set(1.0))
    wide_full = nn(normed, wide_w) + wide_bias
    packed = (wide_full * wide_scale + wide_one).astype(bf16)
    kv, queries, out_t, log_norms, attended, out_w, hidden_w, proj_w = attend(
        packed, starts, pack_two
    )

    residual = tokens + nn(attended, out_w) + out_b
    inverse_two = inverse_rms(residual)
    normed_two = (residual * inverse_two * gain_two).astype(bf16)
    pre_act = nn(normed_two, hidden_w) + hidden_b
    gate = jax.nn.sigmoid(pre_act)
    activated = (pre_act * gate).astype(bf16)
    layer_out = (residual + nn(activated, proj_w) + proj_b).astype(bf16)

    upstream_low = cotangent.reshape(2 * TOK, D)
    upstream = upstream_low.astype(f32)
    d_pre = (nt(upstream_low, proj_w) * gate * (1.0 + pre_act * (1.0 - gate))).astype(bf16)
    d_normed_two = nt(d_pre, hidden_w)
    d_residual = upstream + norm_back(d_normed_two * gain_two, residual, inverse_two)
    d_branch = d_residual.astype(bf16)
    d_attended = nt(d_branch, out_w).astype(bf16)
    d_scaled, two = attend_back(
        d_attended, kv, queries, starts, out_t, log_norms,
        attended, d_branch, normed_two, d_pre, activated, upstream_low,
    )
    d_scaled = d_scaled.astype(f32)
    query_lanes = lanes_of(zeros, ones, zeros, none)
    scale_terms = jnp.sum(d_scaled * wide_full, axis=0) * query_lanes
    scale_terms = jnp.sum(scale_terms.reshape(H, LANES), axis=0)[HD : 2 * HD]
    d_wide = (d_scaled * wide_scale).astype(bf16)
    d_normed = nt(d_wide, wide_w)
    input_grad = (
        d_residual + norm_back(d_normed * gain_one, tokens, inverse_one)
    ).astype(bf16)

    def total(values):
        return jnp.sum(values.astype(f32), axis=0)

    d_bias = total(d_wide).reshape(H, LANES)
    vector_grads = jnp.stack(
        [
            total(d_normed * tokens * inverse_one),
            d_bias[:, HD : 2 * HD].reshape(D),
            d_bias[:, 2 * HD : 3 * HD].reshape(D),
            total(d_branch),
            total(d_normed_two * residual * inverse_two),
            total(d_pre),
            total(upstream),
        ]
    )
    vector_grads = jnp.pad(vector_grads, ((0, 9), (0, 0))).astype(bf16)
    scale_tile = jnp.pad(scale_terms.reshape(8, 10), ((0, 8), (112, 6))).astype(bf16)
    one = scatter_grads(normed, d_wide, vector_grads, scale_tile)
    rows = jnp.concatenate(
        [one[w * 10 : w * 10 + 10].reshape(10, 5, LANES) for w in range(3)]
        + [one[30:32].reshape(10, 1, LANES)],
        axis=1,
    )
    d_key_w, d_query_w, d_value_w = [
        rows[:, :, i * HD : (i + 1) * HD].reshape(10, D) for i in range(3)
    ]
    vector = [one[i, 240:250] for i in range(7)]
    scale_grad = one[0:8, 496:506].reshape(HD)
    scale_grad = scale_grad * (LOG2E / math.sqrt(HD)) * jax.nn.sigmoid(dim_scale)
    return (
        layer_out.reshape(2, TOK, D),
        input_grad.reshape(2, TOK, D),
        vector[0],
        d_query_w,
        d_key_w,
        d_value_w,
        vector[1],
        vector[2],
        two[0:10],
        vector[3],
        vector[4],
        two[10:20],
        vector[5],
        two[20:30],
        vector[6],
        scale_grad,
    )


def solution(mesh):
    rows = P(("blk", "head"), None)
    vec = P(("blk", "head"))
    tok = P(None, ("blk", "head"), None)
    in_specs = (
        tok, P(), vec, rows, rows, rows, vec, vec, rows, vec, vec, rows, vec, rows, vec, P(), tok
    )
    out_specs = (
        tok, tok, vec, rows, rows, rows, vec, vec, rows, vec, vec, rows, vec, rows, vec, P()
    )
    return jax.shard_map(
        on_device, mesh=mesh, in_specs=in_specs, out_specs=out_specs, check_vma=False
    )
```

```python
import functools
import math

import jax
import jax.numpy as jnp
import numpy as np
from jax import lax
from jax.experimental import pallas as pl
from jax.experimental.pallas import tpu as pltpu
from jax.sharding import PartitionSpec as P

D = 1280
H = 16
HD = 80
FF = 1280
B = 512
TOK = 64
PAIRS = 32
LANES = 256
ROWS = 32
WIDE = H * LANES
OUT_WIDE = H * 128
GROUP = 80
CHUNK = 96
MINE = 512
EPSILON = 1e-06
LOG2E = 1.442695041
NEGATIVE = -1e30
MESH = pl.DeviceIdType.MESH
f32 = jnp.float32
bf16 = jnp.bfloat16

PARTS = (((0, 640), "xyz"), ((640, 640), "xzy"))


def inverse_rms(values):
    return lax.rsqrt(jnp.mean(values * values, axis=-1, keepdims=True) + EPSILON)


def norm_back(upstream, values, inverse):
    return inverse * upstream - values * inverse**3 * jnp.mean(
        upstream * values, axis=-1, keepdims=True
    )


def nn(a, b):
    return lax.dot_general(a, b, (((1,), (0,)), ((), ())), preferred_element_type=f32)


def nt(a, b):
    return lax.dot_general(a, b, (((1,), (1,)), ((), ())), preferred_element_type=f32)


def tn(a, b):
    return lax.dot_general(a, b, (((0,), (0,)), ((), ())), preferred_element_type=f32)


def my_place():
    blk = lax.axis_index("blk")
    head = lax.axis_index("head")
    return {
        "x": (head % 2) * 2 + (blk // 2) % 2,
        "y": head // 2,
        "z": blk // 4,
        "c": blk % 2,
    }


def device_at(place):
    x, y, z, c = place["x"], place["y"], place["z"], place["c"]
    return (z * 4 + (x % 2) * 2 + c, y * 2 + x // 2)


def chunk_of(ref, place, cols, lead=()):
    blk, head = device_at(place)
    return ref.at[(*lead, blk, pl.ds(head * ROWS, ROWS), cols)]


def moved(place, axis, value):
    other = dict(place)
    other[axis] = value
    return other


def greet(peers):
    barrier = pltpu.get_barrier_semaphore()
    for peer in peers:
        pl.semaphore_signal(barrier, inc=1, device_id=peer, device_id_type=MESH)
    pl.semaphore_wait(barrier, len(peers))


def greet_all():
    barrier = pltpu.get_barrier_semaphore()
    me = lax.axis_index("blk") * 8 + lax.axis_index("head")

    @pl.loop(1, 128)
    def _(k):
        other = (me + k) % 128
        pl.semaphore_signal(
            barrier, inc=1, device_id=(other // 8, other % 8), device_id_type=MESH
        )

    pl.semaphore_wait(barrier, 127)


def ring_peers(place):
    peers = [device_at(moved(place, "c", 1 - place["c"]))]
    for axis in "xyz":
        for step in (1, 3, 2):
            peers.append(device_at(moved(place, axis, (place[axis] + step) % 4)))
    return peers


def wait_bytes(ref, sem):
    pltpu.make_async_copy(ref, ref, sem).wait()


def remote(src, dst, send, recv, device):
    return pltpu.make_async_remote_copy(
        src_ref=src, dst_ref=dst, send_sem=send, recv_sem=recv, device_id=device, device_id_type=MESH
    )


def varied(place, axes, number):
    other = dict(place)
    for axis in axes:
        other[axis] = number % 4
        number = number // 4
    return other


def selections():
    spread = np.zeros((288, 256), np.float32)
    join = np.zeros((CHUNK, 256), np.float32)
    order = np.zeros((4 * GROUP, 4 * CHUNK), np.float32)
    for i in range(8):
        for j in range(10):
            spread[32 + i * 10 + j, i * ROWS + j] = 1
            spread[128 + i * 10 + j, i * ROWS + 10 + j] = 1
            spread[208 + i * 10 + j, i * ROWS + 20 + j] = 1
            join[i * 10 + j, i * ROWS + j] = 1
            inner, x_high = i // 2, i % 2
            for y in range(4):
                order[inner * GROUP + (y * 2 + x_high) * 10 + j, y * CHUNK + i * 10 + j] = 1
        for v in range(16):
            join[GROUP + v, i * ROWS + 16 + v] = 1
    share = join.T.copy()
    return spread, join, share, order


SPREAD, JOIN, SHARE, ORDER = selections()
TAKE_T = np.stack([SPREAD[32:112].T, SPREAD[128:208].T, SPREAD[208:288].T])


def row_block(ref, g, count):
    return ref.at[pl.ds(pl.multiple_of(g * count, 16), count)]


class Gather:
    def __init__(self, buf, send, recv, place):
        self.place = place
        self.buf, self.send, self.recv = buf, send, recv
        self.sibling = device_at(moved(place, "c", 1 - place["c"]))

    def begin(self, pack, sem):
        own = pltpu.make_async_copy(
            pack, chunk_of(self.buf, self.place, pl.ds(0, D)), sem
        )
        own.start()
        return own

    def forward(self, part, axes, fixed, count):
        first, width = PARTS[part][0]
        cols = pl.ds(first, width)

        @pl.loop(0, count)
        def _(number):
            where = dict(varied(self.place, axes, number), **fixed)
            piece = chunk_of(self.buf, where, cols)
            remote(
                piece, piece, self.send.at[part, 3], self.recv.at[part, 5], self.sibling
            ).start()

    def stage(self, stage):
        for part, ((first, width), order) in enumerate(PARTS):
            cols = pl.ds(first, width)
            if stage:
                wait_bytes(
                    self.buf.at[0, pl.ds(0, 3 * 4 ** (stage - 1) * ROWS), cols]
                    if stage == 1
                    else self.buf.at[pl.ds(0, 3), pl.ds(0, 4 * ROWS), cols],
                    self.recv.at[part, stage - 1],
                )

            @pl.loop(0, 4**stage)
            def _(number, part=part, cols=cols, order=order):
                piece = chunk_of(self.buf, varied(self.place, order[:stage], number), cols)
                axis = order[stage]
                for step in (1, 3, 2):
                    target = moved(self.place, axis, (self.place[axis] + step) % 4)
                    slot = stage if stage < 2 else 1 + step
                    remote(
                        piece,
                        piece,
                        self.send.at[part, stage],
                        self.recv.at[part, slot],
                        device_at(target),
                    ).start()

        for part, (_, order) in enumerate(PARTS):
            if stage == 0:
                self.forward(part, "", {}, 1)
            else:
                axis = order[stage - 1]
                for step in (1, 3, 2):
                    self.forward(
                        part,
                        order[: stage - 1],
                        {axis: (self.place[axis] + 4 - step) % 4},
                        4 ** (stage - 1),
                    )

    def finish(self):
        for step in (1, 3, 2):
            for part, ((first, width), order) in enumerate(PARTS):
                wait_bytes(
                    self.buf.at[pl.ds(0, 2), :, pl.ds(first, width)],
                    self.recv.at[part, 1 + step],
                )
                axis = order[2]
                self.forward(
                    part, order[:2], {axis: (self.place[axis] + 4 - step) % 4}, 16
                )
        for part, ((first, width), order) in enumerate(PARTS):
            cols = pl.ds(first, width)
            half = self.buf.at[pl.ds(0, 8), :, cols]
            wait_bytes(half, self.recv.at[part, 5])
            wait_bytes(half, self.send.at[part, 3])
            wait_bytes(self.buf.at[0, pl.ds(0, 3 * ROWS), cols], self.send.at[part, 0])
            wait_bytes(
                self.buf.at[pl.ds(0, 3), pl.ds(0, 4 * ROWS), cols], self.send.at[part, 1]
            )
            wait_bytes(self.buf.at[pl.ds(0, 6), :, cols], self.send.at[part, 2])


VMEM = pl.BlockSpec(memory_space=pltpu.VMEM)
HBM = pl.BlockSpec(memory_space=pl.ANY)


def unpack(buf, staged, spread, out_w, hidden_w, proj_w, out_sem):
    spans = ((0, 128, out_w), (128, GROUP, hidden_w), (208, GROUP, proj_w))

    @pl.loop(0, 16)
    def _(g):
        slot = g % 2
        outs = [
            pltpu.make_async_copy(
                staged.at[slot, pl.ds(at, count)], row_block(ref, g, count), out_sem.at[i, slot]
            )
            for i, (at, count, ref) in enumerate(spans)
        ]

        @pl.when(g >= 2)
        def _():
            for out in outs:
                out.wait()

        staged[slot] = nn(spread[...], buf[g]).astype(bf16)
        for out in outs:
            out.start()

    for slot in range(2):
        for i, (at, count, ref) in enumerate(spans):
            pltpu.make_async_copy(
                staged.at[slot, pl.ds(at, count)], row_block(ref, 0, count), out_sem.at[i, slot]
            ).wait()


class Scatter:
    def __init__(self, away, mine, pair, lands, halves, send, recv, place):
        self.away, self.mine, self.pair = away, mine, pair
        self.lands, self.halves = lands, halves
        self.send, self.recv, self.place = send, recv, place
        self.sibling = device_at(moved(place, "c", 1 - place["c"]))

    def swap(self, number):
        return remote(
            self.away.at[number],
            self.pair.at[number],
            self.send.at[len(PARTS), number],
            self.recv.at[len(PARTS), number],
            self.sibling,
        )

    def add_pair(self, number):
        self.swap(number).wait()
        self.mine[number] = (
            self.mine[number].astype(f32) + self.pair[number].astype(f32)
        ).astype(bf16)

    def own_piece(self, where, cols):
        half = where["z"] * 2 + where["x"] % 2
        return self.mine.at[half, pl.ds((where["y"] * 2 + where["x"] // 2) * ROWS, ROWS), cols]

    def start(self, stage):
        for part, ((first, width), order) in enumerate(PARTS):
            cols = pl.ds(first, width)
            axis = order[2 - stage]
            rest = order[: 2 - stage]

            @pl.loop(0, 16 // 4**stage)
            def _(number, part=part, cols=cols, axis=axis, rest=rest):
                for step in (1, 3, 2):
                    target = moved(self.place, axis, (self.place[axis] + step) % 4)
                    if stage == 0:
                        source = self.own_piece(varied(target, rest, number), cols)
                    elif stage == 1:
                        source = self.halves[0].at[target[axis], number, :, cols]
                    else:
                        source = self.halves[1].at[target[axis], :, cols]
                    remote(
                        source,
                        self.lands[stage].at[step - 1, number, :, cols],
                        self.send.at[part, stage],
                        self.recv.at[part, stage],
                        device_at(target),
                    ).start()

    def add(self, stage, out=None):
        for part, ((first, width), order) in enumerate(PARTS):
            cols = pl.ds(first, width)
            axis = order[2 - stage]
            rest = order[: 2 - stage]
            wait_bytes(self.lands[stage].at[:, :, :, cols], self.recv.at[part, stage])

            @pl.loop(0, 16 // 4**stage)
            def _(number, cols=cols, axis=axis, rest=rest):
                if stage == 0:
                    total = self.own_piece(varied(self.place, rest, number), cols)[...]
                elif stage == 1:
                    total = self.halves[0][self.place[axis], number, :, cols]
                else:
                    total = self.halves[1][self.place[axis], :, cols]
                total = total.astype(f32)
                for source in range(3):
                    total = total + self.lands[stage][source, number, :, cols].astype(f32)
                if stage == 0:
                    self.halves[0][number // 4, number % 4, :, cols] = total.astype(bf16)
                elif stage == 1:
                    self.halves[1][number, :, cols] = total.astype(bf16)
                else:
                    out[:, cols] = total

    def finish(self):
        for stage in range(3):
            for part, ((first, width), order) in enumerate(PARTS):
                wait_bytes(
                    self.lands[stage].at[:, :, :, pl.ds(first, width)], self.send.at[part, stage]
                )


def scatter_scratch():
    return [
        pltpu.VMEM((8, 256, D), bf16),
        pltpu.VMEM((8, 256, D), bf16),
        pltpu.VMEM((8, 256, D), bf16),
        pltpu.VMEM((3, 16, ROWS, D), bf16),
        pltpu.VMEM((3, 4, ROWS, D), bf16),
        pltpu.VMEM((3, 1, ROWS, D), bf16),
        pltpu.VMEM((4, 4, ROWS, D), bf16),
        pltpu.VMEM((4, ROWS, D), bf16),
        pltpu.SemaphoreType.DMA((3, 8)),
        pltpu.SemaphoreType.DMA((3, 8)),
    ]


def scatter_of(scratch, place):
    away, mine, pair, l0, l1, l2, h0, h1, send, recv = scratch
    return Scatter(away, mine, pair, (l0, l1, l2), (h0, h1), send, recv, place)


HALVES = ((0, "yz"), (256, "zy"))


def ring_devices(place):
    others = [moved(place, "c", 1 - place["c"])]
    for step in (1, 3, 2):
        there = moved(place, "x", (place["x"] + step) % 4)
        others += [there, moved(there, "c", 1 - place["c"])]
    return others


def ring_number(place):
    return (place["x"] % 2) * 4 + place["c"] * 2 + place["x"] // 2


def tokens_of(ref, place):
    inner = (place["x"] % 2) * 2 + place["c"]
    return ref.at[inner, :, pl.ds((place["x"] // 2) * TOK, TOK)]


def head_of(place):
    return (place["x"] // 2) * 8 + (place["z"] % 2) * 4 + place["y"]


def pair_device(pair, quarter):
    micro, h = pair // H, pair % H
    return ((micro * 2 + (h % 8) // 4) * 4 + quarter, (h % 4) * 2 + h // 8)


def gather_columns(buf, send, recv, place, stage):
    for half, (first, order) in enumerate(HALVES):
        cols = pl.ds(first, 256)
        axis = order[stage]
        if stage:
            wait_bytes(buf.at[0, pl.ds(0, 3 * CHUNK), cols], recv.at[half, 0])
        for number in range(4**stage):
            where = varied(place, order[:stage], number)
            piece = buf.at[where["z"], pl.ds(where["y"] * CHUNK, CHUNK), cols]
            for step in (1, 3, 2):
                target = moved(place, axis, (place[axis] + step) % 4)
                remote(
                    piece, piece, send.at[half, stage], recv.at[half, stage], device_at(target)
                ).start()


def finish_columns(buf, send, recv):
    for half, (first, _) in enumerate(HALVES):
        cols = pl.ds(first, 256)
        wait_bytes(buf.at[pl.ds(0, 3), :, cols], recv.at[half, 1])
        wait_bytes(buf.at[0, pl.ds(0, 3 * CHUNK), cols], send.at[half, 0])
        wait_bytes(buf.at[pl.ds(0, 3), :, cols], send.at[half, 1])


def quarter_of(blk):
    inner = blk % 4
    return jnp.where((blk // 4) % 2 == 0, inner, 3 - inner)


def query_block(quarter, j):
    return j * 4 + jnp.where(j % 2 == 0, quarter, 3 - quarter)


def chip_block(x_low, n):
    z = n // 2
    return z * 4 + 2 * ((z + x_low) % 2) + n % 2


def cell_of(ref, pair, width):
    return ref.at[pl.ds(pair // H * TOK, TOK), pl.ds(pair % H * width, width)]


def mask_of(key_block, block, start):
    key_at = key_block * B + lax.broadcasted_iota(jnp.int32, (B, B), 0)
    query_at = block * B + lax.broadcasted_iota(jnp.int32, (B, B), 1)
    return (key_at >= start) & (key_at <= query_at)


def has_mask(key_block, block):
    return (key_block == 0) | (key_block == block) | (block == 15)


def shift_matrix(rows, cols, by):
    row = lax.broadcasted_iota(jnp.int32, (rows, cols), 0)
    col = lax.broadcasted_iota(jnp.int32, (rows, cols), 1)
    return jnp.where((row - col == by) & (jnp.minimum(row, col) < HD), 1.0, 0.0).astype(bf16)


def wait_cells(ref, sem, fewer, width):
    wait_bytes(ref.at[:, pl.ds(0, 15 * width)], sem)
    wait_bytes(cell_of(ref, 0, width), sem)

    @pl.when(jnp.logical_not(fewer))
    def _():
        wait_bytes(cell_of(ref, 0, width), sem)


def stays_here(place):
    return (place["z"] % 2 == place["x"] % 2) & (place["y"] // 2 == place["c"])


def wait_ring(ref, sem, place):
    wait_bytes(ref.at[pl.ds(0, 3)], sem)
    wait_bytes(ref.at[0, pl.ds(0, 384)], sem)

    @pl.when(jnp.logical_not(stays_here(place)))
    def _():
        wait_bytes(ref.at[0, pl.ds(0, 128)], sem)


def front_kernel(
    tokens, pieces, pack, scale_row, starts, join, order, spread,
    normed_out, packed_out, wide_w, vectors, kv_out, queries, out_t, log_norms, attended,
    out_w, hidden_w, proj_w,
    ring_tokens, ring_pieces, chunks, kv, value_t, tops, totals, rounded, landed, buf, staged,
    x_tok_send, x_tok_recv, c_tok_send, c_tok_recv, piece_send, piece_recv, col_send, col_recv,
    two_send, two_recv, own_sem, send, recv, core_send, core_recv, x_send, x_recv,
    pass_send, pass_recv, back_send, back_recv, kv_sem, out_sem,
):
    blk = lax.axis_index("blk")
    head = lax.axis_index("head")
    core = blk % 2
    x_low = (blk // 2) % 2
    quarter = blk % 4
    even = (blk // 4) % 2 == 0
    place = my_place()
    pair = (place["z"] // 2) * H + head_of(place)
    turn = place["x"] * 2 + core
    sibling = (blk + 1 - 2 * core, head)
    partner = (blk + 2 - 4 * x_low, head)
    two = Gather(buf, two_send, two_recv, place)
    own = two.begin(pack, own_sem.at[0])
    own_tokens = pltpu.make_async_copy(tokens, tokens_of(ring_tokens, place), own_sem.at[1])
    own_tokens.start()
    number = ring_number(place)
    pltpu.make_async_copy(pieces.at[turn], ring_pieces.at[number], piece_recv).start()
    greet_all()
    for there in ring_devices(place):
        remote(
            pieces.at[there["x"] * 2 + there["c"]],
            ring_pieces.at[number],
            piece_send,
            piece_recv,
            device_at(there),
        ).start()
    mine = tokens_of(ring_tokens, place)
    for step in (1, 3, 2):
        there = moved(place, "x", (place["x"] + step) % 4)
        remote(
            tokens, mine, x_tok_send.at[step - 1], x_tok_recv.at[step - 1], device_at(there)
        ).start()
    remote(tokens, mine, c_tok_send, c_tok_recv, sibling).start()
    own.wait()
    two.stage(0)
    wait_bytes(ring_pieces, piece_recv)
    joined = nn(join[...], ring_pieces[...].reshape(256, MINE)).astype(bf16)
    chunks[place["z"], pl.ds(pl.multiple_of(place["y"] * CHUNK, 32), CHUNK)] = joined
    gather_columns(chunks, col_send, col_recv, place, 0)
    gather_columns(chunks, col_send, col_recv, place, 1)
    for step in (1, 3, 2):
        wait_bytes(tokens, x_tok_recv.at[step - 1])
        there = moved(place, "x", (place["x"] + 4 - step) % 4)
        arrived = tokens_of(ring_tokens, there)
        remote(arrived, arrived, c_tok_send, c_tok_recv, sibling).start()
    own_tokens.wait()
    finish_columns(chunks, col_send, col_recv)
    vector_rows = jnp.zeros((16, MINE), f32)
    for z in range(4):
        wide_w[z * 4 * GROUP : (z + 1) * 4 * GROUP] = nn(order[...], chunks[z]).astype(bf16)
        for y in range(4):
            at = y * CHUNK + GROUP
            vector_rows = vector_rows + chunks[z, at : at + 16].astype(f32)
    vectors[...] = vector_rows
    bias = vector_rows[0:1]
    gain = jnp.concatenate([vector_rows[1:2], vector_rows[2:3], vector_rows[3:4, :256]], axis=1)
    one_lane = jnp.where(
        lax.broadcasted_iota(jnp.int32, (1, MINE), 1) % LANES == 3 * HD, 1.0, 0.0
    )
    wait_bytes(ring_tokens.at[pl.ds(0, 2)], c_tok_recv)

    @pl.loop(0, 4)
    def _(inner):
        values = ring_tokens[inner].reshape(256, D).astype(f32)
        normed = (values * inverse_rms(values) * gain).astype(bf16)
        normed_out[inner] = normed
        full = nn(normed, wide_w[...])
        packed = ((full + bias) * scale_row[0:1] + one_lane).astype(bf16)
        packed_out[inner] = packed.reshape(2, 128, MINE)
        block = place["z"] * 4 + inner
        to_quarter = quarter_of(block)
        for m in range(2):
            for h in range(2):
                blk_to, head_to = pair_device(m * H + turn * 2 + h, to_quarter)
                src = packed_out.at[inner, m, :, pl.ds(h * LANES, LANES)]
                dst = kv.at[block, pl.ds(place["y"] * 128, 128)]
                stays = (blk_to == blk) & (head_to == head)

                @pl.when(stays)
                def _():
                    pltpu.make_async_copy(src, dst, recv).start()

                @pl.when(jnp.logical_not(stays))
                def _():
                    remote(src, dst, send, recv, (blk_to, head_to)).start()

    two.stage(1)
    wait_bytes(kv.at[pl.ds(0, 4)], recv)

    @pl.loop(0, 4)
    def _(j):
        block = kv.at[query_block(quarter, j)]
        remote(block, block, core_send, core_recv, sibling).start()
        remote(block, block, x_send, x_recv, partner).start()

    pick = shift_matrix(LANES, 128, HD)

    @pl.loop(0, 4)
    def _(j):
        queries[j] = nn(kv[query_block(quarter, j)], pick).astype(bf16)
        tops[j] = jnp.full((1, B), NEGATIVE, f32)
        totals[j] = jnp.zeros((1, B), f32)
        out_t[j] = jnp.zeros((128, B), f32)

    wait_bytes(kv.at[pl.ds(0, 4)], core_recv)

    @pl.loop(0, 8)
    def _(n):
        b = chip_block(x_low, n)
        value_t[b] = kv[b, :, 128:].T

    two.stage(2)

    def step(j, block, key_block):
        def tile(masked):
            s = nt(kv[key_block, :, :128], queries[j])
            if masked:
                s = jnp.where(mask_of(key_block, block, starts[j]), s, NEGATIVE)
            top = tops[j]
            new_top = jnp.maximum(top, jnp.max(s, axis=0, keepdims=True))
            p = jnp.exp(s - new_top)
            scale = jnp.exp(top - new_top)
            tops[j] = new_top
            totals[j] = totals[j] * scale + jnp.sum(p, axis=0, keepdims=True)
            out_t[j] = out_t[j] * scale + nn(value_t[key_block], p.astype(bf16))

        masked = has_mask(key_block, block)
        pl.when(masked)(lambda: tile(True))
        pl.when(jnp.logical_not(masked))(lambda: tile(False))

    @pl.loop(0, 4)
    def _(j):
        block = query_block(quarter, j)

        @pl.loop(0, 2 * j + block % 2 + 1)
        def _(n):
            step(j, block, chip_block(x_low, n))

    wait_bytes(kv.at[pl.ds(0, 4)], x_recv)

    @pl.loop(0, 4)
    def _(j):
        block = kv.at[query_block((quarter + 2) % 4, j)]
        remote(block, block, pass_send, pass_recv, sibling).start()

    wait_bytes(kv.at[pl.ds(0, 4)], pass_recv)
    keep = pltpu.make_async_copy(kv, kv_out, kv_sem)
    keep.start()

    @pl.loop(0, 8)
    def _(n):
        b = chip_block(1 - x_low, n)
        value_t[b] = kv[b, :, 128:].T

    @pl.loop(0, 4)
    def _(i):
        j = 3 - i
        block = query_block(quarter, j)

        @pl.loop(0, 2 * j + 2 * ((j + x_low) % 2))
        def _(n):
            step(j, block, chip_block(1 - x_low, n))

        acc = out_t[j]
        result = acc / acc[112:113]
        out_t[j] = result
        log_norms[j] = tops[j] + jnp.log(totals[j])
        rounded[j] = result.T.astype(bf16)

        @pl.loop(0, 8)
        def _(k):
            h = (head + k) % 8
            src = rounded.at[j, pl.ds(h * TOK, TOK)]
            dst = cell_of(landed, pair, 128)
            mine = (k == 0) & (block == blk)

            @pl.when(mine)
            def _():
                pltpu.make_async_copy(src, dst, back_recv).start()

            @pl.when(jnp.logical_not(mine))
            def _():
                remote(src, dst, back_send, back_recv, (block, h)).start()

    two.finish()
    unpack(buf, staged, spread, out_w, hidden_w, proj_w, out_sem)
    wait_bytes(landed, back_recv)
    attended[...] = landed[...]
    keep.wait()
    for sem in (core_send, x_send, pass_send):
        wait_bytes(kv.at[pl.ds(0, 4)], sem)
    wait_cells(landed, back_send, even, 128)
    wait_bytes(ring_pieces.at[pl.ds(0, 7)], piece_send)
    for step_at in range(3):
        wait_bytes(tokens, x_tok_send.at[step_at])
    wait_bytes(ring_tokens.at[pl.ds(0, 2)], c_tok_send)
    wait_ring(kv, send, place)


def front(*operands):
    dma = pltpu.SemaphoreType.DMA
    return pl.pallas_call(
        front_kernel,
        out_shape=(
            jax.ShapeDtypeStruct((4, 256, D), bf16),
            jax.ShapeDtypeStruct((4, 2, 128, MINE), bf16),
            jax.ShapeDtypeStruct((D, MINE), bf16),
            jax.ShapeDtypeStruct((16, MINE), f32),
            jax.ShapeDtypeStruct((16, B, LANES), bf16),
            jax.ShapeDtypeStruct((4, B, 128), bf16),
            jax.ShapeDtypeStruct((4, 128, B), f32),
            jax.ShapeDtypeStruct((4, 1, B), f32),
            jax.ShapeDtypeStruct((2 * TOK, OUT_WIDE), bf16),
            jax.ShapeDtypeStruct((OUT_WIDE, D), bf16),
            jax.ShapeDtypeStruct((D, D), bf16),
            jax.ShapeDtypeStruct((D, D), bf16),
        ),
        in_specs=[VMEM] * 8,
        out_specs=(VMEM, VMEM, VMEM, VMEM, HBM, VMEM, VMEM, VMEM, VMEM, HBM, HBM, HBM),
        scratch_shapes=[
            pltpu.VMEM((4, 2, 128, D), bf16),
            pltpu.VMEM((8, ROWS, MINE), bf16),
            pltpu.VMEM((4, 4 * CHUNK, MINE), bf16),
            pltpu.VMEM((16, B, LANES), bf16),
            pltpu.VMEM((16, 128, B), bf16),
            pltpu.VMEM((4, 1, B), f32),
            pltpu.VMEM((4, 1, B), f32),
            pltpu.VMEM((4, B, 128), bf16),
            pltpu.VMEM((2 * TOK, OUT_WIDE), bf16),
            pltpu.VMEM((16, 256, D), bf16),
            pltpu.VMEM((2, 288, D), bf16),
            dma((3,)), dma((3,)), dma, dma, dma, dma, dma((2, 2)), dma((2, 2)),
            dma((2, 4)), dma((2, 6)), dma((2,)),
        ]
        + [dma] * 11
        + [dma((3, 2))],
        compiler_params=pltpu.CompilerParams(
            collective_id=0, has_side_effects=True, vmem_limit_bytes=56 * 2**20
        ),
        name="front",
    )(
        *operands,
        jnp.asarray(JOIN, bf16),
        jnp.asarray(ORDER, bf16),
        jnp.asarray(SPREAD, bf16),
    )


def rear_kernel(
    pack, kv, queries, starts, out_t, log_norms,
    attended, d_branch, normed_two, d_pre, activated, upstream,
    normed, packed, wide_w, vectors, vector_grads, scale_row, take_t, share, order_t,
    d_normed, pieces_out, two_out,
    d_out, key_t, deltas, d_query, d_kv, mine_kv, half, half_in, cross, cross_in, final, d_wide,
    attended_t, normed_two_t, activated_t, right,
    partial_in, sum_in, grad_chunks, first_in, second_in, first_y, first_z,
    joined, shares, shares_in,
    send, recv, core_send, core_recv, x_send, x_recv, back_send, back_recv,
    normed_sem, c_send, c_recv, sum_send, sum_recv, col_send, col_recv, share_send, share_recv,
    *scratch,
):
    blk = lax.axis_index("blk")
    head = lax.axis_index("head")
    core = blk % 2
    x_low = (blk // 2) % 2
    quarter = blk % 4
    place = my_place()
    my_head = head_of(place)
    pair = (place["z"] // 2) * H + my_head
    to_quarter = quarter_of(blk)
    even = (blk // 4) % 2 == 0
    two = scatter_of(scratch, place)
    greet_all()

    @pl.loop(0, PAIRS)
    def _(k):
        p = (pair + k) % PAIRS
        src = cell_of(pack, p, 128)
        dst = d_out.at[blk // 4, pl.ds(head * TOK, TOK)]
        mine = (k == 0) & even

        @pl.when(mine)
        def _():
            pltpu.make_async_copy(src, dst, recv).start()

        @pl.when(jnp.logical_not(mine))
        def _():
            remote(src, dst, send, recv, pair_device(p, to_quarter)).start()

    for n in range(D // 128):
        lanes = slice(n * 128, n * 128 + 128)
        normed_two_t[lanes] = normed_two[:, lanes].T
        activated_t[lanes] = activated[:, lanes].T
    for n in range(H):
        lanes = slice(n * 128, n * 128 + 128)
        attended_t[lanes] = attended[:, lanes].T
    right[0:128] = d_branch[...]
    right[128:256] = d_pre[...]
    right[256:384] = upstream[...]

    def produce(number, of_core, into):
        group = number * 2 + of_core
        rows = pl.ds(pl.multiple_of(group * GROUP, 16), GROUP)
        out_rows = pl.ds(pl.multiple_of(group * 128 + 32, 16), GROUP)
        left = jnp.concatenate(
            [
                nn(take_t[0], attended_t[out_rows]).astype(bf16),
                nn(take_t[1], normed_two_t[rows]).astype(bf16),
                nn(take_t[2], activated_t[rows]).astype(bf16),
            ],
            axis=1,
        )
        for cell in range(5):
            lanes = slice(cell * LANES, (cell + 1) * LANES)
            into[number, :, lanes] = nn(left, right[:, lanes]).astype(bf16)

    @pl.loop(0, 8)
    def _(number):
        produce(number, 1 - core, two.away)
        two.swap(number).start()

    @pl.loop(0, 8)
    def _(number):
        produce(number, core, two.mine)

    @pl.loop(0, 16)
    def _(b):
        key_t[b] = kv[b, :, :128].T

    @pl.loop(0, 8)
    def _(number):
        two.add_pair(number)

    load_normed = pltpu.make_async_copy(normed, two.pair.at[pl.ds(0, 4)], normed_sem)
    load_normed.start()
    two.start(0)
    wait_bytes(d_out, recv)

    @pl.loop(0, 4)
    def _(j):
        deltas[j] = jnp.sum(d_out[j].astype(f32).T * out_t[j], axis=0, keepdims=True)
        d_query[j] = jnp.zeros((128, B), f32)

    sibling = (blk + 1 - 2 * core, head)
    partner = (blk + 2 - 4 * x_low, head)

    def step(j, block, key_block):
        def tile(masked):
            q = queries[j]
            do = d_out[j]
            p = jnp.exp(nt(kv[key_block, :, :128], q) - log_norms[j])
            if masked:
                p = jnp.where(mask_of(key_block, block, starts[j]), p, 0.0)
            dp = nt(kv[key_block, :, 128:], do)
            ds = (p * (dp - deltas[j])).astype(bf16)
            d_kv[:, :128] += nn(ds, q)
            d_kv[:, 128:] += nn(p.astype(bf16), do)
            d_query[j] += nn(key_t[key_block], ds)

        masked = has_mask(key_block, block)
        pl.when(masked)(lambda: tile(True))
        pl.when(jnp.logical_not(masked))(lambda: tile(False))

    def swap(n):
        return remote(
            half.at[n], half_in.at[n], core_send.at[n], core_recv.at[n], sibling
        )

    def cross_swap(z):
        return remote(cross.at[z], cross_in.at[z], x_send.at[z], x_recv.at[z], partner)

    def own_number(z):
        return 2 * z + (x_low + z) % 2

    def core_sum(z):
        own = own_number(z)
        other = 4 * z + 1 - own
        swap(other).wait()
        cross[z] = (mine_kv[other] + half_in[other].astype(f32)).astype(bf16)
        cross_swap(z).start()
        swap(own).wait()
        mine_kv[own] = mine_kv[own] + half_in[own].astype(f32)

    shift = shift_matrix(128, LANES, -HD)

    def finish(z):
        block = query_block(quarter, z)
        cross_swap(z).wait()
        final[z] = (
            mine_kv[own_number(z)]
            + cross_in[z].astype(f32)
            + nn(d_query[z].T.astype(bf16), shift)
        ).astype(bf16)

        @pl.loop(0, 4)
        def _(k):
            y = (place["y"] + k) % 4
            there = {"x": my_head // 4, "y": y, "z": z, "c": (my_head // 2) % 2}
            src = final.at[z, pl.ds(y * 128, 128)]
            dst = d_wide.at[
                block % 4, place["z"] // 2, :, pl.ds((my_head % 2) * LANES, LANES)
            ]
            blk_to, head_to = device_at(there)
            stays = (blk_to == blk) & (head_to == head)

            @pl.when(stays)
            def _():
                pltpu.make_async_copy(src, dst, back_recv).start()

            @pl.when(jnp.logical_not(stays))
            def _():
                remote(src, dst, back_send, back_recv, (blk_to, head_to)).start()

    @pl.loop(0, 8)
    def _(part):
        z = part // 2

        @pl.loop(2 * part, 2 * part + 2)
        def _(key_block):
            d_kv[...] = jnp.zeros((B, LANES), f32)
            first = z + (query_block(quarter, z) < key_block).astype(jnp.int32)

            @pl.loop(first, 4)
            def _(j):
                step(j, query_block(quarter, j), key_block)

            n = 2 * z + (key_block % 4) // 2

            @pl.when((key_block + z + core) % 2 == 0)
            def _():
                mine_kv[n] = d_kv[...]

            @pl.when((key_block + z + core) % 2 == 1)
            def _():
                half[n] = d_kv[...].astype(bf16)
                swap(n).start()

        @pl.when((part % 2 == 0) & (part > 0))
        def _():
            core_sum(z - 1)

        @pl.when((part % 2 == 1) & (part > 1))
        def _():
            finish(z - 1)

        @pl.when(part == 4)
        def _():
            two.add(0)
            two.start(1)

        @pl.when(part == 6)
        def _():
            two.add(1)
            two.start(2)

    core_sum(3)
    two.add(2, two_out)
    finish(3)
    two.finish()
    wait_bytes(d_wide, back_recv)

    load_normed.wait()
    partial, normed_here = two.away, two.pair
    scale = scale_row[0:1]
    gain = jnp.concatenate([vectors[1:2], vectors[2:3], vectors[3:4, :256]], axis=1)
    bias_sum = jnp.zeros((1, MINE), f32)
    scale_sum = jnp.zeros((1, MINE), f32)
    gain_sum = jnp.zeros((1, D), f32)
    for inner in range(4):
        grad = d_wide[inner].reshape(256, MINE).astype(f32)
        scale_sum = scale_sum + jnp.sum(
            grad * packed[inner].reshape(256, MINE).astype(f32), axis=0, keepdims=True
        )
        grad = (grad * scale).astype(bf16)
        d_wide[inner] = grad.reshape(2, 128, MINE)
        bias_sum = bias_sum + jnp.sum(grad.astype(f32), axis=0, keepdims=True)
        back = nt(grad, wide_w[...])
        gain_sum = gain_sum + jnp.sum(
            back * normed_here[inner].astype(f32), axis=0, keepdims=True
        )
        partial[inner] = back.astype(bf16)
    sibling_at = (blk + 1 - 2 * core, head)
    c_swaps = []
    for low in range(2):
        c_swaps.append(
            remote(
                partial.at[low * 2 + 1 - core],
                partial_in.at[low],
                c_send.at[low],
                c_recv.at[low],
                sibling_at,
            )
        )
        c_swaps[-1].start()
    gain_sum = gain_sum / gain
    scale_sum = scale_sum[:, :LANES] + scale_sum[:, LANES:]
    rows = vector_grads[...] + jnp.concatenate(
        [
            bias_sum,
            gain_sum[:, :512],
            gain_sum[:, 512:1024],
            jnp.concatenate([gain_sum[:, 1024:], scale_sum], axis=1),
            jnp.zeros((12, MINE), f32),
        ],
        axis=0,
    )
    rows = rows.astype(bf16)
    for z in range(4):
        left = jnp.concatenate(
            [normed_here[inner, :, z * 320 // 128 * 128 : z * 320 // 128 * 128 + 384]
             for inner in range(4)],
            axis=0,
        )
        skip = z * 320 % 128
        grads = tn(left, d_wide[...].reshape(1024, MINE))[skip : skip + 320].astype(bf16)
        grad_chunks[z] = nn(order_t[...], grads).astype(bf16)
        for y in range(4):
            grad_chunks[z, y * CHUNK + GROUP : y * CHUNK + GROUP + 16] = rows

    def chunk_rows(y):
        return pl.ds(pl.multiple_of(y * CHUNK, 32), CHUNK)

    for step_at in (1, 3, 2):
        z = (place["z"] + step_at) % 4
        remote(
            grad_chunks.at[z, :, pl.ds(0, 256)],
            first_in.at[0, step_at - 1],
            col_send.at[0, 0],
            col_recv.at[0, 0],
            device_at(moved(place, "z", z)),
        ).start()
        y = (place["y"] + step_at) % 4
        for plane in range(4):
            remote(
                grad_chunks.at[plane, chunk_rows(y), pl.ds(256, 256)],
                first_in.at[1, step_at - 1, chunk_rows(plane)],
                col_send.at[1, 0],
                col_recv.at[1, 0],
                device_at(moved(place, "y", y)),
            ).start()
    for low in range(2):
        c_swaps[low].wait()
        partial[4 + low] = (
            partial[low * 2 + core].astype(f32) + partial_in[low].astype(f32)
        ).astype(bf16)
    for step_at in (1, 3, 2):
        there = moved(place, "x", (place["x"] + step_at) % 4)
        for m in range(2):
            remote(
                partial.at[4 + there["x"] % 2, pl.ds(m * 128 + (there["x"] // 2) * TOK, TOK)],
                sum_in.at[step_at - 1, pl.ds(m * TOK, TOK)],
                sum_send,
                sum_recv,
                device_at(there),
            ).start()
    wait_bytes(first_in.at[0], col_recv.at[0, 0])
    total = grad_chunks[place["z"], :, 0:256].astype(f32)
    for source in range(3):
        total = total + first_in[0, source].astype(f32)
    first_y[...] = total.astype(bf16)
    wait_bytes(first_in.at[1], col_recv.at[1, 0])
    for plane in range(4):
        total = grad_chunks[plane, chunk_rows(place["y"]), 256:512].astype(f32)
        for source in range(3):
            total = total + first_in[1, source, chunk_rows(plane)].astype(f32)
        first_z[plane] = total.astype(bf16)
    for step_at in (1, 3, 2):
        y = (place["y"] + step_at) % 4
        remote(
            first_y.at[chunk_rows(y)],
            second_in.at[0, step_at - 1],
            col_send.at[0, 1],
            col_recv.at[0, 1],
            device_at(moved(place, "y", y)),
        ).start()
        z = (place["z"] + step_at) % 4
        remote(
            first_z.at[z],
            second_in.at[1, step_at - 1],
            col_send.at[1, 1],
            col_recv.at[1, 1],
            device_at(moved(place, "z", z)),
        ).start()
    wait_bytes(second_in.at[0], col_recv.at[0, 1])
    wait_bytes(second_in.at[1], col_recv.at[1, 1])
    total_y = first_y[chunk_rows(place["y"])].astype(f32)
    total_z = first_z[place["z"]].astype(f32)
    for source in range(3):
        total_y = total_y + second_in[0, source].astype(f32)
        total_z = total_z + second_in[1, source].astype(f32)
    joined[:, 0:256] = total_y.astype(bf16)
    joined[:, 256:512] = total_z.astype(bf16)
    shares[...] = nn(share[...], joined[...]).astype(bf16).reshape(8, ROWS, MINE)
    turn = place["x"] * 2 + core
    for there in ring_devices(place):
        remote(
            shares.at[ring_number(there)],
            shares_in.at[turn],
            share_send,
            share_recv,
            device_at(there),
        ).start()
    pltpu.make_async_copy(
        shares.at[ring_number(place)], shares_in.at[turn], share_recv
    ).start()
    wait_bytes(sum_in, sum_recv)
    for m in range(2):
        at = pl.multiple_of(m * 128 + (place["x"] // 2) * TOK, TOK)
        total = partial[4 + x_low, pl.ds(at, TOK)].astype(f32)
        for source in range(3):
            total = total + sum_in[source, m * TOK : (m + 1) * TOK].astype(f32)
        d_normed[m * TOK : (m + 1) * TOK] = total
    wait_bytes(shares_in, share_recv)
    pieces_out[...] = shares_in[...]
    wait_cells(pack, send, even, 128)
    wait_bytes(final.at[pl.ds(0, 3)], back_send)
    wait_bytes(final.at[0, pl.ds(0, 384)], back_send)

    @pl.when(jnp.logical_not(stays_here(place)))
    def _():
        wait_bytes(final.at[0, pl.ds(0, 128)], back_send)

    wait_bytes(sum_in, sum_send)
    for number in range(2):
        wait_bytes(first_in.at[number], col_send.at[number, 0])
        wait_bytes(second_in.at[number], col_send.at[number, 1])
    wait_bytes(shares.at[pl.ds(0, 7)], share_send)


def rear(*operands):
    dma = pltpu.SemaphoreType.DMA
    return pl.pallas_call(
        rear_kernel,
        out_shape=(
            jax.ShapeDtypeStruct((2 * TOK, D), f32),
            jax.ShapeDtypeStruct((8, ROWS, MINE), bf16),
            jax.ShapeDtypeStruct((ROWS, D), f32),
        ),
        in_specs=[VMEM] * 12 + [HBM] + [VMEM] * 8,
        out_specs=(VMEM, VMEM, VMEM),
        scratch_shapes=[
            pltpu.VMEM((4, B, 128), bf16),
            pltpu.VMEM((16, 128, B), bf16),
            pltpu.VMEM((4, 1, B), f32),
            pltpu.VMEM((4, 128, B), f32),
            pltpu.VMEM((B, LANES), f32),
            pltpu.VMEM((8, B, LANES), f32),
            pltpu.VMEM((8, B, LANES), bf16),
            pltpu.VMEM((8, B, LANES), bf16),
            pltpu.VMEM((4, B, LANES), bf16),
            pltpu.VMEM((4, B, LANES), bf16),
            pltpu.VMEM((4, B, LANES), bf16),
            pltpu.VMEM((4, 2, 128, MINE), bf16),
            pltpu.VMEM((OUT_WIDE, 128), bf16),
            pltpu.VMEM((D, 128), bf16),
            pltpu.VMEM((D, 128), bf16),
            pltpu.VMEM((384, D), bf16),
            pltpu.VMEM((2, 256, D), bf16),
            pltpu.VMEM((3, 2 * TOK, D), bf16),
            pltpu.VMEM((4, 4 * CHUNK, MINE), bf16),
            pltpu.VMEM((2, 3, 4 * CHUNK, 256), bf16),
            pltpu.VMEM((2, 3, CHUNK, 256), bf16),
            pltpu.VMEM((4 * CHUNK, 256), bf16),
            pltpu.VMEM((4, CHUNK, 256), bf16),
            pltpu.VMEM((CHUNK, MINE), bf16),
            pltpu.VMEM((8, ROWS, MINE), bf16),
            pltpu.VMEM((8, ROWS, MINE), bf16),
            dma, dma, dma((8,)), dma((8,)), dma((4,)), dma((4,)), dma, dma,
            dma, dma((2,)), dma((2,)), dma, dma, dma((2, 2)), dma((2, 2)), dma, dma,
        ]
        + scatter_scratch(),
        compiler_params=pltpu.CompilerParams(
            collective_id=1, has_side_effects=True, vmem_limit_bytes=63 * 2**20
        ),
        name="rear",
    )(
        *operands,
        jnp.asarray(TAKE_T, bf16),
        jnp.asarray(SHARE, bf16),
        jnp.asarray(ORDER.T, bf16),
    )


def on_device(
    inputs,
    segment_ids,
    norm1_gain,
    w_query,
    w_key,
    w_value,
    query_bias,
    value_bias,
    w_out,
    out_bias,
    norm2_gain,
    w_hidden,
    hidden_bias,
    w_proj,
    proj_bias,
    dim_scale,
    cotangent,
):
    blk = lax.axis_index("blk")
    head = lax.axis_index("head")
    at = (blk * 8 + head) * 10
    spread_heads = jnp.zeros((H, LANES), bf16)
    for i, vector in ((1, query_bias), (2, value_bias)):
        spread_heads = lax.dynamic_update_slice(
            spread_heads, vector[None], (blk, i * HD + head * 10)
        )
    natural = jnp.stack([norm1_gain, out_bias, norm2_gain, hidden_bias, proj_bias])
    natural = lax.dynamic_update_slice(jnp.zeros((5, 3 * MINE), bf16), natural, (0, at))
    columns = jnp.concatenate(
        [w.reshape(10, H, HD) for w in (w_key, w_query, w_value)]
        + [jnp.zeros((10, H, LANES - 3 * HD), bf16)],
        axis=2,
    )
    columns = columns.reshape(10, 8, MINE).transpose(1, 0, 2)
    pieces = jnp.concatenate(
        [
            columns,
            jnp.zeros((8, 6, MINE), bf16),
            spread_heads.reshape(8, 1, MINE),
            jnp.broadcast_to(natural.reshape(1, 15, MINE), (8, 15, MINE)),
        ],
        axis=1,
    )
    pack = jnp.concatenate([w_out, w_hidden, w_proj, jnp.zeros((2, D), bf16)], axis=0)
    softplus_scale = LOG2E / math.sqrt(HD) * jax.nn.softplus(dim_scale)
    ones = jnp.ones((HD,), f32)
    scale_row = jnp.concatenate(
        [ones, softplus_scale, ones, jnp.zeros((LANES - 3 * HD,), f32)] * 2
    )
    scale_row = jnp.broadcast_to(scale_row, (8, MINE))

    micro = blk // 8
    segment_row = lax.dynamic_index_in_dim(segment_ids, micro, 0, keepdims=False)
    starts = jnp.zeros_like(segment_row)
    for value in range(1, 9):
        before = jnp.sum((segment_row < value).astype(jnp.int32))
        starts = jnp.where(segment_row == value, before, starts)
    quarter = blk % 4
    starts = starts.reshape(16, 1, B)
    starts = jnp.stack([starts[query_block(quarter, j)] for j in range(4)])

    (
        ring_normed, packed, wide_w, vectors, kv, queries, out_t, log_norms, attended,
        out_w, hidden_w, proj_w,
    ) = front(inputs, pieces, pack, scale_row, starts)
    every = vectors[1:].reshape(5, 3 * MINE)[:, :D]
    gain_one, out_b, gain_two, hidden_b, proj_b = [every[i] for i in range(5)]

    tokens = inputs.reshape(2 * TOK, D).astype(f32)
    residual = tokens + nn(attended, out_w) + out_b
    inverse_two = inverse_rms(residual)
    normed_two = (residual * inverse_two * gain_two).astype(bf16)
    pre_act = nn(normed_two, hidden_w) + hidden_b
    gate = jax.nn.sigmoid(pre_act)
    activated = (pre_act * gate).astype(bf16)
    layer_out = (residual + nn(activated, proj_w) + proj_b).astype(bf16)

    upstream_low = cotangent.reshape(2 * TOK, D)
    upstream = upstream_low.astype(f32)
    d_pre = (nt(upstream_low, proj_w) * gate * (1.0 + pre_act * (1.0 - gate))).astype(bf16)
    d_normed_two = nt(d_pre, hidden_w)
    d_residual = upstream + norm_back(d_normed_two * gain_two, residual, inverse_two)
    d_branch = d_residual.astype(bf16)
    d_attended = nt(d_branch, out_w).astype(bf16)

    def total(values):
        return jnp.sum(values.astype(f32), axis=0)

    vector_grads = jnp.stack(
        [
            total(d_branch),
            total(d_normed_two * residual * inverse_two),
            total(d_pre),
            total(upstream),
        ]
    )
    vector_grads = jnp.pad(vector_grads, ((0, 0), (0, 3 * MINE - D))).reshape(12, MINE)
    vector_grads = jnp.pad(vector_grads, ((4, 0), (0, 0)))
    d_normed, shares, two = rear(
        d_attended, kv, queries, starts, out_t, log_norms,
        attended, d_branch, normed_two, d_pre, activated, upstream_low,
        ring_normed, packed, wide_w, vectors, vector_grads, scale_row,
    )
    inverse_one = inverse_rms(tokens)
    input_grad = (
        d_residual + norm_back(d_normed * gain_one, tokens, inverse_one)
    ).astype(bf16)

    shares = shares.astype(f32)
    columns = shares[:, :10].transpose(1, 0, 2).reshape(10, H, LANES)
    d_key_w, d_query_w, d_value_w = [
        columns[:, :, i * HD : (i + 1) * HD].reshape(10, D) for i in range(3)
    ]
    by_head = shares[:, 16].reshape(H, LANES)
    d_query_bias, d_value_bias = [
        lax.dynamic_slice(by_head, (blk, i * HD + head * 10), (1, 10)).reshape(10) for i in (1, 2)
    ]
    summed = jnp.sum(shares[:, 17:], axis=0)
    scale_grad = summed[2, LANES + HD : LANES + 2 * HD] / softplus_scale
    scale_grad = scale_grad * (LOG2E / math.sqrt(HD)) * jax.nn.sigmoid(dim_scale)
    natural = lax.dynamic_slice(summed.reshape(5, 3 * MINE), (0, at), (5, 10))
    return (
        layer_out.reshape(2, TOK, D),
        input_grad.reshape(2, TOK, D),
        natural[0],
        d_query_w,
        d_key_w,
        d_value_w,
        d_query_bias,
        d_value_bias,
        two[0:10],
        natural[1],
        natural[2],
        two[10:20],
        natural[3],
        two[20:30],
        natural[4],
        scale_grad,
    )


def solution(mesh):
    rows = P(("blk", "head"), None)
    vec = P(("blk", "head"))
    tok = P(None, ("blk", "head"), None)
    in_specs = (
        tok, P(), vec, rows, rows, rows, vec, vec, rows, vec, vec, rows, vec, rows, vec, P(), tok
    )
    out_specs = (
        tok, tok, vec, rows, rows, rows, vec, vec, rows, vec, vec, rows, vec, rows, vec, P()
    )
    return jax.shard_map(
        on_device, mesh=mesh, in_specs=in_specs, out_specs=out_specs, check_vma=False
    )
```

```python
import functools
import math

import jax
import jax.numpy as jnp
import numpy as np
from jax import lax
from jax.experimental import pallas as pl
from jax.experimental.pallas import tpu as pltpu
from jax.sharding import PartitionSpec as P

D = 1280
H = 16
HD = 80
FF = 1280
B = 512
TOK = 64
PAIRS = 32
LANES = 256
ROWS = 32
WIDE = H * LANES
OUT_WIDE = H * 128
GROUP = 80
CHUNK = 96
MINE = 512
EPSILON = 1e-06
LOG2E = 1.442695041
NEGATIVE = -1e30
MESH = pl.DeviceIdType.MESH
f32 = jnp.float32
bf16 = jnp.bfloat16

PARTS = (((0, 512), "xyz"), ((512, 384), "yzx"), ((896, 384), "zxy"))
PARTS_BACK = (((0, 640), "xyz"), ((640, 640), "xzy"))


def inverse_rms(values):
    return lax.rsqrt(jnp.mean(values * values, axis=-1, keepdims=True) + EPSILON)


def norm_back(upstream, values, inverse):
    return inverse * upstream - values * inverse**3 * jnp.mean(
        upstream * values, axis=-1, keepdims=True
    )


def nn(a, b):
    return lax.dot_general(a, b, (((1,), (0,)), ((), ())), preferred_element_type=f32)


def nt(a, b):
    return lax.dot_general(a, b, (((1,), (1,)), ((), ())), preferred_element_type=f32)


def tn(a, b):
    return lax.dot_general(a, b, (((0,), (0,)), ((), ())), preferred_element_type=f32)


def my_place():
    blk = lax.axis_index("blk")
    head = lax.axis_index("head")
    return {
        "x": (head % 2) * 2 + (blk // 2) % 2,
        "y": head // 2,
        "z": blk // 4,
        "c": blk % 2,
    }


def device_at(place):
    x, y, z, c = place["x"], place["y"], place["z"], place["c"]
    return (z * 4 + (x % 2) * 2 + c, y * 2 + x // 2)


def span(place, free, core=True):
    x, y, z = place["x"], place["y"], place["z"]
    whole = slice(None)
    at = [
        whole if "z" in free else z,
        whole if "x" in free else x % 2,
        place["c"],
        whole if "y" in free else y,
        whole if "x" in free else x // 2,
    ]
    return tuple(at if core else at[:2] + at[3:])


def moved(place, axis, value):
    other = dict(place)
    other[axis] = value
    return other


def greet(peers):
    barrier = pltpu.get_barrier_semaphore()
    for peer in peers:
        pl.semaphore_signal(barrier, inc=1, device_id=peer, device_id_type=MESH)
    pl.semaphore_wait(barrier, len(peers))


def greet_all():
    barrier = pltpu.get_barrier_semaphore()
    me = lax.axis_index("blk") * 8 + lax.axis_index("head")

    @pl.loop(1, 128)
    def _(k):
        other = (me + k) % 128
        pl.semaphore_signal(
            barrier, inc=1, device_id=(other // 8, other % 8), device_id_type=MESH
        )

    pl.semaphore_wait(barrier, 127)


def ring_peers(place):
    peers = [device_at(moved(place, "c", 1 - place["c"]))]
    for axis in "xyz":
        for step in (1, 3, 2):
            peers.append(device_at(moved(place, axis, (place[axis] + step) % 4)))
    return peers


def wait_bytes(ref, sem):
    pltpu.make_async_copy(ref, ref, sem).wait()


def remote(src, dst, send, recv, device):
    return pltpu.make_async_remote_copy(
        src_ref=src, dst_ref=dst, send_sem=send, recv_sem=recv, device_id=device, device_id_type=MESH
    )


def varied(place, axes, number):
    other = dict(place)
    for axis in axes:
        other[axis] = number % 4
        number = number // 4
    return other


def selections():
    take = np.zeros((240, 256), np.float32)
    join = np.zeros((CHUNK, 256), np.float32)
    order = np.zeros((4 * GROUP, 4 * CHUNK), np.float32)
    for i in range(8):
        for j in range(10):
            for w in range(3):
                take[w * GROUP + i * 10 + j, i * ROWS + w * 10 + j] = 1
            join[i * 10 + j, i * ROWS + j] = 1
            inner, x_high = i // 2, i % 2
            for y in range(4):
                order[inner * GROUP + (y * 2 + x_high) * 10 + j, y * CHUNK + i * 10 + j] = 1
        for v in range(16):
            join[GROUP + v, i * ROWS + 16 + v] = 1
    share = join.T.copy()
    return take, join, share, order


TAKE, JOIN, SHARE, ORDER = selections()
TAKE_T = TAKE.reshape(3, GROUP, 256).transpose(0, 2, 1)


def row_block(ref, g, count):
    return ref.at[pl.ds(pl.multiple_of(g * count, 16), count)]


class Gather:
    def __init__(self, buf, send, recv, place):
        self.place = place
        self.buf, self.send, self.recv = buf, send, recv
        self.sibling = device_at(moved(place, "c", 1 - place["c"]))

    def begin(self, pack, sem):
        own = pltpu.make_async_copy(pack, self.buf.at[span(self.place, "")], sem)
        own.start()
        return own

    def piece(self, part, where, free):
        first, width = PARTS[part][0]
        return self.buf.at[(*span(where, free), slice(None), pl.ds(first, width))]

    def pieces(self, part, count):
        cols = pl.ds(*PARTS[part][0])
        whole = slice(None)
        at = {
            3: (pl.ds(0, 3), 0, 0, 0, 0),
            12: (pl.ds(0, 3), 0, 0, whole, 0),
            16: (0, whole, 0, whole, whole),
            48: (pl.ds(0, 3), whole, 0, whole, whole),
            64: (whole, whole, 0, whole, whole),
        }[count]
        return self.buf.at[(*at, whole, cols)]

    def forward(self, part, where, free):
        piece = self.piece(part, where, free)
        remote(piece, piece, self.send.at[part, 3], self.recv.at[part, 5], self.sibling).start()

    def stage(self, stage):
        for part, (_, order) in enumerate(PARTS):
            if stage:
                wait_bytes(self.pieces(part, 3 * 4 ** (stage - 1)), self.recv.at[part, stage - 1])
            piece = self.piece(part, self.place, order[:stage])
            axis = order[stage]
            for step in (1, 3, 2) if stage < 2 else (1, 3):
                target = moved(self.place, axis, (self.place[axis] + step) % 4)
                slot = stage if stage < 2 else 1 + step
                remote(
                    piece,
                    piece,
                    self.send.at[part, stage],
                    self.recv.at[part, slot],
                    device_at(target),
                ).start()
        for part, (_, order) in enumerate(PARTS):
            if stage == 0:
                self.forward(part, self.place, "")
            else:
                axis = order[stage - 1]
                for step in (1, 3, 2):
                    there = moved(self.place, axis, (self.place[axis] + 4 - step) % 4)
                    self.forward(part, there, order[: stage - 1])

    def relay(self):
        for part, ((first, width), order) in enumerate(PARTS):
            axis, halved = order[2], order[1]
            here = self.place[axis]
            for step in (1, 3):
                wait_bytes(self.pieces(part, 16), self.recv.at[part, 1 + step])
                there = moved(self.place, axis, (here + 4 - step) % 4)
                at = list(span(there, order[:2]))
                half = step // 2
                if halved == "x":
                    at[4] = half
                else:
                    at[0 if halved == "z" else 3] = pl.ds(half * 2, 2)
                piece = self.buf.at[(*at, slice(None), pl.ds(first, width))]
                target = device_at(moved(self.place, axis, (here + step) % 4))
                remote(
                    piece, piece, self.send.at[part, 2], self.recv.at[part, 3], target
                ).start()
                self.forward(part, there, order[:2])

    def finish(self):
        for part, (_, order) in enumerate(PARTS):
            wait_bytes(self.pieces(part, 16), self.recv.at[part, 3])
            axis = order[2]
            there = moved(self.place, axis, (self.place[axis] + 2) % 4)
            self.forward(part, there, order[:2])
        for part in range(3):
            wait_bytes(self.pieces(part, 64), self.recv.at[part, 5])
            wait_bytes(self.pieces(part, 64), self.send.at[part, 3])
            wait_bytes(self.pieces(part, 3), self.send.at[part, 0])
            wait_bytes(self.pieces(part, 12), self.send.at[part, 1])
            wait_bytes(self.pieces(part, 48), self.send.at[part, 2])


VMEM = pl.BlockSpec(memory_space=pltpu.VMEM)
HBM = pl.BlockSpec(memory_space=pl.ANY)


def unpack(buf, staged, take, out_w, hidden_w, proj_w, out_sem):
    spans = ((0, 128, out_w), (128, GROUP, hidden_w), (208, GROUP, proj_w))
    staged[:, 0:32] = jnp.zeros((2, 32, D), bf16)
    staged[:, 112:128] = jnp.zeros((2, 16, D), bf16)

    @pl.loop(0, 16)
    def _(g):
        slot = g % 2
        outs = [
            pltpu.make_async_copy(
                staged.at[slot, pl.ds(at, count)], row_block(ref, g, count), out_sem.at[i, slot]
            )
            for i, (at, count, ref) in enumerate(spans)
        ]

        @pl.when(g >= 2)
        def _():
            for out in outs:
                out.wait()

        rows = nn(take[...], buf[g // 4, (g // 2) % 2, g % 2].reshape(256, D)).astype(bf16)
        staged[slot, 32:112] = rows[0:80]
        staged[slot, 128:288] = rows[80:240]
        for out in outs:
            out.start()

    for slot in range(2):
        for i, (at, count, ref) in enumerate(spans):
            pltpu.make_async_copy(
                staged.at[slot, pl.ds(at, count)], row_block(ref, 0, count), out_sem.at[i, slot]
            ).wait()


class Scatter:
    def __init__(self, away, mine, pair, lands, halves, send, recv, place):
        self.away, self.mine, self.pair = away, mine, pair
        self.lands, self.halves = lands, halves
        self.send, self.recv, self.place = send, recv, place
        self.sibling = device_at(moved(place, "c", 1 - place["c"]))

    def swap(self, number):
        at = (number // 2, number % 2)
        sems = (len(PARTS_BACK), number)
        return remote(
            self.away.at[at], self.pair.at[at], self.send.at[sems], self.recv.at[sems], self.sibling
        )

    def add_pair(self, number):
        self.swap(number).wait()
        at = (number // 2, number % 2)
        self.mine[at] = (self.mine[at].astype(f32) + self.pair[at].astype(f32)).astype(bf16)

    def source(self, part, stage, where):
        (first, width), order = PARTS_BACK[part]
        if stage == 0:
            at = span(where, order[:2], core=False)
            return self.mine.at[(*at, slice(None), pl.ds(first, width))]
        at = [
            slice(None) if axis in order[: 2 - stage] else value
            for axis, value in zip("zxyx", span(where, "", core=False))
            if axis in order[: 3 - stage]
        ]
        return self.halves[stage - 1][part].at[tuple(at)]

    def start(self, stage):
        for part, (_, order) in enumerate(PARTS_BACK):
            axis = order[2 - stage]
            for step in (1, 3, 2):
                target = moved(self.place, axis, (self.place[axis] + step) % 4)
                remote(
                    self.source(part, stage, target),
                    self.lands[stage][part].at[step - 1],
                    self.send.at[part, stage],
                    self.recv.at[part, stage],
                    device_at(target),
                ).start()

    def add(self, stage, out=None):
        for part, ((first, width), order) in enumerate(PARTS_BACK):
            land = self.lands[stage][part]
            wait_bytes(land, self.recv.at[part, stage])
            own = self.source(part, stage, self.place)
            lead = land.shape[1:-2]

            @pl.loop(0, math.prod(lead))
            def _(number):
                at = []
                for size in reversed(lead):
                    at.insert(0, number % size)
                    number = number // size
                at = tuple(at)
                total = own[at].astype(f32)
                for source in range(3):
                    total = total + land[(source, *at)].astype(f32)
                if stage < 2:
                    self.halves[stage][part][at] = total.astype(bf16)
                else:
                    out[:, first : first + width] = total

    def finish(self):
        for stage in range(3):
            for part in range(len(PARTS_BACK)):
                wait_bytes(self.lands[stage][part], self.send.at[part, stage])


def lead_of(axes):
    sizes = {"z": (4,), "x": (2, 2), "y": (4,)}
    if axes == {"x", "y"}:
        return (2, 4, 2)
    if axes == {"x", "z"}:
        return (4, 2, 2)
    return sum((sizes[axis] for axis in "zyx" if axis in axes), ())


def scatter_scratch():
    whole = pltpu.VMEM((4, 2, 4, 2, ROWS, D), bf16)
    lands, halves = [], []
    for stage in range(3):
        for (_, width), order in PARTS_BACK:
            lead = lead_of(set(order[: 2 - stage]))
            lands.append(pltpu.VMEM((3, *lead, ROWS, width), bf16))
            if stage < 2:
                halves.append(pltpu.VMEM((*lead, ROWS, width), bf16))
    semaphores = [pltpu.SemaphoreType.DMA((3, 8))] * 2
    return [whole] * 3 + lands + halves + semaphores


def scatter_of(scratch, place):
    away, mine, pair = scratch[:3]
    parts = len(PARTS_BACK)
    lands = [scratch[3 + parts * stage : 3 + parts * (stage + 1)] for stage in range(3)]
    halves = [scratch[3 + parts * stage : 3 + parts * (stage + 1)] for stage in (3, 4)]
    return Scatter(away, mine, pair, lands, halves, scratch[-2], scratch[-1], place)


HALVES = ((0, "yz"), (256, "zy"))


def ring_devices(place):
    others = [moved(place, "c", 1 - place["c"])]
    for step in (1, 3, 2):
        there = moved(place, "x", (place["x"] + step) % 4)
        others += [there, moved(there, "c", 1 - place["c"])]
    return others


def ring_number(place):
    return (place["x"] % 2) * 4 + place["c"] * 2 + place["x"] // 2


def tokens_of(ref, place):
    inner = (place["x"] % 2) * 2 + place["c"]
    return ref.at[inner, :, pl.ds((place["x"] // 2) * TOK, TOK)]


def head_of(place):
    return (place["x"] // 2) * 8 + (place["z"] % 2) * 4 + place["y"]


def pair_device(pair, quarter):
    micro, h = pair // H, pair % H
    return ((micro * 2 + (h % 8) // 4) * 4 + quarter, (h % 4) * 2 + h // 8)


def column_pieces(buf, half, place, free):
    at = [slice(None) if axis in free else place[axis] for axis in "zy"]
    return buf.at[(*at, slice(None), pl.ds(HALVES[half][0], 256))]


def gather_columns(buf, send, recv, place, stage):
    for half, (first, order) in enumerate(HALVES):
        axis = order[stage]
        if stage:
            wait_bytes(buf.at[0, pl.ds(0, 3), :, pl.ds(first, 256)], recv.at[half, 0])
        piece = column_pieces(buf, half, place, order[:stage])
        for step in (1, 3, 2):
            target = moved(place, axis, (place[axis] + step) % 4)
            remote(
                piece, piece, send.at[half, stage], recv.at[half, stage], device_at(target)
            ).start()


def finish_columns(buf, send, recv):
    for half, (first, _) in enumerate(HALVES):
        cols = pl.ds(first, 256)
        wait_bytes(buf.at[pl.ds(0, 3), :, :, cols], recv.at[half, 1])
        wait_bytes(buf.at[0, pl.ds(0, 3), :, cols], send.at[half, 0])
        wait_bytes(buf.at[pl.ds(0, 3), :, :, cols], send.at[half, 1])


def quarter_of(blk):
    inner = blk % 4
    return jnp.where((blk // 4) % 2 == 0, inner, 3 - inner)


def query_block(quarter, j):
    return j * 4 + jnp.where(j % 2 == 0, quarter, 3 - quarter)


def cell_of(ref, pair, width):
    return ref.at[pl.ds(pair // H * TOK, TOK), pl.ds(pair % H * width, width)]


def mask_of(key_block, block, start):
    key_at = key_block * B + lax.broadcasted_iota(jnp.int32, (B, B), 0)
    query_at = block * B + lax.broadcasted_iota(jnp.int32, (B, B), 1)
    return (key_at >= start) & (key_at <= query_at)


def has_mask(key_block, block):
    return (key_block == 0) | (key_block == block) | (block == 15)


def shift_matrix(rows, cols, by):
    row = lax.broadcasted_iota(jnp.int32, (rows, cols), 0)
    col = lax.broadcasted_iota(jnp.int32, (rows, cols), 1)
    return jnp.where((row - col == by) & (jnp.minimum(row, col) < HD), 1.0, 0.0).astype(bf16)


def wait_cells(ref, sem, fewer, width):
    wait_bytes(ref.at[:, pl.ds(0, 15 * width)], sem)
    wait_bytes(cell_of(ref, 0, width), sem)

    @pl.when(jnp.logical_not(fewer))
    def _():
        wait_bytes(cell_of(ref, 0, width), sem)


def stays_here(place):
    return (place["z"] % 2 == place["x"] % 2) & (place["y"] // 2 == place["c"])


def wait_ring(ref, sem, place):
    wait_bytes(ref.at[pl.ds(0, 3)], sem)
    wait_bytes(ref.at[0, pl.ds(0, 384)], sem)

    @pl.when(jnp.logical_not(stays_here(place)))
    def _():
        wait_bytes(ref.at[0, pl.ds(0, 128)], sem)


def front_kernel(
    tokens, pieces, pack, scale_row, segments, join, order, take,
    normed_out, packed_out, wide_w, vectors, starts, kv_out, queries, out_t, log_norms, attended,
    out_w, hidden_w, proj_w,
    ring_tokens, ring_pieces, chunks, kv, value_t, tops, totals, rounded, landed, buf, staged,
    x_tok_send, x_tok_recv, c_tok_send, c_tok_recv, piece_send, piece_recv, col_send, col_recv,
    two_send, two_recv, own_sem, send, recv, core_send, core_recv, x_send, x_recv,
    pass_send, pass_recv, back_send, back_recv, kv_sem, out_sem,
):
    blk = lax.axis_index("blk")
    head = lax.axis_index("head")
    core = blk % 2
    x_low = (blk // 2) % 2
    quarter = blk % 4
    even = (blk // 4) % 2 == 0
    place = my_place()
    pair = (place["z"] // 2) * H + head_of(place)
    turn = place["x"] * 2 + core
    sibling = (blk + 1 - 2 * core, head)
    two = Gather(buf, two_send, two_recv, place)
    own = two.begin(pack, own_sem.at[0])
    own_tokens = pltpu.make_async_copy(tokens, tokens_of(ring_tokens, place), own_sem.at[1])
    own_tokens.start()
    number = ring_number(place)
    pltpu.make_async_copy(pieces.at[turn], ring_pieces.at[number], piece_recv).start()
    greet_all()
    for there in ring_devices(place):
        remote(
            pieces.at[there["x"] * 2 + there["c"]],
            ring_pieces.at[number],
            piece_send,
            piece_recv,
            device_at(there),
        ).start()
    mine = tokens_of(ring_tokens, place)
    for step in (1, 3, 2):
        there = moved(place, "x", (place["x"] + step) % 4)
        remote(
            tokens, mine, x_tok_send.at[step - 1], x_tok_recv.at[step - 1], device_at(there)
        ).start()
    remote(tokens, mine, c_tok_send, c_tok_recv, sibling).start()
    own.wait()
    two.stage(0)
    ids = segments[place["z"] // 2]
    before = [jnp.sum((ids < value).astype(jnp.int32)) for value in range(1, 9)]
    for j in range(4):
        row = segments[place["z"] // 2, pl.ds(query_block(quarter, j), 1)]
        start = jnp.zeros_like(row)
        for value in range(1, 9):
            start = jnp.where(row == value, before[value - 1], start)
        starts[j] = start
    wait_bytes(ring_pieces, piece_recv)
    joined = nn(join[...], ring_pieces[...].reshape(256, MINE)).astype(bf16)
    chunks[place["z"], place["y"]] = joined
    gather_columns(chunks, col_send, col_recv, place, 0)
    gather_columns(chunks, col_send, col_recv, place, 1)
    for step in (1, 3, 2):
        wait_bytes(tokens, x_tok_recv.at[step - 1])
        there = moved(place, "x", (place["x"] + 4 - step) % 4)
        arrived = tokens_of(ring_tokens, there)
        remote(arrived, arrived, c_tok_send, c_tok_recv, sibling).start()
    own_tokens.wait()
    finish_columns(chunks, col_send, col_recv)
    vector_rows = jnp.zeros((16, MINE), f32)
    for z in range(4):
        wide_w[z * 4 * GROUP : (z + 1) * 4 * GROUP] = nn(order[...], chunks[z].reshape(4 * CHUNK, MINE)).astype(bf16)
        for y in range(4):
            vector_rows = vector_rows + chunks[z, y, GROUP:].astype(f32)
    vectors[...] = vector_rows
    bias = vector_rows[0:1]
    gain = jnp.concatenate([vector_rows[1:2], vector_rows[2:3], vector_rows[3:4, :256]], axis=1)
    one_lane = jnp.where(
        lax.broadcasted_iota(jnp.int32, (1, MINE), 1) % LANES == 3 * HD, 1.0, 0.0
    )
    wait_bytes(ring_tokens.at[pl.ds(0, 2)], c_tok_recv)

    def deliver(inner, aside, send, recv):
        block = place["z"] * 4 + inner
        to_quarter = (quarter_of(block) + aside) % 4
        for m in range(2):
            for h in range(2):
                blk_to, head_to = pair_device(m * H + turn * 2 + h, to_quarter)
                src = packed_out.at[inner, m, :, pl.ds(h * LANES, LANES)]
                dst = kv.at[block, pl.ds(place["y"] * 128, 128)]
                stays = (blk_to == blk) & (head_to == head)

                @pl.when(stays)
                def _():
                    pltpu.make_async_copy(src, dst, recv).start()

                @pl.when(jnp.logical_not(stays))
                def _():
                    remote(src, dst, send, recv, (blk_to, head_to)).start()

    @pl.loop(0, 4)
    def _(inner):
        values = ring_tokens[inner].reshape(256, D).astype(f32)
        normed = (values * inverse_rms(values) * gain).astype(bf16)
        normed_out[inner] = normed.reshape(4, 2, ROWS, D)
        full = nn(normed, wide_w[...])
        packed = ((full + bias) * scale_row[0:1] + one_lane).astype(bf16)
        packed_out[inner] = packed.reshape(2, 128, MINE)
        deliver(inner, 0, send, recv)

    @pl.loop(0, 4)
    def _(inner):
        deliver(inner, 2, x_send, x_recv)

    two.stage(1)
    wait_bytes(kv.at[pl.ds(0, 4)], recv)

    @pl.loop(0, 4)
    def _(j):
        block = kv.at[query_block(quarter, j)]
        remote(block, block, core_send, core_recv, sibling).start()

    def turn_values(of_quarter):
        @pl.loop(0, 4)
        def _(j):
            b = query_block(of_quarter, j)
            value_t[b] = kv[b, :, 128:].T

    pick = shift_matrix(LANES, 128, HD)

    @pl.loop(0, 4)
    def _(j):
        queries[j] = nn(kv[query_block(quarter, j)], pick).astype(bf16)
        tops[j] = jnp.full((1, B), NEGATIVE, f32)
        totals[j] = jnp.zeros((1, B), f32)
        out_t[j] = jnp.zeros((128, B), f32)

    turn_values(quarter)

    def step(j, block, key_block):
        def tile(masked):
            s = nt(kv[key_block, :, :128], queries[j])
            if masked:
                s = jnp.where(mask_of(key_block, block, starts[j]), s, NEGATIVE)
            top = tops[j]
            new_top = jnp.maximum(top, jnp.max(s, axis=0, keepdims=True))
            p = jnp.exp(s - new_top)
            scale = jnp.exp(top - new_top)
            tops[j] = new_top
            totals[j] = totals[j] * scale + jnp.sum(p, axis=0, keepdims=True)
            out_t[j] = out_t[j] * scale + nn(value_t[key_block], p.astype(bf16))

        masked = has_mask(key_block, block)
        pl.when(masked)(lambda: tile(True))
        pl.when(jnp.logical_not(masked))(lambda: tile(False))

    def key_pass(j, of_quarter, count):
        block = query_block(quarter, j)

        @pl.loop(0, count)
        def _(n):
            step(j, block, query_block(of_quarter, n))

    @pl.loop(0, 4)
    def _(j):
        key_pass(j, quarter, j + 1)

    two.stage(2)
    wait_bytes(kv.at[pl.ds(0, 4)], core_recv)
    beside = quarter + 1 - 2 * core
    turn_values(beside)

    @pl.loop(0, 4)
    def _(j):
        key_pass(j, beside, j + query_block(quarter, j) % 2)

    wait_bytes(kv.at[pl.ds(0, 4)], x_recv)
    across = (quarter + 2) % 4
    for_sibling = [kv.at[query_block(across, j)] for j in range(4)]
    for block in for_sibling:
        remote(block, block, pass_send, pass_recv, sibling).start()
    turn_values(across)

    @pl.loop(0, 4)
    def _(j):
        key_pass(j, across, j + (j + x_low) % 2)

    two.relay()
    wait_bytes(kv.at[pl.ds(0, 4)], pass_recv)
    keep = pltpu.make_async_copy(kv, kv_out, kv_sem)
    keep.start()
    across_beside = across + 1 - 2 * core
    turn_values(across_beside)

    @pl.loop(0, 4)
    def _(i):
        j = 3 - i
        block = query_block(quarter, j)
        key_pass(j, across_beside, j + (j + x_low) % 2)
        acc = out_t[j]
        result = acc / acc[112:113]
        out_t[j] = result
        log_norms[j] = tops[j] + jnp.log(totals[j])
        rounded[j] = result.T.astype(bf16)

        @pl.loop(0, 8)
        def _(k):
            h = (head + k) % 8
            src = rounded.at[j, pl.ds(h * TOK, TOK)]
            dst = cell_of(landed, pair, 128)
            mine = (k == 0) & (block == blk)

            @pl.when(mine)
            def _():
                pltpu.make_async_copy(src, dst, back_recv).start()

            @pl.when(jnp.logical_not(mine))
            def _():
                remote(src, dst, back_send, back_recv, (block, h)).start()

    two.finish()
    unpack(buf, staged, take, out_w, hidden_w, proj_w, out_sem)
    wait_bytes(landed, back_recv)
    attended[...] = landed[...]
    keep.wait()
    for sem in (core_send, pass_send):
        wait_bytes(kv.at[pl.ds(0, 4)], sem)
    wait_cells(landed, back_send, even, 128)
    wait_bytes(ring_pieces.at[pl.ds(0, 7)], piece_send)
    for step_at in range(3):
        wait_bytes(tokens, x_tok_send.at[step_at])
    wait_bytes(ring_tokens.at[pl.ds(0, 2)], c_tok_send)
    wait_ring(kv, send, place)
    wait_ring(kv, x_send, place)


def front(*operands):
    dma = pltpu.SemaphoreType.DMA
    return pl.pallas_call(
        front_kernel,
        out_shape=(
            jax.ShapeDtypeStruct((4, 4, 2, ROWS, D), bf16),
            jax.ShapeDtypeStruct((4, 2, 128, MINE), bf16),
            jax.ShapeDtypeStruct((D, MINE), bf16),
            jax.ShapeDtypeStruct((16, MINE), f32),
            jax.ShapeDtypeStruct((4, 1, B), jnp.int32),
            jax.ShapeDtypeStruct((16, B, LANES), bf16),
            jax.ShapeDtypeStruct((4, B, 128), bf16),
            jax.ShapeDtypeStruct((4, 128, B), f32),
            jax.ShapeDtypeStruct((4, 1, B), f32),
            jax.ShapeDtypeStruct((2 * TOK, OUT_WIDE), bf16),
            jax.ShapeDtypeStruct((OUT_WIDE, D), bf16),
            jax.ShapeDtypeStruct((D, D), bf16),
            jax.ShapeDtypeStruct((D, D), bf16),
        ),
        in_specs=[VMEM] * 8,
        out_specs=(VMEM,) * 5 + (HBM,) + (VMEM,) * 4 + (HBM,) * 3,
        scratch_shapes=[
            pltpu.VMEM((4, 2, 128, D), bf16),
            pltpu.VMEM((8, ROWS, MINE), bf16),
            pltpu.VMEM((4, 4, CHUNK, MINE), bf16),
            pltpu.VMEM((16, B, LANES), bf16),
            pltpu.VMEM((16, 128, B), bf16),
            pltpu.VMEM((4, 1, B), f32),
            pltpu.VMEM((4, 1, B), f32),
            pltpu.VMEM((4, B, 128), bf16),
            pltpu.VMEM((2 * TOK, OUT_WIDE), bf16),
            pltpu.VMEM((4, 2, 2, 4, 2, ROWS, D), bf16),
            pltpu.VMEM((2, 288, D), bf16),
            dma((3,)), dma((3,)), dma, dma, dma, dma, dma((2, 2)), dma((2, 2)),
            dma((3, 4)), dma((3, 6)), dma((2,)),
        ]
        + [dma] * 11
        + [dma((3, 2))],
        compiler_params=pltpu.CompilerParams(
            collective_id=0, has_side_effects=True, vmem_limit_bytes=56 * 2**20
        ),
        name="front",
    )(
        *operands,
        jnp.asarray(JOIN, bf16),
        jnp.asarray(ORDER, bf16),
        jnp.asarray(TAKE, bf16),
    )


def rear_kernel(
    pack, kv, queries, starts, out_t, log_norms,
    attended, d_branch, normed_two, d_pre, activated, upstream,
    normed, packed, wide_w, vector_grads, scale_row, take_t, share, order_t,
    d_normed, pieces_out, two_out,
    d_out, key_t, deltas, d_query, d_kv, mine_kv, half, half_in, cross, cross_in, final, d_wide,
    attended_t, normed_two_t, activated_t, right,
    partial_in, sum_in, grad_chunks, first_in, second_in, first_sum,
    joined, shares, shares_in,
    send, recv, core_send, core_recv, x_send, x_recv, back_send, back_recv,
    normed_sem, c_send, c_recv, sum_send, sum_recv, col_send, col_recv, share_send, share_recv,
    *scratch,
):
    blk = lax.axis_index("blk")
    head = lax.axis_index("head")
    core = blk % 2
    x_low = (blk // 2) % 2
    quarter = blk % 4
    place = my_place()
    my_head = head_of(place)
    pair = (place["z"] // 2) * H + my_head
    to_quarter = quarter_of(blk)
    even = (blk // 4) % 2 == 0
    two = scatter_of(scratch, place)
    greet_all()

    @pl.loop(0, PAIRS)
    def _(k):
        p = (pair + k) % PAIRS
        src = cell_of(pack, p, 128)
        dst = d_out.at[blk // 4, pl.ds(head * TOK, TOK)]
        mine = (k == 0) & even

        @pl.when(mine)
        def _():
            pltpu.make_async_copy(src, dst, recv).start()

        @pl.when(jnp.logical_not(mine))
        def _():
            remote(src, dst, send, recv, pair_device(p, to_quarter)).start()

    for n in range(D // 128):
        lanes = slice(n * 128, n * 128 + 128)
        normed_two_t[lanes] = normed_two[:, lanes].T
        activated_t[lanes] = activated[:, lanes].T
    for n in range(H):
        lanes = slice(n * 128, n * 128 + 128)
        attended_t[lanes] = attended[:, lanes].T
    right[0:128] = d_branch[...]
    right[128:256] = d_pre[...]
    right[256:384] = upstream[...]

    def produce(number, of_core, into):
        group = number * 2 + of_core
        rows = pl.ds(pl.multiple_of(group * GROUP, 16), GROUP)
        out_rows = pl.ds(pl.multiple_of(group * 128 + 32, 16), GROUP)
        left = jnp.concatenate(
            [
                nn(take_t[0], attended_t[out_rows]).astype(bf16),
                nn(take_t[1], normed_two_t[rows]).astype(bf16),
                nn(take_t[2], activated_t[rows]).astype(bf16),
            ],
            axis=1,
        )
        for cell in range(5):
            lanes = slice(cell * LANES, (cell + 1) * LANES)
            block = nn(left, right[:, lanes]).astype(bf16)
            into[number // 2, number % 2, :, :, :, lanes] = block.reshape(4, 2, ROWS, LANES)

    @pl.loop(0, 8)
    def _(number):
        produce(number, 1 - core, two.away)
        two.swap(number).start()

    @pl.loop(0, 8)
    def _(number):
        produce(number, core, two.mine)

    @pl.loop(0, 16)
    def _(b):
        key_t[b] = kv[b, :, :128].T

    load_normed = pltpu.make_async_copy(normed, two.pair.at[:, 0], normed_sem)
    wait_bytes(d_out, recv)

    @pl.loop(0, 4)
    def _(j):
        deltas[j] = jnp.sum(d_out[j].astype(f32).T * out_t[j], axis=0, keepdims=True)
        d_query[j] = jnp.zeros((128, B), f32)

    sibling = (blk + 1 - 2 * core, head)

    def step(j, block, key_block):
        def tile(masked):
            q = queries[j]
            do = d_out[j]
            p = jnp.exp(nt(kv[key_block, :, :128], q) - log_norms[j])
            if masked:
                p = jnp.where(mask_of(key_block, block, starts[j]), p, 0.0)
            dp = nt(kv[key_block, :, 128:], do)
            ds = (p * (dp - deltas[j])).astype(bf16)
            d_kv[:, :128] += nn(ds, q)
            d_kv[:, 128:] += nn(p.astype(bf16), do)
            d_query[j] += nn(key_t[key_block], ds)

        masked = has_mask(key_block, block)
        pl.when(masked)(lambda: tile(True))
        pl.when(jnp.logical_not(masked))(lambda: tile(False))

    def swap(n):
        return remote(
            half.at[n], half_in.at[n], core_send.at[n], core_recv.at[n], sibling
        )

    shift = shift_matrix(128, LANES, -HD)

    partner = (blk + 2 - 4 * x_low, head)

    def cross_swap(z):
        return remote(cross.at[z], cross_in.at[z], x_send.at[z], x_recv.at[z], partner)

    def core_sum(z):
        own = 2 * z + (x_low + z) % 2
        other = 4 * z + 1 - own
        swap(other).wait()
        cross[z] = (mine_kv[other] + half_in[other].astype(f32)).astype(bf16)
        cross_swap(z).start()
        swap(own).wait()
        mine_kv[own] = (
            mine_kv[own]
            + half_in[own].astype(f32)
            + nn(d_query[z].T.astype(bf16), shift)
        )

    def finish(z):
        cross_swap(z).wait()
        own = 2 * z + (x_low + z) % 2
        final[z] = (mine_kv[own] + cross_in[z].astype(f32)).astype(bf16)
        inner = query_block(quarter, z) % 4
        dst = d_wide.at[inner, place["z"] // 2, :, pl.ds((my_head % 2) * LANES, LANES)]

        @pl.loop(0, 4)
        def _(k):
            y = (place["y"] + k) % 4
            there = {"x": my_head // 4, "y": y, "z": z, "c": (my_head // 2) % 2}
            src = final.at[z, pl.ds(y * 128, 128)]
            blk_to, head_to = device_at(there)
            stays = (blk_to == blk) & (head_to == head)

            @pl.when(stays)
            def _():
                pltpu.make_async_copy(src, dst, back_recv).start()

            @pl.when(jnp.logical_not(stays))
            def _():
                remote(src, dst, back_send, back_recv, (blk_to, head_to)).start()

    @pl.loop(0, 8)
    def _(part):
        z = part // 2

        @pl.loop(2 * part, 2 * part + 2)
        def _(key_block):
            d_kv[...] = jnp.zeros((B, LANES), f32)
            first = z + (query_block(quarter, z) < key_block).astype(jnp.int32)

            @pl.loop(first, 4)
            def _(j):
                step(j, query_block(quarter, j), key_block)

            n = 2 * z + (key_block % 4) // 2

            @pl.when((key_block + z + core) % 2 == 0)
            def _():
                mine_kv[n] = d_kv[...]

            @pl.when((key_block + z + core) % 2 == 1)
            def _():
                half[n] = d_kv[...].astype(bf16)
                swap(n).start()

        @pl.when((part % 2 == 0) & (part > 0))
        def _():
            core_sum(z - 1)

        @pl.when((part % 2 == 1) & (part > 1))
        def _():
            finish(z - 1)

        @pl.when(part == 0)
        def _():
            @pl.loop(0, 8)
            def _(number):
                two.add_pair(number)

            load_normed.start()
            two.start(0)

    core_sum(3)
    two.add(0)
    two.start(1)
    finish(3)
    wait_bytes(d_wide, back_recv)

    load_normed.wait()
    partial, normed_here = two.away.at[:, 0], two.pair.at[:, 0]
    summed = two.away.at[:, 1]
    scale = scale_row[0:1]
    bias_sum = jnp.zeros((1, MINE), f32)
    scale_sum = jnp.zeros((1, MINE), f32)
    for inner in range(4):
        grad = d_wide[inner].reshape(256, MINE).astype(f32)
        scale_sum = scale_sum + jnp.sum(
            grad * packed[inner].reshape(256, MINE).astype(f32), axis=0, keepdims=True
        )
        grad = (grad * scale).astype(bf16)
        d_wide[inner] = grad.reshape(2, 128, MINE)
        bias_sum = bias_sum + jnp.sum(grad.astype(f32), axis=0, keepdims=True)
    scale_sum = scale_sum[:, :LANES] + scale_sum[:, LANES:]
    rows = vector_grads[...] + jnp.concatenate(
        [bias_sum, jnp.concatenate([scale_sum, scale_sum], axis=1), jnp.zeros((14, MINE), f32)],
        axis=0,
    )
    rows = rows.astype(bf16)
    for z in range(4):
        left = jnp.concatenate(
            [normed_here[inner, :, :, :, z * 320 // 128 * 128 : z * 320 // 128 * 128 + 384].reshape(256, 384)
             for inner in range(4)],
            axis=0,
        )
        skip = z * 320 % 128
        grads = tn(left, d_wide[...].reshape(1024, MINE))[skip : skip + 320].astype(bf16)
        grad_chunks[z] = nn(order_t[...], grads).astype(bf16).reshape(4, CHUNK, MINE)
        for y in range(4):
            grad_chunks[z, y, GROUP:] = rows

    for step_at in (1, 3, 2):
        for half, axis in enumerate("zy"):
            there = moved(place, axis, (place[axis] + step_at) % 4)
            remote(
                column_pieces(grad_chunks, half, there, "y" if half == 0 else "z"),
                first_in.at[half, step_at - 1],
                col_send.at[half, 0],
                col_recv.at[half, 0],
                device_at(there),
            ).start()
    sibling_at = (blk + 1 - 2 * core, head)
    c_swaps = [
        remote(
            partial.at[low * 2 + 1 - core],
            partial_in.at[low],
            c_send.at[low],
            c_recv.at[low],
            sibling_at,
        )
        for low in range(2)
    ]
    for number in range(4):
        inner = (number % 2) * 2 + (1 - core if number < 2 else core)
        back = nt(d_wide[inner].reshape(256, MINE), wide_w[...])
        partial[inner] = back.astype(bf16).reshape(4, 2, ROWS, D)
        if number < 2:
            c_swaps[number].start()
    for low in range(2):
        c_swaps[low].wait()
        summed[low] = (
            partial[low * 2 + core].astype(f32) + partial_in[low].astype(f32)
        ).astype(bf16)
    for step_at in (1, 3, 2):
        there = moved(place, "x", (place["x"] + step_at) % 4)
        for m in range(2):
            remote(
                summed.at[there["x"] % 2, m * 2 + there["x"] // 2],
                sum_in.at[step_at - 1, m],
                sum_send,
                sum_recv,
                device_at(there),
            ).start()
    two.add(1)
    two.start(2)
    for half in range(2):
        wait_bytes(first_in.at[half], col_recv.at[half, 0])
        own = column_pieces(grad_chunks, half, place, "y" if half == 0 else "z")
        for number in range(4):
            total = own[number].astype(f32)
            for source in range(3):
                total = total + first_in[half, source, number].astype(f32)
            first_sum[half, number] = total.astype(bf16)
    for step_at in (1, 3, 2):
        for half, axis in enumerate("yz"):
            there = moved(place, axis, (place[axis] + step_at) % 4)
            remote(
                first_sum.at[half, there[axis]],
                second_in.at[half, step_at - 1],
                col_send.at[half, 1],
                col_recv.at[half, 1],
                device_at(there),
            ).start()
    totals = []
    for half, axis in enumerate("yz"):
        wait_bytes(second_in.at[half], col_recv.at[half, 1])
        total = first_sum[half, place[axis]].astype(f32)
        for source in range(3):
            total = total + second_in[half, source].astype(f32)
        totals.append(total)
    total_y, total_z = totals
    joined[:, 0:256] = total_y.astype(bf16)
    joined[:, 256:512] = total_z.astype(bf16)
    shares[...] = nn(share[...], joined[...]).astype(bf16).reshape(8, ROWS, MINE)
    turn = place["x"] * 2 + core
    for there in ring_devices(place):
        remote(
            shares.at[ring_number(there)],
            shares_in.at[turn],
            share_send,
            share_recv,
            device_at(there),
        ).start()
    pltpu.make_async_copy(
        shares.at[ring_number(place)], shares_in.at[turn], share_recv
    ).start()
    two.add(2, two_out)
    two.finish()
    wait_bytes(sum_in, sum_recv)
    for m in range(2):
        total = summed[x_low, m * 2 + place["x"] // 2].astype(f32)
        for source in range(3):
            total = total + sum_in[source, m].astype(f32)
        d_normed[m * TOK : (m + 1) * TOK] = total.reshape(TOK, D)
    wait_bytes(shares_in, share_recv)
    pieces_out[...] = shares_in[...]
    wait_cells(pack, send, even, 128)
    wait_ring(final, back_send, place)
    wait_bytes(sum_in, sum_send)
    for number in range(2):
        wait_bytes(first_in.at[number], col_send.at[number, 0])
        wait_bytes(second_in.at[number], col_send.at[number, 1])
    wait_bytes(shares.at[pl.ds(0, 7)], share_send)


def rear(*operands):
    dma = pltpu.SemaphoreType.DMA
    return pl.pallas_call(
        rear_kernel,
        out_shape=(
            jax.ShapeDtypeStruct((2 * TOK, D), f32),
            jax.ShapeDtypeStruct((8, ROWS, MINE), bf16),
            jax.ShapeDtypeStruct((ROWS, D), f32),
        ),
        in_specs=[VMEM] * 12 + [HBM] + [VMEM] * 7,
        out_specs=(VMEM, VMEM, VMEM),
        scratch_shapes=[
            pltpu.VMEM((4, B, 128), bf16),
            pltpu.VMEM((16, 128, B), bf16),
            pltpu.VMEM((4, 1, B), f32),
            pltpu.VMEM((4, 128, B), f32),
            pltpu.VMEM((B, LANES), f32),
            pltpu.VMEM((8, B, LANES), f32),
            pltpu.VMEM((8, B, LANES), bf16),
            pltpu.VMEM((8, B, LANES), bf16),
            pltpu.VMEM((4, B, LANES), bf16),
            pltpu.VMEM((4, B, LANES), bf16),
            pltpu.VMEM((4, B, LANES), bf16),
            pltpu.VMEM((4, 2, 128, MINE), bf16),
            pltpu.VMEM((OUT_WIDE, 128), bf16),
            pltpu.VMEM((D, 128), bf16),
            pltpu.VMEM((D, 128), bf16),
            pltpu.VMEM((384, D), bf16),
            pltpu.VMEM((2, 4, 2, ROWS, D), bf16),
            pltpu.VMEM((3, 2, 2, ROWS, D), bf16),
            pltpu.VMEM((4, 4, CHUNK, MINE), bf16),
            pltpu.VMEM((2, 3, 4, CHUNK, 256), bf16),
            pltpu.VMEM((2, 3, CHUNK, 256), bf16),
            pltpu.VMEM((2, 4, CHUNK, 256), bf16),
            pltpu.VMEM((CHUNK, MINE), bf16),
            pltpu.VMEM((8, ROWS, MINE), bf16),
            pltpu.VMEM((8, ROWS, MINE), bf16),
            dma, dma, dma((8,)), dma((8,)), dma((4,)), dma((4,)), dma, dma,
            dma, dma((2,)), dma((2,)), dma, dma, dma((2, 2)), dma((2, 2)), dma, dma,
        ]
        + scatter_scratch(),
        compiler_params=pltpu.CompilerParams(
            collective_id=1, has_side_effects=True, vmem_limit_bytes=63 * 2**20
        ),
        name="rear",
    )(
        *operands,
        jnp.asarray(TAKE_T, bf16),
        jnp.asarray(SHARE, bf16),
        jnp.asarray(ORDER.T, bf16),
    )


def on_device(
    inputs,
    segment_ids,
    norm1_gain,
    w_query,
    w_key,
    w_value,
    query_bias,
    value_bias,
    w_out,
    out_bias,
    norm2_gain,
    w_hidden,
    hidden_bias,
    w_proj,
    proj_bias,
    dim_scale,
    cotangent,
):
    blk = lax.axis_index("blk")
    head = lax.axis_index("head")
    at = (blk * 8 + head) * 10
    spread_heads = jnp.zeros((H, LANES), bf16)
    for i, vector in ((1, query_bias), (2, value_bias)):
        spread_heads = lax.dynamic_update_slice(
            spread_heads, vector[None], (blk, i * HD + head * 10)
        )
    natural = jnp.stack([norm1_gain, out_bias, norm2_gain, hidden_bias, proj_bias])
    natural = lax.dynamic_update_slice(jnp.zeros((5, 3 * MINE), bf16), natural, (0, at))
    columns = jnp.concatenate(
        [w.reshape(10, H, HD) for w in (w_key, w_query, w_value)]
        + [jnp.zeros((10, H, LANES - 3 * HD), bf16)],
        axis=2,
    )
    columns = columns.reshape(10, 8, MINE).transpose(1, 0, 2)
    pieces = jnp.concatenate(
        [
            columns,
            jnp.zeros((8, 6, MINE), bf16),
            spread_heads.reshape(8, 1, MINE),
            jnp.broadcast_to(natural.reshape(1, 15, MINE), (8, 15, MINE)),
        ],
        axis=1,
    )
    pack = jnp.concatenate([w_out, w_hidden, w_proj, jnp.zeros((2, D), bf16)], axis=0)
    softplus_scale = LOG2E / math.sqrt(HD) * jax.nn.softplus(dim_scale)
    ones = jnp.ones((HD,), f32)
    scale_row = jnp.concatenate(
        [ones, softplus_scale, ones, jnp.zeros((LANES - 3 * HD,), f32)] * 2
    )
    scale_row = jnp.broadcast_to(scale_row, (8, MINE))

    (
        ring_normed, packed, wide_w, vectors, starts, kv, queries, out_t, log_norms, attended,
        out_w, hidden_w, proj_w,
    ) = front(inputs, pieces, pack, scale_row, segment_ids.reshape(2, 16, B))
    every = vectors[1:].reshape(5, 3 * MINE)[:, :D]
    gain_one, out_b, gain_two, hidden_b, proj_b = [every[i] for i in range(5)]

    tokens = inputs.reshape(2 * TOK, D).astype(f32)
    residual = tokens + nn(attended, out_w) + out_b
    inverse_two = inverse_rms(residual)
    normed_two = (residual * inverse_two * gain_two).astype(bf16)
    pre_act = nn(normed_two, hidden_w) + hidden_b
    gate = jax.nn.sigmoid(pre_act)
    activated = (pre_act * gate).astype(bf16)
    layer_out = (residual + nn(activated, proj_w) + proj_b).astype(bf16)

    upstream_low = cotangent.reshape(2 * TOK, D)
    upstream = upstream_low.astype(f32)
    d_pre = (nt(upstream_low, proj_w) * gate * (1.0 + pre_act * (1.0 - gate))).astype(bf16)
    d_normed_two = nt(d_pre, hidden_w)
    d_residual = upstream + norm_back(d_normed_two * gain_two, residual, inverse_two)
    d_branch = d_residual.astype(bf16)
    d_attended = nt(d_branch, out_w).astype(bf16)

    def total(values):
        return jnp.sum(values.astype(f32), axis=0)

    vector_grads = jnp.stack(
        [
            total(d_branch),
            total(d_normed_two * residual * inverse_two),
            total(d_pre),
            total(upstream),
        ]
    )
    vector_grads = jnp.pad(vector_grads, ((0, 0), (0, 3 * MINE - D))).reshape(12, MINE)
    vector_grads = jnp.pad(vector_grads, ((4, 0), (0, 0)))
    d_normed, shares, two = rear(
        d_attended, kv, queries, starts, out_t, log_norms,
        attended, d_branch, normed_two, d_pre, activated, upstream_low,
        ring_normed, packed, wide_w, vector_grads, scale_row,
    )
    inverse_one = inverse_rms(tokens)
    input_grad = (
        d_residual + norm_back(d_normed * gain_one, tokens, inverse_one)
    ).astype(bf16)

    shares = shares.astype(f32)
    columns = shares[:, :10].transpose(1, 0, 2).reshape(10, H, LANES)
    d_key_w, d_query_w, d_value_w = [
        columns[:, :, i * HD : (i + 1) * HD].reshape(10, D) for i in range(3)
    ]
    by_head = shares[:, 16].reshape(H, LANES)
    d_query_bias, d_value_bias = [
        lax.dynamic_slice(by_head, (blk, i * HD + head * 10), (1, 10)).reshape(10) for i in (1, 2)
    ]
    summed = jnp.sum(shares[:, 17:], axis=0)
    scale_grad = summed[0, HD : 2 * HD] / softplus_scale
    scale_grad = scale_grad * (LOG2E / math.sqrt(HD)) * jax.nn.sigmoid(dim_scale)
    natural = lax.dynamic_slice(summed.reshape(5, 3 * MINE), (0, at), (5, 10))
    norm1_gain_grad = sum(
        jnp.sum(w.astype(f32) * grad, axis=1)
        for w, grad in ((w_query, d_query_w), (w_key, d_key_w), (w_value, d_value_w))
    ) / norm1_gain.astype(f32)
    return (
        layer_out.reshape(2, TOK, D),
        input_grad.reshape(2, TOK, D),
        norm1_gain_grad,
        d_query_w,
        d_key_w,
        d_value_w,
        d_query_bias,
        d_value_bias,
        two[0:10],
        natural[1],
        natural[2],
        two[10:20],
        natural[3],
        two[20:30],
        natural[4],
        scale_grad,
    )


def solution(mesh):
    rows = P(("blk", "head"), None)
    vec = P(("blk", "head"))
    tok = P(None, ("blk", "head"), None)
    in_specs = (
        tok, P(), vec, rows, rows, rows, vec, vec, rows, vec, vec, rows, vec, rows, vec, P(), tok
    )
    out_specs = (
        tok, tok, vec, rows, rows, rows, vec, vec, rows, vec, vec, rows, vec, rows, vec, P()
    )
    return jax.shard_map(
        on_device, mesh=mesh, in_specs=in_specs, out_specs=out_specs, check_vma=False
    )
```

```python
import functools
import math

import jax
import jax.numpy as jnp
import numpy as np
from jax import lax
from jax.experimental import pallas as pl
from jax.experimental.pallas import tpu as pltpu
from jax.sharding import PartitionSpec as P

D = 1280
H = 16
HD = 80
FF = 1280
B = 512
TOK = 64
PAIRS = 32
LANES = 256
ROWS = 32
WIDE = H * LANES
OUT_WIDE = H * 128
GROUP = 80
CHUNK = 96
MINE = 512
EPSILON = 1e-06
LOG2E = 1.442695041
NEGATIVE = -1e30
MESH = pl.DeviceIdType.MESH
f32 = jnp.float32
bf16 = jnp.bfloat16

PARTS = (((0, 512), "xyz"), ((512, 384), "yzx"), ((896, 384), "zxy"))
PARTS_BACK = (((0, 512), "xyz"), ((512, 512), "xzy"), ((1024, 256), "yzx"))


def inverse_rms(values):
    return lax.rsqrt(jnp.mean(values * values, axis=-1, keepdims=True) + EPSILON)


def norm_back(upstream, values, inverse):
    return inverse * upstream - values * inverse**3 * jnp.mean(
        upstream * values, axis=-1, keepdims=True
    )


def nn(a, b):
    return lax.dot_general(a, b, (((1,), (0,)), ((), ())), preferred_element_type=f32)


def nt(a, b):
    return lax.dot_general(a, b, (((1,), (1,)), ((), ())), preferred_element_type=f32)


def tn(a, b):
    return lax.dot_general(a, b, (((0,), (0,)), ((), ())), preferred_element_type=f32)


def my_place():
    blk = lax.axis_index("blk")
    head = lax.axis_index("head")
    return {
        "x": (head % 2) * 2 + (blk // 2) % 2,
        "y": head // 2,
        "z": blk // 4,
        "c": blk % 2,
    }


def device_at(place):
    x, y, z, c = place["x"], place["y"], place["z"], place["c"]
    return (z * 4 + (x % 2) * 2 + c, y * 2 + x // 2)


def span(place, free, core=True):
    x, y, z = place["x"], place["y"], place["z"]
    whole = slice(None)
    at = [
        whole if "z" in free else z,
        whole if "x" in free else x % 2,
        place["c"],
        whole if "y" in free else y,
        whole if "x" in free else x // 2,
    ]
    return tuple(at if core else at[:2] + at[3:])


def moved(place, axis, value):
    other = dict(place)
    other[axis] = value
    return other


def greet(peers):
    barrier = pltpu.get_barrier_semaphore()
    for peer in peers:
        pl.semaphore_signal(barrier, inc=1, device_id=peer, device_id_type=MESH)
    pl.semaphore_wait(barrier, len(peers))


def greet_all():
    barrier = pltpu.get_barrier_semaphore()
    me = lax.axis_index("blk") * 8 + lax.axis_index("head")

    @pl.loop(1, 128)
    def _(k):
        other = (me + k) % 128
        pl.semaphore_signal(
            barrier, inc=1, device_id=(other // 8, other % 8), device_id_type=MESH
        )

    pl.semaphore_wait(barrier, 127)


def ring_peers(place):
    peers = [device_at(moved(place, "c", 1 - place["c"]))]
    for axis in "xyz":
        for step in (1, 3, 2):
            peers.append(device_at(moved(place, axis, (place[axis] + step) % 4)))
    return peers


def wait_bytes(ref, sem):
    pltpu.make_async_copy(ref, ref, sem).wait()


def remote(src, dst, send, recv, device):
    return pltpu.make_async_remote_copy(
        src_ref=src, dst_ref=dst, send_sem=send, recv_sem=recv, device_id=device, device_id_type=MESH
    )


def varied(place, axes, number):
    other = dict(place)
    for axis in axes:
        other[axis] = number % 4
        number = number // 4
    return other


def selections():
    take = np.zeros((240, 256), np.float32)
    join = np.zeros((CHUNK, 256), np.float32)
    order = np.zeros((4 * GROUP, 4 * CHUNK), np.float32)
    for i in range(8):
        for j in range(10):
            for w in range(3):
                take[w * GROUP + i * 10 + j, i * ROWS + w * 10 + j] = 1
            join[i * 10 + j, i * ROWS + j] = 1
            inner, x_high = i // 2, i % 2
            for y in range(4):
                order[inner * GROUP + (y * 2 + x_high) * 10 + j, y * CHUNK + i * 10 + j] = 1
        for v in range(16):
            join[GROUP + v, i * ROWS + 16 + v] = 1
    share = join.T.copy()
    return take, join, share, order


TAKE, JOIN, SHARE, ORDER = selections()
TAKE_T = TAKE.reshape(3, GROUP, 256).transpose(0, 2, 1)


def row_block(ref, g, count):
    return ref.at[pl.ds(pl.multiple_of(g * count, 16), count)]


class Gather:
    def __init__(self, buf, send, recv, place):
        self.place = place
        self.buf, self.send, self.recv = buf, send, recv
        self.sibling = device_at(moved(place, "c", 1 - place["c"]))

    def begin(self, pack, sem):
        own = pltpu.make_async_copy(pack, self.buf.at[span(self.place, "")], sem)
        own.start()
        return own

    def piece(self, part, where, free):
        first, width = PARTS[part][0]
        return self.buf.at[(*span(where, free), slice(None), pl.ds(first, width))]

    def pieces(self, part, count):
        cols = pl.ds(*PARTS[part][0])
        whole = slice(None)
        at = {
            3: (pl.ds(0, 3), 0, 0, 0, 0),
            12: (pl.ds(0, 3), 0, 0, whole, 0),
            16: (0, whole, 0, whole, whole),
            48: (pl.ds(0, 3), whole, 0, whole, whole),
            64: (whole, whole, 0, whole, whole),
        }[count]
        return self.buf.at[(*at, whole, cols)]

    def forward(self, part, where, free):
        piece = self.piece(part, where, free)
        remote(piece, piece, self.send.at[part, 3], self.recv.at[part, 5], self.sibling).start()

    def stage(self, stage):
        for part, (_, order) in enumerate(PARTS):
            if stage:
                wait_bytes(self.pieces(part, 3 * 4 ** (stage - 1)), self.recv.at[part, stage - 1])
            piece = self.piece(part, self.place, order[:stage])
            axis = order[stage]
            for step in (1, 3, 2) if stage < 2 else (1, 3):
                target = moved(self.place, axis, (self.place[axis] + step) % 4)
                slot = stage if stage < 2 else 1 + step
                remote(
                    piece,
                    piece,
                    self.send.at[part, stage],
                    self.recv.at[part, slot],
                    device_at(target),
                ).start()
        for part, (_, order) in enumerate(PARTS):
            if stage == 0:
                self.forward(part, self.place, "")
            else:
                axis = order[stage - 1]
                for step in (1, 3, 2):
                    there = moved(self.place, axis, (self.place[axis] + 4 - step) % 4)
                    self.forward(part, there, order[: stage - 1])

    def relay(self):
        for part, ((first, width), order) in enumerate(PARTS):
            axis, halved = order[2], order[1]
            here = self.place[axis]
            for step in (1, 3):
                wait_bytes(self.pieces(part, 16), self.recv.at[part, 1 + step])
                there = moved(self.place, axis, (here + 4 - step) % 4)
                at = list(span(there, order[:2]))
                half = step // 2
                if halved == "x":
                    at[4] = half
                else:
                    at[0 if halved == "z" else 3] = pl.ds(half * 2, 2)
                piece = self.buf.at[(*at, slice(None), pl.ds(first, width))]
                target = device_at(moved(self.place, axis, (here + step) % 4))
                remote(
                    piece, piece, self.send.at[part, 2], self.recv.at[part, 3], target
                ).start()
                self.forward(part, there, order[:2])

    def finish(self):
        for part, (_, order) in enumerate(PARTS):
            wait_bytes(self.pieces(part, 16), self.recv.at[part, 3])
            axis = order[2]
            there = moved(self.place, axis, (self.place[axis] + 2) % 4)
            self.forward(part, there, order[:2])
        for part in range(3):
            wait_bytes(self.pieces(part, 64), self.recv.at[part, 5])
            wait_bytes(self.pieces(part, 64), self.send.at[part, 3])
            wait_bytes(self.pieces(part, 3), self.send.at[part, 0])
            wait_bytes(self.pieces(part, 12), self.send.at[part, 1])
            wait_bytes(self.pieces(part, 48), self.send.at[part, 2])


VMEM = pl.BlockSpec(memory_space=pltpu.VMEM)
HBM = pl.BlockSpec(memory_space=pl.ANY)


def unpack(buf, staged, take, out_w, hidden_w, proj_w, out_sem):
    spans = ((0, 128, out_w), (128, GROUP, hidden_w), (208, GROUP, proj_w))
    staged[:, 0:32] = jnp.zeros((2, 32, D), bf16)
    staged[:, 112:128] = jnp.zeros((2, 16, D), bf16)

    @pl.loop(0, 16)
    def _(g):
        slot = g % 2
        outs = [
            pltpu.make_async_copy(
                staged.at[slot, pl.ds(at, count)], row_block(ref, g, count), out_sem.at[i, slot]
            )
            for i, (at, count, ref) in enumerate(spans)
        ]

        @pl.when(g >= 2)
        def _():
            for out in outs:
                out.wait()

        rows = nn(take[...], buf[g // 4, (g // 2) % 2, g % 2].reshape(256, D)).astype(bf16)
        staged[slot, 32:112] = rows[0:80]
        staged[slot, 128:288] = rows[80:240]
        for out in outs:
            out.start()

    for slot in range(2):
        for i, (at, count, ref) in enumerate(spans):
            pltpu.make_async_copy(
                staged.at[slot, pl.ds(at, count)], row_block(ref, 0, count), out_sem.at[i, slot]
            ).wait()


class Scatter:
    def __init__(self, away, mine, pair, lands, halves, send, recv, place):
        self.away, self.mine, self.pair = away, mine, pair
        self.lands, self.halves = lands, halves
        self.send, self.recv, self.place = send, recv, place
        self.sibling = device_at(moved(place, "c", 1 - place["c"]))

    def swap(self, number):
        at = (number // 2, number % 2)
        sems = (len(PARTS_BACK), number)
        return remote(
            self.away.at[at], self.pair.at[at], self.send.at[sems], self.recv.at[sems], self.sibling
        )

    def add_pair(self, number):
        self.swap(number).wait()
        at = (number // 2, number % 2)
        self.mine[at] = (self.mine[at].astype(f32) + self.pair[at].astype(f32)).astype(bf16)

    def source(self, part, stage, where):
        (first, width), order = PARTS_BACK[part]
        if stage == 0:
            at = span(where, order[:2], core=False)
            return self.mine.at[(*at, slice(None), pl.ds(first, width))]
        at = [
            slice(None) if axis in order[: 2 - stage] else value
            for axis, value in zip("zxyx", span(where, "", core=False))
            if axis in order[: 3 - stage]
        ]
        return self.halves[stage - 1][part].at[tuple(at)]

    def start(self, stage):
        for part, (_, order) in enumerate(PARTS_BACK):
            axis = order[2 - stage]
            for step in (1, 3, 2):
                target = moved(self.place, axis, (self.place[axis] + step) % 4)
                remote(
                    self.source(part, stage, target),
                    self.lands[stage][part].at[step - 1],
                    self.send.at[part, stage],
                    self.recv.at[part, stage],
                    device_at(target),
                ).start()

    def add(self, stage, out=None):
        for part, ((first, width), order) in enumerate(PARTS_BACK):
            land = self.lands[stage][part]
            wait_bytes(land, self.recv.at[part, stage])
            own = self.source(part, stage, self.place)
            lead = land.shape[1:-2]

            @pl.loop(0, math.prod(lead))
            def _(number):
                at = []
                for size in reversed(lead):
                    at.insert(0, number % size)
                    number = number // size
                at = tuple(at)
                total = own[at].astype(f32)
                for source in range(3):
                    total = total + land[(source, *at)].astype(f32)
                if stage < 2:
                    self.halves[stage][part][at] = total.astype(bf16)
                else:
                    out[:, first : first + width] = total

    def finish(self):
        for stage in range(3):
            for part in range(len(PARTS_BACK)):
                wait_bytes(self.lands[stage][part], self.send.at[part, stage])


def lead_of(axes):
    sizes = {"z": (4,), "x": (2, 2), "y": (4,)}
    if axes == {"x", "y"}:
        return (2, 4, 2)
    if axes == {"x", "z"}:
        return (4, 2, 2)
    return sum((sizes[axis] for axis in "zyx" if axis in axes), ())


def scatter_scratch():
    whole = pltpu.VMEM((4, 2, 4, 2, ROWS, D), bf16)
    lands, halves = [], []
    for stage in range(3):
        for (_, width), order in PARTS_BACK:
            lead = lead_of(set(order[: 2 - stage]))
            lands.append(pltpu.VMEM((3, *lead, ROWS, width), bf16))
            if stage < 2:
                halves.append(pltpu.VMEM((*lead, ROWS, width), bf16))
    semaphores = [pltpu.SemaphoreType.DMA((4, 8))] * 2
    return [whole] * 3 + lands + halves + semaphores


def scatter_of(scratch, place):
    away, mine, pair = scratch[:3]
    parts = len(PARTS_BACK)
    lands = [scratch[3 + parts * stage : 3 + parts * (stage + 1)] for stage in range(3)]
    halves = [scratch[3 + parts * stage : 3 + parts * (stage + 1)] for stage in (3, 4)]
    return Scatter(away, mine, pair, lands, halves, scratch[-2], scratch[-1], place)


HALVES = ((0, "yz"), (256, "zy"))


def ring_devices(place):
    others = [moved(place, "c", 1 - place["c"])]
    for step in (1, 3, 2):
        there = moved(place, "x", (place["x"] + step) % 4)
        others += [there, moved(there, "c", 1 - place["c"])]
    return others


def ring_number(place):
    return (place["x"] % 2) * 4 + place["c"] * 2 + place["x"] // 2


def tokens_of(ref, place):
    inner = (place["x"] % 2) * 2 + place["c"]
    return ref.at[inner, :, pl.ds((place["x"] // 2) * TOK, TOK)]


def head_of(place):
    return (place["x"] // 2) * 8 + (place["z"] % 2) * 4 + place["y"]


def pair_device(pair, quarter):
    micro, h = pair // H, pair % H
    return ((micro * 2 + (h % 8) // 4) * 4 + quarter, (h % 4) * 2 + h // 8)


def column_pieces(buf, half, place, free):
    at = [slice(None) if axis in free else place[axis] for axis in "zy"]
    return buf.at[(*at, slice(None), pl.ds(HALVES[half][0], 256))]


def gather_columns(buf, send, recv, place, stage):
    for half, (first, order) in enumerate(HALVES):
        axis = order[stage]
        if stage:
            wait_bytes(buf.at[0, pl.ds(0, 3), :, pl.ds(first, 256)], recv.at[half, 0])
        piece = column_pieces(buf, half, place, order[:stage])
        for step in (1, 3, 2):
            target = moved(place, axis, (place[axis] + step) % 4)
            remote(
                piece, piece, send.at[half, stage], recv.at[half, stage], device_at(target)
            ).start()


def finish_columns(buf, send, recv):
    for half, (first, _) in enumerate(HALVES):
        cols = pl.ds(first, 256)
        wait_bytes(buf.at[pl.ds(0, 3), :, :, cols], recv.at[half, 1])
        wait_bytes(buf.at[0, pl.ds(0, 3), :, cols], send.at[half, 0])
        wait_bytes(buf.at[pl.ds(0, 3), :, :, cols], send.at[half, 1])


def quarter_of(blk):
    inner = blk % 4
    return jnp.where((blk // 4) % 2 == 0, inner, 3 - inner)


def query_block(quarter, j):
    return j * 4 + jnp.where(j % 2 == 0, quarter, 3 - quarter)


def cell_of(ref, pair, width):
    return ref.at[pl.ds(pair // H * TOK, TOK), pl.ds(pair % H * width, width)]


def mask_of(key_block, block, start):
    key_at = key_block * B + lax.broadcasted_iota(jnp.int32, (B, B), 0)
    query_at = block * B + lax.broadcasted_iota(jnp.int32, (B, B), 1)
    return (key_at >= start) & (key_at <= query_at)


def has_mask(key_block, block):
    return (key_block == 0) | (key_block == block) | (block == 15)


def shift_matrix(rows, cols, by):
    row = lax.broadcasted_iota(jnp.int32, (rows, cols), 0)
    col = lax.broadcasted_iota(jnp.int32, (rows, cols), 1)
    return jnp.where((row - col == by) & (jnp.minimum(row, col) < HD), 1.0, 0.0).astype(bf16)


def wait_cells(ref, sem, fewer, width):
    wait_bytes(ref.at[:, pl.ds(0, 15 * width)], sem)
    wait_bytes(cell_of(ref, 0, width), sem)

    @pl.when(jnp.logical_not(fewer))
    def _():
        wait_bytes(cell_of(ref, 0, width), sem)


def stays_here(place):
    return (place["z"] % 2 == place["x"] % 2) & (place["y"] // 2 == place["c"])


def wait_ring(ref, sem, place):
    wait_bytes(ref.at[pl.ds(0, 3)], sem)
    wait_bytes(ref.at[0, pl.ds(0, 384)], sem)

    @pl.when(jnp.logical_not(stays_here(place)))
    def _():
        wait_bytes(ref.at[0, pl.ds(0, 128)], sem)


def front_kernel(
    tokens, pieces, pack, scale_row, segments, join, order, take,
    normed_hbm, packed_hbm, wide_hbm, vectors, starts, kv_out, queries, out_t, log_norms, attended,
    out_w, hidden_w, proj_w,
    normed_out, normed_t, packed_out, wide_w, keep_sems, ring_tokens, ring_pieces, chunks, kv, value_t, tops, totals, rounded, landed, buf, staged,
    x_tok_send, x_tok_recv, c_tok_send, c_tok_recv, piece_send, piece_recv, col_send, col_recv,
    two_send, two_recv, own_sem, send, recv, core_send, core_recv, x_send, x_recv,
    pass_send, pass_recv, back_send, back_recv, kv_sem, out_sem,
):
    blk = lax.axis_index("blk")
    head = lax.axis_index("head")
    core = blk % 2
    x_low = (blk // 2) % 2
    quarter = blk % 4
    even = (blk // 4) % 2 == 0
    place = my_place()
    pair = (place["z"] // 2) * H + head_of(place)
    turn = place["x"] * 2 + core
    sibling = (blk + 1 - 2 * core, head)
    two = Gather(buf, two_send, two_recv, place)
    own = two.begin(pack, own_sem.at[0])
    own_tokens = pltpu.make_async_copy(tokens, tokens_of(ring_tokens, place), own_sem.at[1])
    own_tokens.start()
    number = ring_number(place)
    pltpu.make_async_copy(pieces.at[turn], ring_pieces.at[number], piece_recv).start()
    greet_all()
    for there in ring_devices(place):
        remote(
            pieces.at[there["x"] * 2 + there["c"]],
            ring_pieces.at[number],
            piece_send,
            piece_recv,
            device_at(there),
        ).start()
    mine = tokens_of(ring_tokens, place)
    for step in (1, 3, 2):
        there = moved(place, "x", (place["x"] + step) % 4)
        remote(
            tokens, mine, x_tok_send.at[step - 1], x_tok_recv.at[step - 1], device_at(there)
        ).start()
    remote(tokens, mine, c_tok_send, c_tok_recv, sibling).start()
    own.wait()
    two.stage(0)
    ids = segments[place["z"] // 2]
    before = [jnp.sum((ids < value).astype(jnp.int32)) for value in range(1, 9)]
    for j in range(4):
        row = segments[place["z"] // 2, pl.ds(query_block(quarter, j), 1)]
        start = jnp.zeros_like(row)
        for value in range(1, 9):
            start = jnp.where(row == value, before[value - 1], start)
        starts[j] = start
    wait_bytes(ring_pieces, piece_recv)
    joined = nn(join[...], ring_pieces[...].reshape(256, MINE)).astype(bf16)
    chunks[place["z"], place["y"]] = joined
    gather_columns(chunks, col_send, col_recv, place, 0)
    gather_columns(chunks, col_send, col_recv, place, 1)
    for step in (1, 3, 2):
        wait_bytes(tokens, x_tok_recv.at[step - 1])
        there = moved(place, "x", (place["x"] + 4 - step) % 4)
        arrived = tokens_of(ring_tokens, there)
        remote(arrived, arrived, c_tok_send, c_tok_recv, sibling).start()
    own_tokens.wait()
    finish_columns(chunks, col_send, col_recv)

    @pl.loop(0, 4)
    def _(z):
        rows = pl.ds(pl.multiple_of(z * 4 * GROUP, 64), 4 * GROUP)
        wide_w[rows] = nn(order[...], chunks[z].reshape(4 * CHUNK, MINE)).astype(bf16)

    vector_rows = jnp.zeros((16, MINE), f32)
    for z in range(4):
        for y in range(4):
            vector_rows = vector_rows + chunks[z, y, GROUP:].astype(f32)
    vectors[...] = vector_rows
    bias = vector_rows[0:1]
    gain = jnp.concatenate([vector_rows[1:2], vector_rows[2:3], vector_rows[3:4, :256]], axis=1)
    one_lane = jnp.where(
        lax.broadcasted_iota(jnp.int32, (1, MINE), 1) % LANES == 3 * HD, 1.0, 0.0
    )
    wait_bytes(ring_tokens.at[pl.ds(0, 2)], c_tok_recv)

    def deliver(inner, aside, send, recv):
        block = place["z"] * 4 + inner
        to_quarter = (quarter_of(block) + aside) % 4
        for m in range(2):
            for h in range(2):
                blk_to, head_to = pair_device(m * H + turn * 2 + h, to_quarter)
                src = packed_out.at[inner, m, :, pl.ds(h * LANES, LANES)]
                dst = kv.at[block, pl.ds(place["y"] * 128, 128)]
                stays = (blk_to == blk) & (head_to == head)

                @pl.when(stays)
                def _():
                    pltpu.make_async_copy(src, dst, recv).start()

                @pl.when(jnp.logical_not(stays))
                def _():
                    remote(src, dst, send, recv, (blk_to, head_to)).start()

    @pl.loop(0, 4)
    def _(inner):
        values = ring_tokens[inner].reshape(256, D).astype(f32)
        normed = (values * inverse_rms(values) * gain).astype(bf16)
        normed_out[inner] = normed
        full = nn(normed, wide_w[...])
        packed = ((full + bias) * scale_row[0:1] + one_lane).astype(bf16)
        packed_out[inner] = packed.reshape(2, 128, MINE)
        deliver(inner, 0, send, recv)

    @pl.loop(0, 4)
    def _(inner):
        deliver(inner, 2, x_send, x_recv)

    two.stage(1)

    @pl.loop(0, 4)
    def _(inner):
        @pl.loop(0, D // 128)
        def _(n):
            lanes = pl.ds(pl.multiple_of(n * 128, 128), 128)
            normed_t[inner, lanes] = normed_out[inner, :, lanes].T

    keeps = [
        pltpu.make_async_copy(ref, out, keep_sems.at[i])
        for i, (ref, out) in enumerate(
            ((normed_t, normed_hbm), (packed_out, packed_hbm), (wide_w, wide_hbm))
        )
    ]
    for keep in keeps:
        keep.start()
    wait_bytes(kv.at[pl.ds(0, 4)], recv)

    @pl.loop(0, 4)
    def _(j):
        block = kv.at[query_block(quarter, j)]
        remote(block, block, core_send, core_recv, sibling).start()

    pick = shift_matrix(LANES, 128, HD)

    @pl.loop(0, 4)
    def _(j):
        queries[j] = nn(kv[query_block(quarter, j)], pick).astype(bf16)
        tops[j] = jnp.full((1, B), NEGATIVE, f32)
        totals[j] = jnp.zeros((1, B), f32)
        out_t[j] = jnp.zeros((128, B), f32)


    def step(j, block, key_blocks):
        def tiles(masked):
            scores = []
            for key_block in key_blocks:
                s = nt(kv[key_block, :, :128], queries[j])
                if masked:
                    s = jnp.where(mask_of(key_block, block, starts[j]), s, NEGATIVE)
                scores.append(s)
            top = tops[j]
            new_top = top
            for s in scores:
                new_top = jnp.maximum(new_top, jnp.max(s, axis=0, keepdims=True))
            scale = jnp.exp(top - new_top)
            total = totals[j] * scale
            acc = out_t[j] * scale
            for key_block, s in zip(key_blocks, scores):
                p = jnp.exp(s - new_top)
                total = total + jnp.sum(p, axis=0, keepdims=True)
                acc = acc + nn(value_t[key_block], p.astype(bf16))
            tops[j] = new_top
            totals[j] = total
            out_t[j] = acc

        masked = has_mask(key_blocks[0], block)
        for key_block in key_blocks[1:]:
            masked = masked | has_mask(key_block, block)
        pl.when(masked)(lambda: tiles(True))
        pl.when(jnp.logical_not(masked))(lambda: tiles(False))

    def key_pass(j, of_quarter, count):
        block = query_block(quarter, j)

        @pl.loop(0, count // 2)
        def _(n):
            last = count - 1 - 2 * n
            step(j, block, (query_block(of_quarter, last), query_block(of_quarter, last - 1)))

        @pl.when(count % 2 == 1)
        def _():
            step(j, block, (query_block(of_quarter, 0),))

    def give(j, block):
        acc = out_t[j]
        result = acc / acc[112:113]
        out_t[j] = result
        log_norms[j] = tops[j] + jnp.log(totals[j])
        rounded[j] = result.T.astype(bf16)

        @pl.loop(0, 8)
        def _(k):
            h = (head + k) % 8
            src = rounded.at[j, pl.ds(h * TOK, TOK)]
            dst = cell_of(landed, pair, 128)
            mine = (k == 0) & (block == blk)

            @pl.when(mine)
            def _():
                pltpu.make_async_copy(src, dst, back_recv).start()

            @pl.when(jnp.logical_not(mine))
            def _():
                remote(src, dst, back_send, back_recv, (block, h)).start()

    keep_kv = pltpu.make_async_copy(kv, kv_out, kv_sem)

    @pl.loop(0, 4)
    def _(turn_at):
        of_quarter = (quarter + 2 * (turn_at // 2)) % 4 + (turn_at % 2) * (1 - 2 * core)

        @pl.when(turn_at == 1)
        def _():
            two.stage(2)
            wait_bytes(kv.at[pl.ds(0, 4)], core_recv)

        @pl.when(turn_at == 2)
        def _():
            wait_bytes(kv.at[pl.ds(0, 4)], x_recv)

            @pl.loop(0, 4)
            def _(j):
                block = kv.at[query_block(of_quarter, j)]
                remote(block, block, pass_send, pass_recv, sibling).start()

        @pl.when(turn_at == 3)
        def _():
            two.relay()
            wait_bytes(kv.at[pl.ds(0, 4)], pass_recv)
            keep_kv.start()

        @pl.loop(0, 4)
        def _(j):
            b = query_block(of_quarter, j)
            value_t[b] = kv[b, :, 128:].T

        @pl.loop(0, 4)
        def _(i):
            j = 3 - i
            block = query_block(quarter, j)
            more = jnp.where(
                turn_at == 0, 1, jnp.where(turn_at == 1, block % 2, (j + x_low) % 2)
            )
            key_pass(j, of_quarter, j + more)
            pl.when(turn_at == 3)(lambda: give(j, block))

    two.finish()
    unpack(buf, staged, take, out_w, hidden_w, proj_w, out_sem)
    wait_bytes(landed, back_recv)
    attended[...] = landed[...]
    for keep in keeps + [keep_kv]:
        keep.wait()
    for sem in (core_send, pass_send):
        wait_bytes(kv.at[pl.ds(0, 4)], sem)
    wait_cells(landed, back_send, even, 128)
    wait_bytes(ring_pieces.at[pl.ds(0, 7)], piece_send)
    for step_at in range(3):
        wait_bytes(tokens, x_tok_send.at[step_at])
    wait_bytes(ring_tokens.at[pl.ds(0, 2)], c_tok_send)
    wait_ring(kv, send, place)
    wait_ring(kv, x_send, place)


def front(*operands):
    dma = pltpu.SemaphoreType.DMA
    return pl.pallas_call(
        front_kernel,
        out_shape=(
            jax.ShapeDtypeStruct((4, D, 256), bf16),
            jax.ShapeDtypeStruct((4, 2, 128, MINE), bf16),
            jax.ShapeDtypeStruct((D, MINE), bf16),
            jax.ShapeDtypeStruct((16, MINE), f32),
            jax.ShapeDtypeStruct((4, 1, B), jnp.int32),
            jax.ShapeDtypeStruct((16, B, LANES), bf16),
            jax.ShapeDtypeStruct((4, B, 128), bf16),
            jax.ShapeDtypeStruct((4, 128, B), f32),
            jax.ShapeDtypeStruct((4, 1, B), f32),
            jax.ShapeDtypeStruct((2 * TOK, OUT_WIDE), bf16),
            jax.ShapeDtypeStruct((OUT_WIDE, D), bf16),
            jax.ShapeDtypeStruct((D, D), bf16),
            jax.ShapeDtypeStruct((D, D), bf16),
        ),
        in_specs=[VMEM] * 8,
        out_specs=(HBM,) * 3 + (VMEM,) * 2 + (HBM,) + (VMEM,) * 4 + (HBM,) * 3,
        scratch_shapes=[
            pltpu.VMEM((4, 256, D), bf16),
            pltpu.VMEM((4, D, 256), bf16),
            pltpu.VMEM((4, 2, 128, MINE), bf16),
            pltpu.VMEM((D, MINE), bf16),
            dma((3,)),
            pltpu.VMEM((4, 2, 128, D), bf16),
            pltpu.VMEM((8, ROWS, MINE), bf16),
            pltpu.VMEM((4, 4, CHUNK, MINE), bf16),
            pltpu.VMEM((16, B, LANES), bf16),
            pltpu.VMEM((16, 128, B), bf16),
            pltpu.VMEM((4, 1, B), f32),
            pltpu.VMEM((4, 1, B), f32),
            pltpu.VMEM((4, B, 128), bf16),
            pltpu.VMEM((2 * TOK, OUT_WIDE), bf16),
            pltpu.VMEM((4, 2, 2, 4, 2, ROWS, D), bf16),
            pltpu.VMEM((2, 288, D), bf16),
            dma((3,)), dma((3,)), dma, dma, dma, dma, dma((2, 2)), dma((2, 2)),
            dma((3, 4)), dma((3, 6)), dma((2,)),
        ]
        + [dma] * 11
        + [dma((3, 2))],
        compiler_params=pltpu.CompilerParams(
            collective_id=0, has_side_effects=True, vmem_limit_bytes=56 * 2**20
        ),
        name="front",
    )(
        *operands,
        jnp.asarray(JOIN, bf16),
        jnp.asarray(ORDER, bf16),
        jnp.asarray(TAKE, bf16),
    )


def rear_kernel(
    pack, kv_hbm, queries, starts, out_t, log_norms,
    attended, d_branch, normed_two, d_pre, activated, upstream,
    normed_hbm, packed_hbm, wide_hbm, vector_grads, scale_row, take_t, share, order_t,
    d_normed, pieces_out, two_out,
    kv, packed, wide_w, load_sems,
    d_out, key_t, deltas, d_query, d_kv, mine_kv, half, half_in, cross, cross_in, final, d_wide,
    attended_t, normed_two_t, activated_t, right,
    sum_in, grad_chunks, first_in, second_in, first_sum,
    joined, shares, shares_in,
    send, recv, core_send, core_recv, x_send, x_recv, back_send, back_recv,
    c_send, c_recv, sum_send, sum_recv, col_send, col_recv, share_send, share_recv,
    *scratch,
):
    blk = lax.axis_index("blk")
    head = lax.axis_index("head")
    core = blk % 2
    x_low = (blk // 2) % 2
    quarter = blk % 4
    place = my_place()
    my_head = head_of(place)
    pair = (place["z"] // 2) * H + my_head
    to_quarter = quarter_of(blk)
    even = (blk // 4) % 2 == 0
    two = scatter_of(scratch, place)
    loads = [
        pltpu.make_async_copy(src, dst, load_sems.at[i])
        for i, (src, dst) in enumerate(
            ((kv_hbm, kv), (packed_hbm, packed), (wide_hbm, wide_w))
        )
    ]
    for load in loads:
        load.start()
    greet_all()

    @pl.loop(0, PAIRS)
    def _(k):
        p = (pair + k) % PAIRS
        src = cell_of(pack, p, 128)
        dst = d_out.at[blk // 4, pl.ds(head * TOK, TOK)]
        mine = (k == 0) & even

        @pl.when(mine)
        def _():
            pltpu.make_async_copy(src, dst, recv).start()

        @pl.when(jnp.logical_not(mine))
        def _():
            remote(src, dst, send, recv, pair_device(p, to_quarter)).start()


    @pl.loop(0, D // 128)
    def _(n):
        lanes = pl.ds(pl.multiple_of(n * 128, 128), 128)
        normed_two_t[lanes] = normed_two[:, lanes].T
        activated_t[lanes] = activated[:, lanes].T

    @pl.loop(0, H)
    def _(n):
        lanes = pl.ds(pl.multiple_of(n * 128, 128), 128)
        attended_t[lanes] = attended[:, lanes].T

    right[0:128] = d_branch[...]
    right[128:256] = d_pre[...]
    right[256:384] = upstream[...]

    def produce(number, of_core, into):
        group = number * 2 + of_core
        rows = pl.ds(pl.multiple_of(group * GROUP, 16), GROUP)
        out_rows = pl.ds(pl.multiple_of(group * 128 + 32, 16), GROUP)
        left = jnp.concatenate(
            [
                nn(take_t[0], attended_t[out_rows]).astype(bf16),
                nn(take_t[1], normed_two_t[rows]).astype(bf16),
                nn(take_t[2], activated_t[rows]).astype(bf16),
            ],
            axis=1,
        )
        for cell in range(5):
            lanes = slice(cell * LANES, (cell + 1) * LANES)
            block = nn(left, right[:, lanes]).astype(bf16)
            into[number // 2, number % 2, :, :, :, lanes] = block.reshape(4, 2, ROWS, LANES)

    @pl.loop(0, 8)
    def _(number):
        produce(number, 1 - core, two.away)
        two.swap(number).start()

    @pl.loop(0, 8)
    def _(number):
        produce(number, core, two.mine)

    loads[0].wait()

    def keys_at(block, lane):
        return kv[pl.ds(pl.multiple_of(block * B, B), B), lane : lane + 128]

    @pl.loop(0, 16)
    def _(b):
        key_t[b] = keys_at(b, 0).T

    @pl.loop(0, 8)
    def _(number):
        two.add_pair(number)

    two.start(0)
    wait_bytes(d_out, recv)

    @pl.loop(0, 4)
    def _(j):
        deltas[j] = jnp.sum(d_out[j].astype(f32).T * out_t[j], axis=0, keepdims=True)
        d_query[j] = jnp.zeros((128, B), f32)

    sibling = (blk + 1 - 2 * core, head)

    def step(numbers, key_block):
        def tiles(masked):
            found = []
            for j in numbers:
                q = queries[j]
                do = d_out[j]
                p = jnp.exp(nt(keys_at(key_block, 0), q) - log_norms[j])
                if masked:
                    allowed = mask_of(key_block, query_block(quarter, j), starts[j])
                    p = jnp.where(allowed, p, 0.0)
                dp = nt(keys_at(key_block, 128), do)
                found.append((q, do, p.astype(bf16), (p * (dp - deltas[j])).astype(bf16)))
            d_kv[:, :128] += sum(nn(ds, q) for q, do, p, ds in found)
            d_kv[:, 128:] += sum(nn(p, do) for q, do, p, ds in found)
            for j, (q, do, p, ds) in zip(numbers, found):
                d_query[j] += nn(key_t[key_block], ds)

        masked = has_mask(key_block, query_block(quarter, numbers[0]))
        for j in numbers[1:]:
            masked = masked | has_mask(key_block, query_block(quarter, j))
        pl.when(masked)(lambda: tiles(True))
        pl.when(jnp.logical_not(masked))(lambda: tiles(False))

    def swap(n):
        return remote(
            half.at[n], half_in.at[n], core_send.at[n], core_recv.at[n], sibling
        )

    shift = shift_matrix(128, LANES, -HD)

    partner = (blk + 2 - 4 * x_low, head)

    def cross_swap(z):
        return remote(cross.at[z], cross_in.at[z], x_send.at[z], x_recv.at[z], partner)

    def core_sum(z):
        own = 2 * z + (x_low + z) % 2
        other = 4 * z + 1 - own
        swap(other).wait()
        cross[z] = (mine_kv[other] + half_in[other].astype(f32)).astype(bf16)
        cross_swap(z).start()
        swap(own).wait()
        mine_kv[own] = (
            mine_kv[own]
            + half_in[own].astype(f32)
            + nn(d_query[z].T.astype(bf16), shift)
        )

    def finish(z):
        cross_swap(z).wait()
        own = 2 * z + (x_low + z) % 2
        final[z] = (mine_kv[own] + cross_in[z].astype(f32)).astype(bf16)
        inner = query_block(quarter, z) % 4
        dst = d_wide.at[inner, place["z"] // 2, :, pl.ds((my_head % 2) * LANES, LANES)]

        @pl.loop(0, 4)
        def _(k):
            y = (place["y"] + k) % 4
            there = {"x": my_head // 4, "y": y, "z": z, "c": (my_head // 2) % 2}
            src = final.at[z, pl.ds(y * 128, 128)]
            blk_to, head_to = device_at(there)
            stays = (blk_to == blk) & (head_to == head)

            @pl.when(stays)
            def _():
                pltpu.make_async_copy(src, dst, back_recv).start()

            @pl.when(jnp.logical_not(stays))
            def _():
                remote(src, dst, back_send, back_recv, (blk_to, head_to)).start()

    load_normed = pltpu.make_async_copy(normed_hbm, kv.at[pl.ds(0, 4 * D)], load_sems.at[3])

    def key_steps(key_block):
        z = key_block // 4
        d_kv[...] = jnp.zeros((B, LANES), f32)
        first = z + (query_block(quarter, z) < key_block).astype(jnp.int32)

        @pl.when(first % 2 == 1)
        def _():
            step((first,), key_block)

        @pl.loop((first + 1) // 2, 2)
        def _(n):
            step((2 * n, 2 * n + 1), key_block)

        n = 2 * z + (key_block % 4) // 2

        @pl.when((key_block + z + core) % 2 == 0)
        def _():
            mine_kv[n] = d_kv[...]

        @pl.when((key_block + z + core) % 2 == 1)
        def _():
            half[n] = d_kv[...].astype(bf16)
            swap(n).start()

    @pl.loop(0, 10)
    def _(part):
        z = part // 2

        @pl.when(part < 8)
        def _():
            @pl.loop(2 * part, 2 * part + 2)
            def _(key_block):
                key_steps(key_block)

        @pl.when(part == 8)
        def _():
            load_normed.start()

        @pl.when((part % 2 == 0) & (part > 0))
        def _():
            core_sum(z - 1)

        @pl.when((part % 2 == 1) & (part > 1))
        def _():
            finish(z - 1)

        @pl.when(part == 6)
        def _():
            two.add(0)
            two.start(1)

    two.add(1)
    two.start(2)
    wait_bytes(d_wide, back_recv)

    for load in loads[1:]:
        load.wait()
    load_normed.wait()
    partial = two.away.at[:, 0]
    summed, partial_in = two.away.at[pl.ds(0, 2), 1], two.away.at[pl.ds(2, 2), 1]
    scale = scale_row[0:1]
    bias_sum = jnp.zeros((1, MINE), f32)
    scale_sum = jnp.zeros((1, MINE), f32)

    def scaled_grads(inner, sums):
        bias_sum, scale_sum = sums
        grad = d_wide[inner].reshape(256, MINE).astype(f32)
        scale_sum = scale_sum + jnp.sum(
            grad * packed[inner].reshape(256, MINE).astype(f32), axis=0, keepdims=True
        )
        grad = (grad * scale).astype(bf16)
        d_wide[inner] = grad.reshape(2, 128, MINE)
        return bias_sum + jnp.sum(grad.astype(f32), axis=0, keepdims=True), scale_sum

    bias_sum, scale_sum = lax.fori_loop(0, 4, scaled_grads, (bias_sum, scale_sum))
    scale_sum = scale_sum[:, :LANES] + scale_sum[:, LANES:]
    rows = vector_grads[...] + jnp.concatenate(
        [bias_sum, jnp.concatenate([scale_sum, scale_sum], axis=1), jnp.zeros((14, MINE), f32)],
        axis=0,
    )
    rows = rows.astype(bf16)
    sibling_at = (blk + 1 - 2 * core, head)
    c_swaps = [
        remote(
            partial.at[low * 2 + 1 - core],
            partial_in.at[low],
            c_send.at[low],
            c_recv.at[low],
            sibling_at,
        )
        for low in range(2)
    ]

    def token_grads(inner):
        back = nt(d_wide[inner].reshape(256, MINE), wide_w[...])
        partial[inner] = back.astype(bf16).reshape(4, 2, ROWS, D)

    @pl.loop(0, 2)
    def _(low):
        token_grads(low * 2 + 1 - core)

    for low in range(2):
        c_swaps[low].start()

    @pl.loop(0, 4)
    def _(z):
        def part(inner):
            at = pl.ds(pl.multiple_of(inner * D + z * 320, 64), 320)
            return nn(kv[at], d_wide[inner].reshape(256, MINE))

        grads = sum(part(inner) for inner in range(4)).astype(bf16)
        grad_chunks[z] = nn(order_t[...], grads).astype(bf16).reshape(4, CHUNK, MINE)
        for y in range(4):
            grad_chunks[z, y, GROUP:] = rows


    for step_at in (1, 3, 2):
        for half, axis in enumerate("zy"):
            there = moved(place, axis, (place[axis] + step_at) % 4)
            remote(
                column_pieces(grad_chunks, half, there, "y" if half == 0 else "z"),
                first_in.at[half, step_at - 1],
                col_send.at[half, 0],
                col_recv.at[half, 0],
                device_at(there),
            ).start()

    @pl.loop(0, 2)
    def _(low):
        token_grads(low * 2 + core)

    for low in range(2):
        c_swaps[low].wait()
        summed[low] = (
            partial[low * 2 + core].astype(f32) + partial_in[low].astype(f32)
        ).astype(bf16)
    for step_at in (1, 3, 2):
        there = moved(place, "x", (place["x"] + step_at) % 4)
        for m in range(2):
            remote(
                summed.at[there["x"] % 2, m * 2 + there["x"] // 2],
                sum_in.at[step_at - 1, m],
                sum_send,
                sum_recv,
                device_at(there),
            ).start()
    for half in range(2):
        wait_bytes(first_in.at[half], col_recv.at[half, 0])
        own = column_pieces(grad_chunks, half, place, "y" if half == 0 else "z")
        for number in range(4):
            total = own[number].astype(f32)
            for source in range(3):
                total = total + first_in[half, source, number].astype(f32)
            first_sum[half, number] = total.astype(bf16)
    for step_at in (1, 3, 2):
        for half, axis in enumerate("yz"):
            there = moved(place, axis, (place[axis] + step_at) % 4)
            remote(
                first_sum.at[half, there[axis]],
                second_in.at[half, step_at - 1],
                col_send.at[half, 1],
                col_recv.at[half, 1],
                device_at(there),
            ).start()
    totals = []
    for half, axis in enumerate("yz"):
        wait_bytes(second_in.at[half], col_recv.at[half, 1])
        total = first_sum[half, place[axis]].astype(f32)
        for source in range(3):
            total = total + second_in[half, source].astype(f32)
        totals.append(total)
    total_y, total_z = totals
    joined[:, 0:256] = total_y.astype(bf16)
    joined[:, 256:512] = total_z.astype(bf16)
    shares[...] = nn(share[...], joined[...]).astype(bf16).reshape(8, ROWS, MINE)
    turn = place["x"] * 2 + core
    for there in ring_devices(place):
        remote(
            shares.at[ring_number(there)],
            shares_in.at[turn],
            share_send,
            share_recv,
            device_at(there),
        ).start()
    pltpu.make_async_copy(
        shares.at[ring_number(place)], shares_in.at[turn], share_recv
    ).start()
    two.add(2, two_out)
    two.finish()
    wait_bytes(sum_in, sum_recv)
    for m in range(2):
        total = summed[x_low, m * 2 + place["x"] // 2].astype(f32)
        for source in range(3):
            total = total + sum_in[source, m].astype(f32)
        d_normed[m * TOK : (m + 1) * TOK] = total.reshape(TOK, D)
    wait_bytes(shares_in, share_recv)
    pieces_out[...] = shares_in[...]
    wait_cells(pack, send, even, 128)
    wait_ring(final, back_send, place)
    wait_bytes(sum_in, sum_send)
    for number in range(2):
        wait_bytes(first_in.at[number], col_send.at[number, 0])
        wait_bytes(second_in.at[number], col_send.at[number, 1])
    wait_bytes(shares.at[pl.ds(0, 7)], share_send)


def rear(*operands):
    dma = pltpu.SemaphoreType.DMA
    return pl.pallas_call(
        rear_kernel,
        out_shape=(
            jax.ShapeDtypeStruct((2 * TOK, D), f32),
            jax.ShapeDtypeStruct((8, ROWS, MINE), bf16),
            jax.ShapeDtypeStruct((ROWS, D), f32),
        ),
        in_specs=[VMEM] + [HBM] + [VMEM] * 10 + [HBM] * 3 + [VMEM] * 5,
        out_specs=(VMEM, VMEM, VMEM),
        scratch_shapes=[
            pltpu.VMEM((16 * B, LANES), bf16),
            pltpu.VMEM((4, 2, 128, MINE), bf16),
            pltpu.VMEM((D, MINE), bf16),
            dma((4,)),
            pltpu.VMEM((4, B, 128), bf16),
            pltpu.VMEM((16, 128, B), bf16),
            pltpu.VMEM((4, 1, B), f32),
            pltpu.VMEM((4, 128, B), f32),
            pltpu.VMEM((B, LANES), f32),
            pltpu.VMEM((8, B, LANES), f32),
            pltpu.VMEM((8, B, LANES), bf16),
            pltpu.VMEM((8, B, LANES), bf16),
            pltpu.VMEM((4, B, LANES), bf16),
            pltpu.VMEM((4, B, LANES), bf16),
            pltpu.VMEM((4, B, LANES), bf16),
            pltpu.VMEM((4, 2, 128, MINE), bf16),
            pltpu.VMEM((OUT_WIDE, 128), bf16),
            pltpu.VMEM((D, 128), bf16),
            pltpu.VMEM((D, 128), bf16),
            pltpu.VMEM((384, D), bf16),
            pltpu.VMEM((3, 2, 2, ROWS, D), bf16),
            pltpu.VMEM((4, 4, CHUNK, MINE), bf16),
            pltpu.VMEM((2, 3, 4, CHUNK, 256), bf16),
            pltpu.VMEM((2, 3, CHUNK, 256), bf16),
            pltpu.VMEM((2, 4, CHUNK, 256), bf16),
            pltpu.VMEM((CHUNK, MINE), bf16),
            pltpu.VMEM((8, ROWS, MINE), bf16),
            pltpu.VMEM((8, ROWS, MINE), bf16),
            dma, dma, dma((8,)), dma((8,)), dma((4,)), dma((4,)), dma, dma,
            dma((2,)), dma((2,)), dma, dma, dma((2, 2)), dma((2, 2)), dma, dma,
        ]
        + scatter_scratch(),
        compiler_params=pltpu.CompilerParams(
            collective_id=1, has_side_effects=True, vmem_limit_bytes=63 * 2**20
        ),
        name="rear",
    )(
        *operands,
        jnp.asarray(TAKE_T, bf16),
        jnp.asarray(SHARE, bf16),
        jnp.asarray(ORDER.T, bf16),
    )


def on_device(
    inputs,
    segment_ids,
    norm1_gain,
    w_query,
    w_key,
    w_value,
    query_bias,
    value_bias,
    w_out,
    out_bias,
    norm2_gain,
    w_hidden,
    hidden_bias,
    w_proj,
    proj_bias,
    dim_scale,
    cotangent,
):
    blk = lax.axis_index("blk")
    head = lax.axis_index("head")
    at = (blk * 8 + head) * 10
    spread_heads = jnp.zeros((H, LANES), bf16)
    biases = jnp.concatenate([query_bias, jnp.zeros((HD - 10,), bf16), value_bias])
    spread_heads = lax.dynamic_update_slice(spread_heads, biases[None], (blk, HD + head * 10))
    natural = jnp.stack([norm1_gain, out_bias, norm2_gain, hidden_bias, proj_bias])
    natural = lax.dynamic_update_slice(jnp.zeros((5, 3 * MINE), bf16), natural, (0, at))
    columns = jnp.concatenate(
        [w.reshape(10, H, HD) for w in (w_key, w_query, w_value)]
        + [jnp.zeros((10, H, LANES - 3 * HD), bf16)],
        axis=2,
    )
    columns = columns.reshape(10, 8, MINE).transpose(1, 0, 2)
    pieces = jnp.concatenate(
        [
            columns,
            jnp.zeros((8, 6, MINE), bf16),
            spread_heads.reshape(8, 1, MINE),
            jnp.broadcast_to(natural.reshape(1, 15, MINE), (8, 15, MINE)),
        ],
        axis=1,
    )
    pack = jnp.concatenate([w_out, w_hidden, w_proj, jnp.zeros((2, D), bf16)], axis=0)
    softplus_scale = LOG2E / math.sqrt(HD) * jax.nn.softplus(dim_scale)
    ones = jnp.ones((HD,), f32)
    scale_row = jnp.concatenate(
        [ones, softplus_scale, ones, jnp.zeros((LANES - 3 * HD,), f32)] * 2
    )
    scale_row = jnp.broadcast_to(scale_row, (8, MINE))

    (
        ring_normed, packed, wide_w, vectors, starts, kv, queries, out_t, log_norms, attended,
        out_w, hidden_w, proj_w,
    ) = front(inputs, pieces, pack, scale_row, segment_ids.reshape(2, 16, B))
    every = vectors[1:].reshape(5, 3 * MINE)[:, :D]
    gain_one, out_b, gain_two, hidden_b, proj_b = [every[i] for i in range(5)]

    tokens = inputs.reshape(2 * TOK, D).astype(f32)
    residual = tokens + nn(attended, out_w) + out_b
    inverse_two = inverse_rms(residual)
    normed_two = (residual * inverse_two * gain_two).astype(bf16)
    pre_act = nn(normed_two, hidden_w) + hidden_b
    gate = jax.nn.sigmoid(pre_act)
    activated = (pre_act * gate).astype(bf16)
    layer_out = (residual + nn(activated, proj_w) + proj_b).astype(bf16)

    upstream_low = cotangent.reshape(2 * TOK, D)
    upstream = upstream_low.astype(f32)
    d_pre = (nt(upstream_low, proj_w) * gate * (1.0 + pre_act * (1.0 - gate))).astype(bf16)
    d_normed_two = nt(d_pre, hidden_w)
    d_residual = upstream + norm_back(d_normed_two * gain_two, residual, inverse_two)
    d_branch = d_residual.astype(bf16)
    d_attended = nt(d_branch, out_w).astype(bf16)

    def total(values):
        return jnp.sum(values.astype(f32), axis=0)

    vector_grads = jnp.stack(
        [
            total(d_branch),
            total(d_normed_two * residual * inverse_two),
            total(d_pre),
            total(upstream),
        ]
    )
    vector_grads = jnp.pad(vector_grads, ((0, 0), (0, 3 * MINE - D))).reshape(12, MINE)
    vector_grads = jnp.pad(vector_grads, ((4, 0), (0, 0)))
    d_normed, shares, two = rear(
        d_attended, kv.reshape(16 * B, LANES), queries, starts, out_t, log_norms,
        attended, d_branch, normed_two, d_pre, activated, upstream_low,
        ring_normed.reshape(4 * D, 256), packed, wide_w, vector_grads, scale_row,
    )
    inverse_one = inverse_rms(tokens)
    input_grad = (
        d_residual + norm_back(d_normed * gain_one, tokens, inverse_one)
    ).astype(bf16)

    shares = shares.astype(f32)
    columns = shares[:, :10].transpose(1, 0, 2).reshape(10, H, LANES)
    d_key_w, d_query_w, d_value_w = [
        columns[:, :, i * HD : (i + 1) * HD].reshape(10, D) for i in range(3)
    ]
    by_head = shares[:, 16].reshape(H, LANES)
    d_query_bias, d_value_bias = [
        lax.dynamic_slice(by_head, (blk, i * HD + head * 10), (1, 10)).reshape(10) for i in (1, 2)
    ]
    summed = jnp.sum(shares[:, 17:], axis=0)
    scale_grad = summed[0, HD : 2 * HD] / softplus_scale
    scale_grad = scale_grad * (LOG2E / math.sqrt(HD)) * jax.nn.sigmoid(dim_scale)
    natural = lax.dynamic_slice(summed.reshape(5, 3 * MINE), (0, at), (5, 10))
    norm1_gain_grad = sum(
        jnp.sum(w.astype(f32) * grad, axis=1)
        for w, grad in ((w_query, d_query_w), (w_key, d_key_w), (w_value, d_value_w))
    ) / norm1_gain.astype(f32)
    return (
        layer_out.reshape(2, TOK, D),
        input_grad.reshape(2, TOK, D),
        norm1_gain_grad,
        d_query_w,
        d_key_w,
        d_value_w,
        d_query_bias,
        d_value_bias,
        two[0:10],
        natural[1],
        natural[2],
        two[10:20],
        natural[3],
        two[20:30],
        natural[4],
        scale_grad,
    )


def solution(mesh):
    rows = P(("blk", "head"), None)
    vec = P(("blk", "head"))
    tok = P(None, ("blk", "head"), None)
    in_specs = (
        tok, P(), vec, rows, rows, rows, vec, vec, rows, vec, vec, rows, vec, rows, vec, P(), tok
    )
    out_specs = (
        tok, tok, vec, rows, rows, rows, vec, vec, rows, vec, vec, rows, vec, rows, vec, P()
    )
    return jax.shard_map(
        on_device, mesh=mesh, in_specs=in_specs, out_specs=out_specs, check_vma=False
    )
```

```python
import functools
import math

import jax
import jax.numpy as jnp
import numpy as np
from jax import lax
from jax.experimental import pallas as pl
from jax.experimental.pallas import tpu as pltpu
from jax.sharding import PartitionSpec as P

D = 1280
H = 16
HD = 80
FF = 1280
B = 512
TOK = 64
PAIRS = 32
LANES = 256
ROWS = 32
WIDE = H * LANES
OUT_WIDE = H * 128
GROUP = 80
CHUNK = 96
MINE = 512
EPSILON = 1e-06
LOG2E = 1.442695041
NEGATIVE = -1e30
MESH = pl.DeviceIdType.MESH
f32 = jnp.float32
bf16 = jnp.bfloat16

PARTS = (((0, 512), "xyz"), ((512, 384), "yzx"), ((896, 384), "zxy"))
PARTS_BACK = (((0, 512), "xyz"), ((512, 512), "xzy"), ((1024, 256), "yzx"))


def inverse_rms(values):
    return lax.rsqrt(jnp.mean(values * values, axis=-1, keepdims=True) + EPSILON)


def norm_back(upstream, values, inverse):
    return inverse * upstream - values * inverse**3 * jnp.mean(
        upstream * values, axis=-1, keepdims=True
    )


def nn(a, b):
    return lax.dot_general(a, b, (((1,), (0,)), ((), ())), preferred_element_type=f32)


def nt(a, b):
    return lax.dot_general(a, b, (((1,), (1,)), ((), ())), preferred_element_type=f32)


def tn(a, b):
    return lax.dot_general(a, b, (((0,), (0,)), ((), ())), preferred_element_type=f32)


def my_place():
    blk = lax.axis_index("blk")
    head = lax.axis_index("head")
    return {
        "x": (head % 2) * 2 + (blk // 2) % 2,
        "y": head // 2,
        "z": blk // 4,
        "c": blk % 2,
    }


def device_at(place):
    x, y, z, c = place["x"], place["y"], place["z"], place["c"]
    return (z * 4 + (x % 2) * 2 + c, y * 2 + x // 2)


def span(place, free, core=True):
    x, y, z = place["x"], place["y"], place["z"]
    whole = slice(None)
    at = [
        whole if "z" in free else z,
        whole if "x" in free else x % 2,
        place["c"],
        whole if "y" in free else y,
        whole if "x" in free else x // 2,
    ]
    return tuple(at if core else at[:2] + at[3:])


def moved(place, axis, value):
    other = dict(place)
    other[axis] = value
    return other


def greet(peers):
    barrier = pltpu.get_barrier_semaphore()
    for peer in peers:
        pl.semaphore_signal(barrier, inc=1, device_id=peer, device_id_type=MESH)
    pl.semaphore_wait(barrier, len(peers))


def greet_all():
    barrier = pltpu.get_barrier_semaphore()
    me = lax.axis_index("blk") * 8 + lax.axis_index("head")

    @pl.loop(1, 128)
    def _(k):
        other = (me + k) % 128
        pl.semaphore_signal(
            barrier, inc=1, device_id=(other // 8, other % 8), device_id_type=MESH
        )

    pl.semaphore_wait(barrier, 127)


def ring_peers(place):
    peers = [device_at(moved(place, "c", 1 - place["c"]))]
    for axis in "xyz":
        for step in (1, 3, 2):
            peers.append(device_at(moved(place, axis, (place[axis] + step) % 4)))
    return peers


def wait_bytes(ref, sem):
    pltpu.make_async_copy(ref, ref, sem).wait()


def remote(src, dst, send, recv, device):
    return pltpu.make_async_remote_copy(
        src_ref=src, dst_ref=dst, send_sem=send, recv_sem=recv, device_id=device, device_id_type=MESH
    )


def varied(place, axes, number):
    other = dict(place)
    for axis in axes:
        other[axis] = number % 4
        number = number // 4
    return other


def selections():
    join = np.zeros((CHUNK, 256), np.float32)
    for i in range(8):
        for j in range(10):
            join[i * 10 + j, i * ROWS + j] = 1
        for v in range(16):
            join[GROUP + v, i * ROWS + 16 + v] = 1
    return join, join.T.copy()


JOIN, SHARE = selections()


def rows_of(values, size, starts):
    return jnp.concatenate([values[at : at + size] for at in starts], axis=0)


def row_block(ref, g, count):
    return ref.at[pl.ds(pl.multiple_of(g * count, 16), count)]


class Gather:
    def __init__(self, buf, send, recv, place):
        self.place = place
        self.buf, self.send, self.recv = buf, send, recv
        self.sibling = device_at(moved(place, "c", 1 - place["c"]))

    def begin(self, pack, sem):
        own = pltpu.make_async_copy(pack, self.buf.at[span(self.place, "")], sem)
        own.start()
        return own

    def piece(self, part, where, free):
        first, width = PARTS[part][0]
        return self.buf.at[(*span(where, free), slice(None), pl.ds(first, width))]

    def pieces(self, part, count):
        cols = pl.ds(*PARTS[part][0])
        whole = slice(None)
        at = {
            3: (pl.ds(0, 3), 0, 0, 0, 0),
            12: (pl.ds(0, 3), 0, 0, whole, 0),
            16: (0, whole, 0, whole, whole),
            48: (pl.ds(0, 3), whole, 0, whole, whole),
            64: (whole, whole, 0, whole, whole),
        }[count]
        return self.buf.at[(*at, whole, cols)]

    def forward(self, part, where, free):
        piece = self.piece(part, where, free)
        remote(piece, piece, self.send.at[part, 3], self.recv.at[part, 5], self.sibling).start()

    def stage(self, stage):
        for part, (_, order) in enumerate(PARTS):
            if stage:
                wait_bytes(self.pieces(part, 3 * 4 ** (stage - 1)), self.recv.at[part, stage - 1])
            piece = self.piece(part, self.place, order[:stage])
            axis = order[stage]
            for step in (1, 3, 2) if stage < 2 else (1, 3):
                target = moved(self.place, axis, (self.place[axis] + step) % 4)
                slot = stage if stage < 2 else 1 + step
                remote(
                    piece,
                    piece,
                    self.send.at[part, stage],
                    self.recv.at[part, slot],
                    device_at(target),
                ).start()
        for part, (_, order) in enumerate(PARTS):
            if stage == 0:
                self.forward(part, self.place, "")
            else:
                axis = order[stage - 1]
                for step in (1, 3, 2):
                    there = moved(self.place, axis, (self.place[axis] + 4 - step) % 4)
                    self.forward(part, there, order[: stage - 1])

    def relay(self):
        for part, ((first, width), order) in enumerate(PARTS):
            axis, halved = order[2], order[1]
            here = self.place[axis]
            for step in (1, 3):
                wait_bytes(self.pieces(part, 16), self.recv.at[part, 1 + step])
                there = moved(self.place, axis, (here + 4 - step) % 4)
                at = list(span(there, order[:2]))
                half = step // 2
                if halved == "x":
                    at[4] = half
                else:
                    at[0 if halved == "z" else 3] = pl.ds(half * 2, 2)
                piece = self.buf.at[(*at, slice(None), pl.ds(first, width))]
                target = device_at(moved(self.place, axis, (here + step) % 4))
                remote(
                    piece, piece, self.send.at[part, 2], self.recv.at[part, 3], target
                ).start()
                self.forward(part, there, order[:2])

    def finish(self):
        for part, (_, order) in enumerate(PARTS):
            wait_bytes(self.pieces(part, 16), self.recv.at[part, 3])
            axis = order[2]
            there = moved(self.place, axis, (self.place[axis] + 2) % 4)
            self.forward(part, there, order[:2])
        for part in range(3):
            wait_bytes(self.pieces(part, 64), self.recv.at[part, 5])
            wait_bytes(self.pieces(part, 64), self.send.at[part, 3])
            wait_bytes(self.pieces(part, 3), self.send.at[part, 0])
            wait_bytes(self.pieces(part, 12), self.send.at[part, 1])
            wait_bytes(self.pieces(part, 48), self.send.at[part, 2])


VMEM = pl.BlockSpec(memory_space=pltpu.VMEM)
HBM = pl.BlockSpec(memory_space=pl.ANY)


def unpack(buf, staged, out_w, hidden_w, proj_w, out_sem):
    spans = ((0, 128, out_w), (128, GROUP, hidden_w), (208, GROUP, proj_w))
    staged[:, 0:32] = jnp.zeros((2, 32, D), bf16)
    staged[:, 112:128] = jnp.zeros((2, 16, D), bf16)

    @pl.loop(0, 16)
    def _(g):
        slot = g % 2
        outs = [
            pltpu.make_async_copy(
                staged.at[slot, pl.ds(at, count)], row_block(ref, g, count), out_sem.at[i, slot]
            )
            for i, (at, count, ref) in enumerate(spans)
        ]

        @pl.when(g >= 2)
        def _():
            for out in outs:
                out.wait()

        packed = buf[g // 4, (g // 2) % 2, g % 2].reshape(256, D).astype(f32)
        for w, at in enumerate((32, 128, 208)):
            rows = rows_of(packed, 10, range(w * 10, 256, ROWS))
            staged[slot, at : at + GROUP] = rows.astype(bf16)
        for out in outs:
            out.start()

    for slot in range(2):
        for i, (at, count, ref) in enumerate(spans):
            pltpu.make_async_copy(
                staged.at[slot, pl.ds(at, count)], row_block(ref, 0, count), out_sem.at[i, slot]
            ).wait()


class Scatter:
    def __init__(self, away, mine, pair, lands, halves, send, recv, place):
        self.away, self.mine, self.pair = away, mine, pair
        self.lands, self.halves = lands, halves
        self.send, self.recv, self.place = send, recv, place
        self.sibling = device_at(moved(place, "c", 1 - place["c"]))

    def swap(self, number):
        at = (number // 2, number % 2)
        sems = (len(PARTS_BACK), number)
        return remote(
            self.away.at[at], self.pair.at[at], self.send.at[sems], self.recv.at[sems], self.sibling
        )

    def add_pair(self, number):
        self.swap(number).wait()
        at = (number // 2, number % 2)
        self.mine[at] = (self.mine[at].astype(f32) + self.pair[at].astype(f32)).astype(bf16)

    def source(self, part, stage, where):
        (first, width), order = PARTS_BACK[part]
        if stage == 0:
            at = span(where, order[:2], core=False)
            return self.mine.at[(*at, slice(None), pl.ds(first, width))]
        at = [
            slice(None) if axis in order[: 2 - stage] else value
            for axis, value in zip("zxyx", span(where, "", core=False))
            if axis in order[: 3 - stage]
        ]
        return self.halves[stage - 1][part].at[tuple(at)]

    def start(self, stage):
        for part, (_, order) in enumerate(PARTS_BACK):
            axis = order[2 - stage]
            for step in (1, 3, 2):
                target = moved(self.place, axis, (self.place[axis] + step) % 4)
                remote(
                    self.source(part, stage, target),
                    self.lands[stage][part].at[step - 1],
                    self.send.at[part, stage],
                    self.recv.at[part, stage],
                    device_at(target),
                ).start()

    def add(self, stage, out=None):
        for part, ((first, width), order) in enumerate(PARTS_BACK):
            land = self.lands[stage][part]
            wait_bytes(land, self.recv.at[part, stage])
            own = self.source(part, stage, self.place)
            lead = land.shape[1:-2]

            @pl.loop(0, math.prod(lead))
            def _(number):
                at = []
                for size in reversed(lead):
                    at.insert(0, number % size)
                    number = number // size
                at = tuple(at)
                total = own[at].astype(f32)
                for source in range(3):
                    total = total + land[(source, *at)].astype(f32)
                if stage < 2:
                    self.halves[stage][part][at] = total.astype(bf16)
                else:
                    out[:, first : first + width] = total

    def finish(self):
        for stage in range(3):
            for part in range(len(PARTS_BACK)):
                wait_bytes(self.lands[stage][part], self.send.at[part, stage])


def lead_of(axes):
    sizes = {"z": (4,), "x": (2, 2), "y": (4,)}
    if axes == {"x", "y"}:
        return (2, 4, 2)
    if axes == {"x", "z"}:
        return (4, 2, 2)
    return sum((sizes[axis] for axis in "zyx" if axis in axes), ())


def scatter_scratch():
    whole = pltpu.VMEM((4, 2, 4, 2, ROWS, D), bf16)
    lands, halves = [], []
    for stage in range(3):
        for (_, width), order in PARTS_BACK:
            lead = lead_of(set(order[: 2 - stage]))
            lands.append(pltpu.VMEM((3, *lead, ROWS, width), bf16))
            if stage < 2:
                halves.append(pltpu.VMEM((*lead, ROWS, width), bf16))
    semaphores = [pltpu.SemaphoreType.DMA((4, 8))] * 2
    return [whole] * 3 + lands + halves + semaphores


def scatter_of(scratch, place):
    away, mine, pair = scratch[:3]
    parts = len(PARTS_BACK)
    lands = [scratch[3 + parts * stage : 3 + parts * (stage + 1)] for stage in range(3)]
    halves = [scratch[3 + parts * stage : 3 + parts * (stage + 1)] for stage in (3, 4)]
    return Scatter(away, mine, pair, lands, halves, scratch[-2], scratch[-1], place)


HALVES = ((0, "yz"), (256, "zy"))


def ring_devices(place):
    others = [moved(place, "c", 1 - place["c"])]
    for step in (1, 3, 2):
        there = moved(place, "x", (place["x"] + step) % 4)
        others += [there, moved(there, "c", 1 - place["c"])]
    return others


def ring_number(place):
    return (place["x"] % 2) * 4 + place["c"] * 2 + place["x"] // 2


def tokens_of(ref, place):
    inner = (place["x"] % 2) * 2 + place["c"]
    return ref.at[inner, :, pl.ds((place["x"] // 2) * TOK, TOK)]


def head_of(place):
    return (place["x"] // 2) * 8 + (place["z"] % 2) * 4 + place["y"]


def pair_device(pair, quarter):
    micro, h = pair // H, pair % H
    return ((micro * 2 + (h % 8) // 4) * 4 + quarter, (h % 4) * 2 + h // 8)


def column_pieces(buf, half, place, free):
    at = [slice(None) if axis in free else place[axis] for axis in "zy"]
    return buf.at[(*at, slice(None), pl.ds(HALVES[half][0], 256))]


def gather_columns(buf, send, recv, place, stage):
    for half, (first, order) in enumerate(HALVES):
        axis = order[stage]
        if stage:
            wait_bytes(buf.at[0, pl.ds(0, 3), :, pl.ds(first, 256)], recv.at[half, 0])
        piece = column_pieces(buf, half, place, order[:stage])
        for step in (1, 3, 2):
            target = moved(place, axis, (place[axis] + step) % 4)
            remote(
                piece, piece, send.at[half, stage], recv.at[half, stage], device_at(target)
            ).start()


def finish_columns(buf, send, recv):
    for half, (first, _) in enumerate(HALVES):
        cols = pl.ds(first, 256)
        wait_bytes(buf.at[pl.ds(0, 3), :, :, cols], recv.at[half, 1])
        wait_bytes(buf.at[0, pl.ds(0, 3), :, cols], send.at[half, 0])
        wait_bytes(buf.at[pl.ds(0, 3), :, :, cols], send.at[half, 1])


def quarter_of(blk):
    inner = blk % 4
    return jnp.where((blk // 4) % 2 == 0, inner, 3 - inner)


def query_block(quarter, j):
    return j * 4 + jnp.where(j % 2 == 0, quarter, 3 - quarter)


def cell_of(ref, pair, width):
    return ref.at[pl.ds(pair // H * TOK, TOK), pl.ds(pair % H * width, width)]


def mask_of(key_block, block, start):
    key_at = key_block * B + lax.broadcasted_iota(jnp.int32, (B, B), 0)
    query_at = block * B + lax.broadcasted_iota(jnp.int32, (B, B), 1)
    return (key_at >= start) & (key_at <= query_at)


def has_mask(key_block, block):
    return (key_block == 0) | (key_block == block) | (block == 15)


def shift_matrix(rows, cols, by):
    row = lax.broadcasted_iota(jnp.int32, (rows, cols), 0)
    col = lax.broadcasted_iota(jnp.int32, (rows, cols), 1)
    return jnp.where((row - col == by) & (jnp.minimum(row, col) < HD), 1.0, 0.0).astype(bf16)


def wait_cells(ref, sem, fewer, width):
    wait_bytes(ref.at[:, pl.ds(0, 15 * width)], sem)
    wait_bytes(cell_of(ref, 0, width), sem)

    @pl.when(jnp.logical_not(fewer))
    def _():
        wait_bytes(cell_of(ref, 0, width), sem)


def stays_here(place):
    return (place["z"] % 2 == place["x"] % 2) & (place["y"] // 2 == place["c"])


def wait_ring(ref, sem, place):
    wait_bytes(ref.at[pl.ds(0, 3)], sem)
    wait_bytes(ref.at[0, pl.ds(0, 384)], sem)

    @pl.when(jnp.logical_not(stays_here(place)))
    def _():
        wait_bytes(ref.at[0, pl.ds(0, 128)], sem)


def front_kernel(
    tokens, pieces, pack, scale_row, segments, join,
    normed_hbm, packed_hbm, wide_hbm, vectors, starts, kv_out, queries, out_t, log_norms, attended,
    out_w, hidden_w, proj_w,
    normed_out, normed_t, packed_out, wide_w, keep_sems, ring_tokens, ring_pieces, chunks, kv, value_t, tops, totals, rounded, landed, buf, staged,
    x_tok_send, x_tok_recv, c_tok_send, c_tok_recv, piece_send, piece_recv, col_send, col_recv,
    two_send, two_recv, own_sem, send, recv, core_send, core_recv, x_send, x_recv,
    pass_send, pass_recv, back_send, back_recv, kv_sem, out_sem,
):
    blk = lax.axis_index("blk")
    head = lax.axis_index("head")
    core = blk % 2
    x_low = (blk // 2) % 2
    quarter = blk % 4
    even = (blk // 4) % 2 == 0
    place = my_place()
    pair = (place["z"] // 2) * H + head_of(place)
    turn = place["x"] * 2 + core
    sibling = (blk + 1 - 2 * core, head)
    two = Gather(buf, two_send, two_recv, place)
    own = two.begin(pack, own_sem.at[0])
    own_tokens = pltpu.make_async_copy(tokens, tokens_of(ring_tokens, place), own_sem.at[1])
    own_tokens.start()
    number = ring_number(place)
    pltpu.make_async_copy(pieces.at[turn], ring_pieces.at[number], piece_recv).start()
    greet_all()
    for there in ring_devices(place):
        remote(
            pieces.at[there["x"] * 2 + there["c"]],
            ring_pieces.at[number],
            piece_send,
            piece_recv,
            device_at(there),
        ).start()
    mine = tokens_of(ring_tokens, place)
    for step in (1, 3, 2):
        there = moved(place, "x", (place["x"] + step) % 4)
        remote(
            tokens, mine, x_tok_send.at[step - 1], x_tok_recv.at[step - 1], device_at(there)
        ).start()
    remote(tokens, mine, c_tok_send, c_tok_recv, sibling).start()
    own.wait()
    two.stage(0)
    ids = segments[place["z"] // 2]
    before = [jnp.sum((ids < value).astype(jnp.int32)) for value in range(1, 9)]
    for j in range(4):
        row = segments[place["z"] // 2, pl.ds(query_block(quarter, j), 1)]
        start = jnp.zeros_like(row)
        for value in range(1, 9):
            start = jnp.where(row == value, before[value - 1], start)
        starts[j] = start
    wait_bytes(ring_pieces, piece_recv)
    joined = nn(join[...], ring_pieces[...].reshape(256, MINE)).astype(bf16)
    chunks[place["z"], place["y"]] = joined
    gather_columns(chunks, col_send, col_recv, place, 0)
    gather_columns(chunks, col_send, col_recv, place, 1)
    for step in (1, 3, 2):
        wait_bytes(tokens, x_tok_recv.at[step - 1])
        there = moved(place, "x", (place["x"] + 4 - step) % 4)
        arrived = tokens_of(ring_tokens, there)
        remote(arrived, arrived, c_tok_send, c_tok_recv, sibling).start()
    own_tokens.wait()
    finish_columns(chunks, col_send, col_recv)

    @pl.loop(0, 4)
    def _(z):
        rows = pl.ds(pl.multiple_of(z * 4 * GROUP, 64), 4 * GROUP)
        found = chunks[z].reshape(4 * CHUNK, MINE).astype(f32)
        starts_at = [y * CHUNK + inner * 20 for inner in range(4) for y in range(4)]
        wide_w[rows] = rows_of(found, 20, starts_at).astype(bf16)

    vector_rows = jnp.zeros((16, MINE), f32)
    for z in range(4):
        for y in range(4):
            vector_rows = vector_rows + chunks[z, y, GROUP:].astype(f32)
    for i in range(5):
        three = [vector_rows[1 + 3 * i + k : 2 + 3 * i + k] for k in range(3)]
        vectors[i : i + 1] = jnp.concatenate(three[:2] + [three[2][:, :256]], axis=1)
    bias = vector_rows[0:1]
    gain = vectors[0:1]
    one_lane = jnp.where(
        lax.broadcasted_iota(jnp.int32, (1, MINE), 1) % LANES == 3 * HD, 1.0, 0.0
    )
    wait_bytes(ring_tokens.at[pl.ds(0, 2)], c_tok_recv)

    def deliver(inner, aside, send, recv):
        block = place["z"] * 4 + inner
        to_quarter = (quarter_of(block) + aside) % 4
        for m in range(2):
            for h in range(2):
                blk_to, head_to = pair_device(m * H + turn * 2 + h, to_quarter)
                src = packed_out.at[inner, m, :, pl.ds(h * LANES, LANES)]
                dst = kv.at[block, pl.ds(place["y"] * 128, 128)]
                stays = (blk_to == blk) & (head_to == head)

                @pl.when(stays)
                def _():
                    pltpu.make_async_copy(src, dst, recv).start()

                @pl.when(jnp.logical_not(stays))
                def _():
                    remote(src, dst, send, recv, (blk_to, head_to)).start()

    @pl.loop(0, 4)
    def _(inner):
        values = ring_tokens[inner].reshape(256, D).astype(f32)
        normed = (values * inverse_rms(values) * gain).astype(bf16)
        normed_out[inner] = normed
        full = nn(normed, wide_w[...])
        packed = ((full + bias) * scale_row[0:1] + one_lane).astype(bf16)
        packed_out[inner] = packed.reshape(2, 128, MINE)
        deliver(inner, 0, send, recv)

    @pl.loop(0, 4)
    def _(inner):
        deliver(inner, 2, x_send, x_recv)

    two.stage(1)

    @pl.loop(0, 4)
    def _(inner):
        @pl.loop(0, D // 128)
        def _(n):
            lanes = pl.ds(pl.multiple_of(n * 128, 128), 128)
            normed_t[inner, lanes] = normed_out[inner, :, lanes].T

    keeps = [
        pltpu.make_async_copy(ref, out, keep_sems.at[i])
        for i, (ref, out) in enumerate(
            ((normed_t, normed_hbm), (packed_out, packed_hbm), (wide_w, wide_hbm))
        )
    ]
    for keep in keeps:
        keep.start()
    wait_bytes(kv.at[pl.ds(0, 4)], recv)

    @pl.loop(0, 4)
    def _(j):
        block = kv.at[query_block(quarter, j)]
        remote(block, block, core_send, core_recv, sibling).start()

    pick = shift_matrix(LANES, 128, HD)

    @pl.loop(0, 4)
    def _(j):
        queries[j] = nn(kv[query_block(quarter, j)], pick).astype(bf16)
        tops[j] = jnp.full((1, B), NEGATIVE, f32)
        totals[j] = jnp.zeros((1, B), f32)
        out_t[j] = jnp.zeros((128, B), f32)


    def step(j, block, key_blocks):
        def tiles(masked):
            scores = []
            for key_block in key_blocks:
                s = nt(kv[key_block, :, :128], queries[j])
                if masked:
                    s = jnp.where(mask_of(key_block, block, starts[j]), s, NEGATIVE)
                scores.append(s)
            top = tops[j]
            new_top = top
            for s in scores:
                new_top = jnp.maximum(new_top, jnp.max(s, axis=0, keepdims=True))
            scale = jnp.exp(top - new_top)
            total = totals[j] * scale
            acc = out_t[j] * scale
            for key_block, s in zip(key_blocks, scores):
                p = jnp.exp(s - new_top)
                total = total + jnp.sum(p, axis=0, keepdims=True)
                acc = acc + nn(value_t[key_block], p.astype(bf16))
            tops[j] = new_top
            totals[j] = total
            out_t[j] = acc

        masked = has_mask(key_blocks[0], block)
        for key_block in key_blocks[1:]:
            masked = masked | has_mask(key_block, block)
        pl.when(masked)(lambda: tiles(True))
        pl.when(jnp.logical_not(masked))(lambda: tiles(False))

    def key_pass(j, of_quarter, count):
        block = query_block(quarter, j)

        @pl.loop(0, count // 2)
        def _(n):
            last = count - 1 - 2 * n
            step(j, block, (query_block(of_quarter, last), query_block(of_quarter, last - 1)))

        @pl.when(count % 2 == 1)
        def _():
            step(j, block, (query_block(of_quarter, 0),))

    def give(j, block):
        acc = out_t[j]
        result = acc / acc[112:113]
        out_t[j] = result
        log_norms[j] = tops[j] + jnp.log(totals[j])
        rounded[j] = result.T.astype(bf16)

        @pl.loop(0, 8)
        def _(k):
            h = (head + k) % 8
            src = rounded.at[j, pl.ds(h * TOK, TOK)]
            dst = cell_of(landed, pair, 128)
            mine = (k == 0) & (block == blk)

            @pl.when(mine)
            def _():
                pltpu.make_async_copy(src, dst, back_recv).start()

            @pl.when(jnp.logical_not(mine))
            def _():
                remote(src, dst, back_send, back_recv, (block, h)).start()

    keep_kv = pltpu.make_async_copy(kv, kv_out, kv_sem)

    @pl.loop(0, 4)
    def _(turn_at):
        of_quarter = (quarter + 2 * (turn_at // 2)) % 4 + (turn_at % 2) * (1 - 2 * core)

        @pl.when(turn_at == 1)
        def _():
            two.stage(2)
            wait_bytes(kv.at[pl.ds(0, 4)], core_recv)

        @pl.when(turn_at == 2)
        def _():
            wait_bytes(kv.at[pl.ds(0, 4)], x_recv)

            @pl.loop(0, 4)
            def _(j):
                block = kv.at[query_block(of_quarter, j)]
                remote(block, block, pass_send, pass_recv, sibling).start()

        @pl.when(turn_at == 3)
        def _():
            two.relay()
            wait_bytes(kv.at[pl.ds(0, 4)], pass_recv)
            keep_kv.start()

        @pl.loop(0, 4)
        def _(j):
            b = query_block(of_quarter, j)
            value_t[b] = kv[b, :, 128:].T

        @pl.loop(0, 4)
        def _(i):
            j = 3 - i
            block = query_block(quarter, j)
            more = jnp.where(
                turn_at == 0, 1, jnp.where(turn_at == 1, block % 2, (j + x_low) % 2)
            )
            key_pass(j, of_quarter, j + more)
            pl.when(turn_at == 3)(lambda: give(j, block))

    two.finish()
    unpack(buf, staged, out_w, hidden_w, proj_w, out_sem)
    wait_bytes(landed, back_recv)
    attended[...] = landed[...]
    for keep in keeps + [keep_kv]:
        keep.wait()
    for sem in (core_send, pass_send):
        wait_bytes(kv.at[pl.ds(0, 4)], sem)
    wait_cells(landed, back_send, even, 128)
    wait_bytes(ring_pieces.at[pl.ds(0, 7)], piece_send)
    for step_at in range(3):
        wait_bytes(tokens, x_tok_send.at[step_at])
    wait_bytes(ring_tokens.at[pl.ds(0, 2)], c_tok_send)
    wait_ring(kv, send, place)
    wait_ring(kv, x_send, place)


def front(*operands):
    dma = pltpu.SemaphoreType.DMA
    return pl.pallas_call(
        front_kernel,
        out_shape=(
            jax.ShapeDtypeStruct((4, D, 256), bf16),
            jax.ShapeDtypeStruct((4, 2, 128, MINE), bf16),
            jax.ShapeDtypeStruct((D, MINE), bf16),
            jax.ShapeDtypeStruct((8, D), f32),
            jax.ShapeDtypeStruct((4, 1, B), jnp.int32),
            jax.ShapeDtypeStruct((16, B, LANES), bf16),
            jax.ShapeDtypeStruct((4, B, 128), bf16),
            jax.ShapeDtypeStruct((4, 128, B), f32),
            jax.ShapeDtypeStruct((4, 1, B), f32),
            jax.ShapeDtypeStruct((2 * TOK, OUT_WIDE), bf16),
            jax.ShapeDtypeStruct((OUT_WIDE, D), bf16),
            jax.ShapeDtypeStruct((D, D), bf16),
            jax.ShapeDtypeStruct((D, D), bf16),
        ),
        in_specs=[VMEM] * 6,
        out_specs=(HBM,) * 3 + (VMEM,) * 2 + (HBM,) + (VMEM,) * 4 + (HBM,) * 3,
        scratch_shapes=[
            pltpu.VMEM((4, 256, D), bf16),
            pltpu.VMEM((4, D, 256), bf16),
            pltpu.VMEM((4, 2, 128, MINE), bf16),
            pltpu.VMEM((D, MINE), bf16),
            dma((3,)),
            pltpu.VMEM((4, 2, 128, D), bf16),
            pltpu.VMEM((8, ROWS, MINE), bf16),
            pltpu.VMEM((4, 4, CHUNK, MINE), bf16),
            pltpu.VMEM((16, B, LANES), bf16),
            pltpu.VMEM((16, 128, B), bf16),
            pltpu.VMEM((4, 1, B), f32),
            pltpu.VMEM((4, 1, B), f32),
            pltpu.VMEM((4, B, 128), bf16),
            pltpu.VMEM((2 * TOK, OUT_WIDE), bf16),
            pltpu.VMEM((4, 2, 2, 4, 2, ROWS, D), bf16),
            pltpu.VMEM((2, 288, D), bf16),
            dma((3,)), dma((3,)), dma, dma, dma, dma, dma((2, 2)), dma((2, 2)),
            dma((3, 4)), dma((3, 6)), dma((2,)),
        ]
        + [dma] * 11
        + [dma((3, 2))],
        compiler_params=pltpu.CompilerParams(
            collective_id=0, has_side_effects=True, vmem_limit_bytes=56 * 2**20
        ),
        name="front",
    )(
        *operands,
        jnp.asarray(JOIN, bf16),
    )


def rear_kernel(
    pack, kv_hbm, queries, starts, out_t, log_norms,
    attended, d_branch, normed_two, d_pre, activated, upstream,
    normed_hbm, packed_hbm, wide_hbm, vector_grads, scale_row, tokens, vectors,
    share,
    input_grad, pieces_out, two_out,
    kv, packed, wide_w, load_sems,
    d_out, key_t, deltas, d_query, d_kv, mine_kv, half, half_in, cross, cross_in, final, d_wide,
    attended_t, normed_two_t, activated_t,
    sum_in, grad_chunks, first_in, second_in, first_sum,
    joined, shares, shares_in,
    send, recv, core_send, core_recv, x_send, x_recv, back_send, back_recv,
    c_send, c_recv, sum_send, sum_recv, col_send, col_recv, share_send, share_recv,
    *scratch,
):
    blk = lax.axis_index("blk")
    head = lax.axis_index("head")
    core = blk % 2
    x_low = (blk // 2) % 2
    quarter = blk % 4
    place = my_place()
    my_head = head_of(place)
    pair = (place["z"] // 2) * H + my_head
    to_quarter = quarter_of(blk)
    even = (blk // 4) % 2 == 0
    two = scatter_of(scratch, place)
    loads = [
        pltpu.make_async_copy(src, dst, load_sems.at[i])
        for i, (src, dst) in enumerate(
            ((kv_hbm, kv), (packed_hbm, packed), (wide_hbm, wide_w))
        )
    ]
    for load in loads:
        load.start()
    greet_all()

    @pl.loop(0, PAIRS)
    def _(k):
        p = (pair + k) % PAIRS
        src = cell_of(pack, p, 128)
        dst = d_out.at[blk // 4, pl.ds(head * TOK, TOK)]
        mine = (k == 0) & even

        @pl.when(mine)
        def _():
            pltpu.make_async_copy(src, dst, recv).start()

        @pl.when(jnp.logical_not(mine))
        def _():
            remote(src, dst, send, recv, pair_device(p, to_quarter)).start()


    @pl.loop(0, D // 128)
    def _(n):
        lanes = pl.ds(pl.multiple_of(n * 128, 128), 128)
        normed_two_t[lanes] = normed_two[:, lanes].T
        activated_t[lanes] = activated[:, lanes].T

    @pl.loop(0, H)
    def _(n):
        lanes = pl.ds(pl.multiple_of(n * 128, 128), 128)
        attended_t[lanes] = attended[:, lanes].T


    @pl.loop(0, 8)
    def _(number):
        rows = pl.ds(pl.multiple_of(number * 2 * GROUP, 32), 2 * GROUP)
        heads = [
            attended_t[pl.ds(pl.multiple_of((number * 2 + k) * 128 + 32, 32), GROUP)]
            for k in range(2)
        ]
        found = [
            nn(jnp.concatenate(heads, axis=0), d_branch[...]),
            nn(normed_two_t[rows], d_pre[...]),
            nn(activated_t[rows], upstream[...]),
        ]
        spare = jnp.zeros((2, D), f32)
        for k in range(2):
            block = jnp.concatenate(
                [
                    part
                    for i in range(8)
                    for part in [w[k * GROUP + i * 10 : k * GROUP + i * 10 + 10] for w in found]
                    + [spare]
                ],
                axis=0,
            )
            block = block.astype(bf16).reshape(4, 2, ROWS, D)

            @pl.when(core == k)
            def _():
                two.mine[number // 2, number % 2] = block

            @pl.when(core != k)
            def _():
                two.away[number // 2, number % 2] = block

        two.swap(number).start()

    loads[0].wait()

    def keys_at(block, lane):
        return kv[pl.ds(pl.multiple_of(block * B, B), B), lane : lane + 128]

    @pl.loop(0, 16)
    def _(b):
        key_t[b] = keys_at(b, 0).T

    @pl.loop(0, 8)
    def _(number):
        two.add_pair(number)

    two.start(0)
    wait_bytes(d_out, recv)

    @pl.loop(0, 4)
    def _(j):
        deltas[j] = jnp.sum(d_out[j].astype(f32).T * out_t[j], axis=0, keepdims=True)
        d_query[j] = jnp.zeros((128, B), f32)

    sibling = (blk + 1 - 2 * core, head)

    def step(numbers, key_block):
        def tiles(masked):
            found = []
            for j in numbers:
                q = queries[j]
                do = d_out[j]
                p = jnp.exp(nt(keys_at(key_block, 0), q) - log_norms[j])
                if masked:
                    allowed = mask_of(key_block, query_block(quarter, j), starts[j])
                    p = jnp.where(allowed, p, 0.0)
                dp = nt(keys_at(key_block, 128), do)
                found.append((q, do, p.astype(bf16), (p * (dp - deltas[j])).astype(bf16)))
            d_kv[:, :128] += sum(nn(ds, q) for q, do, p, ds in found)
            d_kv[:, 128:] += sum(nn(p, do) for q, do, p, ds in found)
            for j, (q, do, p, ds) in zip(numbers, found):
                d_query[j] += nn(key_t[key_block], ds)

        masked = has_mask(key_block, query_block(quarter, numbers[0]))
        for j in numbers[1:]:
            masked = masked | has_mask(key_block, query_block(quarter, j))
        pl.when(masked)(lambda: tiles(True))
        pl.when(jnp.logical_not(masked))(lambda: tiles(False))

    def swap(n):
        return remote(
            half.at[n], half_in.at[n], core_send.at[n], core_recv.at[n], sibling
        )

    shift = shift_matrix(128, LANES, -HD)

    partner = (blk + 2 - 4 * x_low, head)

    def cross_swap(z):
        return remote(cross.at[z], cross_in.at[z], x_send.at[z], x_recv.at[z], partner)

    def core_sum(z):
        own = 2 * z + (x_low + z) % 2
        other = 4 * z + 1 - own
        swap(other).wait()
        cross[z] = (mine_kv[other] + half_in[other].astype(f32)).astype(bf16)
        cross_swap(z).start()
        swap(own).wait()
        mine_kv[own] = (
            mine_kv[own]
            + half_in[own].astype(f32)
            + nn(d_query[z].T.astype(bf16), shift)
        )

    def finish(z):
        cross_swap(z).wait()
        own = 2 * z + (x_low + z) % 2
        final[z] = (mine_kv[own] + cross_in[z].astype(f32)).astype(bf16)
        inner = query_block(quarter, z) % 4
        dst = d_wide.at[inner, place["z"] // 2, :, pl.ds((my_head % 2) * LANES, LANES)]

        @pl.loop(0, 4)
        def _(k):
            y = (place["y"] + k) % 4
            there = {"x": my_head // 4, "y": y, "z": z, "c": (my_head // 2) % 2}
            src = final.at[z, pl.ds(y * 128, 128)]
            blk_to, head_to = device_at(there)
            stays = (blk_to == blk) & (head_to == head)

            @pl.when(stays)
            def _():
                pltpu.make_async_copy(src, dst, back_recv).start()

            @pl.when(jnp.logical_not(stays))
            def _():
                remote(src, dst, back_send, back_recv, (blk_to, head_to)).start()

    load_normed = pltpu.make_async_copy(normed_hbm, kv.at[pl.ds(0, 4 * D)], load_sems.at[3])

    def key_steps(key_block):
        z = key_block // 4
        d_kv[...] = jnp.zeros((B, LANES), f32)
        first = z + (query_block(quarter, z) < key_block).astype(jnp.int32)

        @pl.when(first % 2 == 1)
        def _():
            step((first,), key_block)

        @pl.loop((first + 1) // 2, 2)
        def _(n):
            step((2 * n, 2 * n + 1), key_block)

        n = 2 * z + (key_block % 4) // 2

        @pl.when((key_block + z + core) % 2 == 0)
        def _():
            mine_kv[n] = d_kv[...]

        @pl.when((key_block + z + core) % 2 == 1)
        def _():
            half[n] = d_kv[...].astype(bf16)
            swap(n).start()

    @pl.loop(0, 10)
    def _(part):
        z = part // 2

        @pl.when(part < 8)
        def _():
            @pl.loop(2 * part, 2 * part + 2)
            def _(key_block):
                key_steps(key_block)

        @pl.when(part == 8)
        def _():
            load_normed.start()

        @pl.when((part % 2 == 0) & (part > 0))
        def _():
            core_sum(z - 1)

        @pl.when((part % 2 == 1) & (part > 1))
        def _():
            finish(z - 1)

        @pl.when(part == 6)
        def _():
            two.add(0)
            two.start(1)

    two.add(1)
    two.start(2)
    wait_bytes(d_wide, back_recv)

    for load in loads[1:]:
        load.wait()
    load_normed.wait()
    partial = two.away.at[:, 0]
    summed, partial_in = two.away.at[pl.ds(0, 2), 1], two.away.at[pl.ds(2, 2), 1]
    scale = scale_row[0:1]
    bias_sum = jnp.zeros((1, MINE), f32)
    scale_sum = jnp.zeros((1, MINE), f32)

    def scaled_grads(inner, sums):
        bias_sum, scale_sum = sums
        grad = d_wide[inner].reshape(256, MINE).astype(f32)
        scale_sum = scale_sum + jnp.sum(
            grad * packed[inner].reshape(256, MINE).astype(f32), axis=0, keepdims=True
        )
        grad = (grad * scale).astype(bf16)
        d_wide[inner] = grad.reshape(2, 128, MINE)
        return bias_sum + jnp.sum(grad.astype(f32), axis=0, keepdims=True), scale_sum

    bias_sum, scale_sum = lax.fori_loop(0, 4, scaled_grads, (bias_sum, scale_sum))
    scale_sum = scale_sum[:, :LANES] + scale_sum[:, LANES:]
    rows = vector_grads[...] + jnp.concatenate(
        [bias_sum, jnp.concatenate([scale_sum, scale_sum], axis=1), jnp.zeros((14, MINE), f32)],
        axis=0,
    )
    rows = rows.astype(bf16)
    sibling_at = (blk + 1 - 2 * core, head)
    c_swaps = [
        remote(
            partial.at[low * 2 + 1 - core],
            partial_in.at[low],
            c_send.at[low],
            c_recv.at[low],
            sibling_at,
        )
        for low in range(2)
    ]

    def token_grads(inner):
        back = nt(d_wide[inner].reshape(256, MINE), wide_w[...])
        partial[inner] = back.astype(bf16).reshape(4, 2, ROWS, D)

    @pl.loop(0, 2)
    def _(low):
        token_grads(low * 2 + 1 - core)

    for low in range(2):
        c_swaps[low].start()

    @pl.loop(0, 4)
    def _(z):
        def part(inner):
            at = pl.ds(pl.multiple_of(inner * D + z * 320, 64), 320)
            return nn(kv[at], d_wide[inner].reshape(256, MINE))

        grads = sum(part(inner) for inner in range(4))
        for y in range(4):
            found = rows_of(grads, 20, [inner * GROUP + y * 20 for inner in range(4)])
            grad_chunks[z, y, :GROUP] = found.astype(bf16)
            grad_chunks[z, y, GROUP:] = rows


    for step_at in (1, 3, 2):
        for half, axis in enumerate("zy"):
            there = moved(place, axis, (place[axis] + step_at) % 4)
            remote(
                column_pieces(grad_chunks, half, there, "y" if half == 0 else "z"),
                first_in.at[half, step_at - 1],
                col_send.at[half, 0],
                col_recv.at[half, 0],
                device_at(there),
            ).start()

    @pl.loop(0, 2)
    def _(low):
        token_grads(low * 2 + core)

    for low in range(2):
        c_swaps[low].wait()
        summed[low] = (
            partial[low * 2 + core].astype(f32) + partial_in[low].astype(f32)
        ).astype(bf16)
    for step_at in (1, 3, 2):
        there = moved(place, "x", (place["x"] + step_at) % 4)
        for m in range(2):
            remote(
                summed.at[there["x"] % 2, m * 2 + there["x"] // 2],
                sum_in.at[step_at - 1, m],
                sum_send,
                sum_recv,
                device_at(there),
            ).start()
    for half in range(2):
        wait_bytes(first_in.at[half], col_recv.at[half, 0])
        own = column_pieces(grad_chunks, half, place, "y" if half == 0 else "z")
        for number in range(4):
            total = own[number].astype(f32)
            for source in range(3):
                total = total + first_in[half, source, number].astype(f32)
            first_sum[half, number] = total.astype(bf16)
    for step_at in (1, 3, 2):
        for half, axis in enumerate("yz"):
            there = moved(place, axis, (place[axis] + step_at) % 4)
            remote(
                first_sum.at[half, there[axis]],
                second_in.at[half, step_at - 1],
                col_send.at[half, 1],
                col_recv.at[half, 1],
                device_at(there),
            ).start()
    totals = []
    for half, axis in enumerate("yz"):
        wait_bytes(second_in.at[half], col_recv.at[half, 1])
        total = first_sum[half, place[axis]].astype(f32)
        for source in range(3):
            total = total + second_in[half, source].astype(f32)
        totals.append(total)
    total_y, total_z = totals
    joined[:, 0:256] = total_y.astype(bf16)
    joined[:, 256:512] = total_z.astype(bf16)
    shares[...] = nn(share[...], joined[...]).astype(bf16).reshape(8, ROWS, MINE)
    turn = place["x"] * 2 + core
    for there in ring_devices(place):
        remote(
            shares.at[ring_number(there)],
            shares_in.at[turn],
            share_send,
            share_recv,
            device_at(there),
        ).start()
    pltpu.make_async_copy(
        shares.at[ring_number(place)], shares_in.at[turn], share_recv
    ).start()
    two.add(2, two_out)
    two.finish()
    wait_bytes(sum_in, sum_recv)
    for m in range(2):
        total = summed[x_low, m * 2 + place["x"] // 2].astype(f32)
        for source in range(3):
            total = total + sum_in[source, m].astype(f32)
        values = tokens[m].astype(f32)
        upward = total.reshape(TOK, D) * vectors[0:1]
        input_grad[m] = (
            d_branch[m * TOK : (m + 1) * TOK].astype(f32)
            + norm_back(upward, values, inverse_rms(values))
        ).astype(bf16)
    wait_bytes(shares_in, share_recv)
    pieces_out[...] = shares_in[...]
    wait_cells(pack, send, even, 128)
    wait_ring(final, back_send, place)
    wait_bytes(sum_in, sum_send)
    for number in range(2):
        wait_bytes(first_in.at[number], col_send.at[number, 0])
        wait_bytes(second_in.at[number], col_send.at[number, 1])
    wait_bytes(shares.at[pl.ds(0, 7)], share_send)


def rear(*operands):
    dma = pltpu.SemaphoreType.DMA
    return pl.pallas_call(
        rear_kernel,
        out_shape=(
            jax.ShapeDtypeStruct((2, TOK, D), bf16),
            jax.ShapeDtypeStruct((8, ROWS, MINE), bf16),
            jax.ShapeDtypeStruct((ROWS, D), f32),
        ),
        in_specs=[VMEM] + [HBM] + [VMEM] * 10 + [HBM] * 3 + [VMEM] * 5,
        out_specs=(VMEM, VMEM, VMEM),
        scratch_shapes=[
            pltpu.VMEM((16 * B, LANES), bf16),
            pltpu.VMEM((4, 2, 128, MINE), bf16),
            pltpu.VMEM((D, MINE), bf16),
            dma((4,)),
            pltpu.VMEM((4, B, 128), bf16),
            pltpu.VMEM((16, 128, B), bf16),
            pltpu.VMEM((4, 1, B), f32),
            pltpu.VMEM((4, 128, B), f32),
            pltpu.VMEM((B, LANES), f32),
            pltpu.VMEM((8, B, LANES), f32),
            pltpu.VMEM((8, B, LANES), bf16),
            pltpu.VMEM((8, B, LANES), bf16),
            pltpu.VMEM((4, B, LANES), bf16),
            pltpu.VMEM((4, B, LANES), bf16),
            pltpu.VMEM((4, B, LANES), bf16),
            pltpu.VMEM((4, 2, 128, MINE), bf16),
            pltpu.VMEM((OUT_WIDE, 128), bf16),
            pltpu.VMEM((D, 128), bf16),
            pltpu.VMEM((D, 128), bf16),
            pltpu.VMEM((3, 2, 2, ROWS, D), bf16),
            pltpu.VMEM((4, 4, CHUNK, MINE), bf16),
            pltpu.VMEM((2, 3, 4, CHUNK, 256), bf16),
            pltpu.VMEM((2, 3, CHUNK, 256), bf16),
            pltpu.VMEM((2, 4, CHUNK, 256), bf16),
            pltpu.VMEM((CHUNK, MINE), bf16),
            pltpu.VMEM((8, ROWS, MINE), bf16),
            pltpu.VMEM((8, ROWS, MINE), bf16),
            dma, dma, dma((8,)), dma((8,)), dma((4,)), dma((4,)), dma, dma,
            dma((2,)), dma((2,)), dma, dma, dma((2, 2)), dma((2, 2)), dma, dma,
        ]
        + scatter_scratch(),
        compiler_params=pltpu.CompilerParams(
            collective_id=1, has_side_effects=True, vmem_limit_bytes=63 * 2**20
        ),
        name="rear",
    )(
        *operands,
        jnp.asarray(SHARE, bf16),
    )


def on_device(
    inputs,
    segment_ids,
    norm1_gain,
    w_query,
    w_key,
    w_value,
    query_bias,
    value_bias,
    w_out,
    out_bias,
    norm2_gain,
    w_hidden,
    hidden_bias,
    w_proj,
    proj_bias,
    dim_scale,
    cotangent,
):
    blk = lax.axis_index("blk")
    head = lax.axis_index("head")
    at = (blk * 8 + head) * 10
    spread_heads = jnp.zeros((H, LANES), bf16)
    biases = jnp.concatenate([query_bias, jnp.zeros((HD - 10,), bf16), value_bias])
    spread_heads = lax.dynamic_update_slice(spread_heads, biases[None], (blk, HD + head * 10))
    natural = jnp.stack([norm1_gain, out_bias, norm2_gain, hidden_bias, proj_bias])
    natural = lax.dynamic_update_slice(jnp.zeros((5, 3 * MINE), bf16), natural, (0, at))
    columns = jnp.concatenate(
        [w.reshape(10, H, HD) for w in (w_key, w_query, w_value)]
        + [jnp.zeros((10, H, LANES - 3 * HD), bf16)],
        axis=2,
    )
    columns = columns.reshape(10, 8, MINE).transpose(1, 0, 2)
    pieces = jnp.concatenate(
        [
            columns,
            jnp.zeros((8, 6, MINE), bf16),
            spread_heads.reshape(8, 1, MINE),
            jnp.broadcast_to(natural.reshape(1, 15, MINE), (8, 15, MINE)),
        ],
        axis=1,
    )
    pack = jnp.concatenate([w_out, w_hidden, w_proj, jnp.zeros((2, D), bf16)], axis=0)
    softplus_scale = LOG2E / math.sqrt(HD) * jax.nn.softplus(dim_scale)
    ones = jnp.ones((HD,), f32)
    scale_row = jnp.concatenate(
        [ones, softplus_scale, ones, jnp.zeros((LANES - 3 * HD,), f32)] * 2
    )
    scale_row = scale_row[None]

    (
        ring_normed, packed, wide_w, vectors, starts, kv, queries, out_t, log_norms, attended,
        out_w, hidden_w, proj_w,
    ) = front(inputs, pieces, pack, scale_row, segment_ids.reshape(2, 16, B))
    out_b, gain_two, hidden_b, proj_b = [vectors[i] for i in range(1, 5)]

    tokens = inputs.reshape(2 * TOK, D).astype(f32)
    residual = tokens + nn(attended, out_w) + out_b
    inverse_two = inverse_rms(residual)
    normed_two = (residual * inverse_two * gain_two).astype(bf16)
    pre_act = nn(normed_two, hidden_w) + hidden_b
    gate = jax.nn.sigmoid(pre_act)
    activated = (pre_act * gate).astype(bf16)
    layer_out = (residual + nn(activated, proj_w) + proj_b).astype(bf16)

    upstream_low = cotangent.reshape(2 * TOK, D)
    upstream = upstream_low.astype(f32)
    d_pre = (nt(upstream_low, proj_w) * gate * (1.0 + pre_act * (1.0 - gate))).astype(bf16)
    d_normed_two = nt(d_pre, hidden_w)
    d_residual = upstream + norm_back(d_normed_two * gain_two, residual, inverse_two)
    d_branch = d_residual.astype(bf16)
    d_attended = nt(d_branch, out_w).astype(bf16)

    def total(values):
        return jnp.sum(values.astype(f32), axis=0)

    vector_grads = jnp.stack(
        [
            total(d_branch),
            total(d_normed_two * residual * inverse_two),
            total(d_pre),
            total(upstream),
        ]
    )
    vector_grads = jnp.pad(vector_grads, ((0, 0), (0, 3 * MINE - D))).reshape(12, MINE)
    vector_grads = jnp.pad(vector_grads, ((4, 0), (0, 0)))
    input_grad, shares, two = rear(
        d_attended, kv.reshape(16 * B, LANES), queries, starts, out_t, log_norms,
        attended, d_branch, normed_two, d_pre, activated, upstream_low,
        ring_normed.reshape(4 * D, 256), packed, wide_w, vector_grads, scale_row,
        inputs, vectors,
    )
    shares = shares.astype(f32)
    columns = shares[:, :10].transpose(1, 0, 2).reshape(10, H, LANES)
    d_key_w, d_query_w, d_value_w = [
        columns[:, :, i * HD : (i + 1) * HD].reshape(10, D) for i in range(3)
    ]
    by_head = shares[:, 16].reshape(H, LANES)
    d_query_bias, d_value_bias = [
        lax.dynamic_slice(by_head, (blk, i * HD + head * 10), (1, 10)).reshape(10) for i in (1, 2)
    ]
    summed = jnp.sum(shares[:, 17:], axis=0)
    scale_grad = summed[0, HD : 2 * HD] / softplus_scale
    scale_grad = scale_grad * (LOG2E / math.sqrt(HD)) * jax.nn.sigmoid(dim_scale)
    natural = lax.dynamic_slice(summed.reshape(5, 3 * MINE), (0, at), (5, 10))
    norm1_gain_grad = sum(
        jnp.sum(w.astype(f32) * grad, axis=1)
        for w, grad in ((w_query, d_query_w), (w_key, d_key_w), (w_value, d_value_w))
    ) / norm1_gain.astype(f32)
    return (
        layer_out.reshape(2, TOK, D),
        input_grad,
        norm1_gain_grad,
        d_query_w,
        d_key_w,
        d_value_w,
        d_query_bias,
        d_value_bias,
        two[0:10],
        natural[1],
        natural[2],
        two[10:20],
        natural[3],
        two[20:30],
        natural[4],
        scale_grad,
    )


def solution(mesh):
    rows = P(("blk", "head"), None)
    vec = P(("blk", "head"))
    tok = P(None, ("blk", "head"), None)
    in_specs = (
        tok, P(), vec, rows, rows, rows, vec, vec, rows, vec, vec, rows, vec, rows, vec, P(), tok
    )
    out_specs = (
        tok, tok, vec, rows, rows, rows, vec, vec, rows, vec, vec, rows, vec, rows, vec, P()
    )
    return jax.shard_map(
        on_device, mesh=mesh, in_specs=in_specs, out_specs=out_specs, check_vma=False
    )
```

```python
import functools
import math

import jax
import jax.numpy as jnp
import numpy as np
from jax import lax
from jax.experimental import pallas as pl
from jax.experimental.pallas import tpu as pltpu
from jax.sharding import PartitionSpec as P

D = 1280
H = 16
HD = 80
FF = 1280
B = 512
TOK = 64
PAIRS = 32
LANES = 256
ROWS = 32
WIDE = H * LANES
OUT_WIDE = H * 128
GROUP = 80
CHUNK = 96
MINE = 512
EPSILON = 1e-06
LOG2E = 1.442695041
NEGATIVE = -1e30
MESH = pl.DeviceIdType.MESH
f32 = jnp.float32
bf16 = jnp.bfloat16

PARTS = (((0, 384), "xyz"), ((384, 512), "yzx"), ((896, 384), "zxy"))
PARTS_BACK = (((0, 512), "xyz"), ((512, 512), "xzy"), ((1024, 256), "yzx"))


def inverse_rms(values):
    return lax.rsqrt(jnp.mean(values * values, axis=-1, keepdims=True) + EPSILON)


def norm_back(upstream, values, inverse):
    return inverse * upstream - values * inverse**3 * jnp.mean(
        upstream * values, axis=-1, keepdims=True
    )


def nn(a, b):
    return lax.dot_general(a, b, (((1,), (0,)), ((), ())), preferred_element_type=f32)


def nt(a, b):
    return lax.dot_general(a, b, (((1,), (1,)), ((), ())), preferred_element_type=f32)


def tn(a, b):
    return lax.dot_general(a, b, (((0,), (0,)), ((), ())), preferred_element_type=f32)


def my_place():
    blk = lax.axis_index("blk")
    head = lax.axis_index("head")
    return {
        "x": (head % 2) * 2 + (blk // 2) % 2,
        "y": head // 2,
        "z": blk // 4,
        "c": blk % 2,
    }


def device_at(place):
    x, y, z, c = place["x"], place["y"], place["z"], place["c"]
    return (z * 4 + (x % 2) * 2 + c, y * 2 + x // 2)


def span(place, free, core=True):
    x, y, z = place["x"], place["y"], place["z"]
    whole = slice(None)
    at = [
        whole if "z" in free else z,
        whole if "x" in free else x % 2,
        place["c"],
        whole if "y" in free else y,
        whole if "x" in free else x // 2,
    ]
    return tuple(at if core else at[:2] + at[3:])


def moved(place, axis, value):
    other = dict(place)
    other[axis] = value
    return other


def greet(peers):
    barrier = pltpu.get_barrier_semaphore()
    for peer in peers:
        pl.semaphore_signal(barrier, inc=1, device_id=peer, device_id_type=MESH)
    pl.semaphore_wait(barrier, len(peers))


def greet_all():
    barrier = pltpu.get_barrier_semaphore()
    me = lax.axis_index("blk") * 8 + lax.axis_index("head")

    @pl.loop(1, 128)
    def _(k):
        other = (me + k) % 128
        pl.semaphore_signal(
            barrier, inc=1, device_id=(other // 8, other % 8), device_id_type=MESH
        )

    pl.semaphore_wait(barrier, 127)


def ring_peers(place):
    peers = [device_at(moved(place, "c", 1 - place["c"]))]
    for axis in "xyz":
        for step in (1, 3, 2):
            peers.append(device_at(moved(place, axis, (place[axis] + step) % 4)))
    return peers


def wait_bytes(ref, sem):
    pltpu.make_async_copy(ref, ref, sem).wait()


def remote(src, dst, send, recv, device):
    return pltpu.make_async_remote_copy(
        src_ref=src, dst_ref=dst, send_sem=send, recv_sem=recv, device_id=device, device_id_type=MESH
    )


def varied(place, axes, number):
    other = dict(place)
    for axis in axes:
        other[axis] = number % 4
        number = number // 4
    return other


def selections():
    join = np.zeros((CHUNK, 256), np.float32)
    for i in range(8):
        for j in range(10):
            join[i * 10 + j, i * ROWS + j] = 1
        for v in range(16):
            join[GROUP + v, i * ROWS + 16 + v] = 1
    return join, join.T.copy()


JOIN, SHARE = selections()


def rows_of(values, size, starts):
    return jnp.concatenate([values[at : at + size] for at in starts], axis=0)


def row_block(ref, g, count):
    return ref.at[pl.ds(pl.multiple_of(g * count, 16), count)]


class Gather:
    def __init__(self, buf, send, recv, place):
        self.place = place
        self.buf, self.send, self.recv = buf, send, recv
        self.sibling = device_at(moved(place, "c", 1 - place["c"]))

    def begin(self, matrices):
        spare = jnp.zeros((2, D), f32)
        own = [matrix[...].astype(f32) for matrix in matrices] + [spare]
        self.buf[span(self.place, "")] = jnp.concatenate(own, axis=0).astype(bf16)

    def piece(self, part, where, free):
        first, width = PARTS[part][0]
        return self.buf.at[(*span(where, free), slice(None), pl.ds(first, width))]

    def pieces(self, part, count):
        cols = pl.ds(*PARTS[part][0])
        whole = slice(None)
        at = {
            3: (pl.ds(0, 3), 0, 0, 0, 0),
            12: (pl.ds(0, 3), 0, 0, whole, 0),
            16: (0, whole, 0, whole, whole),
            48: (pl.ds(0, 3), whole, 0, whole, whole),
            64: (whole, whole, 0, whole, whole),
        }[count]
        return self.buf.at[(*at, whole, cols)]

    def forward(self, part, where, free):
        piece = self.piece(part, where, free)
        remote(piece, piece, self.send.at[part, 3], self.recv.at[part, 5], self.sibling).start()

    def stage(self, stage):
        for part, (_, order) in enumerate(PARTS):
            if stage:
                wait_bytes(self.pieces(part, 3 * 4 ** (stage - 1)), self.recv.at[part, stage - 1])
            piece = self.piece(part, self.place, order[:stage])
            axis = order[stage]
            for step in (1, 3, 2) if stage < 2 else (1, 3):
                target = moved(self.place, axis, (self.place[axis] + step) % 4)
                slot = stage if stage < 2 else 1 + step
                remote(
                    piece,
                    piece,
                    self.send.at[part, stage],
                    self.recv.at[part, slot],
                    device_at(target),
                ).start()
        for part, (_, order) in enumerate(PARTS):
            if stage == 0:
                self.forward(part, self.place, "")
            else:
                axis = order[stage - 1]
                for step in (1, 3, 2):
                    there = moved(self.place, axis, (self.place[axis] + 4 - step) % 4)
                    self.forward(part, there, order[: stage - 1])

    def relay(self):
        for part, ((first, width), order) in enumerate(PARTS):
            axis, halved = order[2], order[1]
            here = self.place[axis]
            for step in (1, 3):
                wait_bytes(self.pieces(part, 16), self.recv.at[part, 1 + step])
                there = moved(self.place, axis, (here + 4 - step) % 4)
                at = list(span(there, order[:2]))
                half = step // 2
                if halved == "x":
                    at[4] = half
                else:
                    at[0 if halved == "z" else 3] = pl.ds(half * 2, 2)
                piece = self.buf.at[(*at, slice(None), pl.ds(first, width))]
                target = device_at(moved(self.place, axis, (here + step) % 4))
                remote(
                    piece, piece, self.send.at[part, 2], self.recv.at[part, 3], target
                ).start()
                self.forward(part, there, order[:2])

    def finish(self):
        for part, (_, order) in enumerate(PARTS):
            wait_bytes(self.pieces(part, 16), self.recv.at[part, 3])
            axis = order[2]
            there = moved(self.place, axis, (self.place[axis] + 2) % 4)
            self.forward(part, there, order[:2])
        for part in range(3):
            wait_bytes(self.pieces(part, 64), self.recv.at[part, 5])
            wait_bytes(self.pieces(part, 64), self.send.at[part, 3])
            wait_bytes(self.pieces(part, 3), self.send.at[part, 0])
            wait_bytes(self.pieces(part, 12), self.send.at[part, 1])
            wait_bytes(self.pieces(part, 48), self.send.at[part, 2])


VMEM = pl.BlockSpec(memory_space=pltpu.VMEM)
HBM = pl.BlockSpec(memory_space=pl.ANY)


def unpack(buf, staged, out_w, hidden_w, proj_w, out_sem):
    spans = ((0, 128, out_w), (128, GROUP, hidden_w), (208, GROUP, proj_w))
    staged[:, 0:32] = jnp.zeros((2, 32, D), bf16)
    staged[:, 112:128] = jnp.zeros((2, 16, D), bf16)

    @pl.loop(0, 16)
    def _(g):
        slot = g % 2
        outs = [
            pltpu.make_async_copy(
                staged.at[slot, pl.ds(at, count)], row_block(ref, g, count), out_sem.at[i, slot]
            )
            for i, (at, count, ref) in enumerate(spans)
        ]

        @pl.when(g >= 2)
        def _():
            for out in outs:
                out.wait()

        packed = buf[g // 4, (g // 2) % 2, g % 2].reshape(256, D).astype(f32)
        for w, at in enumerate((32, 128, 208)):
            rows = rows_of(packed, 10, range(w * 10, 256, ROWS))
            staged[slot, at : at + GROUP] = rows.astype(bf16)
        for out in outs:
            out.start()

    for slot in range(2):
        for i, (at, count, ref) in enumerate(spans):
            pltpu.make_async_copy(
                staged.at[slot, pl.ds(at, count)], row_block(ref, 0, count), out_sem.at[i, slot]
            ).wait()


class Scatter:
    def __init__(self, away, mine, pair, lands, halves, send, recv, place):
        self.away, self.mine, self.pair = away, mine, pair
        self.lands, self.halves = lands, halves
        self.send, self.recv, self.place = send, recv, place
        self.sibling = device_at(moved(place, "c", 1 - place["c"]))

    def swap(self, number):
        at = (number // 2, number % 2)
        sems = (len(PARTS_BACK), number)
        return remote(
            self.away.at[at], self.pair.at[at], self.send.at[sems], self.recv.at[sems], self.sibling
        )

    def add_pair(self, number):
        self.swap(number).wait()
        at = (number // 2, number % 2)
        self.mine[at] = (self.mine[at].astype(f32) + self.pair[at].astype(f32)).astype(bf16)

    def source(self, part, stage, where):
        (first, width), order = PARTS_BACK[part]
        if stage == 0:
            at = span(where, order[:2], core=False)
            return self.mine.at[(*at, slice(None), pl.ds(first, width))]
        at = [
            slice(None) if axis in order[: 2 - stage] else value
            for axis, value in zip("zxyx", span(where, "", core=False))
            if axis in order[: 3 - stage]
        ]
        return self.halves[stage - 1][part].at[tuple(at)]

    def start(self, stage):
        for part, (_, order) in enumerate(PARTS_BACK):
            axis = order[2 - stage]
            for step in (1, 3, 2):
                target = moved(self.place, axis, (self.place[axis] + step) % 4)
                remote(
                    self.source(part, stage, target),
                    self.lands[stage][part].at[step - 1],
                    self.send.at[part, stage],
                    self.recv.at[part, stage],
                    device_at(target),
                ).start()

    def add(self, stage, out=None):
        for part, ((first, width), order) in enumerate(PARTS_BACK):
            land = self.lands[stage][part]
            wait_bytes(land, self.recv.at[part, stage])
            own = self.source(part, stage, self.place)
            lead = land.shape[1:-2]

            @pl.loop(0, math.prod(lead))
            def _(number):
                at = []
                for size in reversed(lead):
                    at.insert(0, number % size)
                    number = number // size
                at = tuple(at)
                total = own[at].astype(f32)
                for source in range(3):
                    total = total + land[(source, *at)].astype(f32)
                if stage < 2:
                    self.halves[stage][part][at] = total.astype(bf16)
                else:
                    out[:, first : first + width] = total

    def finish(self):
        for stage in range(3):
            for part in range(len(PARTS_BACK)):
                wait_bytes(self.lands[stage][part], self.send.at[part, stage])


def lead_of(axes):
    sizes = {"z": (4,), "x": (2, 2), "y": (4,)}
    if axes == {"x", "y"}:
        return (2, 4, 2)
    if axes == {"x", "z"}:
        return (4, 2, 2)
    return sum((sizes[axis] for axis in "zyx" if axis in axes), ())


def scatter_scratch():
    whole = pltpu.VMEM((4, 2, 4, 2, ROWS, D), bf16)
    lands, halves = [], []
    for stage in range(3):
        for (_, width), order in PARTS_BACK:
            lead = lead_of(set(order[: 2 - stage]))
            lands.append(pltpu.VMEM((3, *lead, ROWS, width), bf16))
            if stage < 2:
                halves.append(pltpu.VMEM((*lead, ROWS, width), bf16))
    semaphores = [pltpu.SemaphoreType.DMA((4, 8))] * 2
    return [whole] * 3 + lands + halves + semaphores


def scatter_of(scratch, place):
    away, mine, pair = scratch[:3]
    parts = len(PARTS_BACK)
    lands = [scratch[3 + parts * stage : 3 + parts * (stage + 1)] for stage in range(3)]
    halves = [scratch[3 + parts * stage : 3 + parts * (stage + 1)] for stage in (3, 4)]
    return Scatter(away, mine, pair, lands, halves, scratch[-2], scratch[-1], place)


HALVES = ((0, "yz"), (256, "zy"))


def ring_devices(place):
    others = [moved(place, "c", 1 - place["c"])]
    for step in (1, 3, 2):
        there = moved(place, "x", (place["x"] + step) % 4)
        others += [there, moved(there, "c", 1 - place["c"])]
    return others


def ring_number(place):
    return (place["x"] % 2) * 4 + place["c"] * 2 + place["x"] // 2


def tokens_of(ref, place):
    inner = (place["x"] % 2) * 2 + place["c"]
    return ref.at[inner, :, pl.ds((place["x"] // 2) * TOK, TOK)]


def head_of(place):
    return (place["x"] // 2) * 8 + (place["z"] % 2) * 4 + place["y"]


def pair_device(pair, quarter):
    micro, h = pair // H, pair % H
    return ((micro * 2 + (h % 8) // 4) * 4 + quarter, (h % 4) * 2 + h // 8)


def column_pieces(buf, half, place, free):
    at = [slice(None) if axis in free else place[axis] for axis in "zy"]
    return buf.at[(*at, slice(None), pl.ds(HALVES[half][0], 256))]


def gather_columns(buf, send, recv, place, stage):
    for half, (first, order) in enumerate(HALVES):
        axis = order[stage]
        if stage:
            wait_bytes(buf.at[0, pl.ds(0, 3), :, pl.ds(first, 256)], recv.at[half, 0])
        piece = column_pieces(buf, half, place, order[:stage])
        for step in (1, 3, 2):
            target = moved(place, axis, (place[axis] + step) % 4)
            remote(
                piece, piece, send.at[half, stage], recv.at[half, stage], device_at(target)
            ).start()


def finish_columns(buf, send, recv):
    for half, (first, _) in enumerate(HALVES):
        cols = pl.ds(first, 256)
        wait_bytes(buf.at[pl.ds(0, 3), :, :, cols], recv.at[half, 1])
        wait_bytes(buf.at[0, pl.ds(0, 3), :, cols], send.at[half, 0])
        wait_bytes(buf.at[pl.ds(0, 3), :, :, cols], send.at[half, 1])


def quarter_of(blk):
    inner = blk % 4
    return jnp.where((blk // 4) % 2 == 0, inner, 3 - inner)


def query_block(quarter, j):
    return j * 4 + jnp.where(j % 2 == 0, quarter, 3 - quarter)


def cell_of(ref, pair, width):
    return ref.at[pl.ds(pair // H * TOK, TOK), pl.ds(pair % H * width, width)]


def mask_of(key_block, block, start):
    key_at = key_block * B + lax.broadcasted_iota(jnp.int32, (B, B), 0)
    query_at = block * B + lax.broadcasted_iota(jnp.int32, (B, B), 1)
    return (key_at >= start) & (key_at <= query_at)


def has_mask(key_block, block):
    return (key_block == 0) | (key_block == block) | (block == 15)


def shift_matrix(rows, cols, by):
    row = lax.broadcasted_iota(jnp.int32, (rows, cols), 0)
    col = lax.broadcasted_iota(jnp.int32, (rows, cols), 1)
    return jnp.where((row - col == by) & (jnp.minimum(row, col) < HD), 1.0, 0.0).astype(bf16)


def wait_cells(ref, sem, fewer, width):
    wait_bytes(ref.at[:, pl.ds(0, 15 * width)], sem)
    wait_bytes(cell_of(ref, 0, width), sem)

    @pl.when(jnp.logical_not(fewer))
    def _():
        wait_bytes(cell_of(ref, 0, width), sem)


def stays_here(place):
    return (place["z"] % 2 == place["x"] % 2) & (place["y"] // 2 == place["c"])


def wait_ring(ref, sem, place):
    wait_bytes(ref.at[pl.ds(0, 3)], sem)
    wait_bytes(ref.at[0, pl.ds(0, 384)], sem)

    @pl.when(jnp.logical_not(stays_here(place)))
    def _():
        wait_bytes(ref.at[0, pl.ds(0, 128)], sem)


def front_kernel(
    tokens, pieces, w_out, w_hidden, w_proj, scale_row, segments, join,
    normed_hbm, packed_hbm, wide_hbm, vectors, starts, kv_out, queries, out_t, log_norms, attended,
    out_w, hidden_w, proj_w,
    normed_out, normed_t, packed_out, wide_w, keep_sems, ring_tokens, ring_pieces, chunks, kv, value_t, tops, totals, rounded, landed, buf, staged,
    x_tok_send, x_tok_recv, c_tok_send, c_tok_recv, piece_send, piece_recv, col_send, col_recv,
    two_send, two_recv, own_sem, send, recv, core_send, core_recv, x_send, x_recv,
    pass_send, pass_recv, back_send, back_recv, kv_sem, out_sem,
):
    blk = lax.axis_index("blk")
    head = lax.axis_index("head")
    core = blk % 2
    x_low = (blk // 2) % 2
    quarter = blk % 4
    even = (blk // 4) % 2 == 0
    place = my_place()
    pair = (place["z"] // 2) * H + head_of(place)
    turn = place["x"] * 2 + core
    sibling = (blk + 1 - 2 * core, head)
    two = Gather(buf, two_send, two_recv, place)
    own_tokens = pltpu.make_async_copy(tokens, tokens_of(ring_tokens, place), own_sem)
    own_tokens.start()
    number = ring_number(place)
    pltpu.make_async_copy(pieces.at[turn], ring_pieces.at[number], piece_recv).start()
    greet_all()
    for there in ring_devices(place):
        remote(
            pieces.at[there["x"] * 2 + there["c"]],
            ring_pieces.at[number],
            piece_send,
            piece_recv,
            device_at(there),
        ).start()
    mine = tokens_of(ring_tokens, place)
    for step in (1, 3, 2):
        there = moved(place, "x", (place["x"] + step) % 4)
        remote(
            tokens, mine, x_tok_send.at[step - 1], x_tok_recv.at[step - 1], device_at(there)
        ).start()
    remote(tokens, mine, c_tok_send, c_tok_recv, sibling).start()
    two.begin((w_out, w_hidden, w_proj))
    two.stage(0)
    ids = segments[place["z"] // 2]
    before = [jnp.sum((ids < value).astype(jnp.int32)) for value in range(1, 9)]
    for j in range(4):
        row = segments[place["z"] // 2, pl.ds(query_block(quarter, j), 1)]
        start = jnp.zeros_like(row)
        for value in range(1, 9):
            start = jnp.where(row == value, before[value - 1], start)
        starts[j] = start
    wait_bytes(ring_pieces, piece_recv)
    joined = nn(join[...], ring_pieces[...].reshape(256, MINE)).astype(bf16)
    chunks[place["z"], place["y"]] = joined
    gather_columns(chunks, col_send, col_recv, place, 0)
    gather_columns(chunks, col_send, col_recv, place, 1)
    for step in (1, 3, 2):
        wait_bytes(tokens, x_tok_recv.at[step - 1])
        there = moved(place, "x", (place["x"] + 4 - step) % 4)
        arrived = tokens_of(ring_tokens, there)
        remote(arrived, arrived, c_tok_send, c_tok_recv, sibling).start()
    own_tokens.wait()
    finish_columns(chunks, col_send, col_recv)

    @pl.loop(0, 4)
    def _(z):
        rows = pl.ds(pl.multiple_of(z * 4 * GROUP, 64), 4 * GROUP)
        found = chunks[z].reshape(4 * CHUNK, MINE).astype(f32)
        starts_at = [y * CHUNK + inner * 20 for inner in range(4) for y in range(4)]
        wide_w[rows] = rows_of(found, 20, starts_at).astype(bf16)

    vector_rows = jnp.zeros((16, MINE), f32)
    for z in range(4):
        for y in range(4):
            vector_rows = vector_rows + chunks[z, y, GROUP:].astype(f32)
    for i in range(5):
        three = [vector_rows[1 + 3 * i + k : 2 + 3 * i + k] for k in range(3)]
        vectors[i : i + 1] = jnp.concatenate(three[:2] + [three[2][:, :256]], axis=1)
    bias = vector_rows[0:1]
    gain = vectors[0:1]
    one_lane = jnp.where(
        lax.broadcasted_iota(jnp.int32, (1, MINE), 1) % LANES == 3 * HD, 1.0, 0.0
    )
    wait_bytes(ring_tokens.at[pl.ds(0, 2)], c_tok_recv)

    def deliver(inner, aside, send, recv):
        block = place["z"] * 4 + inner
        to_quarter = (quarter_of(block) + aside) % 4
        for m in range(2):
            for h in range(2):
                blk_to, head_to = pair_device(m * H + turn * 2 + h, to_quarter)
                src = packed_out.at[inner, m, :, pl.ds(h * LANES, LANES)]
                dst = kv.at[block, pl.ds(place["y"] * 128, 128)]
                stays = (blk_to == blk) & (head_to == head)

                @pl.when(stays)
                def _():
                    pltpu.make_async_copy(src, dst, recv).start()

                @pl.when(jnp.logical_not(stays))
                def _():
                    remote(src, dst, send, recv, (blk_to, head_to)).start()

    @pl.loop(0, 4)
    def _(inner):
        values = ring_tokens[inner].reshape(256, D).astype(f32)
        normed = (values * inverse_rms(values) * gain).astype(bf16)
        normed_out[inner] = normed
        full = nn(normed, wide_w[...])
        packed = ((full + bias) * scale_row[0:1] + one_lane).astype(bf16)
        packed_out[inner] = packed.reshape(2, 128, MINE)
        deliver(inner, 0, send, recv)

    @pl.loop(0, 4)
    def _(inner):
        deliver(inner, 2, x_send, x_recv)

    two.stage(1)

    @pl.loop(0, 4)
    def _(inner):
        @pl.loop(0, D // 128)
        def _(n):
            lanes = pl.ds(pl.multiple_of(n * 128, 128), 128)
            normed_t[inner, lanes] = normed_out[inner, :, lanes].T

    keeps = [
        pltpu.make_async_copy(ref, out, keep_sems.at[i])
        for i, (ref, out) in enumerate(
            ((normed_t, normed_hbm), (packed_out, packed_hbm), (wide_w, wide_hbm))
        )
    ]
    for keep in keeps:
        keep.start()
    wait_bytes(kv.at[pl.ds(0, 4)], recv)

    @pl.loop(0, 4)
    def _(j):
        block = kv.at[query_block(quarter, j)]
        remote(block, block, core_send, core_recv, sibling).start()

    pick = shift_matrix(LANES, 128, HD)

    @pl.loop(0, 4)
    def _(j):
        queries[j] = nn(kv[query_block(quarter, j)], pick).astype(bf16)
        tops[j] = jnp.full((1, B), NEGATIVE, f32)
        totals[j] = jnp.zeros((1, B), f32)
        out_t[j] = jnp.zeros((128, B), f32)


    def step(j, block, key_blocks):
        def tiles(masked):
            scores = []
            for key_block in key_blocks:
                s = nt(kv[key_block, :, :128], queries[j])
                if masked:
                    s = jnp.where(mask_of(key_block, block, starts[j]), s, NEGATIVE)
                scores.append(s)
            top = tops[j]
            new_top = top
            for s in scores:
                new_top = jnp.maximum(new_top, jnp.max(s, axis=0, keepdims=True))
            scale = jnp.exp(top - new_top)
            total = totals[j] * scale
            acc = out_t[j] * scale
            for key_block, s in zip(key_blocks, scores):
                p = jnp.exp(s - new_top)
                total = total + jnp.sum(p, axis=0, keepdims=True)
                acc = acc + nn(value_t[key_block], p.astype(bf16))
            tops[j] = new_top
            totals[j] = total
            out_t[j] = acc

        masked = has_mask(key_blocks[0], block)
        for key_block in key_blocks[1:]:
            masked = masked | has_mask(key_block, block)
        pl.when(masked)(lambda: tiles(True))
        pl.when(jnp.logical_not(masked))(lambda: tiles(False))

    def key_pass(j, of_quarter, count):
        block = query_block(quarter, j)

        @pl.when(count == 4)
        def _():
            step(j, block, tuple(query_block(of_quarter, n) for n in range(4)))

        @pl.loop(0, jnp.where(count == 4, 0, count // 2))
        def _(n):
            last = count - 1 - 2 * n
            step(j, block, (query_block(of_quarter, last), query_block(of_quarter, last - 1)))

        @pl.when(count % 2 == 1)
        def _():
            step(j, block, (query_block(of_quarter, 0),))

    def give(j, block):
        acc = out_t[j]
        result = acc / acc[112:113]
        out_t[j] = result
        log_norms[j] = tops[j] + jnp.log(totals[j])
        rounded[j] = result.T.astype(bf16)

        @pl.loop(0, 8)
        def _(k):
            h = (head + k) % 8
            src = rounded.at[j, pl.ds(h * TOK, TOK)]
            dst = cell_of(landed, pair, 128)
            mine = (k == 0) & (block == blk)

            @pl.when(mine)
            def _():
                pltpu.make_async_copy(src, dst, back_recv).start()

            @pl.when(jnp.logical_not(mine))
            def _():
                remote(src, dst, back_send, back_recv, (block, h)).start()

    keep_kv = pltpu.make_async_copy(kv, kv_out, kv_sem)

    @pl.loop(0, 4)
    def _(turn_at):
        of_quarter = (quarter + 2 * (turn_at // 2)) % 4 + (turn_at % 2) * (1 - 2 * core)

        @pl.when(turn_at == 1)
        def _():
            two.stage(2)
            wait_bytes(kv.at[pl.ds(0, 4)], core_recv)

        @pl.when(turn_at == 2)
        def _():
            wait_bytes(kv.at[pl.ds(0, 4)], x_recv)

            @pl.loop(0, 4)
            def _(j):
                block = kv.at[query_block(of_quarter, j)]
                remote(block, block, pass_send, pass_recv, sibling).start()

        @pl.when(turn_at == 3)
        def _():
            two.relay()
            wait_bytes(kv.at[pl.ds(0, 4)], pass_recv)
            keep_kv.start()

        @pl.loop(0, 4)
        def _(j):
            b = query_block(of_quarter, j)
            value_t[b] = kv[b, :, 128:].T

        @pl.loop(0, 4)
        def _(i):
            j = 3 - i
            block = query_block(quarter, j)
            more = jnp.where(
                turn_at == 0, 1, jnp.where(turn_at == 1, block % 2, (j + x_low) % 2)
            )
            key_pass(j, of_quarter, j + more)
            pl.when(turn_at == 3)(lambda: give(j, block))

    two.finish()
    unpack(buf, staged, out_w, hidden_w, proj_w, out_sem)
    wait_bytes(landed, back_recv)
    attended[...] = landed[...]
    for keep in keeps + [keep_kv]:
        keep.wait()
    for sem in (core_send, pass_send):
        wait_bytes(kv.at[pl.ds(0, 4)], sem)
    wait_cells(landed, back_send, even, 128)
    wait_bytes(ring_pieces.at[pl.ds(0, 7)], piece_send)
    for step_at in range(3):
        wait_bytes(tokens, x_tok_send.at[step_at])
    wait_bytes(ring_tokens.at[pl.ds(0, 2)], c_tok_send)
    wait_ring(kv, send, place)
    wait_ring(kv, x_send, place)


def front(*operands):
    dma = pltpu.SemaphoreType.DMA
    return pl.pallas_call(
        front_kernel,
        out_shape=(
            jax.ShapeDtypeStruct((4, D, 256), bf16),
            jax.ShapeDtypeStruct((4, 2, 128, MINE), bf16),
            jax.ShapeDtypeStruct((D, MINE), bf16),
            jax.ShapeDtypeStruct((8, D), f32),
            jax.ShapeDtypeStruct((4, 1, B), jnp.int32),
            jax.ShapeDtypeStruct((16, B, LANES), bf16),
            jax.ShapeDtypeStruct((4, B, 128), bf16),
            jax.ShapeDtypeStruct((4, 128, B), f32),
            jax.ShapeDtypeStruct((4, 1, B), f32),
            jax.ShapeDtypeStruct((2 * TOK, OUT_WIDE), bf16),
            jax.ShapeDtypeStruct((OUT_WIDE, D), bf16),
            jax.ShapeDtypeStruct((D, D), bf16),
            jax.ShapeDtypeStruct((D, D), bf16),
        ),
        in_specs=[VMEM] * 8,
        out_specs=(HBM,) * 3 + (VMEM,) * 2 + (HBM,) + (VMEM,) * 4 + (HBM,) * 3,
        scratch_shapes=[
            pltpu.VMEM((4, 256, D), bf16),
            pltpu.VMEM((4, D, 256), bf16),
            pltpu.VMEM((4, 2, 128, MINE), bf16),
            pltpu.VMEM((D, MINE), bf16),
            dma((3,)),
            pltpu.VMEM((4, 2, 128, D), bf16),
            pltpu.VMEM((8, ROWS, MINE), bf16),
            pltpu.VMEM((4, 4, CHUNK, MINE), bf16),
            pltpu.VMEM((16, B, LANES), bf16),
            pltpu.VMEM((16, 128, B), bf16),
            pltpu.VMEM((4, 1, B), f32),
            pltpu.VMEM((4, 1, B), f32),
            pltpu.VMEM((4, B, 128), bf16),
            pltpu.VMEM((2 * TOK, OUT_WIDE), bf16),
            pltpu.VMEM((4, 2, 2, 4, 2, ROWS, D), bf16),
            pltpu.VMEM((2, 288, D), bf16),
            dma((3,)), dma((3,)), dma, dma, dma, dma, dma((2, 2)), dma((2, 2)),
            dma((3, 4)), dma((3, 6)), dma,
        ]
        + [dma] * 11
        + [dma((3, 2))],
        compiler_params=pltpu.CompilerParams(
            collective_id=0, has_side_effects=True, vmem_limit_bytes=56 * 2**20
        ),
        name="front",
    )(
        *operands,
        jnp.asarray(JOIN, bf16),
    )


def rear_kernel(
    pack, kv_hbm, queries_hbm, starts, out_t_hbm, log_norms,
    attended, d_branch, normed_two, d_pre, activated, upstream,
    normed_hbm, packed_hbm, wide_hbm, vector_grads, scale_row, tokens, vectors,
    share,
    input_grad, pieces_out, two_out,
    kv, queries, out_t, packed, wide_w, load_sems,
    d_out, key_t, deltas, d_query, d_kv, mine_kv, half, half_in, cross, cross_in, final, d_wide,
    attended_t, normed_two_t, activated_t,
    sum_in, grad_chunks, first_in, second_in, first_sum,
    joined, shares, shares_in,
    send, recv, core_send, core_recv, x_send, x_recv, back_send, back_recv,
    c_send, c_recv, sum_send, sum_recv, col_send, col_recv, share_send, share_recv,
    *scratch,
):
    blk = lax.axis_index("blk")
    head = lax.axis_index("head")
    core = blk % 2
    x_low = (blk // 2) % 2
    quarter = blk % 4
    place = my_place()
    my_head = head_of(place)
    pair = (place["z"] // 2) * H + my_head
    to_quarter = quarter_of(blk)
    even = (blk // 4) % 2 == 0
    two = scatter_of(scratch, place)
    loads = [
        pltpu.make_async_copy(src, dst, load_sems.at[i])
        for i, (src, dst) in enumerate(
            (
                (kv_hbm, kv),
                (queries_hbm, queries),
                (out_t_hbm, out_t),
                (packed_hbm, packed),
                (wide_hbm, wide_w),
            )
        )
    ]
    for load in loads:
        load.start()
    greet_all()

    @pl.loop(0, PAIRS)
    def _(k):
        p = (pair + k) % PAIRS
        src = cell_of(pack, p, 128)
        dst = d_out.at[blk // 4, pl.ds(head * TOK, TOK)]
        mine = (k == 0) & even

        @pl.when(mine)
        def _():
            pltpu.make_async_copy(src, dst, recv).start()

        @pl.when(jnp.logical_not(mine))
        def _():
            remote(src, dst, send, recv, pair_device(p, to_quarter)).start()


    @pl.loop(0, D // 128)
    def _(n):
        lanes = pl.ds(pl.multiple_of(n * 128, 128), 128)
        normed_two_t[lanes] = normed_two[:, lanes].T
        activated_t[lanes] = activated[:, lanes].T

    @pl.loop(0, H)
    def _(n):
        lanes = pl.ds(pl.multiple_of(n * 128, 128), 128)
        attended_t[lanes] = attended[:, lanes].T


    @pl.loop(0, 8)
    def _(number):
        rows = pl.ds(pl.multiple_of(number * 2 * GROUP, 32), 2 * GROUP)
        heads = [
            attended_t[pl.ds(pl.multiple_of((number * 2 + k) * 128 + 32, 32), GROUP)]
            for k in range(2)
        ]
        found = [
            nn(jnp.concatenate(heads, axis=0), d_branch[...]),
            nn(normed_two_t[rows], d_pre[...]),
            nn(activated_t[rows], upstream[...]),
        ]
        spare = jnp.zeros((2, D), f32)
        for k in range(2):
            block = jnp.concatenate(
                [
                    part
                    for i in range(8)
                    for part in [w[k * GROUP + i * 10 : k * GROUP + i * 10 + 10] for w in found]
                    + [spare]
                ],
                axis=0,
            )
            block = block.astype(bf16).reshape(4, 2, ROWS, D)

            @pl.when(core == k)
            def _():
                two.mine[number // 2, number % 2] = block

            @pl.when(core != k)
            def _():
                two.away[number // 2, number % 2] = block

        two.swap(number).start()

    for load in loads[:3]:
        load.wait()

    def keys_at(block, lane):
        return kv[pl.ds(pl.multiple_of(block * B, B), B), lane : lane + 128]

    @pl.loop(0, 16)
    def _(b):
        key_t[b] = keys_at(b, 0).T

    @pl.loop(0, 8)
    def _(number):
        two.add_pair(number)

    two.start(0)
    wait_bytes(d_out, recv)

    @pl.loop(0, 4)
    def _(j):
        deltas[j] = jnp.sum(d_out[j].astype(f32).T * out_t[j], axis=0, keepdims=True)
        d_query[j] = jnp.zeros((128, B), f32)

    sibling = (blk + 1 - 2 * core, head)

    def step(numbers, key_block):
        def tiles(masked):
            found = []
            for j in numbers:
                q = queries[j]
                do = d_out[j]
                p = jnp.exp(nt(keys_at(key_block, 0), q) - log_norms[j])
                if masked:
                    allowed = mask_of(key_block, query_block(quarter, j), starts[j])
                    p = jnp.where(allowed, p, 0.0)
                dp = nt(keys_at(key_block, 128), do)
                found.append((q, do, p.astype(bf16), (p * (dp - deltas[j])).astype(bf16)))
            d_kv[:, :128] += sum(nn(ds, q) for q, do, p, ds in found)
            d_kv[:, 128:] += sum(nn(p, do) for q, do, p, ds in found)
            for j, (q, do, p, ds) in zip(numbers, found):
                d_query[j] += nn(key_t[key_block], ds)

        masked = has_mask(key_block, query_block(quarter, numbers[0]))
        for j in numbers[1:]:
            masked = masked | has_mask(key_block, query_block(quarter, j))
        pl.when(masked)(lambda: tiles(True))
        pl.when(jnp.logical_not(masked))(lambda: tiles(False))

    def swap(n):
        return remote(
            half.at[n], half_in.at[n], core_send.at[n], core_recv.at[n], sibling
        )

    shift = shift_matrix(128, LANES, -HD)

    partner = (blk + 2 - 4 * x_low, head)

    def cross_swap(z):
        return remote(cross.at[z], cross_in.at[z], x_send.at[z], x_recv.at[z], partner)

    def core_sum(z):
        own = 2 * z + (x_low + z) % 2
        other = 4 * z + 1 - own
        swap(other).wait()
        cross[z] = (mine_kv[other] + half_in[other].astype(f32)).astype(bf16)
        cross_swap(z).start()
        swap(own).wait()
        mine_kv[own] = (
            mine_kv[own]
            + half_in[own].astype(f32)
            + nn(d_query[z].T.astype(bf16), shift)
        )

    def finish(z):
        cross_swap(z).wait()
        own = 2 * z + (x_low + z) % 2
        final[z] = (mine_kv[own] + cross_in[z].astype(f32)).astype(bf16)
        inner = query_block(quarter, z) % 4
        dst = d_wide.at[inner, place["z"] // 2, :, pl.ds((my_head % 2) * LANES, LANES)]

        @pl.loop(0, 4)
        def _(k):
            y = (place["y"] + k) % 4
            there = {"x": my_head // 4, "y": y, "z": z, "c": (my_head // 2) % 2}
            src = final.at[z, pl.ds(y * 128, 128)]
            blk_to, head_to = device_at(there)
            stays = (blk_to == blk) & (head_to == head)

            @pl.when(stays)
            def _():
                pltpu.make_async_copy(src, dst, back_recv).start()

            @pl.when(jnp.logical_not(stays))
            def _():
                remote(src, dst, back_send, back_recv, (blk_to, head_to)).start()

    load_normed = pltpu.make_async_copy(normed_hbm, kv.at[pl.ds(0, 4 * D)], load_sems.at[5])

    def key_steps(key_block):
        z = key_block // 4
        d_kv[...] = jnp.zeros((B, LANES), f32)
        first = z + (query_block(quarter, z) < key_block).astype(jnp.int32)

        @pl.when(first % 2 == 1)
        def _():
            step((first,), key_block)

        @pl.loop((first + 1) // 2, 2)
        def _(n):
            step((2 * n, 2 * n + 1), key_block)

        n = 2 * z + (key_block % 4) // 2

        @pl.when((key_block + z + core) % 2 == 0)
        def _():
            mine_kv[n] = d_kv[...]

        @pl.when((key_block + z + core) % 2 == 1)
        def _():
            half[n] = d_kv[...].astype(bf16)
            swap(n).start()

    @pl.loop(0, 10)
    def _(part):
        z = part // 2

        @pl.when(part < 8)
        def _():
            @pl.loop(2 * part, 2 * part + 2)
            def _(key_block):
                key_steps(key_block)

        @pl.when(part == 8)
        def _():
            load_normed.start()

        @pl.when((part % 2 == 0) & (part > 0))
        def _():
            core_sum(z - 1)

        @pl.when((part % 2 == 1) & (part > 1))
        def _():
            finish(z - 1)

        @pl.when(part == 6)
        def _():
            two.add(0)
            two.start(1)

    two.add(1)
    two.start(2)
    wait_bytes(d_wide, back_recv)

    for load in loads[3:]:
        load.wait()
    load_normed.wait()
    partial = two.away.at[:, 0]
    summed, partial_in = two.away.at[pl.ds(0, 2), 1], two.away.at[pl.ds(2, 2), 1]
    scale = scale_row[0:1]
    bias_sum = jnp.zeros((1, MINE), f32)
    scale_sum = jnp.zeros((1, MINE), f32)

    def scaled_grads(inner, sums):
        bias_sum, scale_sum = sums
        grad = d_wide[inner].reshape(256, MINE).astype(f32)
        scale_sum = scale_sum + jnp.sum(
            grad * packed[inner].reshape(256, MINE).astype(f32), axis=0, keepdims=True
        )
        grad = (grad * scale).astype(bf16)
        d_wide[inner] = grad.reshape(2, 128, MINE)
        return bias_sum + jnp.sum(grad.astype(f32), axis=0, keepdims=True), scale_sum

    bias_sum, scale_sum = lax.fori_loop(0, 4, scaled_grads, (bias_sum, scale_sum))
    scale_sum = scale_sum[:, :LANES] + scale_sum[:, LANES:]
    rows = vector_grads[...] + jnp.concatenate(
        [bias_sum, jnp.concatenate([scale_sum, scale_sum], axis=1), jnp.zeros((14, MINE), f32)],
        axis=0,
    )
    rows = rows.astype(bf16)
    sibling_at = (blk + 1 - 2 * core, head)
    c_swaps = [
        remote(
            partial.at[low * 2 + 1 - core],
            partial_in.at[low],
            c_send.at[low],
            c_recv.at[low],
            sibling_at,
        )
        for low in range(2)
    ]

    def token_grads(inner):
        back = nt(d_wide[inner].reshape(256, MINE), wide_w[...])
        partial[inner] = back.astype(bf16).reshape(4, 2, ROWS, D)

    @pl.loop(0, 2)
    def _(low):
        token_grads(low * 2 + 1 - core)

    for low in range(2):
        c_swaps[low].start()

    @pl.loop(0, 4)
    def _(z):
        def part(inner):
            at = pl.ds(pl.multiple_of(inner * D + z * 320, 64), 320)
            return nn(kv[at], d_wide[inner].reshape(256, MINE))

        grads = sum(part(inner) for inner in range(4))
        for y in range(4):
            found = rows_of(grads, 20, [inner * GROUP + y * 20 for inner in range(4)])
            grad_chunks[z, y, :GROUP] = found.astype(bf16)
            grad_chunks[z, y, GROUP:] = rows


    for step_at in (1, 3, 2):
        for half, axis in enumerate("zy"):
            there = moved(place, axis, (place[axis] + step_at) % 4)
            remote(
                column_pieces(grad_chunks, half, there, "y" if half == 0 else "z"),
                first_in.at[half, step_at - 1],
                col_send.at[half, 0],
                col_recv.at[half, 0],
                device_at(there),
            ).start()

    @pl.loop(0, 2)
    def _(low):
        token_grads(low * 2 + core)

    for low in range(2):
        c_swaps[low].wait()
        summed[low] = (
            partial[low * 2 + core].astype(f32) + partial_in[low].astype(f32)
        ).astype(bf16)
    for step_at in (1, 3, 2):
        there = moved(place, "x", (place["x"] + step_at) % 4)
        for m in range(2):
            remote(
                summed.at[there["x"] % 2, m * 2 + there["x"] // 2],
                sum_in.at[step_at - 1, m],
                sum_send,
                sum_recv,
                device_at(there),
            ).start()
    for half in range(2):
        wait_bytes(first_in.at[half], col_recv.at[half, 0])
        own = column_pieces(grad_chunks, half, place, "y" if half == 0 else "z")
        for number in range(4):
            total = own[number].astype(f32)
            for source in range(3):
                total = total + first_in[half, source, number].astype(f32)
            first_sum[half, number] = total.astype(bf16)
    for step_at in (1, 3, 2):
        for half, axis in enumerate("yz"):
            there = moved(place, axis, (place[axis] + step_at) % 4)
            remote(
                first_sum.at[half, there[axis]],
                second_in.at[half, step_at - 1],
                col_send.at[half, 1],
                col_recv.at[half, 1],
                device_at(there),
            ).start()
    totals = []
    for half, axis in enumerate("yz"):
        wait_bytes(second_in.at[half], col_recv.at[half, 1])
        total = first_sum[half, place[axis]].astype(f32)
        for source in range(3):
            total = total + second_in[half, source].astype(f32)
        totals.append(total)
    total_y, total_z = totals
    joined[:, 0:256] = total_y.astype(bf16)
    joined[:, 256:512] = total_z.astype(bf16)
    shares[...] = nn(share[...], joined[...]).astype(bf16).reshape(8, ROWS, MINE)
    turn = place["x"] * 2 + core
    for there in ring_devices(place):
        remote(
            shares.at[ring_number(there)],
            shares_in.at[turn],
            share_send,
            share_recv,
            device_at(there),
        ).start()
    pltpu.make_async_copy(
        shares.at[ring_number(place)], shares_in.at[turn], share_recv
    ).start()
    two.add(2, two_out)
    two.finish()
    wait_bytes(sum_in, sum_recv)
    for m in range(2):
        total = summed[x_low, m * 2 + place["x"] // 2].astype(f32)
        for source in range(3):
            total = total + sum_in[source, m].astype(f32)
        values = tokens[m].astype(f32)
        upward = total.reshape(TOK, D) * vectors[0:1]
        input_grad[m] = (
            d_branch[m * TOK : (m + 1) * TOK].astype(f32)
            + norm_back(upward, values, inverse_rms(values))
        ).astype(bf16)
    wait_bytes(shares_in, share_recv)
    pieces_out[...] = shares_in[...]
    wait_cells(pack, send, even, 128)
    wait_ring(final, back_send, place)
    wait_bytes(sum_in, sum_send)
    for number in range(2):
        wait_bytes(first_in.at[number], col_send.at[number, 0])
        wait_bytes(second_in.at[number], col_send.at[number, 1])
    wait_bytes(shares.at[pl.ds(0, 7)], share_send)


def rear(*operands):
    dma = pltpu.SemaphoreType.DMA
    return pl.pallas_call(
        rear_kernel,
        out_shape=(
            jax.ShapeDtypeStruct((2, TOK, D), bf16),
            jax.ShapeDtypeStruct((8, ROWS, MINE), bf16),
            jax.ShapeDtypeStruct((ROWS, D), f32),
        ),
        in_specs=[HBM] * 3 + [VMEM, HBM] + [VMEM] * 7 + [HBM] * 3 + [VMEM] * 5,
        out_specs=(VMEM, VMEM, VMEM),
        scratch_shapes=[
            pltpu.VMEM((16 * B, LANES), bf16),
            pltpu.VMEM((4, B, 128), bf16),
            pltpu.VMEM((4, 128, B), f32),
            pltpu.VMEM((4, 2, 128, MINE), bf16),
            pltpu.VMEM((D, MINE), bf16),
            dma((6,)),
            pltpu.VMEM((4, B, 128), bf16),
            pltpu.VMEM((16, 128, B), bf16),
            pltpu.VMEM((4, 1, B), f32),
            pltpu.VMEM((4, 128, B), f32),
            pltpu.VMEM((B, LANES), f32),
            pltpu.VMEM((8, B, LANES), f32),
            pltpu.VMEM((8, B, LANES), bf16),
            pltpu.VMEM((8, B, LANES), bf16),
            pltpu.VMEM((4, B, LANES), bf16),
            pltpu.VMEM((4, B, LANES), bf16),
            pltpu.VMEM((4, B, LANES), bf16),
            pltpu.VMEM((4, 2, 128, MINE), bf16),
            pltpu.VMEM((OUT_WIDE, 128), bf16),
            pltpu.VMEM((D, 128), bf16),
            pltpu.VMEM((D, 128), bf16),
            pltpu.VMEM((3, 2, 2, ROWS, D), bf16),
            pltpu.VMEM((4, 4, CHUNK, MINE), bf16),
            pltpu.VMEM((2, 3, 4, CHUNK, 256), bf16),
            pltpu.VMEM((2, 3, CHUNK, 256), bf16),
            pltpu.VMEM((2, 4, CHUNK, 256), bf16),
            pltpu.VMEM((CHUNK, MINE), bf16),
            pltpu.VMEM((8, ROWS, MINE), bf16),
            pltpu.VMEM((8, ROWS, MINE), bf16),
            dma, dma, dma((8,)), dma((8,)), dma((4,)), dma((4,)), dma, dma,
            dma((2,)), dma((2,)), dma, dma, dma((2, 2)), dma((2, 2)), dma, dma,
        ]
        + scatter_scratch(),
        compiler_params=pltpu.CompilerParams(
            collective_id=1, has_side_effects=True, vmem_limit_bytes=63 * 2**20
        ),
        name="rear",
    )(
        *operands,
        jnp.asarray(SHARE, bf16),
    )


def on_device(
    inputs,
    segment_ids,
    norm1_gain,
    w_query,
    w_key,
    w_value,
    query_bias,
    value_bias,
    w_out,
    out_bias,
    norm2_gain,
    w_hidden,
    hidden_bias,
    w_proj,
    proj_bias,
    dim_scale,
    cotangent,
):
    blk = lax.axis_index("blk")
    head = lax.axis_index("head")
    at = (blk * 8 + head) * 10
    spread_heads = jnp.zeros((H, LANES), bf16)
    biases = jnp.concatenate([query_bias, jnp.zeros((HD - 10,), bf16), value_bias])
    spread_heads = lax.dynamic_update_slice(spread_heads, biases[None], (blk, HD + head * 10))
    natural = jnp.stack([norm1_gain, out_bias, norm2_gain, hidden_bias, proj_bias])
    natural = lax.dynamic_update_slice(jnp.zeros((5, 3 * MINE), bf16), natural, (0, at))
    columns = jnp.concatenate(
        [w.reshape(10, H, HD) for w in (w_key, w_query, w_value)]
        + [jnp.zeros((10, H, LANES - 3 * HD), bf16)],
        axis=2,
    )
    columns = columns.reshape(10, 8, MINE).transpose(1, 0, 2)
    pieces = jnp.concatenate(
        [
            columns,
            jnp.zeros((8, 6, MINE), bf16),
            spread_heads.reshape(8, 1, MINE),
            jnp.broadcast_to(natural.reshape(1, 15, MINE), (8, 15, MINE)),
        ],
        axis=1,
    )
    softplus_scale = LOG2E / math.sqrt(HD) * jax.nn.softplus(dim_scale)
    ones = jnp.ones((HD,), f32)
    scale_row = jnp.concatenate(
        [ones, softplus_scale, ones, jnp.zeros((LANES - 3 * HD,), f32)] * 2
    )
    scale_row = scale_row[None]

    (
        ring_normed, packed, wide_w, vectors, starts, kv, queries, out_t, log_norms, attended,
        out_w, hidden_w, proj_w,
    ) = front(
        inputs, pieces, w_out, w_hidden, w_proj, scale_row, segment_ids.reshape(2, 16, B)
    )
    out_b, gain_two, hidden_b, proj_b = [vectors[i] for i in range(1, 5)]

    tokens = inputs.reshape(2 * TOK, D).astype(f32)
    residual = tokens + nn(attended, out_w) + out_b
    inverse_two = inverse_rms(residual)
    normed_two = (residual * inverse_two * gain_two).astype(bf16)
    pre_act = nn(normed_two, hidden_w) + hidden_b
    gate = jax.nn.sigmoid(pre_act)
    activated = (pre_act * gate).astype(bf16)
    layer_out = (residual + nn(activated, proj_w) + proj_b).astype(bf16)

    upstream_low = cotangent.reshape(2 * TOK, D)
    upstream = upstream_low.astype(f32)
    d_pre = (nt(upstream_low, proj_w) * gate * (1.0 + pre_act * (1.0 - gate))).astype(bf16)
    d_normed_two = nt(d_pre, hidden_w)
    d_residual = upstream + norm_back(d_normed_two * gain_two, residual, inverse_two)
    d_branch = d_residual.astype(bf16)
    d_attended = nt(d_branch, out_w).astype(bf16)

    def total(values):
        return jnp.sum(values.astype(f32), axis=0)

    vector_grads = jnp.stack(
        [
            total(d_branch),
            total(d_normed_two * residual * inverse_two),
            total(d_pre),
            total(upstream),
        ]
    )
    vector_grads = jnp.pad(vector_grads, ((0, 0), (0, 3 * MINE - D))).reshape(12, MINE)
    vector_grads = jnp.pad(vector_grads, ((4, 0), (0, 0)))
    input_grad, shares, two = rear(
        d_attended, kv.reshape(16 * B, LANES), queries, starts, out_t, log_norms,
        attended, d_branch, normed_two, d_pre, activated, upstream_low,
        ring_normed.reshape(4 * D, 256), packed, wide_w, vector_grads, scale_row,
        inputs, vectors,
    )
    shares = shares.astype(f32)
    columns = shares[:, :10].transpose(1, 0, 2).reshape(10, H, LANES)
    d_key_w, d_query_w, d_value_w = [
        columns[:, :, i * HD : (i + 1) * HD].reshape(10, D) for i in range(3)
    ]
    by_head = shares[:, 16].reshape(H, LANES)
    d_query_bias, d_value_bias = [
        lax.dynamic_slice(by_head, (blk, i * HD + head * 10), (1, 10)).reshape(10) for i in (1, 2)
    ]
    summed = jnp.sum(shares[:, 17:], axis=0)
    scale_grad = summed[0, HD : 2 * HD] / softplus_scale
    scale_grad = scale_grad * (LOG2E / math.sqrt(HD)) * jax.nn.sigmoid(dim_scale)
    natural = lax.dynamic_slice(summed.reshape(5, 3 * MINE), (0, at), (5, 10))
    norm1_gain_grad = sum(
        jnp.sum(w.astype(f32) * grad, axis=1)
        for w, grad in ((w_query, d_query_w), (w_key, d_key_w), (w_value, d_value_w))
    ) / norm1_gain.astype(f32)
    return (
        layer_out.reshape(2, TOK, D),
        input_grad,
        norm1_gain_grad,
        d_query_w,
        d_key_w,
        d_value_w,
        d_query_bias,
        d_value_bias,
        two[0:10],
        natural[1],
        natural[2],
        two[10:20],
        natural[3],
        two[20:30],
        natural[4],
        scale_grad,
    )


def solution(mesh):
    rows = P(("blk", "head"), None)
    vec = P(("blk", "head"))
    tok = P(None, ("blk", "head"), None)
    in_specs = (
        tok, P(), vec, rows, rows, rows, vec, vec, rows, vec, vec, rows, vec, rows, vec, P(), tok
    )
    out_specs = (
        tok, tok, vec, rows, rows, rows, vec, vec, rows, vec, vec, rows, vec, rows, vec, P()
    )
    return jax.shard_map(
        on_device, mesh=mesh, in_specs=in_specs, out_specs=out_specs, check_vma=False
    )
```

```python
import functools
import math

import jax
import jax.numpy as jnp
import numpy as np
from jax import lax
from jax.experimental import pallas as pl
from jax.experimental.pallas import tpu as pltpu
from jax.sharding import PartitionSpec as P

D = 1280
H = 16
HD = 80
FF = 1280
B = 512
TOK = 64
PAIRS = 32
LANES = 256
ROWS = 32
WIDE = H * LANES
OUT_WIDE = H * 128
GROUP = 80
CHUNK = 96
MINE = 512
EPSILON = 1e-06
LOG2E = 1.442695041
NEGATIVE = -1e30
MESH = pl.DeviceIdType.MESH
f32 = jnp.float32
bf16 = jnp.bfloat16

PARTS = (((0, 384), "xyz"), ((384, 512), "yzx"), ((896, 384), "zxy"))
PARTS_BACK = (((0, 512), "xyz"), ((512, 512), "xzy"), ((1024, 256), "yzx"))


def inverse_rms(values):
    return lax.rsqrt(jnp.mean(values * values, axis=-1, keepdims=True) + EPSILON)


def norm_back(upstream, values, inverse):
    return inverse * upstream - values * inverse**3 * jnp.mean(
        upstream * values, axis=-1, keepdims=True
    )


def nn(a, b):
    return lax.dot_general(a, b, (((1,), (0,)), ((), ())), preferred_element_type=f32)


def nt(a, b):
    return lax.dot_general(a, b, (((1,), (1,)), ((), ())), preferred_element_type=f32)


def tn(a, b):
    return lax.dot_general(a, b, (((0,), (0,)), ((), ())), preferred_element_type=f32)


def my_place():
    blk = lax.axis_index("blk")
    head = lax.axis_index("head")
    return {
        "x": (head % 2) * 2 + (blk // 2) % 2,
        "y": head // 2,
        "z": blk // 4,
        "c": blk % 2,
    }


def device_at(place):
    x, y, z, c = place["x"], place["y"], place["z"], place["c"]
    return (z * 4 + (x % 2) * 2 + c, y * 2 + x // 2)


def span(place, free, core=True):
    x, y, z = place["x"], place["y"], place["z"]
    whole = slice(None)
    at = [
        whole if "z" in free else z,
        whole if "x" in free else x % 2,
        place["c"],
        whole if "y" in free else y,
        whole if "x" in free else x // 2,
    ]
    return tuple(at if core else at[:2] + at[3:])


def moved(place, axis, value):
    other = dict(place)
    other[axis] = value
    return other


def greet(peers):
    barrier = pltpu.get_barrier_semaphore()
    for peer in peers:
        pl.semaphore_signal(barrier, inc=1, device_id=peer, device_id_type=MESH)
    pl.semaphore_wait(barrier, len(peers))


def greet_all():
    barrier = pltpu.get_barrier_semaphore()
    blk = lax.axis_index("blk")
    head = lax.axis_index("head")
    heads = [(head + h) % 8 for h in range(8)]
    for h in range(1, 8):
        pl.semaphore_signal(barrier, inc=1, device_id=(blk, heads[h]), device_id_type=MESH)

    @pl.loop(1, 16)
    def _(b):
        other = (blk + b) % 16
        for h in range(8):
            pl.semaphore_signal(barrier, inc=1, device_id=(other, heads[h]), device_id_type=MESH)

    pl.semaphore_wait(barrier, 127)


def ring_peers(place):
    peers = [device_at(moved(place, "c", 1 - place["c"]))]
    for axis in "xyz":
        for step in (1, 3, 2):
            peers.append(device_at(moved(place, axis, (place[axis] + step) % 4)))
    return peers


def wait_bytes(ref, sem):
    pltpu.make_async_copy(ref, ref, sem).wait()


def remote(src, dst, send, recv, device):
    return pltpu.make_async_remote_copy(
        src_ref=src, dst_ref=dst, send_sem=send, recv_sem=recv, device_id=device, device_id_type=MESH
    )


def varied(place, axes, number):
    other = dict(place)
    for axis in axes:
        other[axis] = number % 4
        number = number // 4
    return other


def selections():
    join = np.zeros((CHUNK, 256), np.float32)
    for i in range(8):
        for j in range(10):
            join[i * 10 + j, i * ROWS + j] = 1
        for v in range(16):
            join[GROUP + v, i * ROWS + 16 + v] = 1
    return join, join.T.copy()


JOIN, SHARE = selections()


def rows_of(values, size, starts):
    return jnp.concatenate([values[at : at + size] for at in starts], axis=0)


def row_block(ref, g, count):
    return ref.at[pl.ds(pl.multiple_of(g * count, 16), count)]


class Gather:
    def __init__(self, buf, send, recv, place):
        self.place = place
        self.buf, self.send, self.recv = buf, send, recv
        self.sibling = device_at(moved(place, "c", 1 - place["c"]))

    def begin(self, matrices):
        spare = jnp.zeros((2, D), f32)
        own = [matrix[...].astype(f32) for matrix in matrices] + [spare]
        self.buf[span(self.place, "")] = jnp.concatenate(own, axis=0).astype(bf16)

    def piece(self, part, where, free):
        first, width = PARTS[part][0]
        return self.buf.at[(*span(where, free), slice(None), pl.ds(first, width))]

    def pieces(self, part, count):
        cols = pl.ds(*PARTS[part][0])
        whole = slice(None)
        at = {
            3: (pl.ds(0, 3), 0, 0, 0, 0),
            12: (pl.ds(0, 3), 0, 0, whole, 0),
            16: (0, whole, 0, whole, whole),
            48: (pl.ds(0, 3), whole, 0, whole, whole),
            64: (whole, whole, 0, whole, whole),
        }[count]
        return self.buf.at[(*at, whole, cols)]

    def forward(self, part, where, free):
        piece = self.piece(part, where, free)
        remote(piece, piece, self.send.at[part, 3], self.recv.at[part, 5], self.sibling).start()

    def stage(self, stage):
        for part, (_, order) in enumerate(PARTS):
            if stage:
                wait_bytes(self.pieces(part, 3 * 4 ** (stage - 1)), self.recv.at[part, stage - 1])
            piece = self.piece(part, self.place, order[:stage])
            axis = order[stage]
            for step in (1, 3, 2) if stage < 2 else (1, 3):
                target = moved(self.place, axis, (self.place[axis] + step) % 4)
                slot = stage if stage < 2 else 1 + step
                remote(
                    piece,
                    piece,
                    self.send.at[part, stage],
                    self.recv.at[part, slot],
                    device_at(target),
                ).start()
        for part, (_, order) in enumerate(PARTS):
            if stage == 0:
                self.forward(part, self.place, "")
            else:
                axis = order[stage - 1]
                for step in (1, 3, 2):
                    there = moved(self.place, axis, (self.place[axis] + 4 - step) % 4)
                    self.forward(part, there, order[: stage - 1])

    def relay(self):
        for part, ((first, width), order) in enumerate(PARTS):
            axis, halved = order[2], order[1]
            here = self.place[axis]
            for step in (1, 3):
                wait_bytes(self.pieces(part, 16), self.recv.at[part, 1 + step])
                there = moved(self.place, axis, (here + 4 - step) % 4)
                at = list(span(there, order[:2]))
                half = step // 2
                if halved == "x":
                    at[4] = half
                else:
                    at[0 if halved == "z" else 3] = pl.ds(half * 2, 2)
                piece = self.buf.at[(*at, slice(None), pl.ds(first, width))]
                target = device_at(moved(self.place, axis, (here + step) % 4))
                remote(
                    piece, piece, self.send.at[part, 2], self.recv.at[part, 3], target
                ).start()
                self.forward(part, there, order[:2])

    def finish(self):
        for part, (_, order) in enumerate(PARTS):
            wait_bytes(self.pieces(part, 16), self.recv.at[part, 3])
            axis = order[2]
            there = moved(self.place, axis, (self.place[axis] + 2) % 4)
            self.forward(part, there, order[:2])
        for part in range(3):
            wait_bytes(self.pieces(part, 64), self.recv.at[part, 5])
            wait_bytes(self.pieces(part, 64), self.send.at[part, 3])
            wait_bytes(self.pieces(part, 3), self.send.at[part, 0])
            wait_bytes(self.pieces(part, 12), self.send.at[part, 1])
            wait_bytes(self.pieces(part, 48), self.send.at[part, 2])


VMEM = pl.BlockSpec(memory_space=pltpu.VMEM)
HBM = pl.BlockSpec(memory_space=pl.ANY)


def unpack(buf, staged, out_w, hidden_w, proj_w, out_sem):
    spans = ((0, 128, out_w), (128, GROUP, hidden_w), (208, GROUP, proj_w))
    staged[:, 0:32] = jnp.zeros((2, 32, D), bf16)
    staged[:, 112:128] = jnp.zeros((2, 16, D), bf16)

    @pl.loop(0, 16)
    def _(g):
        slot = g % 2
        outs = [
            pltpu.make_async_copy(
                staged.at[slot, pl.ds(at, count)], row_block(ref, g, count), out_sem.at[i, slot]
            )
            for i, (at, count, ref) in enumerate(spans)
        ]

        @pl.when(g >= 2)
        def _():
            for out in outs:
                out.wait()

        packed = buf[g // 4, (g // 2) % 2, g % 2].reshape(256, D).astype(f32)
        for w, at in enumerate((32, 128, 208)):
            rows = rows_of(packed, 10, range(w * 10, 256, ROWS))
            staged[slot, at : at + GROUP] = rows.astype(bf16)
        for out in outs:
            out.start()

    for slot in range(2):
        for i, (at, count, ref) in enumerate(spans):
            pltpu.make_async_copy(
                staged.at[slot, pl.ds(at, count)], row_block(ref, 0, count), out_sem.at[i, slot]
            ).wait()


class Scatter:
    def __init__(self, away, mine, pair, lands, halves, send, recv, place):
        self.away, self.mine, self.pair = away, mine, pair
        self.lands, self.halves = lands, halves
        self.send, self.recv, self.place = send, recv, place
        self.sibling = device_at(moved(place, "c", 1 - place["c"]))

    def swap(self, number):
        at = (number // 2, number % 2)
        sems = (len(PARTS_BACK), number)
        return remote(
            self.away.at[at], self.pair.at[at], self.send.at[sems], self.recv.at[sems], self.sibling
        )

    def add_pair(self, number):
        self.swap(number).wait()
        at = (number // 2, number % 2)
        self.mine[at] = (self.mine[at].astype(f32) + self.pair[at].astype(f32)).astype(bf16)

    def source(self, part, stage, where):
        (first, width), order = PARTS_BACK[part]
        if stage == 0:
            at = span(where, order[:2], core=False)
            return self.mine.at[(*at, slice(None), pl.ds(first, width))]
        at = [
            slice(None) if axis in order[: 2 - stage] else value
            for axis, value in zip("zxyx", span(where, "", core=False))
            if axis in order[: 3 - stage]
        ]
        return self.halves[stage - 1][part].at[tuple(at)]

    def start(self, stage):
        for part, (_, order) in enumerate(PARTS_BACK):
            axis = order[2 - stage]
            for step in (1, 3, 2):
                target = moved(self.place, axis, (self.place[axis] + step) % 4)
                remote(
                    self.source(part, stage, target),
                    self.lands[stage][part].at[step - 1],
                    self.send.at[part, stage],
                    self.recv.at[part, stage],
                    device_at(target),
                ).start()

    def add(self, stage, out=None):
        for part, ((first, width), order) in enumerate(PARTS_BACK):
            land = self.lands[stage][part]
            wait_bytes(land, self.recv.at[part, stage])
            own = self.source(part, stage, self.place)
            lead = land.shape[1:-2]

            @pl.loop(0, math.prod(lead))
            def _(number):
                at = []
                for size in reversed(lead):
                    at.insert(0, number % size)
                    number = number // size
                at = tuple(at)
                total = own[at].astype(f32)
                for source in range(3):
                    total = total + land[(source, *at)].astype(f32)
                if stage < 2:
                    self.halves[stage][part][at] = total.astype(bf16)
                else:
                    out[:, first : first + width] = total

    def finish(self):
        for stage in range(3):
            for part in range(len(PARTS_BACK)):
                wait_bytes(self.lands[stage][part], self.send.at[part, stage])


def lead_of(axes):
    sizes = {"z": (4,), "x": (2, 2), "y": (4,)}
    if axes == {"x", "y"}:
        return (2, 4, 2)
    if axes == {"x", "z"}:
        return (4, 2, 2)
    return sum((sizes[axis] for axis in "zyx" if axis in axes), ())


def scatter_scratch():
    whole = pltpu.VMEM((4, 2, 4, 2, ROWS, D), bf16)
    lands, halves = [], []
    for stage in range(3):
        for (_, width), order in PARTS_BACK:
            lead = lead_of(set(order[: 2 - stage]))
            lands.append(pltpu.VMEM((3, *lead, ROWS, width), bf16))
            if stage < 2:
                halves.append(pltpu.VMEM((*lead, ROWS, width), bf16))
    semaphores = [pltpu.SemaphoreType.DMA((4, 8))] * 2
    return [whole] * 3 + lands + halves + semaphores


def scatter_of(scratch, place):
    away, mine, pair = scratch[:3]
    parts = len(PARTS_BACK)
    lands = [scratch[3 + parts * stage : 3 + parts * (stage + 1)] for stage in range(3)]
    halves = [scratch[3 + parts * stage : 3 + parts * (stage + 1)] for stage in (3, 4)]
    return Scatter(away, mine, pair, lands, halves, scratch[-2], scratch[-1], place)


HALVES = ((0, "yz"), (256, "zy"))


def ring_devices(place):
    others = [moved(place, "c", 1 - place["c"])]
    for step in (1, 3, 2):
        there = moved(place, "x", (place["x"] + step) % 4)
        others += [there, moved(there, "c", 1 - place["c"])]
    return others


def ring_number(place):
    return (place["x"] % 2) * 4 + place["c"] * 2 + place["x"] // 2


def tokens_of(ref, place):
    inner = (place["x"] % 2) * 2 + place["c"]
    return ref.at[inner, :, pl.ds((place["x"] // 2) * TOK, TOK)]


def head_of(place):
    return (place["x"] // 2) * 8 + (place["z"] % 2) * 4 + place["y"]


def pair_device(pair, quarter):
    micro, h = pair // H, pair % H
    return ((micro * 2 + (h % 8) // 4) * 4 + quarter, (h % 4) * 2 + h // 8)


def column_pieces(buf, half, place, free):
    at = [slice(None) if axis in free else place[axis] for axis in "zy"]
    return buf.at[(*at, slice(None), pl.ds(HALVES[half][0], 256))]


def gather_columns(buf, send, recv, place, stage):
    for half, (first, order) in enumerate(HALVES):
        axis = order[stage]
        if stage:
            wait_bytes(buf.at[0, pl.ds(0, 3), :, pl.ds(first, 256)], recv.at[half, 0])
        piece = column_pieces(buf, half, place, order[:stage])
        for step in (1, 3, 2):
            target = moved(place, axis, (place[axis] + step) % 4)
            remote(
                piece, piece, send.at[half, stage], recv.at[half, stage], device_at(target)
            ).start()


def finish_columns(buf, send, recv):
    for half, (first, _) in enumerate(HALVES):
        cols = pl.ds(first, 256)
        wait_bytes(buf.at[pl.ds(0, 3), :, :, cols], recv.at[half, 1])
        wait_bytes(buf.at[0, pl.ds(0, 3), :, cols], send.at[half, 0])
        wait_bytes(buf.at[pl.ds(0, 3), :, :, cols], send.at[half, 1])


def quarter_of(blk):
    inner = blk % 4
    return jnp.where((blk // 4) % 2 == 0, inner, 3 - inner)


def query_block(quarter, j):
    return j * 4 + jnp.where(j % 2 == 0, quarter, 3 - quarter)


def cell_of(ref, pair, width):
    return ref.at[pl.ds(pair // H * TOK, TOK), pl.ds(pair % H * width, width)]


def mask_of(key_block, block, start):
    key_at = key_block * B + lax.broadcasted_iota(jnp.int32, (B, B), 0)
    query_at = block * B + lax.broadcasted_iota(jnp.int32, (B, B), 1)
    return (key_at >= start) & (key_at <= query_at)


def has_mask(key_block, block):
    return (key_block == 0) | (key_block == block) | (block == 15)


def shift_matrix(rows, cols, by):
    row = lax.broadcasted_iota(jnp.int32, (rows, cols), 0)
    col = lax.broadcasted_iota(jnp.int32, (rows, cols), 1)
    return jnp.where((row - col == by) & (jnp.minimum(row, col) < HD), 1.0, 0.0).astype(bf16)


def wait_cells(ref, sem, fewer, width):
    wait_bytes(ref.at[:, pl.ds(0, 15 * width)], sem)
    wait_bytes(cell_of(ref, 0, width), sem)

    @pl.when(jnp.logical_not(fewer))
    def _():
        wait_bytes(cell_of(ref, 0, width), sem)


def stays_here(place):
    return (place["z"] % 2 == place["x"] % 2) & (place["y"] // 2 == place["c"])


def wait_ring(ref, sem, place):
    wait_bytes(ref.at[pl.ds(0, 3)], sem)
    wait_bytes(ref.at[0, pl.ds(0, 384)], sem)

    @pl.when(jnp.logical_not(stays_here(place)))
    def _():
        wait_bytes(ref.at[0, pl.ds(0, 128)], sem)


def front_kernel(
    tokens, pieces, w_out, w_hidden, w_proj, scale_row, segments, join,
    normed_hbm, packed_hbm, wide_hbm, vectors, starts, kv_out, queries, out_t, log_norms, attended,
    out_w, hidden_w, proj_w,
    normed_out, normed_t, packed_out, wide_w, keep_sems, ring_tokens, ring_pieces, chunks, kv, value_t, tops, totals, rounded, landed, buf, staged,
    x_tok_send, x_tok_recv, c_tok_send, c_tok_recv, piece_send, piece_recv, col_send, col_recv,
    two_send, two_recv, own_sem, send, recv, core_send, core_recv, x_send, x_recv,
    pass_send, pass_recv, back_send, back_recv, kv_sem, out_sem,
):
    blk = lax.axis_index("blk")
    head = lax.axis_index("head")
    core = blk % 2
    x_low = (blk // 2) % 2
    quarter = blk % 4
    even = (blk // 4) % 2 == 0
    place = my_place()
    pair = (place["z"] // 2) * H + head_of(place)
    turn = place["x"] * 2 + core
    sibling = (blk + 1 - 2 * core, head)
    two = Gather(buf, two_send, two_recv, place)
    own_tokens = pltpu.make_async_copy(tokens, tokens_of(ring_tokens, place), own_sem)
    own_tokens.start()
    number = ring_number(place)
    pltpu.make_async_copy(pieces.at[turn], ring_pieces.at[number], piece_recv).start()
    greet_all()
    for there in ring_devices(place):
        remote(
            pieces.at[there["x"] * 2 + there["c"]],
            ring_pieces.at[number],
            piece_send,
            piece_recv,
            device_at(there),
        ).start()
    mine = tokens_of(ring_tokens, place)
    for step in (1, 3, 2):
        there = moved(place, "x", (place["x"] + step) % 4)
        remote(
            tokens, mine, x_tok_send.at[step - 1], x_tok_recv.at[step - 1], device_at(there)
        ).start()
    remote(tokens, mine, c_tok_send, c_tok_recv, sibling).start()
    two.begin((w_out, w_hidden, w_proj))
    two.stage(0)
    ids = segments[place["z"] // 2]
    before = [jnp.sum((ids < value).astype(jnp.int32)) for value in range(1, 9)]
    for j in range(4):
        row = segments[place["z"] // 2, pl.ds(query_block(quarter, j), 1)]
        start = jnp.zeros_like(row)
        for value in range(1, 9):
            start = jnp.where(row == value, before[value - 1], start)
        starts[j] = start
    wait_bytes(ring_pieces, piece_recv)
    joined = nn(join[...], ring_pieces[...].reshape(256, MINE)).astype(bf16)
    chunks[place["z"], place["y"]] = joined
    gather_columns(chunks, col_send, col_recv, place, 0)
    gather_columns(chunks, col_send, col_recv, place, 1)
    for step in (1, 3, 2):
        wait_bytes(tokens, x_tok_recv.at[step - 1])
        there = moved(place, "x", (place["x"] + 4 - step) % 4)
        arrived = tokens_of(ring_tokens, there)
        remote(arrived, arrived, c_tok_send, c_tok_recv, sibling).start()
    own_tokens.wait()
    finish_columns(chunks, col_send, col_recv)

    @pl.loop(0, 4)
    def _(z):
        rows = pl.ds(pl.multiple_of(z * 4 * GROUP, 64), 4 * GROUP)
        found = chunks[z].reshape(4 * CHUNK, MINE).astype(f32)
        starts_at = [y * CHUNK + inner * 20 for inner in range(4) for y in range(4)]
        wide_w[rows] = rows_of(found, 20, starts_at).astype(bf16)

    vector_rows = jnp.zeros((16, MINE), f32)
    for z in range(4):
        for y in range(4):
            vector_rows = vector_rows + chunks[z, y, GROUP:].astype(f32)
    for i in range(5):
        three = [vector_rows[1 + 3 * i + k : 2 + 3 * i + k] for k in range(3)]
        vectors[i : i + 1] = jnp.concatenate(three[:2] + [three[2][:, :256]], axis=1)
    bias = vector_rows[0:1]
    gain = vectors[0:1]
    one_lane = jnp.where(
        lax.broadcasted_iota(jnp.int32, (1, MINE), 1) % LANES == 3 * HD, 1.0, 0.0
    )
    wait_bytes(ring_tokens.at[pl.ds(0, 2)], c_tok_recv)

    def deliver(inner, aside, send, recv):
        block = place["z"] * 4 + inner
        to_quarter = (quarter_of(block) + aside) % 4
        for m in range(2):
            for h in range(2):
                blk_to, head_to = pair_device(m * H + turn * 2 + h, to_quarter)
                src = packed_out.at[inner, m, :, pl.ds(h * LANES, LANES)]
                dst = kv.at[block, pl.ds(place["y"] * 128, 128)]
                stays = (blk_to == blk) & (head_to == head)

                @pl.when(stays)
                def _():
                    pltpu.make_async_copy(src, dst, recv).start()

                @pl.when(jnp.logical_not(stays))
                def _():
                    remote(src, dst, send, recv, (blk_to, head_to)).start()

    @pl.loop(0, 4)
    def _(inner):
        values = ring_tokens[inner].reshape(256, D).astype(f32)
        normed = (values * inverse_rms(values) * gain).astype(bf16)
        normed_out[inner] = normed
        full = nn(normed, wide_w[...])
        packed = ((full + bias) * scale_row[0:1] + one_lane).astype(bf16)
        packed_out[inner] = packed.reshape(2, 128, MINE)
        deliver(inner, 0, send, recv)

    @pl.loop(0, 4)
    def _(inner):
        deliver(inner, 2, x_send, x_recv)

    two.stage(1)

    @pl.loop(0, 4)
    def _(inner):
        @pl.loop(0, D // 128)
        def _(n):
            lanes = pl.ds(pl.multiple_of(n * 128, 128), 128)
            normed_t[inner, lanes] = normed_out[inner, :, lanes].T

    keeps = [
        pltpu.make_async_copy(ref, out, keep_sems.at[i])
        for i, (ref, out) in enumerate(
            ((normed_t, normed_hbm), (packed_out, packed_hbm), (wide_w, wide_hbm))
        )
    ]
    for keep in keeps:
        keep.start()
    wait_bytes(kv.at[pl.ds(0, 4)], recv)

    @pl.loop(0, 4)
    def _(j):
        block = kv.at[query_block(quarter, j)]
        remote(block, block, core_send, core_recv, sibling).start()

    pick = shift_matrix(LANES, 128, HD)

    @pl.loop(0, 4)
    def _(j):
        queries[j] = nn(kv[query_block(quarter, j)], pick).astype(bf16)
        tops[j] = jnp.full((1, B), NEGATIVE, f32)
        totals[j] = jnp.zeros((1, B), f32)
        out_t[j] = jnp.zeros((128, B), f32)


    def step(j, block, key_blocks):
        def tiles(masked):
            scores = []
            for key_block in key_blocks:
                s = nt(kv[key_block, :, :128], queries[j])
                if masked:
                    s = jnp.where(mask_of(key_block, block, starts[j]), s, NEGATIVE)
                scores.append(s)
            top = tops[j]
            new_top = top
            for s in scores:
                new_top = jnp.maximum(new_top, jnp.max(s, axis=0, keepdims=True))
            scale = jnp.exp(top - new_top)
            total = totals[j] * scale
            acc = out_t[j] * scale
            for key_block, s in zip(key_blocks, scores):
                p = jnp.exp(s - new_top)
                total = total + jnp.sum(p, axis=0, keepdims=True)
                acc = acc + nn(value_t[key_block], p.astype(bf16))
            tops[j] = new_top
            totals[j] = total
            out_t[j] = acc

        masked = has_mask(key_blocks[0], block)
        for key_block in key_blocks[1:]:
            masked = masked | has_mask(key_block, block)
        pl.when(masked)(lambda: tiles(True))
        pl.when(jnp.logical_not(masked))(lambda: tiles(False))

    def key_pass(j, of_quarter, count):
        block = query_block(quarter, j)

        @pl.when(count == 4)
        def _():
            step(j, block, tuple(query_block(of_quarter, n) for n in range(4)))

        @pl.loop(0, jnp.where(count == 4, 0, count // 2))
        def _(n):
            last = count - 1 - 2 * n
            step(j, block, (query_block(of_quarter, last), query_block(of_quarter, last - 1)))

        @pl.when(count % 2 == 1)
        def _():
            step(j, block, (query_block(of_quarter, 0),))

    def give(j, block):
        acc = out_t[j]
        result = acc / acc[112:113]
        out_t[j] = result
        log_norms[j] = tops[j] + jnp.log(totals[j])
        rounded[j] = result.T.astype(bf16)

        @pl.loop(0, 8)
        def _(k):
            h = (head + k) % 8
            src = rounded.at[j, pl.ds(h * TOK, TOK)]
            dst = cell_of(landed, pair, 128)
            mine = (k == 0) & (block == blk)

            @pl.when(mine)
            def _():
                pltpu.make_async_copy(src, dst, back_recv).start()

            @pl.when(jnp.logical_not(mine))
            def _():
                remote(src, dst, back_send, back_recv, (block, h)).start()

    keep_kv = pltpu.make_async_copy(kv, kv_out, kv_sem)

    @pl.loop(0, 4)
    def _(turn_at):
        of_quarter = (quarter + 2 * (turn_at // 2)) % 4 + (turn_at % 2) * (1 - 2 * core)

        @pl.when(turn_at == 1)
        def _():
            two.stage(2)
            wait_bytes(kv.at[pl.ds(0, 4)], core_recv)

        @pl.when(turn_at == 2)
        def _():
            wait_bytes(kv.at[pl.ds(0, 4)], x_recv)

            @pl.loop(0, 4)
            def _(j):
                block = kv.at[query_block(of_quarter, j)]
                remote(block, block, pass_send, pass_recv, sibling).start()

        @pl.when(turn_at == 3)
        def _():
            two.relay()
            wait_bytes(kv.at[pl.ds(0, 4)], pass_recv)
            keep_kv.start()

        @pl.loop(0, 4)
        def _(j):
            b = query_block(of_quarter, j)
            value_t[b] = kv[b, :, 128:].T

        @pl.loop(0, 4)
        def _(i):
            j = 3 - i
            block = query_block(quarter, j)
            more = jnp.where(
                turn_at == 0, 1, jnp.where(turn_at == 1, block % 2, (j + x_low) % 2)
            )
            key_pass(j, of_quarter, j + more)
            pl.when(turn_at == 3)(lambda: give(j, block))

    two.finish()
    unpack(buf, staged, out_w, hidden_w, proj_w, out_sem)
    wait_bytes(landed, back_recv)
    attended[...] = landed[...]
    for keep in keeps + [keep_kv]:
        keep.wait()
    for sem in (core_send, pass_send):
        wait_bytes(kv.at[pl.ds(0, 4)], sem)
    wait_cells(landed, back_send, even, 128)
    wait_bytes(ring_pieces.at[pl.ds(0, 7)], piece_send)
    for step_at in range(3):
        wait_bytes(tokens, x_tok_send.at[step_at])
    wait_bytes(ring_tokens.at[pl.ds(0, 2)], c_tok_send)
    wait_ring(kv, send, place)
    wait_ring(kv, x_send, place)


def front(*operands):
    dma = pltpu.SemaphoreType.DMA
    return pl.pallas_call(
        front_kernel,
        out_shape=(
            jax.ShapeDtypeStruct((4, D, 256), bf16),
            jax.ShapeDtypeStruct((4, 2, 128, MINE), bf16),
            jax.ShapeDtypeStruct((D, MINE), bf16),
            jax.ShapeDtypeStruct((8, D), f32),
            jax.ShapeDtypeStruct((4, 1, B), jnp.int32),
            jax.ShapeDtypeStruct((16, B, LANES), bf16),
            jax.ShapeDtypeStruct((4, B, 128), bf16),
            jax.ShapeDtypeStruct((4, 128, B), f32),
            jax.ShapeDtypeStruct((4, 1, B), f32),
            jax.ShapeDtypeStruct((2 * TOK, OUT_WIDE), bf16),
            jax.ShapeDtypeStruct((OUT_WIDE, D), bf16),
            jax.ShapeDtypeStruct((D, D), bf16),
            jax.ShapeDtypeStruct((D, D), bf16),
        ),
        in_specs=[VMEM] * 8,
        out_specs=(HBM,) * 3 + (VMEM,) * 2 + (HBM,) + (VMEM,) * 4 + (HBM,) * 3,
        scratch_shapes=[
            pltpu.VMEM((4, 256, D), bf16),
            pltpu.VMEM((4, D, 256), bf16),
            pltpu.VMEM((4, 2, 128, MINE), bf16),
            pltpu.VMEM((D, MINE), bf16),
            dma((3,)),
            pltpu.VMEM((4, 2, 128, D), bf16),
            pltpu.VMEM((8, ROWS, MINE), bf16),
            pltpu.VMEM((4, 4, CHUNK, MINE), bf16),
            pltpu.VMEM((16, B, LANES), bf16),
            pltpu.VMEM((16, 128, B), bf16),
            pltpu.VMEM((4, 1, B), f32),
            pltpu.VMEM((4, 1, B), f32),
            pltpu.VMEM((4, B, 128), bf16),
            pltpu.VMEM((2 * TOK, OUT_WIDE), bf16),
            pltpu.VMEM((4, 2, 2, 4, 2, ROWS, D), bf16),
            pltpu.VMEM((2, 288, D), bf16),
            dma((3,)), dma((3,)), dma, dma, dma, dma, dma((2, 2)), dma((2, 2)),
            dma((3, 4)), dma((3, 6)), dma,
        ]
        + [dma] * 11
        + [dma((3, 2))],
        compiler_params=pltpu.CompilerParams(
            collective_id=0, has_side_effects=True, vmem_limit_bytes=56 * 2**20
        ),
        name="front",
    )(
        *operands,
        jnp.asarray(JOIN, bf16),
    )


def rear_kernel(
    pack, kv_hbm, queries_hbm, starts, out_t_hbm, log_norms,
    attended, d_branch, normed_two, d_pre, activated, upstream,
    normed_hbm, packed_hbm, wide_hbm, vector_grads, scale_row, tokens, vectors,
    share,
    input_grad, pieces_out, two_out,
    kv, queries, out_t, packed, wide_w, load_sems,
    d_out, key_t, deltas, d_query, d_kv, mine_kv, half, half_in, cross, cross_in, final, d_wide,
    attended_t, normed_two_t, activated_t,
    sum_in, grad_chunks, first_in, second_in, first_sum,
    joined, shares, shares_in,
    send, recv, core_send, core_recv, x_send, x_recv, back_send, back_recv,
    c_send, c_recv, sum_send, sum_recv, col_send, col_recv, share_send, share_recv,
    *scratch,
):
    blk = lax.axis_index("blk")
    head = lax.axis_index("head")
    core = blk % 2
    x_low = (blk // 2) % 2
    quarter = blk % 4
    place = my_place()
    my_head = head_of(place)
    pair = (place["z"] // 2) * H + my_head
    to_quarter = quarter_of(blk)
    even = (blk // 4) % 2 == 0
    two = scatter_of(scratch, place)
    loads = [
        pltpu.make_async_copy(src, dst, load_sems.at[i])
        for i, (src, dst) in enumerate(
            (
                (kv_hbm, kv),
                (queries_hbm, queries),
                (out_t_hbm, out_t),
                (packed_hbm, packed),
                (wide_hbm, wide_w),
            )
        )
    ]
    for load in loads:
        load.start()
    greet_all()

    @pl.loop(0, PAIRS)
    def _(k):
        p = (pair + k) % PAIRS
        src = cell_of(pack, p, 128)
        dst = d_out.at[blk // 4, pl.ds(head * TOK, TOK)]
        mine = (k == 0) & even

        @pl.when(mine)
        def _():
            pltpu.make_async_copy(src, dst, recv).start()

        @pl.when(jnp.logical_not(mine))
        def _():
            remote(src, dst, send, recv, pair_device(p, to_quarter)).start()


    @pl.loop(0, D // 128)
    def _(n):
        lanes = pl.ds(pl.multiple_of(n * 128, 128), 128)
        normed_two_t[lanes] = normed_two[:, lanes].T
        activated_t[lanes] = activated[:, lanes].T

    @pl.loop(0, H)
    def _(n):
        lanes = pl.ds(pl.multiple_of(n * 128, 128), 128)
        attended_t[lanes] = attended[:, lanes].T


    @pl.loop(0, 8)
    def _(number):
        rows = pl.ds(pl.multiple_of(number * 2 * GROUP, 32), 2 * GROUP)
        heads = [
            attended_t[pl.ds(pl.multiple_of((number * 2 + k) * 128 + 32, 32), GROUP)]
            for k in range(2)
        ]
        found = [
            nn(jnp.concatenate(heads, axis=0), d_branch[...]),
            nn(normed_two_t[rows], d_pre[...]),
            nn(activated_t[rows], upstream[...]),
        ]
        spare = jnp.zeros((2, D), f32)
        for k in range(2):
            block = jnp.concatenate(
                [
                    part
                    for i in range(8)
                    for part in [w[k * GROUP + i * 10 : k * GROUP + i * 10 + 10] for w in found]
                    + [spare]
                ],
                axis=0,
            )
            block = block.astype(bf16).reshape(4, 2, ROWS, D)

            @pl.when(core == k)
            def _():
                two.mine[number // 2, number % 2] = block

            @pl.when(core != k)
            def _():
                two.away[number // 2, number % 2] = block

        two.swap(number).start()

    for load in loads[:3]:
        load.wait()

    def keys_at(block, lane):
        return kv[pl.ds(pl.multiple_of(block * B, B), B), lane : lane + 128]

    @pl.loop(0, 16)
    def _(b):
        key_t[b] = keys_at(b, 0).T

    @pl.loop(0, 8)
    def _(number):
        two.add_pair(number)

    two.start(0)
    wait_bytes(d_out, recv)

    @pl.loop(0, 4)
    def _(j):
        deltas[j] = jnp.sum(d_out[j].astype(f32).T * out_t[j], axis=0, keepdims=True)
        d_query[j] = jnp.zeros((128, B), f32)

    sibling = (blk + 1 - 2 * core, head)

    def step(numbers, key_block):
        def tiles(masked):
            found = []
            for j in numbers:
                q = queries[j]
                do = d_out[j]
                p = jnp.exp(nt(keys_at(key_block, 0), q) - log_norms[j])
                if masked:
                    allowed = mask_of(key_block, query_block(quarter, j), starts[j])
                    p = jnp.where(allowed, p, 0.0)
                dp = nt(keys_at(key_block, 128), do)
                found.append((q, do, p.astype(bf16), (p * (dp - deltas[j])).astype(bf16)))
            d_kv[:, :128] += sum(nn(ds, q) for q, do, p, ds in found)
            d_kv[:, 128:] += sum(nn(p, do) for q, do, p, ds in found)
            for j, (q, do, p, ds) in zip(numbers, found):
                d_query[j] += nn(key_t[key_block], ds)

        masked = has_mask(key_block, query_block(quarter, numbers[0]))
        for j in numbers[1:]:
            masked = masked | has_mask(key_block, query_block(quarter, j))
        pl.when(masked)(lambda: tiles(True))
        pl.when(jnp.logical_not(masked))(lambda: tiles(False))

    def swap(n):
        return remote(
            half.at[n], half_in.at[n], core_send.at[n], core_recv.at[n], sibling
        )

    shift = shift_matrix(128, LANES, -HD)

    partner = (blk + 2 - 4 * x_low, head)

    def cross_swap(z):
        return remote(cross.at[z], cross_in.at[z], x_send.at[z], x_recv.at[z], partner)

    def core_sum(z):
        own = 2 * z + (x_low + z) % 2
        other = 4 * z + 1 - own
        swap(other).wait()
        cross[z] = (mine_kv[other] + half_in[other].astype(f32)).astype(bf16)
        cross_swap(z).start()
        swap(own).wait()
        mine_kv[own] = (
            mine_kv[own]
            + half_in[own].astype(f32)
            + nn(d_query[z].T.astype(bf16), shift)
        )

    def finish(z):
        cross_swap(z).wait()
        own = 2 * z + (x_low + z) % 2
        final[z] = (mine_kv[own] + cross_in[z].astype(f32)).astype(bf16)
        inner = query_block(quarter, z) % 4
        dst = d_wide.at[inner, place["z"] // 2, :, pl.ds((my_head % 2) * LANES, LANES)]

        @pl.loop(0, 4)
        def _(k):
            y = (place["y"] + k) % 4
            there = {"x": my_head // 4, "y": y, "z": z, "c": (my_head // 2) % 2}
            src = final.at[z, pl.ds(y * 128, 128)]
            blk_to, head_to = device_at(there)
            stays = (blk_to == blk) & (head_to == head)

            @pl.when(stays)
            def _():
                pltpu.make_async_copy(src, dst, back_recv).start()

            @pl.when(jnp.logical_not(stays))
            def _():
                remote(src, dst, back_send, back_recv, (blk_to, head_to)).start()

    load_normed = pltpu.make_async_copy(normed_hbm, kv.at[pl.ds(0, 4 * D)], load_sems.at[5])

    def key_steps(key_block):
        z = key_block // 4
        d_kv[...] = jnp.zeros((B, LANES), f32)
        first = z + (query_block(quarter, z) < key_block).astype(jnp.int32)

        @pl.when(first % 2 == 1)
        def _():
            step((first,), key_block)

        @pl.loop((first + 1) // 2, 2)
        def _(n):
            step((2 * n, 2 * n + 1), key_block)

        n = 2 * z + (key_block % 4) // 2

        @pl.when((key_block + z + core) % 2 == 0)
        def _():
            mine_kv[n] = d_kv[...]

        @pl.when((key_block + z + core) % 2 == 1)
        def _():
            half[n] = d_kv[...].astype(bf16)
            swap(n).start()

    @pl.loop(0, 10)
    def _(part):
        z = part // 2

        @pl.when(part < 8)
        def _():
            @pl.loop(2 * part, 2 * part + 2)
            def _(key_block):
                key_steps(key_block)

        @pl.when(part == 8)
        def _():
            load_normed.start()

        @pl.when((part % 2 == 0) & (part > 0))
        def _():
            core_sum(z - 1)

        @pl.when((part % 2 == 1) & (part > 1))
        def _():
            finish(z - 1)

        @pl.when(part == 6)
        def _():
            two.add(0)
            two.start(1)

    two.add(1)
    two.start(2)
    wait_bytes(d_wide, back_recv)

    for load in loads[3:]:
        load.wait()
    load_normed.wait()
    partial = two.away.at[:, 0]
    summed, partial_in = two.away.at[pl.ds(0, 2), 1], two.away.at[pl.ds(2, 2), 1]
    scale = scale_row[0:1]
    bias_sum = jnp.zeros((1, MINE), f32)
    scale_sum = jnp.zeros((1, MINE), f32)

    def scaled_grads(inner, sums):
        bias_sum, scale_sum = sums
        grad = d_wide[inner].reshape(256, MINE).astype(f32)
        scale_sum = scale_sum + jnp.sum(
            grad * packed[inner].reshape(256, MINE).astype(f32), axis=0, keepdims=True
        )
        grad = (grad * scale).astype(bf16)
        d_wide[inner] = grad.reshape(2, 128, MINE)
        return bias_sum + jnp.sum(grad.astype(f32), axis=0, keepdims=True), scale_sum

    bias_sum, scale_sum = lax.fori_loop(0, 4, scaled_grads, (bias_sum, scale_sum))
    scale_sum = scale_sum[:, :LANES] + scale_sum[:, LANES:]
    rows = vector_grads[...] + jnp.concatenate(
        [bias_sum, jnp.concatenate([scale_sum, scale_sum], axis=1), jnp.zeros((14, MINE), f32)],
        axis=0,
    )
    rows = rows.astype(bf16)
    sibling_at = (blk + 1 - 2 * core, head)
    c_swaps = [
        remote(
            partial.at[low * 2 + 1 - core],
            partial_in.at[low],
            c_send.at[low],
            c_recv.at[low],
            sibling_at,
        )
        for low in range(2)
    ]

    def token_grads(inner):
        back = nt(d_wide[inner].reshape(256, MINE), wide_w[...])
        partial[inner] = back.astype(bf16).reshape(4, 2, ROWS, D)

    @pl.loop(0, 2)
    def _(low):
        token_grads(low * 2 + 1 - core)

    for low in range(2):
        c_swaps[low].start()

    @pl.loop(0, 4)
    def _(z):
        def part(inner):
            at = pl.ds(pl.multiple_of(inner * D + z * 320, 64), 320)
            return nn(kv[at], d_wide[inner].reshape(256, MINE))

        grads = sum(part(inner) for inner in range(4))
        for y in range(4):
            found = rows_of(grads, 20, [inner * GROUP + y * 20 for inner in range(4)])
            grad_chunks[z, y, :GROUP] = found.astype(bf16)
            grad_chunks[z, y, GROUP:] = rows


    for step_at in (1, 3, 2):
        for half, axis in enumerate("zy"):
            there = moved(place, axis, (place[axis] + step_at) % 4)
            remote(
                column_pieces(grad_chunks, half, there, "y" if half == 0 else "z"),
                first_in.at[half, step_at - 1],
                col_send.at[half, 0],
                col_recv.at[half, 0],
                device_at(there),
            ).start()

    @pl.loop(0, 2)
    def _(low):
        token_grads(low * 2 + core)

    for low in range(2):
        c_swaps[low].wait()
        summed[low] = (
            partial[low * 2 + core].astype(f32) + partial_in[low].astype(f32)
        ).astype(bf16)
    for step_at in (1, 3, 2):
        there = moved(place, "x", (place["x"] + step_at) % 4)
        for m in range(2):
            remote(
                summed.at[there["x"] % 2, m * 2 + there["x"] // 2],
                sum_in.at[step_at - 1, m],
                sum_send,
                sum_recv,
                device_at(there),
            ).start()
    for half in range(2):
        wait_bytes(first_in.at[half], col_recv.at[half, 0])
        own = column_pieces(grad_chunks, half, place, "y" if half == 0 else "z")
        for number in range(4):
            total = own[number].astype(f32)
            for source in range(3):
                total = total + first_in[half, source, number].astype(f32)
            first_sum[half, number] = total.astype(bf16)
    for step_at in (1, 3, 2):
        for half, axis in enumerate("yz"):
            there = moved(place, axis, (place[axis] + step_at) % 4)
            remote(
                first_sum.at[half, there[axis]],
                second_in.at[half, step_at - 1],
                col_send.at[half, 1],
                col_recv.at[half, 1],
                device_at(there),
            ).start()
    totals = []
    for half, axis in enumerate("yz"):
        wait_bytes(second_in.at[half], col_recv.at[half, 1])
        total = first_sum[half, place[axis]].astype(f32)
        for source in range(3):
            total = total + second_in[half, source].astype(f32)
        totals.append(total)
    total_y, total_z = totals
    joined[:, 0:256] = total_y.astype(bf16)
    joined[:, 256:512] = total_z.astype(bf16)
    shares[...] = nn(share[...], joined[...]).astype(bf16).reshape(8, ROWS, MINE)
    turn = place["x"] * 2 + core
    for there in ring_devices(place):
        remote(
            shares.at[ring_number(there)],
            shares_in.at[turn],
            share_send,
            share_recv,
            device_at(there),
        ).start()
    pltpu.make_async_copy(
        shares.at[ring_number(place)], shares_in.at[turn], share_recv
    ).start()
    two.add(2, two_out)
    two.finish()
    wait_bytes(sum_in, sum_recv)
    for m in range(2):
        total = summed[x_low, m * 2 + place["x"] // 2].astype(f32)
        for source in range(3):
            total = total + sum_in[source, m].astype(f32)
        values = tokens[m].astype(f32)
        upward = total.reshape(TOK, D) * vectors[0:1]
        input_grad[m] = (
            d_branch[m * TOK : (m + 1) * TOK].astype(f32)
            + norm_back(upward, values, inverse_rms(values))
        ).astype(bf16)
    wait_bytes(shares_in, share_recv)
    pieces_out[...] = shares_in[...]
    wait_cells(pack, send, even, 128)
    wait_ring(final, back_send, place)
    wait_bytes(sum_in, sum_send)
    for number in range(2):
        wait_bytes(first_in.at[number], col_send.at[number, 0])
        wait_bytes(second_in.at[number], col_send.at[number, 1])
    wait_bytes(shares.at[pl.ds(0, 7)], share_send)


def rear(*operands):
    dma = pltpu.SemaphoreType.DMA
    return pl.pallas_call(
        rear_kernel,
        out_shape=(
            jax.ShapeDtypeStruct((2, TOK, D), bf16),
            jax.ShapeDtypeStruct((8, ROWS, MINE), bf16),
            jax.ShapeDtypeStruct((ROWS, D), f32),
        ),
        in_specs=[HBM] * 3 + [VMEM, HBM] + [VMEM] * 7 + [HBM] * 3 + [VMEM] * 5,
        out_specs=(VMEM, VMEM, VMEM),
        scratch_shapes=[
            pltpu.VMEM((16 * B, LANES), bf16),
            pltpu.VMEM((4, B, 128), bf16),
            pltpu.VMEM((4, 128, B), f32),
            pltpu.VMEM((4, 2, 128, MINE), bf16),
            pltpu.VMEM((D, MINE), bf16),
            dma((6,)),
            pltpu.VMEM((4, B, 128), bf16),
            pltpu.VMEM((16, 128, B), bf16),
            pltpu.VMEM((4, 1, B), f32),
            pltpu.VMEM((4, 128, B), f32),
            pltpu.VMEM((B, LANES), f32),
            pltpu.VMEM((8, B, LANES), f32),
            pltpu.VMEM((8, B, LANES), bf16),
            pltpu.VMEM((8, B, LANES), bf16),
            pltpu.VMEM((4, B, LANES), bf16),
            pltpu.VMEM((4, B, LANES), bf16),
            pltpu.VMEM((4, B, LANES), bf16),
            pltpu.VMEM((4, 2, 128, MINE), bf16),
            pltpu.VMEM((OUT_WIDE, 128), bf16),
            pltpu.VMEM((D, 128), bf16),
            pltpu.VMEM((D, 128), bf16),
            pltpu.VMEM((3, 2, 2, ROWS, D), bf16),
            pltpu.VMEM((4, 4, CHUNK, MINE), bf16),
            pltpu.VMEM((2, 3, 4, CHUNK, 256), bf16),
            pltpu.VMEM((2, 3, CHUNK, 256), bf16),
            pltpu.VMEM((2, 4, CHUNK, 256), bf16),
            pltpu.VMEM((CHUNK, MINE), bf16),
            pltpu.VMEM((8, ROWS, MINE), bf16),
            pltpu.VMEM((8, ROWS, MINE), bf16),
            dma, dma, dma((8,)), dma((8,)), dma((4,)), dma((4,)), dma, dma,
            dma((2,)), dma((2,)), dma, dma, dma((2, 2)), dma((2, 2)), dma, dma,
        ]
        + scatter_scratch(),
        compiler_params=pltpu.CompilerParams(
            collective_id=1, has_side_effects=True, vmem_limit_bytes=63 * 2**20
        ),
        name="rear",
    )(
        *operands,
        jnp.asarray(SHARE, bf16),
    )


def on_device(
    inputs,
    segment_ids,
    norm1_gain,
    w_query,
    w_key,
    w_value,
    query_bias,
    value_bias,
    w_out,
    out_bias,
    norm2_gain,
    w_hidden,
    hidden_bias,
    w_proj,
    proj_bias,
    dim_scale,
    cotangent,
):
    blk = lax.axis_index("blk")
    head = lax.axis_index("head")
    at = (blk * 8 + head) * 10
    spread_heads = jnp.zeros((H, LANES), bf16)
    biases = jnp.concatenate([query_bias, jnp.zeros((HD - 10,), bf16), value_bias])
    spread_heads = lax.dynamic_update_slice(spread_heads, biases[None], (blk, HD + head * 10))
    natural = jnp.stack([norm1_gain, out_bias, norm2_gain, hidden_bias, proj_bias])
    natural = lax.dynamic_update_slice(jnp.zeros((5, 3 * MINE), bf16), natural, (0, at))
    columns = jnp.concatenate(
        [w.reshape(10, H, HD) for w in (w_key, w_query, w_value)]
        + [jnp.zeros((10, H, LANES - 3 * HD), bf16)],
        axis=2,
    )
    columns = columns.reshape(10, 8, MINE).transpose(1, 0, 2)
    pieces = jnp.concatenate(
        [
            columns,
            jnp.zeros((8, 6, MINE), bf16),
            spread_heads.reshape(8, 1, MINE),
            jnp.broadcast_to(natural.reshape(1, 15, MINE), (8, 15, MINE)),
        ],
        axis=1,
    )
    softplus_scale = LOG2E / math.sqrt(HD) * jax.nn.softplus(dim_scale)
    ones = jnp.ones((HD,), f32)
    scale_row = jnp.concatenate(
        [ones, softplus_scale, ones, jnp.zeros((LANES - 3 * HD,), f32)] * 2
    )
    scale_row = scale_row[None]

    (
        ring_normed, packed, wide_w, vectors, starts, kv, queries, out_t, log_norms, attended,
        out_w, hidden_w, proj_w,
    ) = front(
        inputs, pieces, w_out, w_hidden, w_proj, scale_row, segment_ids.reshape(2, 16, B)
    )
    out_b, gain_two, hidden_b, proj_b = [vectors[i] for i in range(1, 5)]

    tokens = inputs.reshape(2 * TOK, D).astype(f32)
    residual = tokens + nn(attended, out_w) + out_b
    inverse_two = inverse_rms(residual)
    normed_two = (residual * inverse_two * gain_two).astype(bf16)
    pre_act = nn(normed_two, hidden_w) + hidden_b
    gate = jax.nn.sigmoid(pre_act)
    activated = (pre_act * gate).astype(bf16)
    layer_out = (residual + nn(activated, proj_w) + proj_b).astype(bf16)

    upstream_low = cotangent.reshape(2 * TOK, D)
    upstream = upstream_low.astype(f32)
    d_pre = (nt(upstream_low, proj_w) * gate * (1.0 + pre_act * (1.0 - gate))).astype(bf16)
    d_normed_two = nt(d_pre, hidden_w)
    d_residual = upstream + norm_back(d_normed_two * gain_two, residual, inverse_two)
    d_branch = d_residual.astype(bf16)
    d_attended = nt(d_branch, out_w).astype(bf16)

    def total(values):
        return jnp.sum(values.astype(f32), axis=0)

    vector_grads = jnp.stack(
        [
            total(d_branch),
            total(d_normed_two * residual * inverse_two),
            total(d_pre),
            total(upstream),
        ]
    )
    vector_grads = jnp.pad(vector_grads, ((0, 0), (0, 3 * MINE - D))).reshape(12, MINE)
    vector_grads = jnp.pad(vector_grads, ((4, 0), (0, 0)))
    input_grad, shares, two = rear(
        d_attended, kv.reshape(16 * B, LANES), queries, starts, out_t, log_norms,
        attended, d_branch, normed_two, d_pre, activated, upstream_low,
        ring_normed.reshape(4 * D, 256), packed, wide_w, vector_grads, scale_row,
        inputs, vectors,
    )
    shares = shares.astype(f32)
    columns = shares[:, :10].transpose(1, 0, 2).reshape(10, H, LANES)
    d_key_w, d_query_w, d_value_w = [
        columns[:, :, i * HD : (i + 1) * HD].reshape(10, D) for i in range(3)
    ]
    by_head = shares[:, 16].reshape(H, LANES)
    d_query_bias, d_value_bias = [
        lax.dynamic_slice(by_head, (blk, i * HD + head * 10), (1, 10)).reshape(10) for i in (1, 2)
    ]
    summed = jnp.sum(shares[:, 17:], axis=0)
    scale_grad = summed[0, HD : 2 * HD] / softplus_scale
    scale_grad = scale_grad * (LOG2E / math.sqrt(HD)) * jax.nn.sigmoid(dim_scale)
    natural = lax.dynamic_slice(summed.reshape(5, 3 * MINE), (0, at), (5, 10))
    norm1_gain_grad = sum(
        jnp.sum(w.astype(f32) * grad, axis=1)
        for w, grad in ((w_query, d_query_w), (w_key, d_key_w), (w_value, d_value_w))
    ) / norm1_gain.astype(f32)
    return (
        layer_out.reshape(2, TOK, D),
        input_grad,
        norm1_gain_grad,
        d_query_w,
        d_key_w,
        d_value_w,
        d_query_bias,
        d_value_bias,
        two[0:10],
        natural[1],
        natural[2],
        two[10:20],
        natural[3],
        two[20:30],
        natural[4],
        scale_grad,
    )


def solution(mesh):
    rows = P(("blk", "head"), None)
    vec = P(("blk", "head"))
    tok = P(None, ("blk", "head"), None)
    in_specs = (
        tok, P(), vec, rows, rows, rows, vec, vec, rows, vec, vec, rows, vec, rows, vec, P(), tok
    )
    out_specs = (
        tok, tok, vec, rows, rows, rows, vec, vec, rows, vec, vec, rows, vec, rows, vec, P()
    )
    return jax.shard_map(
        on_device, mesh=mesh, in_specs=in_specs, out_specs=out_specs, check_vma=False
    )
```

```python
import functools
import math

import jax
import jax.numpy as jnp
import numpy as np
from jax import lax
from jax.experimental import pallas as pl
from jax.experimental.pallas import tpu as pltpu
from jax.sharding import PartitionSpec as P

D = 1280
H = 16
HD = 80
FF = 1280
B = 512
TOK = 64
PAIRS = 32
LANES = 256
ROWS = 32
WIDE = H * LANES
OUT_WIDE = H * 128
GROUP = 80
CHUNK = 96
MINE = 512
EPSILON = 1e-06
LOG2E = 1.442695041
NEGATIVE = -1e30
MESH = pl.DeviceIdType.MESH
f32 = jnp.float32
bf16 = jnp.bfloat16

PARTS = (((0, 384), "xyz"), ((384, 512), "yzx"), ((896, 384), "zxy"))
PARTS_BACK = (((0, 512), "xyz"), ((512, 512), "xzy"), ((1024, 256), "yzx"))


def inverse_rms(values):
    return lax.rsqrt(jnp.mean(values * values, axis=-1, keepdims=True) + EPSILON)


def norm_back(upstream, values, inverse):
    return inverse * upstream - values * inverse**3 * jnp.mean(
        upstream * values, axis=-1, keepdims=True
    )


def nn(a, b):
    return lax.dot_general(a, b, (((1,), (0,)), ((), ())), preferred_element_type=f32)


def nt(a, b):
    return lax.dot_general(a, b, (((1,), (1,)), ((), ())), preferred_element_type=f32)


def tn(a, b):
    return lax.dot_general(a, b, (((0,), (0,)), ((), ())), preferred_element_type=f32)


def my_place():
    blk = lax.axis_index("blk")
    head = lax.axis_index("head")
    return {
        "x": (head % 2) * 2 + (blk // 2) % 2,
        "y": head // 2,
        "z": blk // 4,
        "c": blk % 2,
    }


def device_at(place):
    x, y, z, c = place["x"], place["y"], place["z"], place["c"]
    return (z * 4 + (x % 2) * 2 + c, y * 2 + x // 2)


def span(place, free, core=True):
    x, y, z = place["x"], place["y"], place["z"]
    whole = slice(None)
    at = [
        whole if "z" in free else z,
        whole if "x" in free else x % 2,
        place["c"],
        whole if "y" in free else y,
        whole if "x" in free else x // 2,
    ]
    return tuple(at if core else at[:2] + at[3:])


def moved(place, axis, value):
    other = dict(place)
    other[axis] = value
    return other


def greet(peers):
    barrier = pltpu.get_barrier_semaphore()
    for peer in peers:
        pl.semaphore_signal(barrier, inc=1, device_id=peer, device_id_type=MESH)
    pl.semaphore_wait(barrier, len(peers))


def greet_all():
    barrier = pltpu.get_barrier_semaphore()
    blk = lax.axis_index("blk")
    head = lax.axis_index("head")
    heads = [(head + h) % 8 for h in range(8)]
    for h in range(1, 8):
        pl.semaphore_signal(barrier, inc=1, device_id=(blk, heads[h]), device_id_type=MESH)

    @pl.loop(1, 16)
    def _(b):
        other = (blk + b) % 16
        for h in range(8):
            pl.semaphore_signal(barrier, inc=1, device_id=(other, heads[h]), device_id_type=MESH)

    pl.semaphore_wait(barrier, 127)


def ring_peers(place):
    peers = [device_at(moved(place, "c", 1 - place["c"]))]
    for axis in "xyz":
        for step in (1, 3, 2):
            peers.append(device_at(moved(place, axis, (place[axis] + step) % 4)))
    return peers


def wait_bytes(ref, sem):
    pltpu.make_async_copy(ref, ref, sem).wait()


def remote(src, dst, send, recv, device):
    return pltpu.make_async_remote_copy(
        src_ref=src, dst_ref=dst, send_sem=send, recv_sem=recv, device_id=device, device_id_type=MESH
    )


def varied(place, axes, number):
    other = dict(place)
    for axis in axes:
        other[axis] = number % 4
        number = number // 4
    return other


def selections():
    join = np.zeros((CHUNK, 256), np.float32)
    for i in range(8):
        for j in range(10):
            join[i * 10 + j, i * ROWS + j] = 1
        for v in range(16):
            join[GROUP + v, i * ROWS + 16 + v] = 1
    return join, join.T.copy()


JOIN, SHARE = selections()


def rows_of(values, size, starts):
    return jnp.concatenate([values[at : at + size] for at in starts], axis=0)


def row_block(ref, g, count):
    return ref.at[pl.ds(pl.multiple_of(g * count, 16), count)]


class Gather:
    def __init__(self, buf, send, recv, place):
        self.place = place
        self.buf, self.send, self.recv = buf, send, recv
        self.sibling = device_at(moved(place, "c", 1 - place["c"]))

    def begin(self, matrices):
        spare = jnp.zeros((2, D), f32)
        own = [matrix[...].astype(f32) for matrix in matrices] + [spare]
        self.buf[span(self.place, "")] = jnp.concatenate(own, axis=0).astype(bf16)

    def piece(self, part, where, free):
        first, width = PARTS[part][0]
        return self.buf.at[(*span(where, free), slice(None), pl.ds(first, width))]

    def pieces(self, part, count):
        cols = pl.ds(*PARTS[part][0])
        whole = slice(None)
        at = {
            3: (pl.ds(0, 3), 0, 0, 0, 0),
            12: (pl.ds(0, 3), 0, 0, whole, 0),
            16: (0, whole, 0, whole, whole),
            48: (pl.ds(0, 3), whole, 0, whole, whole),
            64: (whole, whole, 0, whole, whole),
        }[count]
        return self.buf.at[(*at, whole, cols)]

    def forward(self, part, where, free):
        piece = self.piece(part, where, free)
        remote(piece, piece, self.send.at[part, 3], self.recv.at[part, 5], self.sibling).start()

    def stage(self, stage):
        for part, (_, order) in enumerate(PARTS):
            if stage:
                wait_bytes(self.pieces(part, 3 * 4 ** (stage - 1)), self.recv.at[part, stage - 1])
            piece = self.piece(part, self.place, order[:stage])
            axis = order[stage]
            for step in (1, 3, 2) if stage < 2 else (1, 3):
                target = moved(self.place, axis, (self.place[axis] + step) % 4)
                slot = stage if stage < 2 else 1 + step
                remote(
                    piece,
                    piece,
                    self.send.at[part, stage],
                    self.recv.at[part, slot],
                    device_at(target),
                ).start()
        for part, (_, order) in enumerate(PARTS):
            if stage == 0:
                self.forward(part, self.place, "")
            else:
                axis = order[stage - 1]
                for step in (1, 3, 2):
                    there = moved(self.place, axis, (self.place[axis] + 4 - step) % 4)
                    self.forward(part, there, order[: stage - 1])

    def relay(self):
        for part, ((first, width), order) in enumerate(PARTS):
            axis, halved = order[2], order[1]
            here = self.place[axis]
            for step in (1, 3):
                wait_bytes(self.pieces(part, 16), self.recv.at[part, 1 + step])
                there = moved(self.place, axis, (here + 4 - step) % 4)
                at = list(span(there, order[:2]))
                half = step // 2
                if halved == "x":
                    at[4] = half
                else:
                    at[0 if halved == "z" else 3] = pl.ds(half * 2, 2)
                piece = self.buf.at[(*at, slice(None), pl.ds(first, width))]
                target = device_at(moved(self.place, axis, (here + step) % 4))
                remote(
                    piece, piece, self.send.at[part, 2], self.recv.at[part, 3], target
                ).start()
                self.forward(part, there, order[:2])

    def finish(self):
        for part, (_, order) in enumerate(PARTS):
            wait_bytes(self.pieces(part, 16), self.recv.at[part, 3])
            axis = order[2]
            there = moved(self.place, axis, (self.place[axis] + 2) % 4)
            self.forward(part, there, order[:2])
        for part in range(3):
            wait_bytes(self.pieces(part, 64), self.recv.at[part, 5])
            wait_bytes(self.pieces(part, 64), self.send.at[part, 3])
            wait_bytes(self.pieces(part, 3), self.send.at[part, 0])
            wait_bytes(self.pieces(part, 12), self.send.at[part, 1])
            wait_bytes(self.pieces(part, 48), self.send.at[part, 2])


VMEM = pl.BlockSpec(memory_space=pltpu.VMEM)
HBM = pl.BlockSpec(memory_space=pl.ANY)


def unpack(buf, staged, out_w, hidden_w, proj_w, out_sem):
    spans = ((0, 128, out_w), (128, GROUP, hidden_w), (208, GROUP, proj_w))
    staged[:, 0:32] = jnp.zeros((2, 32, D), bf16)
    staged[:, 112:128] = jnp.zeros((2, 16, D), bf16)

    @pl.loop(0, 16)
    def _(g):
        slot = g % 2
        outs = [
            pltpu.make_async_copy(
                staged.at[slot, pl.ds(at, count)], row_block(ref, g, count), out_sem.at[i, slot]
            )
            for i, (at, count, ref) in enumerate(spans)
        ]

        @pl.when(g >= 2)
        def _():
            for out in outs:
                out.wait()

        packed = buf[g // 4, (g // 2) % 2, g % 2].reshape(256, D).astype(f32)
        for w, at in enumerate((32, 128, 208)):
            rows = rows_of(packed, 10, range(w * 10, 256, ROWS))
            staged[slot, at : at + GROUP] = rows.astype(bf16)
        for out in outs:
            out.start()

    for slot in range(2):
        for i, (at, count, ref) in enumerate(spans):
            pltpu.make_async_copy(
                staged.at[slot, pl.ds(at, count)], row_block(ref, 0, count), out_sem.at[i, slot]
            ).wait()


class Scatter:
    def __init__(self, away, mine, pair, lands, halves, send, recv, place):
        self.away, self.mine, self.pair = away, mine, pair
        self.lands, self.halves = lands, halves
        self.send, self.recv, self.place = send, recv, place
        self.sibling = device_at(moved(place, "c", 1 - place["c"]))

    def swap(self, number):
        at = (number // 2, number % 2)
        sems = (len(PARTS_BACK), number)
        return remote(
            self.away.at[at], self.pair.at[at], self.send.at[sems], self.recv.at[sems], self.sibling
        )

    def add_pair(self, number):
        self.swap(number).wait()
        at = (number // 2, number % 2)
        self.mine[at] = (self.mine[at].astype(f32) + self.pair[at].astype(f32)).astype(bf16)

    def source(self, part, stage, where):
        (first, width), order = PARTS_BACK[part]
        if stage == 0:
            at = span(where, order[:2], core=False)
            return self.mine.at[(*at, slice(None), pl.ds(first, width))]
        at = [
            slice(None) if axis in order[: 2 - stage] else value
            for axis, value in zip("zxyx", span(where, "", core=False))
            if axis in order[: 3 - stage]
        ]
        return self.halves[stage - 1][part].at[tuple(at)]

    def start(self, stage):
        for part, (_, order) in enumerate(PARTS_BACK):
            axis = order[2 - stage]
            for step in (1, 3, 2):
                target = moved(self.place, axis, (self.place[axis] + step) % 4)
                remote(
                    self.source(part, stage, target),
                    self.lands[stage][part].at[step - 1],
                    self.send.at[part, stage],
                    self.recv.at[part, stage],
                    device_at(target),
                ).start()

    def add(self, stage, out=None):
        for part, ((first, width), order) in enumerate(PARTS_BACK):
            land = self.lands[stage][part]
            wait_bytes(land, self.recv.at[part, stage])
            own = self.source(part, stage, self.place)
            lead = land.shape[1:-2]

            @pl.loop(0, math.prod(lead))
            def _(number):
                at = []
                for size in reversed(lead):
                    at.insert(0, number % size)
                    number = number // size
                at = tuple(at)
                total = own[at].astype(f32)
                for source in range(3):
                    total = total + land[(source, *at)].astype(f32)
                if stage < 2:
                    self.halves[stage][part][at] = total.astype(bf16)
                else:
                    out[:, first : first + width] = total

    def finish(self):
        for stage in range(3):
            for part in range(len(PARTS_BACK)):
                wait_bytes(self.lands[stage][part], self.send.at[part, stage])


def lead_of(axes):
    sizes = {"z": (4,), "x": (2, 2), "y": (4,)}
    if axes == {"x", "y"}:
        return (2, 4, 2)
    if axes == {"x", "z"}:
        return (4, 2, 2)
    return sum((sizes[axis] for axis in "zyx" if axis in axes), ())


def scatter_scratch():
    whole = pltpu.VMEM((4, 2, 4, 2, ROWS, D), bf16)
    lands, halves = [], []
    for stage in range(3):
        for (_, width), order in PARTS_BACK:
            lead = lead_of(set(order[: 2 - stage]))
            lands.append(pltpu.VMEM((3, *lead, ROWS, width), bf16))
            if stage < 2:
                halves.append(pltpu.VMEM((*lead, ROWS, width), bf16))
    semaphores = [pltpu.SemaphoreType.DMA((4, 8))] * 2
    return [whole] * 3 + lands + halves + semaphores


def scatter_of(scratch, place):
    away, mine, pair = scratch[:3]
    parts = len(PARTS_BACK)
    lands = [scratch[3 + parts * stage : 3 + parts * (stage + 1)] for stage in range(3)]
    halves = [scratch[3 + parts * stage : 3 + parts * (stage + 1)] for stage in (3, 4)]
    return Scatter(away, mine, pair, lands, halves, scratch[-2], scratch[-1], place)


HALVES = ((0, "yz"), (256, "zy"))


def ring_devices(place):
    others = [moved(place, "c", 1 - place["c"])]
    for step in (1, 3, 2):
        there = moved(place, "x", (place["x"] + step) % 4)
        others += [there, moved(there, "c", 1 - place["c"])]
    return others


def ring_number(place):
    return (place["x"] % 2) * 4 + place["c"] * 2 + place["x"] // 2


def tokens_of(ref, place):
    inner = (place["x"] % 2) * 2 + place["c"]
    return ref.at[inner, :, pl.ds((place["x"] // 2) * TOK, TOK)]


def head_of(place):
    return (place["x"] // 2) * 8 + (place["z"] % 2) * 4 + place["y"]


def pair_device(pair, quarter):
    micro, h = pair // H, pair % H
    return ((micro * 2 + (h % 8) // 4) * 4 + quarter, (h % 4) * 2 + h // 8)


def column_pieces(buf, half, place, free):
    at = [slice(None) if axis in free else place[axis] for axis in "zy"]
    return buf.at[(*at, slice(None), pl.ds(HALVES[half][0], 256))]


def gather_columns(buf, send, recv, place, stage):
    for half, (first, order) in enumerate(HALVES):
        axis = order[stage]
        if stage:
            wait_bytes(buf.at[0, pl.ds(0, 3), :, pl.ds(first, 256)], recv.at[half, 0])
        piece = column_pieces(buf, half, place, order[:stage])
        for step in (1, 3, 2):
            target = moved(place, axis, (place[axis] + step) % 4)
            remote(
                piece, piece, send.at[half, stage], recv.at[half, stage], device_at(target)
            ).start()


def finish_columns(buf, send, recv):
    for half, (first, _) in enumerate(HALVES):
        cols = pl.ds(first, 256)
        wait_bytes(buf.at[pl.ds(0, 3), :, :, cols], recv.at[half, 1])
        wait_bytes(buf.at[0, pl.ds(0, 3), :, cols], send.at[half, 0])
        wait_bytes(buf.at[pl.ds(0, 3), :, :, cols], send.at[half, 1])


def quarter_of(blk):
    inner = blk % 4
    return jnp.where((blk // 4) % 2 == 0, inner, 3 - inner)


def query_block(quarter, j):
    return j * 4 + jnp.where(j % 2 == 0, quarter, 3 - quarter)


def cell_of(ref, pair, width):
    return ref.at[pl.ds(pair // H * TOK, TOK), pl.ds(pair % H * width, width)]


def mask_of(key_block, block, start):
    key_at = key_block * B + lax.broadcasted_iota(jnp.int32, (B, B), 0)
    query_at = block * B + lax.broadcasted_iota(jnp.int32, (B, B), 1)
    return (key_at >= start) & (key_at <= query_at)


def has_mask(key_block, block):
    return (key_block == 0) | (key_block == block) | (block == 15)


def shift_matrix(rows, cols, by):
    row = lax.broadcasted_iota(jnp.int32, (rows, cols), 0)
    col = lax.broadcasted_iota(jnp.int32, (rows, cols), 1)
    return jnp.where((row - col == by) & (jnp.minimum(row, col) < HD), 1.0, 0.0).astype(bf16)


def wait_cells(ref, sem, fewer, width):
    wait_bytes(ref.at[:, pl.ds(0, 15 * width)], sem)
    wait_bytes(cell_of(ref, 0, width), sem)

    @pl.when(jnp.logical_not(fewer))
    def _():
        wait_bytes(cell_of(ref, 0, width), sem)


def stays_here(place):
    return (place["z"] % 2 == place["x"] % 2) & (place["y"] // 2 == place["c"])


def wait_ring(ref, sem, place):
    wait_bytes(ref.at[pl.ds(0, 3)], sem)
    wait_bytes(ref.at[0, pl.ds(0, 384)], sem)

    @pl.when(jnp.logical_not(stays_here(place)))
    def _():
        wait_bytes(ref.at[0, pl.ds(0, 128)], sem)


def front_kernel(
    tokens, pieces, w_out, w_hidden, w_proj, scale_row, segments, join,
    normed_hbm, packed_hbm, wide_hbm, vectors, starts, kv_out, queries, out_t, log_norms, attended,
    out_w, hidden_w, proj_w,
    normed_out, normed_t, packed_out, wide_w, keep_sems, ring_tokens, ring_pieces, chunks, kv, value_t, tops, totals, rounded, landed, buf, staged,
    x_tok_send, x_tok_recv, c_tok_send, c_tok_recv, piece_send, piece_recv, col_send, col_recv,
    two_send, two_recv, own_sem, send, recv, core_send, core_recv, x_send, x_recv,
    pass_send, pass_recv, back_send, back_recv, kv_sem, out_sem,
):
    blk = lax.axis_index("blk")
    head = lax.axis_index("head")
    core = blk % 2
    x_low = (blk // 2) % 2
    quarter = blk % 4
    even = (blk // 4) % 2 == 0
    place = my_place()
    pair = (place["z"] // 2) * H + head_of(place)
    turn = place["x"] * 2 + core
    sibling = (blk + 1 - 2 * core, head)
    two = Gather(buf, two_send, two_recv, place)
    own_tokens = pltpu.make_async_copy(tokens, tokens_of(ring_tokens, place), own_sem)
    own_tokens.start()
    number = ring_number(place)
    pltpu.make_async_copy(pieces.at[turn], ring_pieces.at[number], piece_recv).start()
    greet_all()
    for there in ring_devices(place):
        remote(
            pieces.at[there["x"] * 2 + there["c"]],
            ring_pieces.at[number],
            piece_send,
            piece_recv,
            device_at(there),
        ).start()
    mine = tokens_of(ring_tokens, place)
    for step in (1, 3, 2):
        there = moved(place, "x", (place["x"] + step) % 4)
        remote(
            tokens, mine, x_tok_send.at[step - 1], x_tok_recv.at[step - 1], device_at(there)
        ).start()
    remote(tokens, mine, c_tok_send, c_tok_recv, sibling).start()
    two.begin((w_out, w_hidden, w_proj))
    two.stage(0)
    ids = segments[place["z"] // 2]
    before = [jnp.sum((ids < value).astype(jnp.int32)) for value in range(1, 9)]
    for j in range(4):
        row = segments[place["z"] // 2, pl.ds(query_block(quarter, j), 1)]
        start = jnp.zeros_like(row)
        for value in range(1, 9):
            start = jnp.where(row == value, before[value - 1], start)
        starts[j] = start
    wait_bytes(ring_pieces, piece_recv)
    joined = nn(join[...], ring_pieces[...].reshape(256, MINE)).astype(bf16)
    chunks[place["z"], place["y"]] = joined
    gather_columns(chunks, col_send, col_recv, place, 0)
    gather_columns(chunks, col_send, col_recv, place, 1)
    for step in (1, 3, 2):
        wait_bytes(tokens, x_tok_recv.at[step - 1])
        there = moved(place, "x", (place["x"] + 4 - step) % 4)
        arrived = tokens_of(ring_tokens, there)
        remote(arrived, arrived, c_tok_send, c_tok_recv, sibling).start()
    own_tokens.wait()
    finish_columns(chunks, col_send, col_recv)

    @pl.loop(0, 4)
    def _(z):
        rows = pl.ds(pl.multiple_of(z * 4 * GROUP, 64), 4 * GROUP)
        found = chunks[z].reshape(4 * CHUNK, MINE).astype(f32)
        starts_at = [y * CHUNK + inner * 20 for inner in range(4) for y in range(4)]
        wide_w[rows] = rows_of(found, 20, starts_at).astype(bf16)

    vector_rows = jnp.zeros((16, MINE), f32)
    for z in range(4):
        for y in range(4):
            vector_rows = vector_rows + chunks[z, y, GROUP:].astype(f32)
    for i in range(5):
        three = [vector_rows[1 + 3 * i + k : 2 + 3 * i + k] for k in range(3)]
        vectors[i : i + 1] = jnp.concatenate(three[:2] + [three[2][:, :256]], axis=1)
    bias = vector_rows[0:1]
    gain = vectors[0:1]
    one_lane = jnp.where(
        lax.broadcasted_iota(jnp.int32, (1, MINE), 1) % LANES == 3 * HD, 1.0, 0.0
    )
    wait_bytes(ring_tokens.at[pl.ds(0, 2)], c_tok_recv)

    def deliver(inner, aside, send, recv):
        block = place["z"] * 4 + inner
        to_quarter = (quarter_of(block) + aside) % 4
        for m in range(2):
            for h in range(2):
                blk_to, head_to = pair_device(m * H + turn * 2 + h, to_quarter)
                src = packed_out.at[inner, m, :, pl.ds(h * LANES, LANES)]
                dst = kv.at[block, pl.ds(place["y"] * 128, 128)]
                stays = (blk_to == blk) & (head_to == head)

                @pl.when(stays)
                def _():
                    pltpu.make_async_copy(src, dst, recv).start()

                @pl.when(jnp.logical_not(stays))
                def _():
                    remote(src, dst, send, recv, (blk_to, head_to)).start()

    @pl.loop(0, 4)
    def _(inner):
        values = ring_tokens[inner].reshape(256, D).astype(f32)
        normed = (values * inverse_rms(values) * gain).astype(bf16)
        normed_out[inner] = normed
        full = nn(normed, wide_w[...])
        packed = ((full + bias) * scale_row[0:1] + one_lane).astype(bf16)
        packed_out[inner] = packed.reshape(2, 128, MINE)
        deliver(inner, 0, send, recv)

    @pl.loop(0, 4)
    def _(inner):
        deliver(inner, 2, x_send, x_recv)

    two.stage(1)

    @pl.loop(0, 4)
    def _(inner):
        @pl.loop(0, D // 128)
        def _(n):
            lanes = pl.ds(pl.multiple_of(n * 128, 128), 128)
            normed_t[inner, lanes] = normed_out[inner, :, lanes].T

    keeps = [
        pltpu.make_async_copy(ref, out, keep_sems.at[i])
        for i, (ref, out) in enumerate(
            ((normed_t, normed_hbm), (packed_out, packed_hbm), (wide_w, wide_hbm))
        )
    ]
    for keep in keeps:
        keep.start()
    wait_bytes(kv.at[pl.ds(0, 4)], recv)

    @pl.loop(0, 4)
    def _(j):
        block = kv.at[query_block(quarter, j)]
        remote(block, block, core_send, core_recv, sibling).start()

    pick = shift_matrix(LANES, 128, HD)

    @pl.loop(0, 4)
    def _(j):
        queries[j] = nn(kv[query_block(quarter, j)], pick).astype(bf16)
        tops[j] = jnp.full((1, B), NEGATIVE, f32)
        totals[j] = jnp.zeros((1, B), f32)
        out_t[j] = jnp.zeros((128, B), f32)


    def step(j, block, key_blocks):
        def tiles(masked):
            scores = []
            for key_block in key_blocks:
                s = nt(kv[key_block, :, :128], queries[j])
                if masked:
                    s = jnp.where(mask_of(key_block, block, starts[j]), s, NEGATIVE)
                scores.append(s)
            top = tops[j]
            new_top = top
            for s in scores:
                new_top = jnp.maximum(new_top, jnp.max(s, axis=0, keepdims=True))
            scale = jnp.exp(top - new_top)
            total = totals[j] * scale
            acc = out_t[j] * scale
            for key_block, s in zip(key_blocks, scores):
                p = jnp.exp(s - new_top)
                total = total + jnp.sum(p, axis=0, keepdims=True)
                acc = acc + nn(value_t[key_block], p.astype(bf16))
            tops[j] = new_top
            totals[j] = total
            out_t[j] = acc

        masked = has_mask(key_blocks[0], block)
        for key_block in key_blocks[1:]:
            masked = masked | has_mask(key_block, block)
        pl.when(masked)(lambda: tiles(True))
        pl.when(jnp.logical_not(masked))(lambda: tiles(False))

    def key_pass(j, of_quarter, count):
        block = query_block(quarter, j)

        @pl.when(count == 4)
        def _():
            step(j, block, tuple(query_block(of_quarter, n) for n in range(4)))

        @pl.loop(0, jnp.where(count == 4, 0, count // 2))
        def _(n):
            last = count - 1 - 2 * n
            step(j, block, (query_block(of_quarter, last), query_block(of_quarter, last - 1)))

        @pl.when(count % 2 == 1)
        def _():
            step(j, block, (query_block(of_quarter, 0),))

    def give(j, block):
        acc = out_t[j]
        result = acc / acc[112:113]
        out_t[j] = result
        log_norms[j] = tops[j] + jnp.log(totals[j])
        rounded[j] = result.T.astype(bf16)

        @pl.loop(0, 8)
        def _(k):
            h = (head + k) % 8
            src = rounded.at[j, pl.ds(h * TOK, TOK)]
            dst = cell_of(landed, pair, 128)
            mine = (k == 0) & (block == blk)

            @pl.when(mine)
            def _():
                pltpu.make_async_copy(src, dst, back_recv).start()

            @pl.when(jnp.logical_not(mine))
            def _():
                remote(src, dst, back_send, back_recv, (block, h)).start()

    keep_kv = pltpu.make_async_copy(kv, kv_out, kv_sem)

    @pl.loop(0, 4)
    def _(turn_at):
        of_quarter = (quarter + 2 * (turn_at // 2)) % 4 + (turn_at % 2) * (1 - 2 * core)

        @pl.when(turn_at == 1)
        def _():
            two.stage(2)
            wait_bytes(kv.at[pl.ds(0, 4)], core_recv)

        @pl.when(turn_at == 2)
        def _():
            wait_bytes(kv.at[pl.ds(0, 4)], x_recv)

            @pl.loop(0, 4)
            def _(j):
                block = kv.at[query_block(of_quarter, j)]
                remote(block, block, pass_send, pass_recv, sibling).start()

        @pl.when(turn_at == 3)
        def _():
            two.relay()
            wait_bytes(kv.at[pl.ds(0, 4)], pass_recv)
            keep_kv.start()

        @pl.loop(0, 4)
        def _(j):
            b = query_block(of_quarter, j)
            value_t[b] = kv[b, :, 128:].T

        @pl.loop(0, 4)
        def _(i):
            j = 3 - i
            block = query_block(quarter, j)
            more = jnp.where(
                turn_at == 0, 1, jnp.where(turn_at == 1, block % 2, (j + x_low) % 2)
            )
            key_pass(j, of_quarter, j + more)
            pl.when(turn_at == 3)(lambda: give(j, block))

    two.finish()
    unpack(buf, staged, out_w, hidden_w, proj_w, out_sem)
    wait_bytes(landed, back_recv)
    attended[...] = landed[...]
    for keep in keeps + [keep_kv]:
        keep.wait()
    for sem in (core_send, pass_send):
        wait_bytes(kv.at[pl.ds(0, 4)], sem)
    wait_cells(landed, back_send, even, 128)
    wait_bytes(ring_pieces.at[pl.ds(0, 7)], piece_send)
    for step_at in range(3):
        wait_bytes(tokens, x_tok_send.at[step_at])
    wait_bytes(ring_tokens.at[pl.ds(0, 2)], c_tok_send)
    wait_ring(kv, send, place)
    wait_ring(kv, x_send, place)


def front(*operands):
    dma = pltpu.SemaphoreType.DMA
    return pl.pallas_call(
        front_kernel,
        out_shape=(
            jax.ShapeDtypeStruct((4, D, 256), bf16),
            jax.ShapeDtypeStruct((4, 2, 128, MINE), bf16),
            jax.ShapeDtypeStruct((D, MINE), bf16),
            jax.ShapeDtypeStruct((8, D), f32),
            jax.ShapeDtypeStruct((4, 1, B), jnp.int32),
            jax.ShapeDtypeStruct((16, B, LANES), bf16),
            jax.ShapeDtypeStruct((4, B, 128), bf16),
            jax.ShapeDtypeStruct((4, 128, B), f32),
            jax.ShapeDtypeStruct((4, 1, B), f32),
            jax.ShapeDtypeStruct((2 * TOK, OUT_WIDE), bf16),
            jax.ShapeDtypeStruct((OUT_WIDE, D), bf16),
            jax.ShapeDtypeStruct((D, D), bf16),
            jax.ShapeDtypeStruct((D, D), bf16),
        ),
        in_specs=[VMEM] * 8,
        out_specs=(HBM,) * 3 + (VMEM,) * 2 + (HBM,) + (VMEM,) * 4 + (HBM,) * 3,
        scratch_shapes=[
            pltpu.VMEM((4, 256, D), bf16),
            pltpu.VMEM((4, D, 256), bf16),
            pltpu.VMEM((4, 2, 128, MINE), bf16),
            pltpu.VMEM((D, MINE), bf16),
            dma((3,)),
            pltpu.VMEM((4, 2, 128, D), bf16),
            pltpu.VMEM((8, ROWS, MINE), bf16),
            pltpu.VMEM((4, 4, CHUNK, MINE), bf16),
            pltpu.VMEM((16, B, LANES), bf16),
            pltpu.VMEM((16, 128, B), bf16),
            pltpu.VMEM((4, 1, B), f32),
            pltpu.VMEM((4, 1, B), f32),
            pltpu.VMEM((4, B, 128), bf16),
            pltpu.VMEM((2 * TOK, OUT_WIDE), bf16),
            pltpu.VMEM((4, 2, 2, 4, 2, ROWS, D), bf16),
            pltpu.VMEM((2, 288, D), bf16),
            dma((3,)), dma((3,)), dma, dma, dma, dma, dma((2, 2)), dma((2, 2)),
            dma((3, 4)), dma((3, 6)), dma,
        ]
        + [dma] * 11
        + [dma((3, 2))],
        compiler_params=pltpu.CompilerParams(
            collective_id=0, has_side_effects=True, vmem_limit_bytes=56 * 2**20
        ),
        name="front",
    )(
        *operands,
        jnp.asarray(JOIN, bf16),
    )


def rear_kernel(
    pack, kv_hbm, queries_hbm, starts, out_t_hbm, log_norms,
    attended, d_branch, normed_two, d_pre, activated, upstream,
    normed_hbm, packed_hbm, wide_hbm, vector_grads, scale_row, tokens, vectors,
    share,
    input_grad, pieces_out, two_out,
    kv, queries, out_t, packed, wide_w, load_sems,
    d_out, key_t, deltas, d_query, d_kv, mine_kv, half, half_in, cross, cross_in, final, d_wide,
    attended_t, normed_two_t, activated_t,
    sum_in, grad_chunks, first_in, second_in, first_sum,
    joined, shares, shares_in,
    send, recv, core_send, core_recv, x_send, x_recv, back_send, back_recv,
    c_send, c_recv, sum_send, sum_recv, col_send, col_recv, share_send, share_recv,
    *scratch,
):
    blk = lax.axis_index("blk")
    head = lax.axis_index("head")
    core = blk % 2
    x_low = (blk // 2) % 2
    quarter = blk % 4
    place = my_place()
    my_head = head_of(place)
    pair = (place["z"] // 2) * H + my_head
    to_quarter = quarter_of(blk)
    even = (blk // 4) % 2 == 0
    two = scatter_of(scratch, place)
    loads = [
        pltpu.make_async_copy(src, dst, load_sems.at[i])
        for i, (src, dst) in enumerate(
            (
                (kv_hbm, kv),
                (queries_hbm, queries),
                (out_t_hbm, out_t),
                (packed_hbm, packed),
                (wide_hbm, wide_w),
            )
        )
    ]
    for load in loads:
        load.start()
    greet_all()

    dst = d_out.at[blk // 4, pl.ds(head * TOK, TOK)]
    heads = [(head + k) % 8 for k in range(8)]
    places_of = [(to % 2) * 8 + to // 2 for to in heads]

    @pl.loop(0, 4)
    def _(step_at):
        z = (place["z"] + step_at) % 4
        rows = pl.ds(z // 2 * TOK, TOK)
        for k in range(8):
            src = pack.at[rows, pl.ds(((z % 2) * 4 + places_of[k]) * 128, 128)]
            copy = remote(src, dst, send, recv, (z * 4 + to_quarter, heads[k]))
            if k:
                copy.start()
                continue
            mine = (step_at == 0) & even
            pl.when(mine)(lambda src=src: pltpu.make_async_copy(src, dst, recv).start())
            pl.when(jnp.logical_not(mine))(copy.start)


    @pl.loop(0, D // 128)
    def _(n):
        lanes = pl.ds(pl.multiple_of(n * 128, 128), 128)
        normed_two_t[lanes] = normed_two[:, lanes].T
        activated_t[lanes] = activated[:, lanes].T

    @pl.loop(0, H)
    def _(n):
        lanes = pl.ds(pl.multiple_of(n * 128, 128), 128)
        attended_t[lanes] = attended[:, lanes].T


    @pl.loop(0, 8)
    def _(number):
        rows = pl.ds(pl.multiple_of(number * 2 * GROUP, 32), 2 * GROUP)
        heads = [
            attended_t[pl.ds(pl.multiple_of((number * 2 + k) * 128 + 32, 32), GROUP)]
            for k in range(2)
        ]
        found = [
            nn(jnp.concatenate(heads, axis=0), d_branch[...]),
            nn(normed_two_t[rows], d_pre[...]),
            nn(activated_t[rows], upstream[...]),
        ]
        spare = jnp.zeros((2, D), f32)
        for k in range(2):
            block = jnp.concatenate(
                [
                    part
                    for i in range(8)
                    for part in [w[k * GROUP + i * 10 : k * GROUP + i * 10 + 10] for w in found]
                    + [spare]
                ],
                axis=0,
            )
            block = block.astype(bf16).reshape(4, 2, ROWS, D)

            @pl.when(core == k)
            def _():
                two.mine[number // 2, number % 2] = block

            @pl.when(core != k)
            def _():
                two.away[number // 2, number % 2] = block

        two.swap(number).start()

    for load in loads[:3]:
        load.wait()

    def keys_at(block, lane):
        return kv[pl.ds(pl.multiple_of(block * B, B), B), lane : lane + 128]

    @pl.loop(0, 16)
    def _(b):
        key_t[b] = keys_at(b, 0).T

    @pl.loop(0, 8)
    def _(number):
        two.add_pair(number)

    two.start(0)
    wait_bytes(d_out, recv)

    @pl.loop(0, 4)
    def _(j):
        deltas[j] = jnp.sum(d_out[j].astype(f32).T * out_t[j], axis=0, keepdims=True)
        d_query[j] = jnp.zeros((128, B), f32)

    sibling = (blk + 1 - 2 * core, head)

    def step(numbers, key_block):
        def tiles(masked):
            found = []
            for j in numbers:
                q = queries[j]
                do = d_out[j]
                p = jnp.exp(nt(keys_at(key_block, 0), q) - log_norms[j])
                if masked:
                    allowed = mask_of(key_block, query_block(quarter, j), starts[j])
                    p = jnp.where(allowed, p, 0.0)
                dp = nt(keys_at(key_block, 128), do)
                found.append((q, do, p.astype(bf16), (p * (dp - deltas[j])).astype(bf16)))
            d_kv[:, :128] += sum(nn(ds, q) for q, do, p, ds in found)
            d_kv[:, 128:] += sum(nn(p, do) for q, do, p, ds in found)
            for j, (q, do, p, ds) in zip(numbers, found):
                d_query[j] += nn(key_t[key_block], ds)

        masked = has_mask(key_block, query_block(quarter, numbers[0]))
        for j in numbers[1:]:
            masked = masked | has_mask(key_block, query_block(quarter, j))
        pl.when(masked)(lambda: tiles(True))
        pl.when(jnp.logical_not(masked))(lambda: tiles(False))

    def swap(n):
        return remote(
            half.at[n], half_in.at[n], core_send.at[n], core_recv.at[n], sibling
        )

    shift = shift_matrix(128, LANES, -HD)

    partner = (blk + 2 - 4 * x_low, head)

    def cross_swap(z):
        return remote(cross.at[z], cross_in.at[z], x_send.at[z], x_recv.at[z], partner)

    def core_sum(z):
        own = 2 * z + (x_low + z) % 2
        other = 4 * z + 1 - own
        swap(other).wait()
        cross[z] = (mine_kv[other] + half_in[other].astype(f32)).astype(bf16)
        cross_swap(z).start()
        swap(own).wait()
        mine_kv[own] = (
            mine_kv[own]
            + half_in[own].astype(f32)
            + nn(d_query[z].T.astype(bf16), shift)
        )

    def finish(z):
        cross_swap(z).wait()
        own = 2 * z + (x_low + z) % 2
        final[z] = (mine_kv[own] + cross_in[z].astype(f32)).astype(bf16)
        inner = query_block(quarter, z) % 4
        dst = d_wide.at[inner, place["z"] // 2, :, pl.ds((my_head % 2) * LANES, LANES)]

        @pl.loop(0, 4)
        def _(k):
            y = (place["y"] + k) % 4
            there = {"x": my_head // 4, "y": y, "z": z, "c": (my_head // 2) % 2}
            src = final.at[z, pl.ds(y * 128, 128)]
            blk_to, head_to = device_at(there)
            stays = (blk_to == blk) & (head_to == head)

            @pl.when(stays)
            def _():
                pltpu.make_async_copy(src, dst, back_recv).start()

            @pl.when(jnp.logical_not(stays))
            def _():
                remote(src, dst, back_send, back_recv, (blk_to, head_to)).start()

    load_normed = pltpu.make_async_copy(normed_hbm, kv.at[pl.ds(0, 4 * D)], load_sems.at[5])

    def key_steps(key_block):
        z = key_block // 4
        d_kv[...] = jnp.zeros((B, LANES), f32)
        first = z + (query_block(quarter, z) < key_block).astype(jnp.int32)

        @pl.when(first % 2 == 1)
        def _():
            step((first,), key_block)

        @pl.loop((first + 1) // 2, 2)
        def _(n):
            step((2 * n, 2 * n + 1), key_block)

        n = 2 * z + (key_block % 4) // 2

        @pl.when((key_block + z + core) % 2 == 0)
        def _():
            mine_kv[n] = d_kv[...]

        @pl.when((key_block + z + core) % 2 == 1)
        def _():
            half[n] = d_kv[...].astype(bf16)
            swap(n).start()

    @pl.loop(0, 10)
    def _(part):
        z = part // 2

        @pl.when(part < 8)
        def _():
            @pl.loop(2 * part, 2 * part + 2)
            def _(key_block):
                key_steps(key_block)

        @pl.when(part == 8)
        def _():
            load_normed.start()

        @pl.when((part % 2 == 0) & (part > 0))
        def _():
            core_sum(z - 1)

        @pl.when((part % 2 == 1) & (part > 1))
        def _():
            finish(z - 1)

        @pl.when(part == 6)
        def _():
            two.add(0)
            two.start(1)

    two.add(1)
    two.start(2)
    wait_bytes(d_wide, back_recv)

    for load in loads[3:]:
        load.wait()
    load_normed.wait()
    partial = two.away.at[:, 0]
    summed, partial_in = two.away.at[pl.ds(0, 2), 1], two.away.at[pl.ds(2, 2), 1]
    scale = scale_row[0:1]
    bias_sum = jnp.zeros((1, MINE), f32)
    scale_sum = jnp.zeros((1, MINE), f32)

    def scaled_grads(inner, sums):
        bias_sum, scale_sum = sums
        grad = d_wide[inner].reshape(256, MINE).astype(f32)
        scale_sum = scale_sum + jnp.sum(
            grad * packed[inner].reshape(256, MINE).astype(f32), axis=0, keepdims=True
        )
        grad = (grad * scale).astype(bf16)
        d_wide[inner] = grad.reshape(2, 128, MINE)
        return bias_sum + jnp.sum(grad.astype(f32), axis=0, keepdims=True), scale_sum

    bias_sum, scale_sum = lax.fori_loop(0, 4, scaled_grads, (bias_sum, scale_sum))
    scale_sum = scale_sum[:, :LANES] + scale_sum[:, LANES:]
    rows = vector_grads[...] + jnp.concatenate(
        [bias_sum, jnp.concatenate([scale_sum, scale_sum], axis=1), jnp.zeros((14, MINE), f32)],
        axis=0,
    )
    rows = rows.astype(bf16)
    sibling_at = (blk + 1 - 2 * core, head)
    c_swaps = [
        remote(
            partial.at[low * 2 + 1 - core],
            partial_in.at[low],
            c_send.at[low],
            c_recv.at[low],
            sibling_at,
        )
        for low in range(2)
    ]

    def token_grads(inner):
        back = nt(d_wide[inner].reshape(256, MINE), wide_w[...])
        partial[inner] = back.astype(bf16).reshape(4, 2, ROWS, D)

    @pl.loop(0, 2)
    def _(low):
        token_grads(low * 2 + 1 - core)

    for low in range(2):
        c_swaps[low].start()

    @pl.loop(0, 4)
    def _(z):
        def part(inner):
            at = pl.ds(pl.multiple_of(inner * D + z * 320, 64), 320)
            return nn(kv[at], d_wide[inner].reshape(256, MINE))

        grads = sum(part(inner) for inner in range(4))
        for y in range(4):
            found = rows_of(grads, 20, [inner * GROUP + y * 20 for inner in range(4)])
            grad_chunks[z, y, :GROUP] = found.astype(bf16)
            grad_chunks[z, y, GROUP:] = rows


    for step_at in (1, 3, 2):
        for half, axis in enumerate("zy"):
            there = moved(place, axis, (place[axis] + step_at) % 4)
            remote(
                column_pieces(grad_chunks, half, there, "y" if half == 0 else "z"),
                first_in.at[half, step_at - 1],
                col_send.at[half, 0],
                col_recv.at[half, 0],
                device_at(there),
            ).start()

    @pl.loop(0, 2)
    def _(low):
        token_grads(low * 2 + core)

    for low in range(2):
        c_swaps[low].wait()
        summed[low] = (
            partial[low * 2 + core].astype(f32) + partial_in[low].astype(f32)
        ).astype(bf16)
    for step_at in (1, 3, 2):
        there = moved(place, "x", (place["x"] + step_at) % 4)
        for m in range(2):
            remote(
                summed.at[there["x"] % 2, m * 2 + there["x"] // 2],
                sum_in.at[step_at - 1, m],
                sum_send,
                sum_recv,
                device_at(there),
            ).start()
    for half in range(2):
        wait_bytes(first_in.at[half], col_recv.at[half, 0])
        own = column_pieces(grad_chunks, half, place, "y" if half == 0 else "z")
        for number in range(4):
            total = own[number].astype(f32)
            for source in range(3):
                total = total + first_in[half, source, number].astype(f32)
            first_sum[half, number] = total.astype(bf16)
    for step_at in (1, 3, 2):
        for half, axis in enumerate("yz"):
            there = moved(place, axis, (place[axis] + step_at) % 4)
            remote(
                first_sum.at[half, there[axis]],
                second_in.at[half, step_at - 1],
                col_send.at[half, 1],
                col_recv.at[half, 1],
                device_at(there),
            ).start()
    totals = []
    for half, axis in enumerate("yz"):
        wait_bytes(second_in.at[half], col_recv.at[half, 1])
        total = first_sum[half, place[axis]].astype(f32)
        for source in range(3):
            total = total + second_in[half, source].astype(f32)
        totals.append(total)
    total_y, total_z = totals
    joined[:, 0:256] = total_y.astype(bf16)
    joined[:, 256:512] = total_z.astype(bf16)
    shares[...] = nn(share[...], joined[...]).astype(bf16).reshape(8, ROWS, MINE)
    turn = place["x"] * 2 + core
    for there in ring_devices(place):
        remote(
            shares.at[ring_number(there)],
            shares_in.at[turn],
            share_send,
            share_recv,
            device_at(there),
        ).start()
    pltpu.make_async_copy(
        shares.at[ring_number(place)], shares_in.at[turn], share_recv
    ).start()
    two.add(2, two_out)
    two.finish()
    wait_bytes(sum_in, sum_recv)
    for m in range(2):
        total = summed[x_low, m * 2 + place["x"] // 2].astype(f32)
        for source in range(3):
            total = total + sum_in[source, m].astype(f32)
        values = tokens[m].astype(f32)
        upward = total.reshape(TOK, D) * vectors[0:1]
        input_grad[m] = (
            d_branch[m * TOK : (m + 1) * TOK].astype(f32)
            + norm_back(upward, values, inverse_rms(values))
        ).astype(bf16)
    wait_bytes(shares_in, share_recv)
    pieces_out[...] = shares_in[...]
    wait_cells(pack, send, even, 128)
    wait_ring(final, back_send, place)
    wait_bytes(sum_in, sum_send)
    for number in range(2):
        wait_bytes(first_in.at[number], col_send.at[number, 0])
        wait_bytes(second_in.at[number], col_send.at[number, 1])
    wait_bytes(shares.at[pl.ds(0, 7)], share_send)


def rear(*operands):
    dma = pltpu.SemaphoreType.DMA
    return pl.pallas_call(
        rear_kernel,
        out_shape=(
            jax.ShapeDtypeStruct((2, TOK, D), bf16),
            jax.ShapeDtypeStruct((8, ROWS, MINE), bf16),
            jax.ShapeDtypeStruct((ROWS, D), f32),
        ),
        in_specs=[HBM] * 3 + [VMEM, HBM] + [VMEM] * 7 + [HBM] * 3 + [VMEM] * 5,
        out_specs=(VMEM, VMEM, VMEM),
        scratch_shapes=[
            pltpu.VMEM((16 * B, LANES), bf16),
            pltpu.VMEM((4, B, 128), bf16),
            pltpu.VMEM((4, 128, B), f32),
            pltpu.VMEM((4, 2, 128, MINE), bf16),
            pltpu.VMEM((D, MINE), bf16),
            dma((6,)),
            pltpu.VMEM((4, B, 128), bf16),
            pltpu.VMEM((16, 128, B), bf16),
            pltpu.VMEM((4, 1, B), f32),
            pltpu.VMEM((4, 128, B), f32),
            pltpu.VMEM((B, LANES), f32),
            pltpu.VMEM((8, B, LANES), f32),
            pltpu.VMEM((8, B, LANES), bf16),
            pltpu.VMEM((8, B, LANES), bf16),
            pltpu.VMEM((4, B, LANES), bf16),
            pltpu.VMEM((4, B, LANES), bf16),
            pltpu.VMEM((4, B, LANES), bf16),
            pltpu.VMEM((4, 2, 128, MINE), bf16),
            pltpu.VMEM((OUT_WIDE, 128), bf16),
            pltpu.VMEM((D, 128), bf16),
            pltpu.VMEM((D, 128), bf16),
            pltpu.VMEM((3, 2, 2, ROWS, D), bf16),
            pltpu.VMEM((4, 4, CHUNK, MINE), bf16),
            pltpu.VMEM((2, 3, 4, CHUNK, 256), bf16),
            pltpu.VMEM((2, 3, CHUNK, 256), bf16),
            pltpu.VMEM((2, 4, CHUNK, 256), bf16),
            pltpu.VMEM((CHUNK, MINE), bf16),
            pltpu.VMEM((8, ROWS, MINE), bf16),
            pltpu.VMEM((8, ROWS, MINE), bf16),
            dma, dma, dma((8,)), dma((8,)), dma((4,)), dma((4,)), dma, dma,
            dma((2,)), dma((2,)), dma, dma, dma((2, 2)), dma((2, 2)), dma, dma,
        ]
        + scatter_scratch(),
        compiler_params=pltpu.CompilerParams(
            collective_id=1, has_side_effects=True, vmem_limit_bytes=63 * 2**20
        ),
        name="rear",
    )(
        *operands,
        jnp.asarray(SHARE, bf16),
    )


def on_device(
    inputs,
    segment_ids,
    norm1_gain,
    w_query,
    w_key,
    w_value,
    query_bias,
    value_bias,
    w_out,
    out_bias,
    norm2_gain,
    w_hidden,
    hidden_bias,
    w_proj,
    proj_bias,
    dim_scale,
    cotangent,
):
    blk = lax.axis_index("blk")
    head = lax.axis_index("head")
    at = (blk * 8 + head) * 10
    spread_heads = jnp.zeros((H, LANES), bf16)
    biases = jnp.concatenate([query_bias, jnp.zeros((HD - 10,), bf16), value_bias])
    spread_heads = lax.dynamic_update_slice(spread_heads, biases[None], (blk, HD + head * 10))
    natural = jnp.stack([norm1_gain, out_bias, norm2_gain, hidden_bias, proj_bias])
    natural = lax.dynamic_update_slice(jnp.zeros((5, 3 * MINE), bf16), natural, (0, at))
    columns = jnp.concatenate(
        [w.reshape(10, H, HD) for w in (w_key, w_query, w_value)]
        + [jnp.zeros((10, H, LANES - 3 * HD), bf16)],
        axis=2,
    )
    columns = columns.reshape(10, 8, MINE).transpose(1, 0, 2)
    pieces = jnp.concatenate(
        [
            columns,
            jnp.zeros((8, 6, MINE), bf16),
            spread_heads.reshape(8, 1, MINE),
            jnp.broadcast_to(natural.reshape(1, 15, MINE), (8, 15, MINE)),
        ],
        axis=1,
    )
    softplus_scale = LOG2E / math.sqrt(HD) * jax.nn.softplus(dim_scale)
    ones = jnp.ones((HD,), f32)
    scale_row = jnp.concatenate(
        [ones, softplus_scale, ones, jnp.zeros((LANES - 3 * HD,), f32)] * 2
    )
    scale_row = scale_row[None]

    (
        ring_normed, packed, wide_w, vectors, starts, kv, queries, out_t, log_norms, attended,
        out_w, hidden_w, proj_w,
    ) = front(
        inputs, pieces, w_out, w_hidden, w_proj, scale_row, segment_ids.reshape(2, 16, B)
    )
    out_b, gain_two, hidden_b, proj_b = [vectors[i] for i in range(1, 5)]

    tokens = inputs.reshape(2 * TOK, D).astype(f32)
    residual = tokens + nn(attended, out_w) + out_b
    inverse_two = inverse_rms(residual)
    normed_two = (residual * inverse_two * gain_two).astype(bf16)
    pre_act = nn(normed_two, hidden_w) + hidden_b
    gate = jax.nn.sigmoid(pre_act)
    activated = (pre_act * gate).astype(bf16)
    layer_out = (residual + nn(activated, proj_w) + proj_b).astype(bf16)

    upstream_low = cotangent.reshape(2 * TOK, D)
    upstream = upstream_low.astype(f32)
    d_pre = (nt(upstream_low, proj_w) * gate * (1.0 + pre_act * (1.0 - gate))).astype(bf16)
    d_normed_two = nt(d_pre, hidden_w)
    d_residual = upstream + norm_back(d_normed_two * gain_two, residual, inverse_two)
    d_branch = d_residual.astype(bf16)
    d_attended = nt(d_branch, out_w).astype(bf16)

    def total(values):
        return jnp.sum(values.astype(f32), axis=0)

    vector_grads = jnp.stack(
        [
            total(d_branch),
            total(d_normed_two * residual * inverse_two),
            total(d_pre),
            total(upstream),
        ]
    )
    vector_grads = jnp.pad(vector_grads, ((0, 0), (0, 3 * MINE - D))).reshape(12, MINE)
    vector_grads = jnp.pad(vector_grads, ((4, 0), (0, 0)))
    input_grad, shares, two = rear(
        d_attended, kv.reshape(16 * B, LANES), queries, starts, out_t, log_norms,
        attended, d_branch, normed_two, d_pre, activated, upstream_low,
        ring_normed.reshape(4 * D, 256), packed, wide_w, vector_grads, scale_row,
        inputs, vectors,
    )
    shares = shares.astype(f32)
    columns = shares[:, :10].transpose(1, 0, 2).reshape(10, H, LANES)
    d_key_w, d_query_w, d_value_w = [
        columns[:, :, i * HD : (i + 1) * HD].reshape(10, D) for i in range(3)
    ]
    by_head = shares[:, 16].reshape(H, LANES)
    d_query_bias, d_value_bias = [
        lax.dynamic_slice(by_head, (blk, i * HD + head * 10), (1, 10)).reshape(10) for i in (1, 2)
    ]
    summed = jnp.sum(shares[:, 17:], axis=0)
    scale_grad = summed[0, HD : 2 * HD] / softplus_scale
    scale_grad = scale_grad * (LOG2E / math.sqrt(HD)) * jax.nn.sigmoid(dim_scale)
    natural = lax.dynamic_slice(summed.reshape(5, 3 * MINE), (0, at), (5, 10))
    norm1_gain_grad = sum(
        jnp.sum(w.astype(f32) * grad, axis=1)
        for w, grad in ((w_query, d_query_w), (w_key, d_key_w), (w_value, d_value_w))
    ) / norm1_gain.astype(f32)
    return (
        layer_out.reshape(2, TOK, D),
        input_grad,
        norm1_gain_grad,
        d_query_w,
        d_key_w,
        d_value_w,
        d_query_bias,
        d_value_bias,
        two[0:10],
        natural[1],
        natural[2],
        two[10:20],
        natural[3],
        two[20:30],
        natural[4],
        scale_grad,
    )


def solution(mesh):
    rows = P(("blk", "head"), None)
    vec = P(("blk", "head"))
    tok = P(None, ("blk", "head"), None)
    in_specs = (
        tok, P(), vec, rows, rows, rows, vec, vec, rows, vec, vec, rows, vec, rows, vec, P(), tok
    )
    out_specs = (
        tok, tok, vec, rows, rows, rows, vec, vec, rows, vec, vec, rows, vec, rows, vec, P()
    )
    return jax.shard_map(
        on_device, mesh=mesh, in_specs=in_specs, out_specs=out_specs, check_vma=False
    )
```
